32 devices in a mesh: member: 2 (over y), lat: 4 (over z), lev: 2 (over x), sub: 2 (over core).
Axes of the slice: x: 2, y: 2, z: 4, core: 2. Of those that a mesh axis runs over, the one named last changes fastest.
Arguments:
- thickness: float32 [32, 64, 1152], P(('member', 'lev', 'sub'), 'lat'), parts along dimension 0, may hold values from 0.5 to 1.5
- wind_u: float32 [32, 64, 1152], P(('member', 'lev', 'sub'), 'lat'), parts along dimension 0, may hold values from -0.2 to 0.2
- wind_v: float32 [32, 64, 1152], P(('member', 'lev', 'sub'), 'lat'), parts along dimension 0, may hold values from -0.2 to 0.2
- tracers: float32 [8, 16, 64, 1152], P('member', ('lev', 'sub'), 'lat'), parts along dimension 0, may hold values from 0 to 1
- level_weights: float32 [16], replicated, may hold values from 0.3 to 3
- cutoff: int32 [64], P('lat'), may hold values from 1 to 576, as said below
Outputs:
- thickness_out: float32 [32, 64, 1152], P(('member', 'lev', 'sub'), 'lat'), parts along dimension 0
- wind_u_out: float32 [32, 64, 1152], P(('member', 'lev', 'sub'), 'lat'), parts along dimension 0
- wind_v_out: float32 [32, 64, 1152], P(('member', 'lev', 'sub'), 'lat'), parts along dimension 0
- tracers_out: float32 [8, 16, 64, 1152], P('member', ('lev', 'sub'), 'lat'), parts along dimension 0
The draws below stay inside these ranges and needn't reach their ends.
There are 2 independent parts, one for each index of `member`. The reference program is written for one: setup_inputs(seed, part) draws one part's arguments, and reference() takes and returns one part's arrays. A program takes and returns all parts, laid end to end along the dimension named above; an argument that names none is the same for every part. Nothing has to cross between parts.
Inputs may be any that keep to these rules, and one draw needn't show every extreme that they name: cutoff is 576 on every row 16 or more rows away from both poles; it is 1 on the two pole rows.
All inputs are finite; a program needn't handle non-finite values.
Results may differ from the reference program's by a relative error of at most 0.0003.
Values sent between devices are 32-bit elements; how exact they have to be, the bound alone decides.
No kernel may reach another device: no remote copies, remote signals or barrier semaphores. Data moves between devices by JAX's collectives and lax.ppermute only.
A program may use at most 64 MiB of HBM per device.

```python
import math
import jax
import jax.numpy as jnp
from jax import lax

NLON = 1152
NTRACER = 4
NLAT = 64
LEVELS = 16
POLAR = 16


def draw_cutoff(key, part):
    key = jax.random.fold_in(key, 11)
    row_ids = jnp.arange(NLAT, dtype=jnp.int32)
    distance = jnp.minimum(row_ids, NLAT - 1 - row_ids)
    nyquist = NLON // 2
    baseline = 1 + (nyquist - 1) * distance // POLAR
    jitter = jax.random.randint(key, (NLAT,), 0, max(nyquist // 8, 1)) * (distance > 0).astype(jnp.int32)
    polar_cut = jnp.minimum(baseline + jitter, nyquist - 1)
    return jnp.where(distance < POLAR, polar_cut, nyquist).astype(jnp.int32)


def steps_of(own_key, dims, cuts, low, high):
    loudness, own = 1.0, jax.random.fold_in(own_key, 6)
    for dim, parts in cuts:
        heights = jnp.exp(jax.random.uniform(jax.random.fold_in(own, dim), (parts,), jnp.float32, low / len(cuts), high / len(cuts)))
        loudness = loudness * jnp.repeat(heights, dims[dim] // parts).reshape([-1 if axis == dim else 1 for axis in range(len(dims))])
    return loudness


def setup_inputs(seed: int = 0, part: int = 0) -> dict:
    arg_keys = jax.random.split(jax.random.key(seed), 7)
    own_keys = jax.random.split(jax.random.fold_in(arg_keys[6], part), 7)
    thickness = jnp.clip(0.5 + 1.0 * jax.random.uniform(own_keys[0], (LEVELS, NLAT, NLON), jnp.float32) ** steps_of(own_keys[0], (LEVELS, NLAT, NLON), ((0, 4), (1, 4)), -0.2, 0.2), 0.5, 1.5)
    wind_u = jnp.clip(jax.random.uniform(own_keys[1], (LEVELS, NLAT, NLON), jnp.float32, -0.2, 0.2) * steps_of(own_keys[1], (LEVELS, NLAT, NLON), ((0, 4), (1, 4)), -0.4, 0.0), -0.2, 0.2)
    wind_v = jnp.clip(jax.random.uniform(own_keys[2], (LEVELS, NLAT, NLON), jnp.float32, -0.2, 0.2) * steps_of(own_keys[2], (LEVELS, NLAT, NLON), ((0, 4), (1, 4)), -0.4, 0.0), -0.2, 0.2)
    tracers = jnp.clip(1.0 * jax.random.uniform(own_keys[3], (NTRACER, LEVELS, NLAT, NLON), jnp.float32) ** steps_of(own_keys[3], (NTRACER, LEVELS, NLAT, NLON), ((1, 4), (2, 4)), -0.2, 0.2), 0.0, 1.0)
    level_weights = jnp.clip(jnp.exp(jax.random.uniform(arg_keys[4], (LEVELS,), jnp.float32, math.log(0.3), math.log(3.0))), 0.3, 3.0)
    cutoff = draw_cutoff(jax.random.fold_in(arg_keys[6], 71), part)
    return {"thickness": thickness, "wind_u": wind_u, "wind_v": wind_v, "tracers": tracers, "level_weights": level_weights, "cutoff": cutoff}


def face_weight(faces, lat_rows):
    inside = (faces > 0) & (faces < lat_rows)
    return jnp.where(inside, jnp.sin(faces.astype(jnp.float32) * (jnp.pi / lat_rows)), 0.0)


def mass_fluxes(thick_ext, u_mid, v_ext, first_row, lat_rows):
    n = u_mid.shape[1]
    row_ids = first_row + jnp.arange(n, dtype=jnp.int32)
    south_wt = face_weight(row_ids, lat_rows)
    north_wt = face_weight(row_ids + 1, lat_rows)
    center = jnp.sin((row_ids.astype(jnp.float32) + 0.5) * (jnp.pi / lat_rows))
    thick_mid = thick_ext[:, 1:-1]
    eastward = u_mid * jnp.where(u_mid > 0, thick_mid, jnp.roll(thick_mid, -1, axis=-1))
    v_north = v_ext[:, 1:-1]
    v_south = v_ext[:, :-2]
    north_flux = v_north * jnp.where(v_north > 0, thick_mid, thick_ext[:, 2:]) * north_wt[:, None]
    south_flux = v_south * jnp.where(v_south > 0, thick_ext[:, :-2], thick_mid) * south_wt[:, None]
    thick_new = thick_mid - (eastward - jnp.roll(eastward, 1, axis=-1)) - (north_flux - south_flux) / center[:, None]
    return thick_new, eastward, north_flux, south_flux, center


def tracer_step(tracer_ext, thick_mid, thick_new, eastward, north_flux, south_flux, v_ext, u_mid, center):
    tracer_mid = tracer_ext[:, :, 1:-1]
    v_north = v_ext[:, 1:-1]
    v_south = v_ext[:, :-2]
    tracer_east = eastward * jnp.where(u_mid > 0, tracer_mid, jnp.roll(tracer_mid, -1, axis=-1))
    tracer_north = north_flux * jnp.where(v_north > 0, tracer_mid, tracer_ext[:, :, 2:])
    tracer_south = south_flux * jnp.where(v_south > 0, tracer_ext[:, :, :-2], tracer_mid)
    changed = thick_mid * tracer_mid - (tracer_east - jnp.roll(tracer_east, 1, axis=-1))
    changed = changed - (tracer_north - tracer_south) / center[:, None]
    return changed / thick_new


def remap(thick_new, fields, weights):
    levels = thick_new.shape[0]
    column_mass = jnp.sum(thick_new, axis=0)
    fraction = weights / jnp.sum(weights)
    targets = column_mass[None] * jnp.cumsum(fraction)[:, None]
    source_low = jnp.cumsum(thick_new, axis=0) - thick_new

    def integrate(target_block):
        w = jnp.minimum(jnp.maximum(target_block[:, None, :] - source_low[None], 0.0), thick_new[None])
        return jnp.sum(fields[:, None] * w[None], axis=2)

    integral = lax.map(integrate, targets.reshape(levels // 4, 4, targets.shape[1]))
    integral = jnp.transpose(integral, (1, 0, 2, 3)).reshape(fields.shape[0], levels, targets.shape[1])
    integral_low = jnp.concatenate([jnp.zeros_like(integral[:, :1]), integral[:, :-1]], axis=1)
    target_thick = column_mass[None] * fraction[:, None]
    return jnp.concatenate([target_thick[None], (integral - integral_low) / target_thick[None]], axis=0)


def reference(thickness, wind_u, wind_v, tracers, level_weights, cutoff):
    lat_rows = thickness.shape[1]
    nyquist = thickness.shape[2]
    thick_ext = jnp.pad(thickness, ((0, 0), (1, 1), (0, 0)))
    v_ext = jnp.pad(wind_v, ((0, 0), (1, 1), (0, 0)))
    tracer_ext = jnp.pad(tracers, ((0, 0), (0, 0), (1, 1), (0, 0)))
    thick_new, eastward, north_flux, south_flux, center = mass_fluxes(thick_ext, wind_u, v_ext, 0, lat_rows)
    tracer_new = tracer_step(tracer_ext, thickness, thick_new, eastward, north_flux, south_flux, v_ext, wind_u, center)
    thick_next = jnp.concatenate([thick_new[:, 1:], jnp.zeros_like(thick_new[:, :1])], axis=1)
    row_ids = jnp.arange(lat_rows, dtype=jnp.int32)
    new_u = wind_u - 0.05 * (jnp.roll(thick_new, -1, axis=-1) - thick_new)
    new_v = (wind_v - 0.05 * (thick_next - thick_new)) * (row_ids < lat_rows - 1)[:, None]
    wave_ids = jnp.arange(nyquist, dtype=jnp.int32)
    wave_num = jnp.minimum(wave_ids, nyquist - wave_ids)
    kept_modes = wave_num[None, :] <= cutoff[:, None]
    wind_pair = jnp.stack([new_u, new_v])
    spectrum = jnp.fft.fft(wind_pair, axis=-1)
    wind_pair = jnp.real(jnp.fft.ifft(spectrum * kept_modes, axis=-1)).astype(thickness.dtype)
    stacked = jnp.concatenate([thick_new[None], wind_pair, tracer_new], axis=0)
    by_rows = jnp.moveaxis(stacked, 2, 0)
    remapped = lax.map(lambda one_row: remap(one_row[0], one_row[1:], level_weights), by_rows)
    remapped = jnp.moveaxis(remapped, 0, 2)
    return remapped[0], remapped[1], remapped[2], remapped[3:]
```

```python
import functools

import jax
import jax.numpy as jnp
import ml_dtypes
import numpy as np
from jax import lax
from jax.experimental import pallas as pl
from jax.experimental.pallas import tpu as pltpu
from jax.sharding import PartitionSpec as P

LANES = 128
VMEM = pl.BlockSpec(memory_space=pltpu.VMEM)
SMEM = pl.BlockSpec(memory_space=pltpu.SMEM)


def params():
    return pltpu.CompilerParams(vmem_limit_bytes=48 * 1024 * 1024)


def cost(flops, bytes_accessed):
    return pl.CostEstimate(flops=int(flops), bytes_accessed=int(bytes_accessed), transcendentals=0)


def geometry_table(lat_rows, band_rows):
    bands = lat_rows // band_rows
    table = np.zeros((bands, band_rows + 8, LANES), np.float32)
    for band in range(bands):
        for j in range(band_rows + 1):
            row = band * band_rows + j
            south = np.sin(row * np.pi / lat_rows) if 0 < row < lat_rows else 0.0
            north = np.sin((row + 1) * np.pi / lat_rows) if row + 1 < lat_rows else 0.0
            table[band, j, 0] = south
            table[band, j, 1] = north
            table[band, j, 2] = 1.0 / np.sin((row + 0.5) * np.pi / lat_rows)
    return table


def east_of(value):
    return pltpu.roll(value, value.shape[1] - 1, 1)


def west_of(value):
    return pltpu.roll(value, 1, 1)


def row_ids(shape):
    return lax.broadcasted_iota(jnp.int32, shape, 0)


def north_of(value, beyond):
    rows = value.shape[0]
    return jnp.where(row_ids(value.shape) == rows - 1, beyond, pltpu.roll(value, rows - 1, 0))


def south_of(value, beyond):
    return jnp.where(row_ids(value.shape) == 0, beyond, pltpu.roll(value, 1, 0))


def fluxes(geo_ref, thick, u, v, thick_s, v_s, thick_n):
    rows = thick.shape[0]
    east = u * jnp.where(u > 0, thick, east_of(thick))
    north = v * jnp.where(v > 0, thick, north_of(thick, thick_n)) * geo_ref[0:rows, 1:2]
    below = v_s * jnp.where(v_s > 0, thick_s, thick[0:1]) * geo_ref[0:1, 0:1]
    return east, north, below


def thickness_kernel(lat_rows, geo_ref, first_ref, thick_ref, u_ref, v_ref, up_ref, down_ref, new_ref, wind_ref, sum_ref):
    rows = thick_ref.shape[1]
    thick, u, v = thick_ref[0], u_ref[0], v_ref[0]
    thick_s, v_s = up_ref[0, 0], up_ref[1, 0]
    thick_n, thick_nn, u_n, v_n = (down_ref[i, 0] for i in range(4))
    east, north, below = fluxes(geo_ref, thick, u, v, thick_s, v_s, thick_n)
    inverse = geo_ref[0:rows, 2:3]
    new = thick - (east - west_of(east)) - (north - south_of(north, below)) * inverse
    east_n = u_n * jnp.where(u_n > 0, thick_n, east_of(thick_n))
    north_n = v_n * jnp.where(v_n > 0, thick_n, thick_nn) * geo_ref[rows : rows + 1, 1:2]
    new_n = (
        thick_n
        - (east_n - west_of(east_n))
        - (north_n - north[rows - 1 : rows]) * geo_ref[rows : rows + 1, 2:3]
    )
    new_ref[0] = new
    wind_ref[0, 0] = u - 0.05 * (east_of(new) - new)
    inside = first_ref[0] + row_ids(new.shape) < lat_rows - 1
    wind_ref[1, 0] = jnp.where(inside, v - 0.05 * (north_of(new, new_n) - new), 0.0)

    @pl.when(pl.program_id(0) == 0)
    def _():
        sum_ref[...] = new

    @pl.when(pl.program_id(0) > 0)
    def _():
        sum_ref[...] += new


def thickness_step(geo, first, lat_rows, thickness, wind_u, wind_v, up, down):
    L, R, N = thickness.shape
    level = pl.BlockSpec((1, R, N), lambda k: (k, 0, 0))
    unit = 4 * R * N
    return pl.pallas_call(
        functools.partial(thickness_kernel, lat_rows),
        grid=(L,),
        in_specs=[
            pl.BlockSpec(geo.shape, lambda k: (0, 0)),
            SMEM,
            level,
            level,
            level,
            pl.BlockSpec((2, 1, 1, N), lambda k: (0, k, 0, 0)),
            pl.BlockSpec((4, 1, 1, N), lambda k: (0, k, 0, 0)),
        ],
        out_specs=[
            level,
            pl.BlockSpec((2, 1, R, N), lambda k: (0, k, 0, 0)),
            pl.BlockSpec((R, N), lambda k: (0, 0)),
        ],
        out_shape=[
            jax.ShapeDtypeStruct((L, R, N), jnp.float32),
            jax.ShapeDtypeStruct((2, L, R, N), jnp.float32),
            jax.ShapeDtypeStruct((R, N), jnp.float32),
        ],
        compiler_params=params(),
        cost_estimate=cost(40 * L * R * N, 7 * L * unit),
        name="thickness_step",
    )(geo, first, thickness, wind_u, wind_v, up, down)


def tracer_kernel(geo_ref, thick_ref, u_ref, v_ref, new_ref, up_ref, down_ref, tracer_ref, up_t_ref, down_t_ref, *out_refs):
    rows = thick_ref.shape[1]
    thick, u, v = thick_ref[0], u_ref[0], v_ref[0]
    east, north, below = fluxes(geo_ref, thick, u, v, up_ref[0, 0], up_ref[1, 0], down_ref[0, 0])
    v_s = up_ref[1, 0]
    inverse = geo_ref[0:rows, 2:3]
    scale = 1.0 / new_ref[0]
    per_out = out_refs[0].shape[0]
    for c in range(tracer_ref.shape[0]):
        q = tracer_ref[c, 0]
        t_east = east * jnp.where(u > 0, q, east_of(q))
        t_north = north * jnp.where(v > 0, q, north_of(q, down_t_ref[c, 0]))
        t_below = below * jnp.where(v_s > 0, up_t_ref[c, 0], q[0:1])
        change = thick * q - (t_east - west_of(t_east))
        change = change - (t_north - south_of(t_north, t_below)) * inverse
        out_refs[c // per_out][c % per_out, 0] = change * scale


def tracer_step(geo, thickness, wind_u, wind_v, thick_new, up, down, tracers, up_t, down_t, parts):
    L, R, N = thickness.shape
    T = tracers.shape[0]
    level = pl.BlockSpec((1, R, N), lambda k: (k, 0, 0))
    edge = lambda n: pl.BlockSpec((n, 1, 1, N), lambda k: (0, k, 0, 0))
    unit = 4 * R * N
    return pl.pallas_call(
        tracer_kernel,
        grid=(L,),
        in_specs=[
            pl.BlockSpec(geo.shape, lambda k: (0, 0)),
            level,
            level,
            level,
            level,
            edge(2),
            edge(1),
            pl.BlockSpec((T, 1, R, N), lambda k: (0, k, 0, 0)),
            edge(T),
            edge(T),
        ],
        out_specs=[pl.BlockSpec((T // parts, 1, R, N), lambda k: (0, k, 0, 0))] * parts,
        out_shape=[jax.ShapeDtypeStruct((T // parts, L, R, N), jnp.float32)] * parts,
        compiler_params=params(),
        cost_estimate=cost(90 * L * R * N, (2 * T + 4) * L * unit),
        name="tracer_step",
    )(geo, thickness, wind_u, wind_v, thick_new, up, down, tracers, up_t, down_t)


def filter_tables(N):
    A = N // LANES
    b = np.arange(LANES)[:, None]
    p = np.arange(LANES)[None, :]
    tables = []
    for q in range(A // 2 + 1):
        angle = 2.0 * np.pi * ((b * (A * p + q)) % N) / N
        c, s = np.cos(angle), np.sin(angle)
        tables.append(np.block([[c, -s], [s, c]]))
    table = np.stack(tables)
    high = table.astype(np.float32).astype(ml_dtypes.bfloat16)
    low = (table - high.astype(np.float64)).astype(np.float32).astype(ml_dtypes.bfloat16)
    return high, low


def split(value):
    high = value.astype(jnp.bfloat16)
    return high, (value - high.astype(jnp.float32)).astype(jnp.bfloat16)


def product(value, high, low, transposed):
    dims = (((1,), (1 if transposed else 0,)), ((), ()))
    dot = lambda x, y: lax.dot_general(x, y, dims, preferred_element_type=jnp.float32)
    v_high, v_low = split(value)
    return dot(v_high, high) + (dot(v_high, low) + dot(v_low, high))


def filter_kernel(N, wind_ref, cutoff_ref, high_ref, low_ref, out_ref):
    A = N // LANES
    half = A // 2
    F, L, R, _ = wind_ref.shape
    rows = F * L * R
    piece = lambda a: wind_ref[:, :, :, a * LANES : (a + 1) * LANES].reshape(rows, LANES)
    x = [piece(a) for a in range(A)]
    even = [x[a] + x[A - a] for a in range(1, half + 1)]
    odd = [x[a] - x[A - a] for a in range(1, half + 1)]
    angle = lambda q, a: 2.0 * np.pi * ((q * a) % A) / A
    cutoff = cutoff_ref[...]
    p = lax.broadcasted_iota(jnp.int32, (R, LANES), 1)
    real, imag = [], []
    for q in range(half + 1):
        re = x[0]
        for a in range(1, half + 1):
            re = re + (even[a - 1] if q == 0 else float(np.cos(angle(q, a))) * even[a - 1])
        if q == 0:
            spectrum = product(re, high_ref[0, 0:LANES], low_ref[0, 0:LANES], False)
        else:
            im = -float(np.sin(angle(q, 1))) * odd[0]
            for a in range(2, half + 1):
                im = im - float(np.sin(angle(q, a))) * odd[a - 1]
            spectrum = product(jnp.concatenate([re, im], axis=1), high_ref[q], low_ref[q], False)
        mode = A * p + q
        factor = 1.0 / N if q == 0 else 2.0 / N
        kept = jnp.where(jnp.minimum(mode, N - mode) <= cutoff, factor, 0.0)
        kept = jnp.concatenate([kept, kept], axis=1)
        spectrum = (spectrum.reshape(F * L, R, 2 * LANES) * kept[None]).reshape(rows, 2 * LANES)
        if q == 0:
            real.append(product(spectrum, high_ref[0, 0:LANES], low_ref[0, 0:LANES], True))
            imag.append(None)
        else:
            back = product(spectrum, high_ref[q], low_ref[q], True)
            real.append(back[:, :LANES])
            imag.append(back[:, LANES:])

    def store(a, value):
        out_ref[:, :, :, a * LANES : (a + 1) * LANES] = value.reshape(F, L, R, LANES)

    first = real[0]
    for q in range(1, half + 1):
        first = first + real[q]
    store(0, first)
    for a in range(1, half + 1):
        even_part = real[0]
        odd_part = None
        for q in range(1, half + 1):
            even_part = even_part + float(np.cos(angle(q, a))) * real[q]
            term = float(np.sin(angle(q, a))) * imag[q]
            odd_part = term if odd_part is None else odd_part + term
        store(a, even_part - odd_part)
        store(A - a, even_part + odd_part)


def fourier_filter(wind, cutoff):
    F, L, R, N = wind.shape
    high, low = filter_tables(N)
    macs = F * L * R * high.size
    return pl.pallas_call(
        functools.partial(filter_kernel, N),
        in_specs=[VMEM] * 4,
        out_specs=VMEM,
        out_shape=jax.ShapeDtypeStruct(wind.shape, jnp.float32),
        compiler_params=params(),
        cost_estimate=cost(2 * 6 * macs, 8 * F * L * R * N + 4 * high.size),
        name="fourier_filter",
    )(wind, jnp.broadcast_to(cutoff[:, None], (R, LANES)), jnp.asarray(high), jnp.asarray(low))


def remap_kernel(lev_count, sub_count, with_thickness, place_ref, cum_ref, frac_ref, inv_ref, *refs):
    S, C = sub_count, lev_count
    thick_refs, refs = refs[:S], refs[S:]
    field_refs, refs = refs[:S], refs[S:]
    other_refs, refs = refs[: (C - 1) * S], refs[(C - 1) * S :]
    out_refs = refs[:C]
    F, L, R, N = field_refs[0].shape
    lev, sub = place_ref[0], place_ref[1]
    spot = [lax.rem(sub + S - t, S) for t in range(S)]

    def tile(rows, columns):
        thick = [[thick_refs[t][m, rows, columns] for m in range(L)] for t in range(S)]
        group = [functools.reduce(jnp.add, levels) for levels in thick]
        mass = functools.reduce(jnp.add, group)
        base = jnp.zeros_like(mass)
        for s in range(1, C):
            other = other_refs[(s - 1) * S][rows, columns]
            for t in range(1, S):
                other = other + other_refs[(s - 1) * S + t][rows, columns]
            mass = mass + other
            base = base + jnp.where(lev >= s, other, 0.0)
        sources = []
        for t in range(S):
            low = base
            for other in range(S):
                if other != t:
                    low = low + jnp.where(spot[other] < spot[t], group[other], 0.0)
            for m in range(L):
                sources.append((t, m, low, thick[t][m]))
                low = low + thick[t][m]
        inverse = 1.0 / mass
        for s in range(C):
            first = (lax.rem(lev + s, C) * S + sub) * L

            def covered(i):
                top = mass * cum_ref[first + i]
                return [jnp.minimum(jnp.maximum(top - low, 0.0), h) for _, _, low, h in sources]

            below = covered(0)
            for i in range(L):
                upto = covered(i + 1)
                part = [a - b for a, b in zip(upto, below)]
                below = upto
                scale = inverse * inv_ref[first + i]
                for f in range(F):
                    total = None
                    for (t, m, _, _), w in zip(sources, part):
                        term = field_refs[t][f, m, rows, columns] * w
                        total = term if total is None else total + term
                    out_refs[s][f, i, rows, columns] = total * scale
                if with_thickness and s == 0:
                    refs[C][i, rows, columns] = mass * frac_ref[first + i]

    for r in range(0, R, 8):

        def body(c, carry):
            tile(slice(r, r + 8), pl.ds(pl.multiple_of(c * LANES, LANES), LANES))
            return carry

        lax.fori_loop(0, N // LANES, body, 0)


def remap_parts(counts, place, cum, frac, inv, thick, fields, others, with_thickness):
    C, S = counts
    F, L, R, N = fields[0].shape
    shape = jax.ShapeDtypeStruct((F, L, R, N), jnp.float32)
    out_shape = [shape] * C
    if with_thickness:
        out_shape = out_shape + [jax.ShapeDtypeStruct((L, R, N), jnp.float32)]
    return pl.pallas_call(
        functools.partial(remap_kernel, C, S, with_thickness),
        in_specs=[SMEM] * 4 + [VMEM] * (2 * S + len(others)),
        out_specs=[VMEM] * len(out_shape),
        out_shape=out_shape,
        compiler_params=params(),
        cost_estimate=cost(C * S * L * L * R * N * (5 + 2 * F), 4 * R * N * L * (F + 1) * (S + C)),
        name="remap_parts",
    )(place, cum, frac, inv, *thick, *fields, *others)


def add_kernel(groups, *refs):
    outs = refs[-1]
    at = 0
    each = len(refs[:-1]) // groups
    for g in range(groups):
        total = refs[g * each][...]
        for i in range(1, each):
            total = total + refs[g * each + i][...]
        n = total.shape[0]
        outs[at : at + n] = total
        at += n


def add_parts(groups):
    flat = [a for group in groups for a in group]
    total = sum(group[0].shape[0] for group in groups)
    L, R, N = flat[0].shape[1:]
    return pl.pallas_call(
        functools.partial(add_kernel, len(groups)),
        in_specs=[VMEM] * len(flat),
        out_specs=VMEM,
        out_shape=jax.ShapeDtypeStruct((total, L, R, N), jnp.float32),
        compiler_params=params(),
        cost_estimate=cost(total * L * R * N, 4 * total * L * R * N * 3),
        name="add_parts",
    )(*flat)


def shifted(value, lev_count, sub_count, s, t):
    if t == 0:
        return lax.ppermute(value, "lev", [(i, (i + s) % lev_count) for i in range(lev_count)])
    if s == 0:
        return lax.ppermute(value, "sub", [(i, (i + t) % sub_count) for i in range(sub_count)])
    pairs = [
        (i * sub_count + j, (i + s) % lev_count * sub_count + (j + t) % sub_count)
        for i in range(lev_count)
        for j in range(sub_count)
    ]
    return lax.ppermute(value, ("lev", "sub"), pairs)


def per_device(thickness, wind_u, wind_v, tracers, level_weights, cutoff):
    L, R, N = thickness.shape
    lat_count = lax.axis_size("lat")
    C, S = lax.axis_size("lev"), lax.axis_size("sub")
    lat_rows = R * lat_count
    send = functools.partial(shifted, lev_count=C, sub_count=S)

    last = jnp.concatenate([thickness[None, :, R - 1 :], wind_v[None, :, R - 1 :], tracers[:, :, R - 1 :]], axis=0)
    leading = jnp.concatenate(
        [
            thickness[None, :, 0:1],
            thickness[None, :, 1:2],
            wind_u[None, :, 0:1],
            wind_v[None, :, 0:1],
            tracers[:, :, 0:1],
        ],
        axis=0,
    )
    northward = [(i, i + 1) for i in range(lat_count - 1)]
    up = lax.ppermute(last, "lat", northward)
    down = lax.ppermute(leading, "lat", [(j, i) for i, j in northward])

    band = lax.axis_index("lat")
    geo = lax.dynamic_index_in_dim(jnp.asarray(geometry_table(lat_rows, R)), band, 0, keepdims=False)
    first = (band * R).astype(jnp.int32).reshape(1)
    place = jnp.stack([lax.axis_index("lev"), lax.axis_index("sub")]).astype(jnp.int32)
    levels = level_weights.shape[0]
    fraction = level_weights / jnp.sum(level_weights)
    lower = np.tril(np.ones((levels + 1, levels), np.float32), -1)
    cum = jnp.sum(jnp.asarray(lower) * fraction[None, :], axis=1)
    inv = 1.0 / fraction

    up_h, up_t = up[:2], up[2:]
    down_h, down_t = down[:4], down[4:]
    thick_new, wind, own_sum = thickness_step(geo, first, lat_rows, thickness, wind_u, wind_v, up_h, down_h)
    others = [send(own_sum, s=s, t=t) for s in range(1, C) for t in range(S)]
    thick = [thick_new] + [send(thick_new, s=0, t=t) for t in range(1, S)]
    parts = 2
    tracer_new = tracer_step(
        geo, thickness, wind_u, wind_v, thick_new, up_h, down_h, tracers, up_t, down_t, parts
    )
    filtered = fourier_filter(wind, cutoff)
    results = []
    thickness_out = None
    for index, own in enumerate(list(tracer_new) + [filtered]):
        fields = [own] + [send(own, s=0, t=t) for t in range(1, S)]
        with_thickness = index == 1
        out = remap_parts((C, S), place, cum, fraction, inv, thick, fields, others, with_thickness)
        if with_thickness:
            thickness_out = out[C]
        results.append([out[0]] + [send(out[s], s=s, t=0) for s in range(1, C)])
    tracers_out = add_parts(results[:parts])
    winds = functools.reduce(jnp.add, results[parts])
    return thickness_out, winds[0], winds[1], tracers_out


def solution(mesh):
    placed = (
        P(("member", "lev", "sub"), "lat", None),
        P(("member", "lev", "sub"), "lat", None),
        P(("member", "lev", "sub"), "lat", None),
        P("member", ("lev", "sub"), "lat", None),
        P(),
        P("lat"),
    )
    return jax.shard_map(
        per_device,
        mesh=mesh,
        in_specs=placed,
        out_specs=(
            P(("member", "lev", "sub"), "lat", None),
            P(("member", "lev", "sub"), "lat", None),
            P(("member", "lev", "sub"), "lat", None),
            P("member", ("lev", "sub"), "lat", None),
        ),
        check_vma=False,
    )
```

```python
import functools

import jax
import jax.numpy as jnp
import ml_dtypes
import numpy as np
from jax import lax
from jax.experimental import pallas as pl
from jax.experimental.pallas import tpu as pltpu
from jax.sharding import PartitionSpec as P

LANES = 128
VMEM = pl.BlockSpec(memory_space=pltpu.VMEM)
SMEM = pl.BlockSpec(memory_space=pltpu.SMEM)


def params():
    return pltpu.CompilerParams(vmem_limit_bytes=48 * 1024 * 1024)


def cost(flops, bytes_accessed):
    return pl.CostEstimate(flops=int(flops), bytes_accessed=int(bytes_accessed), transcendentals=0)


def geometry_table(lat_rows, band_rows):
    bands = lat_rows // band_rows
    table = np.zeros((bands, band_rows + 8, LANES), np.float32)
    for band in range(bands):
        for j in range(band_rows + 1):
            row = band * band_rows + j
            south = np.sin(row * np.pi / lat_rows) if 0 < row < lat_rows else 0.0
            north = np.sin((row + 1) * np.pi / lat_rows) if row + 1 < lat_rows else 0.0
            table[band, j, 0] = south
            table[band, j, 1] = north
            table[band, j, 2] = 1.0 / np.sin((row + 0.5) * np.pi / lat_rows)
    return table


def east_of(value):
    return pltpu.roll(value, value.shape[1] - 1, 1)


def west_of(value):
    return pltpu.roll(value, 1, 1)


def row_ids(shape):
    return lax.broadcasted_iota(jnp.int32, shape, 0)


def north_of(value, beyond):
    rows = value.shape[0]
    return jnp.where(row_ids(value.shape) == rows - 1, beyond, pltpu.roll(value, rows - 1, 0))


def south_of(value, beyond):
    return jnp.where(row_ids(value.shape) == 0, beyond, pltpu.roll(value, 1, 0))


def fluxes(geo, thick, u, v, thick_s, v_s, thick_n):
    rows = thick.shape[0]
    east = u * jnp.where(u > 0, thick, east_of(thick))
    north = v * jnp.where(v > 0, thick, north_of(thick, thick_n)) * geo[0:rows, 1:2]
    below = v_s * jnp.where(v_s > 0, thick_s, thick[0:1]) * geo[0:1, 0:1]
    return east, north, below


def edge_kernel(thick_top, v_top, tracer_top, thick_low, u_low, v_low, tracer_low, last_ref, leading_ref):
    T = tracer_top.shape[0]
    rows = thick_top.shape[1]
    last_ref[0] = thick_top[:, rows - 1 : rows]
    last_ref[1] = v_top[:, rows - 1 : rows]
    last_ref[2 : 2 + T] = tracer_top[:, :, rows - 1 : rows]
    leading_ref[0] = thick_low[:, 0:1]
    leading_ref[1] = thick_low[:, 1:2]
    leading_ref[2] = u_low[:, 0:1]
    leading_ref[3] = v_low[:, 0:1]
    leading_ref[4 : 4 + T] = tracer_low[:, :, 0:1]


def edge_rows(thickness, wind_u, wind_v, tracers):
    L, R, N = thickness.shape
    T = tracers.shape[0]
    block = lambda at: pl.BlockSpec((L, 8, N), lambda i: (0, at, 0))
    blocks = lambda at: pl.BlockSpec((T, L, 8, N), lambda i: (0, 0, at, 0))
    top = R // 8 - 1
    whole = lambda n: pl.BlockSpec((n, L, 1, N), lambda i: (0, 0, 0, 0))
    return pl.pallas_call(
        edge_kernel,
        grid=(1,),
        in_specs=[block(top), block(top), blocks(top), block(0), block(0), block(0), blocks(0)],
        out_specs=[whole(2 + T), whole(4 + T)],
        out_shape=[
            jax.ShapeDtypeStruct((2 + T, L, 1, N), jnp.float32),
            jax.ShapeDtypeStruct((4 + T, L, 1, N), jnp.float32),
        ],
        compiler_params=params(),
        cost_estimate=cost(0, 4 * L * N * 8 * (5 + 2 * T)),
        name="edge_rows",
    )(thickness, wind_v, tracers, thickness, wind_u, wind_v, tracers)


def thickness_kernel(lat_rows, band_ref, table_ref, thick_ref, u_ref, v_ref, up_ref, down_ref, new_ref, wind_ref, sum_ref):
    rows = thick_ref.shape[1]
    geo = table_ref[band_ref[0]]
    thick, u, v = thick_ref[0], u_ref[0], v_ref[0]
    thick_s, v_s = up_ref[0, 0], up_ref[1, 0]
    thick_n, thick_nn, u_n, v_n = (down_ref[i, 0] for i in range(4))
    east, north, below = fluxes(geo, thick, u, v, thick_s, v_s, thick_n)
    inverse = geo[0:rows, 2:3]
    new = thick - (east - west_of(east)) - (north - south_of(north, below)) * inverse
    east_n = u_n * jnp.where(u_n > 0, thick_n, east_of(thick_n))
    north_n = v_n * jnp.where(v_n > 0, thick_n, thick_nn) * geo[rows : rows + 1, 1:2]
    new_n = (
        thick_n
        - (east_n - west_of(east_n))
        - (north_n - north[rows - 1 : rows]) * geo[rows : rows + 1, 2:3]
    )
    new_ref[0] = new
    wind_ref[0, 0] = u - 0.05 * (east_of(new) - new)
    inside = band_ref[0] * rows + row_ids(new.shape) < lat_rows - 1
    wind_ref[1, 0] = jnp.where(inside, v - 0.05 * (north_of(new, new_n) - new), 0.0)

    @pl.when(pl.program_id(0) == 0)
    def _():
        sum_ref[...] = new

    @pl.when(pl.program_id(0) > 0)
    def _():
        sum_ref[...] += new


def thickness_step(band, table, lat_rows, thickness, wind_u, wind_v, up, down):
    L, R, N = thickness.shape
    level = pl.BlockSpec((1, R, N), lambda k: (k, 0, 0))
    unit = 4 * R * N
    return pl.pallas_call(
        functools.partial(thickness_kernel, lat_rows),
        grid=(L,),
        in_specs=[
            SMEM,
            pl.BlockSpec(table.shape, lambda k: (0, 0, 0)),
            level,
            level,
            level,
            pl.BlockSpec((2, 1, 1, N), lambda k: (0, k, 0, 0)),
            pl.BlockSpec((4, 1, 1, N), lambda k: (0, k, 0, 0)),
        ],
        out_specs=[
            level,
            pl.BlockSpec((2, 1, R, N), lambda k: (0, k, 0, 0)),
            pl.BlockSpec((R, N), lambda k: (0, 0)),
        ],
        out_shape=[
            jax.ShapeDtypeStruct((L, R, N), jnp.float32),
            jax.ShapeDtypeStruct((2, L, R, N), jnp.float32),
            jax.ShapeDtypeStruct((R, N), jnp.float32),
        ],
        compiler_params=params(),
        cost_estimate=cost(40 * L * R * N, 7 * L * unit),
        name="thickness_step",
    )(band, table, thickness, wind_u, wind_v, up, down)


def tracer_kernel(band_ref, table_ref, thick_ref, u_ref, v_ref, new_ref, up_ref, down_ref, tracer_ref, up_t_ref, down_t_ref, out_ref):
    rows = thick_ref.shape[1]
    geo = table_ref[band_ref[0]]
    thick, u, v = thick_ref[0], u_ref[0], v_ref[0]
    v_s = up_ref[1, 0]
    east, north, below = fluxes(geo, thick, u, v, up_ref[0, 0], v_s, down_ref[0, 0])
    inverse = geo[0:rows, 2:3]
    scale = 1.0 / new_ref[0]
    count = tracer_ref.shape[0]
    extra = out_ref.shape[0] - count
    if extra:
        out_ref[0, 0] = new_ref[0]
    for c in range(count):
        q = tracer_ref[c, 0]
        t_east = east * jnp.where(u > 0, q, east_of(q))
        t_north = north * jnp.where(v > 0, q, north_of(q, down_t_ref[c, 0]))
        t_below = below * jnp.where(v_s > 0, up_t_ref[c, 0], q[0:1])
        change = thick * q - (t_east - west_of(t_east))
        change = change - (t_north - south_of(t_north, t_below)) * inverse
        out_ref[extra + c, 0] = change * scale


def tracer_step(band, table, thickness, wind_u, wind_v, thick_new, up, down, tracers, begin, count, with_thickness):
    L, R, N = thickness.shape
    level = pl.BlockSpec((1, R, N), lambda k: (k, 0, 0))
    edge = lambda n: pl.BlockSpec((n, 1, 1, N), lambda k: (0, k, 0, 0))
    some = lambda at: pl.BlockSpec(
        (pl.Element(count), pl.Element(1), pl.Element(1), pl.Element(N)), lambda k: (at, k, 0, 0)
    )
    total = count + (1 if with_thickness else 0)
    unit = 4 * R * N
    return pl.pallas_call(
        tracer_kernel,
        grid=(L,),
        in_specs=[
            SMEM,
            pl.BlockSpec(table.shape, lambda k: (0, 0, 0)),
            level,
            level,
            level,
            level,
            edge(2),
            edge(1),
            pl.BlockSpec(
                (pl.Element(count), pl.Element(1), pl.Element(R), pl.Element(N)), lambda k: (begin, k, 0, 0)
            ),
            some(2 + begin),
            some(4 + begin),
        ],
        out_specs=pl.BlockSpec((total, 1, R, N), lambda k: (0, k, 0, 0)),
        out_shape=jax.ShapeDtypeStruct((total, L, R, N), jnp.float32),
        compiler_params=params(),
        cost_estimate=cost(30 * (count + 1) * L * R * N, (2 * count + 5) * L * unit),
        name="tracer_step",
    )(band, table, thickness, wind_u, wind_v, thick_new, up, down, tracers, up, down)


def filter_tables(N):
    A = N // LANES
    b = np.arange(LANES)[:, None]
    p = np.arange(LANES)[None, :]
    tables = []
    for q in range(A // 2 + 1):
        angle = 2.0 * np.pi * ((b * (A * p + q)) % N) / N
        c, s = np.cos(angle), np.sin(angle)
        tables.append(np.block([[c, -s], [s, c]]))
    table = np.stack(tables)
    high = table.astype(np.float32).astype(ml_dtypes.bfloat16)
    low = (table - high.astype(np.float64)).astype(np.float32).astype(ml_dtypes.bfloat16)
    return high, low


def split(value):
    high = value.astype(jnp.bfloat16)
    return high, (value - high.astype(jnp.float32)).astype(jnp.bfloat16)


def product(value, high, low, transposed):
    dims = (((1,), (1 if transposed else 0,)), ((), ()))
    dot = lambda x, y: lax.dot_general(x, y, dims, preferred_element_type=jnp.float32)
    v_high, v_low = split(value)
    return dot(v_high, high) + (dot(v_high, low) + dot(v_low, high))


def filter_kernel(N, wind_ref, cutoff_ref, high_ref, low_ref, out_ref):
    A = N // LANES
    half = A // 2
    F, L, R, _ = wind_ref.shape
    rows = F * L * R
    piece = lambda a: wind_ref[:, :, :, a * LANES : (a + 1) * LANES].reshape(rows, LANES)
    x = [piece(a) for a in range(A)]
    even = [x[a] + x[A - a] for a in range(1, half + 1)]
    odd = [x[a] - x[A - a] for a in range(1, half + 1)]
    angle = lambda q, a: 2.0 * np.pi * ((q * a) % A) / A
    cutoff = cutoff_ref[...]
    p = lax.broadcasted_iota(jnp.int32, (R, LANES), 1)
    real, imag = [], []
    for q in range(half + 1):
        re = x[0]
        for a in range(1, half + 1):
            re = re + (even[a - 1] if q == 0 else float(np.cos(angle(q, a))) * even[a - 1])
        if q == 0:
            spectrum = product(re, high_ref[0, 0:LANES], low_ref[0, 0:LANES], False)
        else:
            im = -float(np.sin(angle(q, 1))) * odd[0]
            for a in range(2, half + 1):
                im = im - float(np.sin(angle(q, a))) * odd[a - 1]
            spectrum = product(jnp.concatenate([re, im], axis=1), high_ref[q], low_ref[q], False)
        mode = A * p + q
        factor = 1.0 / N if q == 0 else 2.0 / N
        kept = jnp.where(jnp.minimum(mode, N - mode) <= cutoff, factor, 0.0)
        kept = jnp.concatenate([kept, kept], axis=1)
        spectrum = (spectrum.reshape(F * L, R, 2 * LANES) * kept[None]).reshape(rows, 2 * LANES)
        if q == 0:
            real.append(product(spectrum, high_ref[0, 0:LANES], low_ref[0, 0:LANES], True))
            imag.append(None)
        else:
            back = product(spectrum, high_ref[q], low_ref[q], True)
            real.append(back[:, :LANES])
            imag.append(back[:, LANES:])

    def store(a, value):
        out_ref[:, :, :, a * LANES : (a + 1) * LANES] = value.reshape(F, L, R, LANES)

    first = real[0]
    for q in range(1, half + 1):
        first = first + real[q]
    store(0, first)
    for a in range(1, half + 1):
        even_part = real[0]
        odd_part = None
        for q in range(1, half + 1):
            even_part = even_part + float(np.cos(angle(q, a))) * real[q]
            term = float(np.sin(angle(q, a))) * imag[q]
            odd_part = term if odd_part is None else odd_part + term
        store(a, even_part - odd_part)
        store(A - a, even_part + odd_part)


def fourier_filter(wind, cutoff):
    F, L, R, N = wind.shape
    high, low = filter_tables(N)
    macs = F * L * R * high.size
    return pl.pallas_call(
        functools.partial(filter_kernel, N),
        in_specs=[VMEM] * 4,
        out_specs=VMEM,
        out_shape=jax.ShapeDtypeStruct(wind.shape, jnp.float32),
        compiler_params=params(),
        cost_estimate=cost(2 * 6 * macs, 8 * F * L * R * N + 4 * high.size),
        name="fourier_filter",
    )(wind, jnp.broadcast_to(cutoff[:, None], (R, LANES)), jnp.asarray(high), jnp.asarray(low))


def remap_kernel(lev_count, sub_count, with_thickness, place_ref, weight_ref, *refs):
    S, C = sub_count, lev_count
    thick_refs, refs = refs[:S], refs[S:]
    field_refs, refs = refs[:S], refs[S:]
    other_refs, refs = refs[: (C - 1) * S], refs[(C - 1) * S :]
    out_refs = refs[:C]
    F, L, R, N = out_refs[0].shape
    extra = field_refs[0].shape[0] - F
    lev, sub = place_ref[0], place_ref[1]
    spot = [lax.rem(sub + S - t, S) for t in range(S)]
    targets = [(lax.rem(lev + s, C) * S + sub) * L for s in range(C)]
    below_sum = [jnp.float32(0.0) for _ in range(C)]
    weight_sum = jnp.float32(0.0)
    for k in range(C * S * L):
        w = weight_ref[k]
        for s in range(C):
            below_sum[s] = below_sum[s] + jnp.where(k < targets[s], w, 0.0)
        weight_sum = weight_sum + w
    weights = [[weight_ref[first + i] for i in range(L)] for first in targets]
    sums = []
    for s in range(C):
        sums.append([below_sum[s]])
        for w in weights[s]:
            sums[s].append(sums[s][-1] + w)

    def tile(rows, columns):
        thick = [[thick_refs[t][0, m, rows, columns] for m in range(L)] for t in range(S)]
        group = [functools.reduce(jnp.add, levels) for levels in thick]
        mass = functools.reduce(jnp.add, group)
        base = jnp.zeros_like(mass)
        for s in range(1, C):
            other = other_refs[(s - 1) * S][rows, columns]
            for t in range(1, S):
                other = other + other_refs[(s - 1) * S + t][rows, columns]
            mass = mass + other
            base = base + jnp.where(lev >= s, other, 0.0)
        sources = []
        for t in range(S):
            low = base
            for other in range(S):
                if other != t:
                    low = low + jnp.where(spot[other] < spot[t], group[other], 0.0)
            for m in range(L):
                sources.append((t, m, low, thick[t][m]))
                low = low + thick[t][m]
        unit = mass / weight_sum
        for s in range(C):

            def covered(i):
                top = unit * sums[s][i]
                return [jnp.minimum(jnp.maximum(top - low, 0.0), h) for _, _, low, h in sources]

            below = covered(0)
            for i in range(L):
                upto = covered(i + 1)
                part = [a - b for a, b in zip(upto, below)]
                below = upto
                target = unit * weights[s][i]
                scale = 1.0 / target
                for f in range(F):
                    total = None
                    for (t, m, _, _), w in zip(sources, part):
                        term = field_refs[t][extra + f, m, rows, columns] * w
                        total = term if total is None else total + term
                    out_refs[s][f, i, rows, columns] = total * scale
                if with_thickness and s == 0:
                    refs[C][i, rows, columns] = target

    for r in range(0, R, 8):

        def body(c, carry):
            tile(slice(r, r + 8), pl.ds(pl.multiple_of(c * LANES, LANES), LANES))
            return carry

        lax.fori_loop(0, N // LANES, body, 0)


def remap_parts(counts, place, weights, thick, fields, others, with_thickness, extra):
    C, S = counts
    F, L, R, N = fields[0].shape
    F = F - extra
    shape = jax.ShapeDtypeStruct((F, L, R, N), jnp.float32)
    out_shape = [shape] * C
    if with_thickness:
        out_shape = out_shape + [jax.ShapeDtypeStruct((L, R, N), jnp.float32)]
    return pl.pallas_call(
        functools.partial(remap_kernel, C, S, with_thickness),
        in_specs=[SMEM] * 2 + [VMEM] * (2 * S + len(others)),
        out_specs=[VMEM] * len(out_shape),
        out_shape=out_shape,
        compiler_params=params(),
        cost_estimate=cost(C * S * L * L * R * N * (5 + 2 * F), 4 * R * N * L * (F + 1) * (S + C)),
        name="remap_parts",
    )(place, weights, *thick, *fields, *others)


def add_kernel(groups, outs_count, *refs):
    outs = refs[len(refs) - outs_count :]
    refs = refs[: len(refs) - outs_count]
    at = 0
    each = len(refs) // groups
    for g in range(groups):
        total = refs[g * each][...]
        for i in range(1, each):
            total = total + refs[g * each + i][...]
        n = total.shape[0]
        if outs_count == 1:
            outs[0][at : at + n] = total
        else:
            for i in range(n):
                outs[at + i][...] = total[i]
        at += n


def add_parts(groups, outs_count):
    flat = [a for group in groups for a in group]
    total = sum(group[0].shape[0] for group in groups)
    L, R, N = flat[0].shape[1:]
    if outs_count == 1:
        out_shape = jax.ShapeDtypeStruct((total, L, R, N), jnp.float32)
    else:
        out_shape = [jax.ShapeDtypeStruct((L, R, N), jnp.float32)] * total
    return pl.pallas_call(
        functools.partial(add_kernel, len(groups), outs_count),
        in_specs=[VMEM] * len(flat),
        out_specs=VMEM if outs_count == 1 else [VMEM] * total,
        out_shape=out_shape,
        compiler_params=params(),
        cost_estimate=cost(total * L * R * N, 4 * total * L * R * N * 3),
        name="add_parts",
    )(*flat)


def shifted(value, lev_count, sub_count, s, t):
    if t == 0:
        return lax.ppermute(value, "lev", [(i, (i + s) % lev_count) for i in range(lev_count)])
    if s == 0:
        return lax.ppermute(value, "sub", [(i, (i + t) % sub_count) for i in range(sub_count)])
    pairs = [
        (i * sub_count + j, (i + s) % lev_count * sub_count + (j + t) % sub_count)
        for i in range(lev_count)
        for j in range(sub_count)
    ]
    return lax.ppermute(value, ("lev", "sub"), pairs)


def per_device(thickness, wind_u, wind_v, tracers, level_weights, cutoff):
    L, R, N = thickness.shape
    lat_count = lax.axis_size("lat")
    C, S = lax.axis_size("lev"), lax.axis_size("sub")
    lat_rows = R * lat_count
    send = functools.partial(shifted, lev_count=C, sub_count=S)

    last, leading = edge_rows(thickness, wind_u, wind_v, tracers)
    northward = [(i, i + 1) for i in range(lat_count - 1)]
    up = lax.ppermute(last, "lat", northward)
    down = lax.ppermute(leading, "lat", [(j, i) for i, j in northward])

    band = lax.axis_index("lat").astype(jnp.int32).reshape(1)
    table = jnp.asarray(geometry_table(lat_rows, R))
    place = jnp.stack([lax.axis_index("lev"), lax.axis_index("sub")]).astype(jnp.int32)

    thick_new, wind, own_sum = thickness_step(band, table, lat_rows, thickness, wind_u, wind_v, up, down)
    others = [send(own_sum, s=s, t=t) for s in range(1, C) for t in range(S)]
    step = functools.partial(tracer_step, band, table, thickness, wind_u, wind_v, thick_new, up, down, tracers)
    T = tracers.shape[0]
    sources = [step(0, 1, True), step(1, T - 1, False), fourier_filter(wind, cutoff)]
    gathered = [[own] + [send(own, s=0, t=t) for t in range(1, S)] for own in sources]
    results = []
    thickness_out = None
    for index, fields in enumerate(gathered):
        with_thickness = index == 2
        extra = 1 if index == 0 else 0
        out = remap_parts((C, S), place, level_weights, gathered[0], fields, others, with_thickness, extra)
        if with_thickness:
            thickness_out = out[C]
        results.append([out[0]] + [send(out[s], s=s, t=0) for s in range(1, C)])
    tracers_out = add_parts(results[:2], 1)
    u_out, v_out = add_parts(results[2:], 2)
    return thickness_out, u_out, v_out, tracers_out


def solution(mesh):
    placed = (
        P(("member", "lev", "sub"), "lat", None),
        P(("member", "lev", "sub"), "lat", None),
        P(("member", "lev", "sub"), "lat", None),
        P("member", ("lev", "sub"), "lat", None),
        P(),
        P("lat"),
    )
    return jax.shard_map(
        per_device,
        mesh=mesh,
        in_specs=placed,
        out_specs=(
            P(("member", "lev", "sub"), "lat", None),
            P(("member", "lev", "sub"), "lat", None),
            P(("member", "lev", "sub"), "lat", None),
            P("member", ("lev", "sub"), "lat", None),
        ),
        check_vma=False,
    )
```

```python
import functools

import jax
import jax.numpy as jnp
import ml_dtypes
import numpy as np
from jax import lax
from jax.experimental import pallas as pl
from jax.experimental.pallas import tpu as pltpu
from jax.sharding import PartitionSpec as P

LANES = 128
VMEM = pl.BlockSpec(memory_space=pltpu.VMEM)
SMEM = pl.BlockSpec(memory_space=pltpu.SMEM)


def params():
    return pltpu.CompilerParams(vmem_limit_bytes=48 * 1024 * 1024)


def cost(flops, bytes_accessed):
    return pl.CostEstimate(flops=int(flops), bytes_accessed=int(bytes_accessed), transcendentals=0)


def after(*arrays):
    return [pl.BlockSpec(memory_space=pl.ANY)] * len(arrays)


def geometry_table(lat_rows, band_rows):
    bands = lat_rows // band_rows
    table = np.zeros((bands, band_rows + 8, LANES), np.float32)
    for band in range(bands):
        for j in range(band_rows + 1):
            row = band * band_rows + j
            south = np.sin(row * np.pi / lat_rows) if 0 < row < lat_rows else 0.0
            north = np.sin((row + 1) * np.pi / lat_rows) if row + 1 < lat_rows else 0.0
            table[band, j, 0] = south
            table[band, j, 1] = north
            table[band, j, 2] = 1.0 / np.sin((row + 0.5) * np.pi / lat_rows)
    return table


def east_of(value):
    return pltpu.roll(value, value.shape[1] - 1, 1)


def west_of(value):
    return pltpu.roll(value, 1, 1)


def row_ids(shape):
    return lax.broadcasted_iota(jnp.int32, shape, 0)


def north_of(value, beyond):
    rows = value.shape[0]
    return jnp.where(row_ids(value.shape) == rows - 1, beyond, pltpu.roll(value, rows - 1, 0))


def south_of(value, beyond):
    return jnp.where(row_ids(value.shape) == 0, beyond, pltpu.roll(value, 1, 0))


def fluxes(geo, thick, u, v, thick_s, v_s, thick_n):
    rows = thick.shape[0]
    east = u * jnp.where(u > 0, thick, east_of(thick))
    north = v * jnp.where(v > 0, thick, north_of(thick, thick_n)) * geo[0:rows, 1:2]
    below = v_s * jnp.where(v_s > 0, thick_s, thick[0:1]) * geo[0:1, 0:1]
    return east, north, below


def edge_kernel(thick_top, v_top, tracer_top, thick_low, u_low, v_low, tracer_low, *refs):
    last_ref, leading_ref = refs[-2:]
    T = tracer_top.shape[0]
    rows = thick_top.shape[1]
    last_ref[0] = thick_top[:, rows - 1 : rows]
    last_ref[1] = v_top[:, rows - 1 : rows]
    last_ref[2 : 2 + T] = tracer_top[:, :, rows - 1 : rows]
    leading_ref[0] = thick_low[:, 0:1]
    leading_ref[1] = thick_low[:, 1:2]
    leading_ref[2] = u_low[:, 0:1]
    leading_ref[3] = v_low[:, 0:1]
    leading_ref[4 : 4 + T] = tracer_low[:, :, 0:1]


def edge_rows(thickness, wind_u, wind_v, tracers, wait):
    L, R, N = thickness.shape
    T = tracers.shape[0]
    block = lambda at: pl.BlockSpec((L, 8, N), lambda i: (0, at, 0))
    blocks = lambda at: pl.BlockSpec((T, L, 8, N), lambda i: (0, 0, at, 0))
    top = R // 8 - 1
    whole = lambda n: pl.BlockSpec((n, L, 1, N), lambda i: (0, 0, 0, 0))
    return pl.pallas_call(
        edge_kernel,
        grid=(1,),
        in_specs=[block(top), block(top), blocks(top), block(0), block(0), block(0), blocks(0)] + after(*wait),
        out_specs=[whole(2 + T), whole(4 + T)],
        out_shape=[
            jax.ShapeDtypeStruct((2 + T, L, 1, N), jnp.float32),
            jax.ShapeDtypeStruct((4 + T, L, 1, N), jnp.float32),
        ],
        compiler_params=params(),
        cost_estimate=cost(0, 4 * L * N * 8 * (5 + 2 * T)),
        name="edge_rows",
    )(thickness, wind_v, tracers, thickness, wind_u, wind_v, tracers, *wait)


def first_kernel(band_ref, table_ref, thick_ref, u_ref, v_ref, new_ref, sum_ref):
    geo = table_ref[band_ref[0]]
    thick, u, v = thick_ref[0], u_ref[0], v_ref[0]
    nothing = jnp.zeros((1, thick.shape[1]), jnp.float32)
    east, north, below = fluxes(geo, thick, u, v, nothing, nothing, nothing)
    new = thick - (east - west_of(east)) - (north - south_of(north, below)) * geo[0 : thick.shape[0], 2:3]
    new_ref[0] = new

    @pl.when(pl.program_id(0) == 0)
    def _():
        sum_ref[...] = new

    @pl.when(pl.program_id(0) > 0)
    def _():
        sum_ref[...] += new


def first_step(band, table, thickness, wind_u, wind_v):
    L, R, N = thickness.shape
    level = pl.BlockSpec((1, R, N), lambda k: (k, 0, 0))
    in_hbm = lambda x: pltpu.with_memory_space_constraint(x, pltpu.HBM)
    return pl.pallas_call(
        first_kernel,
        grid=(L,),
        in_specs=[SMEM, pl.BlockSpec(table.shape, lambda k: (0, 0, 0)), level, level, level],
        out_specs=[level, pl.BlockSpec((R, N), lambda k: (0, 0))],
        out_shape=[
            jax.ShapeDtypeStruct((L, R, N), jnp.float32),
            jax.ShapeDtypeStruct((R, N), jnp.float32),
        ],
        compiler_params=params(),
        cost_estimate=cost(1, 1),
        name="first_step",
    )(band, in_hbm(table), in_hbm(thickness), in_hbm(wind_u), in_hbm(wind_v))


def thickness_kernel(lat_rows, band_ref, table_ref, thick_ref, u_ref, v_ref, up_ref, down_ref, new_ref, wind_ref, sum_ref):
    rows = thick_ref.shape[1]
    geo = table_ref[band_ref[0]]
    thick, u, v = thick_ref[0], u_ref[0], v_ref[0]
    thick_s, v_s = up_ref[0, 0], up_ref[1, 0]
    thick_n, thick_nn, u_n, v_n = (down_ref[i, 0] for i in range(4))
    east, north, below = fluxes(geo, thick, u, v, thick_s, v_s, thick_n)
    inverse = geo[0:rows, 2:3]
    new = thick - (east - west_of(east)) - (north - south_of(north, below)) * inverse
    east_n = u_n * jnp.where(u_n > 0, thick_n, east_of(thick_n))
    north_n = v_n * jnp.where(v_n > 0, thick_n, thick_nn) * geo[rows : rows + 1, 1:2]
    new_n = (
        thick_n
        - (east_n - west_of(east_n))
        - (north_n - north[rows - 1 : rows]) * geo[rows : rows + 1, 2:3]
    )
    new_ref[0] = new
    wind_ref[0, 0] = u - 0.05 * (east_of(new) - new)
    inside = band_ref[0] * rows + row_ids(new.shape) < lat_rows - 1
    wind_ref[1, 0] = jnp.where(inside, v - 0.05 * (north_of(new, new_n) - new), 0.0)

    @pl.when(pl.program_id(0) == 0)
    def _():
        sum_ref[0:1] = new[0:1]
        sum_ref[1:2] = new[rows - 1 : rows]

    @pl.when(pl.program_id(0) > 0)
    def _():
        sum_ref[0:1] += new[0:1]
        sum_ref[1:2] += new[rows - 1 : rows]


def thickness_step(band, table, lat_rows, thickness, wind_u, wind_v, up, down):
    L, R, N = thickness.shape
    level = pl.BlockSpec((1, R, N), lambda k: (k, 0, 0))
    return pl.pallas_call(
        functools.partial(thickness_kernel, lat_rows),
        grid=(L,),
        in_specs=[
            SMEM,
            pl.BlockSpec(table.shape, lambda k: (0, 0, 0)),
            level,
            level,
            level,
            pl.BlockSpec((2, 1, 1, N), lambda k: (0, k, 0, 0)),
            pl.BlockSpec((4, 1, 1, N), lambda k: (0, k, 0, 0)),
        ],
        out_specs=[
            level,
            pl.BlockSpec((2, 1, R, N), lambda k: (0, k, 0, 0)),
            pl.BlockSpec((2, N), lambda k: (0, 0)),
        ],
        out_shape=[
            jax.ShapeDtypeStruct((L, R, N), jnp.float32),
            jax.ShapeDtypeStruct((2, L, R, N), jnp.float32),
            jax.ShapeDtypeStruct((2, N), jnp.float32),
        ],
        compiler_params=params(),
        cost_estimate=cost(1, 1),
        name="thickness_step",
    )(band, table, thickness, wind_u, wind_v, up, down)


def tracer_kernel(edges, band_ref, table_ref, thick_ref, u_ref, v_ref, new_ref, tracer_ref, *refs):
    rows, width = thick_ref.shape[1:]
    out_ref = refs[-1]
    geo = table_ref[band_ref[0]]
    thick, u, v = thick_ref[0], u_ref[0], v_ref[0]
    nothing = jnp.zeros((1, width), jnp.float32)
    if edges:
        up_ref, down_ref = refs[:2]
        thick_s, v_s, thick_n = up_ref[0, 0], up_ref[1, 0], down_ref[0, 0]
    else:
        thick_s, v_s, thick_n = nothing, nothing, nothing
    east, north, below = fluxes(geo, thick, u, v, thick_s, v_s, thick_n)
    inverse = geo[0:rows, 2:3]
    scale = 1.0 / new_ref[0]

    def store(at, value):
        if edges:
            out_ref[at, 0, 0:1] = value[0:1]
            out_ref[at, 0, 1:2] = value[rows - 1 : rows]
        else:
            out_ref[at, 0] = value

    count = tracer_ref.shape[0]
    extra = out_ref.shape[0] - count
    if extra:
        store(0, new_ref[0])
    for c in range(count):
        q = tracer_ref[c, 0]
        q_s, q_n = (up_ref[2 + c, 0], down_ref[4 + c, 0]) if edges else (nothing, nothing)
        t_east = east * jnp.where(u > 0, q, east_of(q))
        t_north = north * jnp.where(v > 0, q, north_of(q, q_n))
        t_below = below * jnp.where(v_s > 0, q_s, q[0:1])
        change = thick * q - (t_east - west_of(t_east))
        change = change - (t_north - south_of(t_north, t_below)) * inverse
        store(extra + c, change * scale)


def tracer_step(band, table, thickness, wind_u, wind_v, thick_new, tracers, begin, count, with_thickness, halo, wait):
    L, R, N = thickness.shape
    level = pl.BlockSpec((1, R, N), lambda k: (k, 0, 0))
    total = count + (1 if with_thickness else 0)
    rows = 2 if halo else R
    return pl.pallas_call(
        functools.partial(tracer_kernel, bool(halo)),
        grid=(L,),
        in_specs=[
            SMEM,
            pl.BlockSpec(table.shape, lambda k: (0, 0, 0)),
            level,
            level,
            level,
            level,
            pl.BlockSpec(
                (pl.Element(count), pl.Element(1), pl.Element(R), pl.Element(N)), lambda k: (begin, k, 0, 0)
            ),
        ]
        + [pl.BlockSpec((a.shape[0], 1, 1, N), lambda k: (0, k, 0, 0)) for a in halo]
        + after(*wait),
        out_specs=pl.BlockSpec((total, 1, rows, N), lambda k: (0, k, 0, 0)),
        out_shape=jax.ShapeDtypeStruct((total, L, rows, N), jnp.float32),
        compiler_params=params(),
        cost_estimate=cost(1, 1),
        name="tracer_step",
    )(band, table, thickness, wind_u, wind_v, thick_new, tracers, *halo, *wait)


def filter_tables(N):
    A = N // LANES
    b = np.arange(LANES)[:, None]
    p = np.arange(LANES)[None, :]
    tables = []
    for q in range(A // 2 + 1):
        angle = 2.0 * np.pi * ((b * (A * p + q)) % N) / N
        c, s = np.cos(angle), np.sin(angle)
        tables.append(np.block([[c, -s], [s, c]]))
    table = np.stack(tables)
    high = table.astype(np.float32).astype(ml_dtypes.bfloat16)
    low = (table - high.astype(np.float64)).astype(np.float32).astype(ml_dtypes.bfloat16)
    return high, low


def split(value):
    high = value.astype(jnp.bfloat16)
    return high, (value - high.astype(jnp.float32)).astype(jnp.bfloat16)


def product(value, high, low, transposed):
    dims = (((1,), (1 if transposed else 0,)), ((), ()))
    dot = lambda x, y: lax.dot_general(x, y, dims, preferred_element_type=jnp.float32)
    v_high, v_low = split(value)
    return dot(v_high, high) + (dot(v_high, low) + dot(v_low, high))


def filter_kernel(N, wind_ref, new_ref, cutoff_ref, high_ref, low_ref, out_ref):
    A = N // LANES
    half = A // 2
    F, L, R, _ = wind_ref.shape
    rows = F * L * R
    piece = lambda a: wind_ref[:, :, :, a * LANES : (a + 1) * LANES].reshape(rows, LANES)
    x = [piece(a) for a in range(A)]
    even = [x[a] + x[A - a] for a in range(1, half + 1)]
    odd = [x[a] - x[A - a] for a in range(1, half + 1)]
    angle = lambda q, a: 2.0 * np.pi * ((q * a) % A) / A
    cutoff = cutoff_ref[...]
    p = lax.broadcasted_iota(jnp.int32, (R, LANES), 1)
    real, imag = [], []
    for q in range(half + 1):
        re = x[0]
        for a in range(1, half + 1):
            re = re + (even[a - 1] if q == 0 else float(np.cos(angle(q, a))) * even[a - 1])
        if q == 0:
            spectrum = product(re, high_ref[0, 0:LANES], low_ref[0, 0:LANES], False)
        else:
            im = -float(np.sin(angle(q, 1))) * odd[0]
            for a in range(2, half + 1):
                im = im - float(np.sin(angle(q, a))) * odd[a - 1]
            spectrum = product(jnp.concatenate([re, im], axis=1), high_ref[q], low_ref[q], False)
        mode = A * p + q
        factor = 1.0 / N if q == 0 else 2.0 / N
        kept = jnp.where(jnp.minimum(mode, N - mode) <= cutoff, factor, 0.0)
        kept = jnp.concatenate([kept, kept], axis=1)
        spectrum = (spectrum.reshape(F * L, R, 2 * LANES) * kept[None]).reshape(rows, 2 * LANES)
        if q == 0:
            real.append(product(spectrum, high_ref[0, 0:LANES], low_ref[0, 0:LANES], True))
            imag.append(None)
        else:
            back = product(spectrum, high_ref[q], low_ref[q], True)
            real.append(back[:, :LANES])
            imag.append(back[:, LANES:])

    def store(a, value):
        out_ref[1:, :, :, a * LANES : (a + 1) * LANES] = value.reshape(F, L, R, LANES)

    out_ref[0] = new_ref[...]
    first = real[0]
    for q in range(1, half + 1):
        first = first + real[q]
    store(0, first)
    for a in range(1, half + 1):
        even_part = real[0]
        odd_part = None
        for q in range(1, half + 1):
            even_part = even_part + float(np.cos(angle(q, a))) * real[q]
            term = float(np.sin(angle(q, a))) * imag[q]
            odd_part = term if odd_part is None else odd_part + term
        store(a, even_part - odd_part)
        store(A - a, even_part + odd_part)


def fourier_filter(wind, thick_new, cutoff):
    F, L, R, N = wind.shape
    high, low = filter_tables(N)
    return pl.pallas_call(
        functools.partial(filter_kernel, N),
        in_specs=[VMEM] * 5,
        out_specs=VMEM,
        out_shape=jax.ShapeDtypeStruct((F + 1, L, R, N), jnp.float32),
        compiler_params=params(),
        cost_estimate=cost(1, 1),
        name="fourier_filter",
    )(wind, thick_new, jnp.broadcast_to(cutoff[:, None], (R, LANES)), jnp.asarray(high), jnp.asarray(low))


def remap_kernel(C, S, steps, begin, compact, with_thickness, others, patches, place_ref, weight_ref, *refs):
    thick_refs, refs = refs[:S], refs[S:]
    field_refs, refs = refs[:S], refs[S:]
    other_refs, refs = refs[:others], refs[others:]
    patch_refs, refs = refs[:patches], refs[patches:]
    out_refs = refs[len(refs) - len(steps) - with_thickness :]
    F = field_refs[0].shape[0] - begin
    _, L, R, N = field_refs[0].shape
    lev, sub = place_ref[0], place_ref[1]
    spot = [lax.rem(sub + S - t, S) for t in range(S)]
    targets = [(lax.rem(lev + s, C) * S + sub) * L for s in steps]
    weight_sum = jnp.float32(0.0)
    below_sum = [jnp.float32(0.0) for _ in steps]
    for k in range(C * S * L):
        w = weight_ref[k]
        below_sum = [b + jnp.where(k < first, w, 0.0) for b, first in zip(below_sum, targets)]
        weight_sum = weight_sum + w
    weights = [[weight_ref[first + i] for i in range(L)] for first in targets]
    sums = []
    for below, row in zip(below_sum, weights):
        sums.append([below])
        for w in row:
            sums[-1].append(sums[-1][-1] + w)

    def tile(r, rows, columns):
        at = slice(r, r + rows)

        def other_sum(index):
            value = other_refs[index][at, columns]
            if patches:
                row = r + lax.broadcasted_iota(jnp.int32, value.shape, 0)
                value = jnp.where(row == 0, patch_refs[index][0:1, columns], value)
                value = jnp.where(row == R - 1, patch_refs[index][1:2, columns], value)
            return value

        thick = [[thick_refs[t][0, m, at, columns] for m in range(L)] for t in range(S)]
        group = [functools.reduce(jnp.add, levels) for levels in thick]
        mass = functools.reduce(jnp.add, group)
        base = jnp.zeros_like(mass)
        for s in range(1, C):
            other = functools.reduce(jnp.add, [other_sum((s - 1) * S + t) for t in range(S)])
            mass = mass + other
            base = base + jnp.where(lev >= s, other, 0.0)
        sources = []
        for t in range(S):
            low = base
            for other in range(S):
                if other != t:
                    low = low + jnp.where(spot[other] < spot[t], group[other], 0.0)
            for m in range(L):
                sources.append((t, m, low, thick[t][m]))
                low = low + thick[t][m]
        unit = mass / weight_sum
        for index, s in enumerate(steps):

            def covered(i):
                top = unit * sums[index][i]
                return [jnp.minimum(jnp.maximum(top - low, 0.0), h) for _, _, low, h in sources]

            below = covered(0)
            for i in range(L):
                upto = covered(i + 1)
                part = [a - b for a, b in zip(upto, below)]
                below = upto
                target = unit * weights[index][i]
                scale = 1.0 / target
                for f in range(F):
                    total = None
                    for (t, m, _, _), w in zip(sources, part):
                        term = field_refs[t][begin + f, m, at, columns] * w
                        total = term if total is None else total + term
                    total = total * scale
                    if compact and s > 0:
                        lower, upper = max(r, 1), min(r + rows, R - 1)
                        start = (f * L + i) * (R - 2) - 1
                        out_refs[index][start + lower : start + upper, columns] = total[lower - r : upper - r]
                    else:
                        out_refs[index][f, i, at, columns] = total
                if with_thickness and s == 0:
                    out_refs[len(steps)][i, at, columns] = target

    rows = min(R, 8)
    for r in range(0, R, rows):

        def body(c, carry):
            tile(r, rows, pl.ds(pl.multiple_of(c * LANES, LANES), LANES))
            return carry

        lax.fori_loop(0, N // LANES, body, 0)


def remap_parts(
    counts, place, weights, thick, fields, others, patches=(), steps=None, begin=0, compact=False, with_thickness=False, wait=()
):
    C, S = counts
    steps = tuple(range(C)) if steps is None else steps
    F, L, R, N = fields[0].shape
    F = F - begin
    whole = jax.ShapeDtypeStruct((F, L, R, N), jnp.float32)
    inner = jax.ShapeDtypeStruct((F * L * (R - 2), N), jnp.float32)
    out_shape = [inner if compact and s > 0 else whole for s in steps]
    if with_thickness:
        out_shape = out_shape + [jax.ShapeDtypeStruct((L, R, N), jnp.float32)]
    return pl.pallas_call(
        functools.partial(
            remap_kernel, C, S, steps, begin, compact, int(with_thickness), len(others), len(patches)
        ),
        in_specs=[SMEM] * 2 + [VMEM] * (2 * S + len(others) + len(patches)) + after(*wait),
        out_specs=[VMEM] * len(out_shape),
        out_shape=out_shape,
        compiler_params=params(),
        cost_estimate=cost(1, 1),
        name="remap_parts",
    )(place, weights, *thick, *fields, *others, *patches, *wait)


def tracer_sum_kernel(chunks, sent, *refs):
    out_ref = refs[-1]
    T, L, R, N = out_ref.shape
    inner, edge = refs[: chunks * (1 + sent)], refs[chunks * (1 + sent) : -1]
    at = 0
    for chunk in range(chunks):
        own, *arrived = inner[chunk * (1 + sent) : (chunk + 1) * (1 + sent)]
        for f in range(own.shape[0]):
            for i in range(L):
                start = (f * L + i) * (R - 2)
                total = own[f, i, 1 : R - 1]
                for ref in arrived:
                    total = total + ref[start : start + R - 2]
                out_ref[at + f, i, 1 : R - 1] = total
        at += own.shape[0]
    for f in range(T):
        for i in range(L):
            total = functools.reduce(jnp.add, [ref[f, i] for ref in edge])
            out_ref[f, i, 0:1] = total[0:1]
            out_ref[f, i, R - 1 : R] = total[1:2]


def tracer_sum(chunks, edge):
    T = edge[0].shape[0]
    _, L, R, N = chunks[0][0].shape
    flat = [a for chunk in chunks for a in chunk] + list(edge)
    return pl.pallas_call(
        functools.partial(tracer_sum_kernel, len(chunks), len(edge) - 1),
        in_specs=[VMEM] * len(flat),
        out_specs=VMEM,
        out_shape=jax.ShapeDtypeStruct((T, L, R, N), jnp.float32),
        compiler_params=params(),
        cost_estimate=cost(1, 1),
        name="tracer_sum",
    )(*flat)


def wind_sum_kernel(parts, *refs):
    u_ref, v_ref = refs[parts:]
    u_ref[...] = functools.reduce(jnp.add, [ref[0] for ref in refs[:parts]])
    v_ref[...] = functools.reduce(jnp.add, [ref[1] for ref in refs[:parts]])


def wind_sum(parts):
    shape = jax.ShapeDtypeStruct(parts[0].shape[1:], jnp.float32)
    return pl.pallas_call(
        functools.partial(wind_sum_kernel, len(parts)),
        in_specs=[VMEM] * len(parts),
        out_specs=[VMEM] * 2,
        out_shape=[shape] * 2,
        compiler_params=params(),
        cost_estimate=cost(1, 1),
        name="wind_sum",
    )(*parts)


def shifted(value, lev_count, sub_count, s, t):
    if t == 0:
        return lax.ppermute(value, "lev", [(i, (i + s) % lev_count) for i in range(lev_count)])
    if s == 0:
        return lax.ppermute(value, "sub", [(i, (i + t) % sub_count) for i in range(sub_count)])
    pairs = [
        (i * sub_count + j, (i + s) % lev_count * sub_count + (j + t) % sub_count)
        for i in range(lev_count)
        for j in range(sub_count)
    ]
    return lax.ppermute(value, ("lev", "sub"), pairs)


def per_device(thickness, wind_u, wind_v, tracers, level_weights, cutoff):
    L, R, N = thickness.shape
    lat_count = lax.axis_size("lat")
    C, S = lax.axis_size("lev"), lax.axis_size("sub")
    lat_rows = R * lat_count
    send = functools.partial(shifted, lev_count=C, sub_count=S)

    T = tracers.shape[0]
    northward = [(i, i + 1) for i in range(lat_count - 1)]
    southward = [(j, i) for i, j in northward]
    band = lax.axis_index("lat").astype(jnp.int32).reshape(1)
    table = jnp.asarray(geometry_table(lat_rows, R))
    place = jnp.stack([lax.axis_index("lev"), lax.axis_index("sub")]).astype(jnp.int32)

    def with_others_of_chip(own):
        return [own] + [send(own, s=0, t=t) for t in range(1, S)]

    def sums_of_other_chips(own):
        return [send(own, s=s, t=t) for s in range(1, C) for t in range(S)]

    def exchanged(parts):
        return [parts[0]] + [send(parts[s], s=s, t=0) for s in range(1, C)]

    remap = functools.partial(remap_parts, (C, S), place, level_weights)
    step = functools.partial(tracer_step, band, table, thickness, wind_u, wind_v)

    new_inner, sum_inner = first_step(band, table, thickness, wind_u, wind_v)
    others = sums_of_other_chips(sum_inner)
    one = step(new_inner, tracers, 0, 1, True, (), ())
    one_group = with_others_of_chip(one)
    rest = step(new_inner, tracers, 1, T - 1, False, (), (one,))
    rest_group = with_others_of_chip(rest)
    one_away = remap(
        one_group, one_group, others, steps=tuple(range(1, C)), begin=1, compact=True, wait=(rest,)
    )
    one_arrived = [send(one_away[s - 1], s=s, t=0) for s in range(1, C)]
    rest_parts = exchanged(remap(one_group, rest_group, others, compact=True, wait=(one_away[0],)))

    last, leading = edge_rows(thickness, wind_u, wind_v, tracers, (rest_parts[0],))
    up = lax.ppermute(last, "lat", northward)
    down = lax.ppermute(leading, "lat", southward)
    thick_new, wind, sum_edge = thickness_step(band, table, lat_rows, thickness, wind_u, wind_v, up, down)
    others_edge = sums_of_other_chips(sum_edge)
    winds = fourier_filter(wind, thick_new, cutoff)
    winds_group = with_others_of_chip(winds)
    edge_group = with_others_of_chip(step(thick_new, tracers, 0, T, True, (up, down), (winds,)))
    edge_parts = exchanged(remap(edge_group, edge_group, others_edge, begin=1))
    wind_out = remap(
        winds_group, winds_group, others, others_edge, begin=1, with_thickness=True, wait=(edge_parts[0],)
    )
    wind_parts = exchanged(wind_out[:C])
    (one_own,) = remap(one_group, one_group, others, steps=(0,), begin=1, wait=(wind_out[0],))

    tracers_out = tracer_sum([[one_own] + one_arrived, rest_parts], edge_parts)
    u_out, v_out = wind_sum(wind_parts)
    return wind_out[C], u_out, v_out, tracers_out


def solution(mesh):
    placed = (
        P(("member", "lev", "sub"), "lat", None),
        P(("member", "lev", "sub"), "lat", None),
        P(("member", "lev", "sub"), "lat", None),
        P("member", ("lev", "sub"), "lat", None),
        P(),
        P("lat"),
    )
    return jax.shard_map(
        per_device,
        mesh=mesh,
        in_specs=placed,
        out_specs=(
            P(("member", "lev", "sub"), "lat", None),
            P(("member", "lev", "sub"), "lat", None),
            P(("member", "lev", "sub"), "lat", None),
            P("member", ("lev", "sub"), "lat", None),
        ),
        check_vma=False,
    )
```

```python
import functools

import jax
import jax.numpy as jnp
import ml_dtypes
import numpy as np
from jax import lax
from jax.experimental import pallas as pl
from jax.experimental.pallas import tpu as pltpu
from jax.sharding import PartitionSpec as P

LANES = 128
VMEM = pl.BlockSpec(memory_space=pltpu.VMEM)
SMEM = pl.BlockSpec(memory_space=pltpu.SMEM)


def params():
    return pltpu.CompilerParams(vmem_limit_bytes=48 * 1024 * 1024)


def cost(flops, bytes_accessed):
    return pl.CostEstimate(flops=int(flops), bytes_accessed=int(bytes_accessed), transcendentals=0)


def after(arrays):
    return [pl.BlockSpec(memory_space=pl.ANY)] * len(arrays)


def geometry_table(lat_rows, band_rows):
    bands = lat_rows // band_rows
    table = np.zeros((bands, band_rows + 8, LANES), np.float32)
    for band in range(bands):
        for j in range(band_rows + 1):
            row = band * band_rows + j
            south = np.sin(row * np.pi / lat_rows) if 0 < row < lat_rows else 0.0
            north = np.sin((row + 1) * np.pi / lat_rows) if row + 1 < lat_rows else 0.0
            table[band, j, 0] = south
            table[band, j, 1] = north
            table[band, j, 2] = 1.0 / np.sin((row + 0.5) * np.pi / lat_rows)
    return table


def east_of(value):
    return pltpu.roll(value, value.shape[1] - 1, 1)


def west_of(value):
    return pltpu.roll(value, 1, 1)


def row_ids(shape):
    return lax.broadcasted_iota(jnp.int32, shape, 0)


def north_of(value, beyond):
    rows = value.shape[0]
    return jnp.where(row_ids(value.shape) == rows - 1, beyond, pltpu.roll(value, rows - 1, 0))


def south_of(value, beyond):
    return jnp.where(row_ids(value.shape) == 0, beyond, pltpu.roll(value, 1, 0))


def fluxes(geo, thick, u, v, thick_s, v_s, thick_n):
    rows = thick.shape[0]
    east = u * jnp.where(u > 0, thick, east_of(thick))
    north = v * jnp.where(v > 0, thick, north_of(thick, thick_n)) * geo[0:rows, 1:2]
    below = v_s * jnp.where(v_s > 0, thick_s, thick[0:1]) * geo[0:1, 0:1]
    return east, north, below


def tracer_change(q, q_s, q_n, thick, u, v, v_s, east, north, below, inverse):
    t_east = east * jnp.where(u > 0, q, east_of(q))
    t_north = north * jnp.where(v > 0, q, north_of(q, q_n))
    t_below = below * jnp.where(v_s > 0, q_s, q[0:1])
    change = thick * q - (t_east - west_of(t_east))
    return change - (t_north - south_of(t_north, t_below)) * inverse


def inner_kernel(band_ref, table_ref, thick_ref, u_ref, v_ref, tracer_ref, out_ref, sum_ref, last_ref, leading_ref):
    rows, width = thick_ref.shape[1:]
    geo = table_ref[band_ref[0]]
    thick, u, v = thick_ref[0], u_ref[0], v_ref[0]
    nothing = jnp.zeros((1, width), jnp.float32)
    east, north, below = fluxes(geo, thick, u, v, nothing, nothing, nothing)
    inverse = geo[0:rows, 2:3]
    new = thick - (east - west_of(east)) - (north - south_of(north, below)) * inverse
    out_ref[0, 0] = new
    last_ref[0, 0] = thick[rows - 1 : rows]
    last_ref[1, 0] = v[rows - 1 : rows]
    leading_ref[0, 0] = thick[0:1]
    leading_ref[1, 0] = thick[1:2]
    leading_ref[2, 0] = u[0:1]
    leading_ref[3, 0] = v[0:1]

    @pl.when(pl.program_id(0) == 0)
    def _():
        sum_ref[...] = new

    @pl.when(pl.program_id(0) > 0)
    def _():
        sum_ref[...] += new

    scale = 1.0 / new
    for c in range(tracer_ref.shape[0]):
        q = tracer_ref[c, 0]
        last_ref[2 + c, 0] = q[rows - 1 : rows]
        leading_ref[4 + c, 0] = q[0:1]
        change = tracer_change(q, nothing, nothing, thick, u, v, nothing, east, north, below, inverse)
        out_ref[1 + c, 0] = change * scale


def inner_step(band, table, thickness, wind_u, wind_v, tracers):
    L, R, N = thickness.shape
    T = tracers.shape[0]
    level = pl.BlockSpec((1, R, N), lambda k: (k, 0, 0))
    some = lambda n, rows: pl.BlockSpec((n, 1, rows, N), lambda k: (0, k, 0, 0))
    in_hbm = lambda x: pltpu.with_memory_space_constraint(x, pltpu.HBM)
    return pl.pallas_call(
        inner_kernel,
        grid=(L,),
        in_specs=[SMEM, pl.BlockSpec(table.shape, lambda k: (0, 0, 0)), level, level, level, some(T, R)],
        out_specs=[some(1 + T, R), pl.BlockSpec((R, N), lambda k: (0, 0)), some(2 + T, 1), some(4 + T, 1)],
        out_shape=[
            jax.ShapeDtypeStruct((1 + T, L, R, N), jnp.float32),
            jax.ShapeDtypeStruct((R, N), jnp.float32),
            jax.ShapeDtypeStruct((2 + T, L, 1, N), jnp.float32),
            jax.ShapeDtypeStruct((4 + T, L, 1, N), jnp.float32),
        ],
        compiler_params=params(),
        cost_estimate=cost(130 * L * R * N, 4 * L * R * N * (8 + 2 * T)),
        name="inner_step",
    )(band, in_hbm(table), in_hbm(thickness), in_hbm(wind_u), in_hbm(wind_v), in_hbm(tracers))


def filter_tables(N):
    A = N // LANES
    b = np.arange(LANES)[:, None]
    p = np.arange(LANES)[None, :]
    tables = []
    for q in range(A // 2 + 1):
        angle = 2.0 * np.pi * ((b * (A * p + q)) % N) / N
        c, s = np.cos(angle), np.sin(angle)
        tables.append(np.block([[c, -s], [s, c]]))
    table = np.stack(tables)
    high = table.astype(np.float32).astype(ml_dtypes.bfloat16)
    low = (table - high.astype(np.float64)).astype(np.float32).astype(ml_dtypes.bfloat16)
    return high, low


def split(value):
    high = value.astype(jnp.bfloat16)
    return high, (value - high.astype(jnp.float32)).astype(jnp.bfloat16)


def product(value, high, low, transposed):
    dims = (((1,), (1 if transposed else 0,)), ((), ()))
    dot = lambda x, y: lax.dot_general(x, y, dims, preferred_element_type=jnp.float32)
    v_high, v_low = split(value)
    return dot(v_high, high) + (dot(v_high, low) + dot(v_low, high))


def filter_rows(x, cutoff, high_ref, low_ref):
    A = len(x)
    N = A * LANES
    half = A // 2
    even = [x[a] + x[A - a] for a in range(1, half + 1)]
    odd = [x[a] - x[A - a] for a in range(1, half + 1)]
    angle = lambda q, a: 2.0 * np.pi * ((q * a) % A) / A
    p = lax.broadcasted_iota(jnp.int32, cutoff.shape, 1)
    real, imag = [], []
    for q in range(half + 1):
        re = x[0]
        for a in range(1, half + 1):
            re = re + (even[a - 1] if q == 0 else float(np.cos(angle(q, a))) * even[a - 1])
        if q == 0:
            high, low = high_ref[0, 0:LANES], low_ref[0, 0:LANES]
            spectrum = product(re, high, low, False)
        else:
            high, low = high_ref[q], low_ref[q]
            im = -float(np.sin(angle(q, 1))) * odd[0]
            for a in range(2, half + 1):
                im = im - float(np.sin(angle(q, a))) * odd[a - 1]
            spectrum = product(jnp.concatenate([re, im], axis=1), high, low, False)
        mode = A * p + q
        factor = 1.0 / N if q == 0 else 2.0 / N
        kept = jnp.where(jnp.minimum(mode, N - mode) <= cutoff, factor, 0.0)
        back = product(spectrum * jnp.concatenate([kept, kept], axis=1), high, low, True)
        real.append(back[:, :LANES])
        imag.append(back[:, LANES:])
    out = [None] * A
    out[0] = functools.reduce(jnp.add, real)
    for a in range(1, half + 1):
        even_part, odd_part = real[0], None
        for q in range(1, half + 1):
            even_part = even_part + float(np.cos(angle(q, a))) * real[q]
            term = float(np.sin(angle(q, a))) * imag[q]
            odd_part = term if odd_part is None else odd_part + term
        out[a] = even_part - odd_part
        out[A - a] = even_part + odd_part
    return out


def second_kernel(
    lat_rows, band_ref, table_ref, thick_ref, u_ref, v_ref, tracer_ref, up_ref, down_ref, cutoff_ref, high_ref, low_ref, *refs
):
    wind_ref, edge_ref, new_wind = refs[-3:]
    k = pl.program_id(0)
    _, L, rows, width = wind_ref.shape
    geo = table_ref[band_ref[0]]
    thick, u, v = thick_ref[0], u_ref[0], v_ref[0]
    thick_s, v_s = up_ref[0, 0], up_ref[1, 0]
    thick_n, thick_nn, u_n, v_n = (down_ref[i, 0] for i in range(4))
    east, north, below = fluxes(geo, thick, u, v, thick_s, v_s, thick_n)
    inverse = geo[0:rows, 2:3]
    new = thick - (east - west_of(east)) - (north - south_of(north, below)) * inverse
    east_n = u_n * jnp.where(u_n > 0, thick_n, east_of(thick_n))
    north_n = v_n * jnp.where(v_n > 0, thick_n, thick_nn) * geo[rows : rows + 1, 1:2]
    new_n = (
        thick_n
        - (east_n - west_of(east_n))
        - (north_n - north[rows - 1 : rows]) * geo[rows : rows + 1, 2:3]
    )
    new_wind[0, k] = u - 0.05 * (east_of(new) - new)
    inside = band_ref[0] * rows + row_ids(new.shape) < lat_rows - 1
    new_wind[1, k] = jnp.where(inside, v - 0.05 * (north_of(new, new_n) - new), 0.0)

    def store_edges(field, level, value):
        edge_ref[field, level, 0:1] = value[0:1]
        edge_ref[field, level, 1:2] = value[rows - 1 : rows]

    store_edges(0, k, new)
    scale = 1.0 / new
    for c in range(tracer_ref.shape[0]):
        change = tracer_change(
            tracer_ref[c, 0], up_ref[2 + c, 0], down_ref[4 + c, 0], thick, u, v, v_s, east, north, below, inverse
        )
        store_edges(3 + c, k, change * scale)

    @pl.when(k == L - 1)
    def _():
        pieces = [
            new_wind[:, :, :, a * LANES : (a + 1) * LANES].reshape(2 * L * rows, LANES) for a in range(width // LANES)
        ]
        cutoff = jnp.broadcast_to(cutoff_ref[...][None], (2 * L, rows, LANES)).reshape(2 * L * rows, LANES)
        for a, piece in enumerate(filter_rows(pieces, cutoff, high_ref, low_ref)):
            wind_ref[:, :, :, a * LANES : (a + 1) * LANES] = piece.reshape(2, L, rows, LANES)
        for f in range(2):
            for level in range(L):
                store_edges(1 + f, level, wind_ref[f, level])


def second_step(band, table, lat_rows, thickness, wind_u, wind_v, tracers, up, down, cutoff, wait):
    L, R, N = thickness.shape
    T = tracers.shape[0]
    high, low = filter_tables(N)
    level = pl.BlockSpec((1, R, N), lambda k: (k, 0, 0))
    some = lambda n, rows: pl.BlockSpec((n, 1, rows, N), lambda k: (0, k, 0, 0))
    whole = lambda shape: pl.BlockSpec(shape, lambda k: (0,) * len(shape))
    return pl.pallas_call(
        functools.partial(second_kernel, lat_rows),
        grid=(L,),
        in_specs=[SMEM, whole(table.shape), level, level, level, some(T, R), some(2 + T, 1), some(4 + T, 1)]
        + [whole((R, LANES)), whole(high.shape), whole(low.shape)]
        + after(wait),
        out_specs=[whole((2, L, R, N)), whole((3 + T, L, 2, N))],
        out_shape=[
            jax.ShapeDtypeStruct((2, L, R, N), jnp.float32),
            jax.ShapeDtypeStruct((3 + T, L, 2, N), jnp.float32),
        ],
        scratch_shapes=[pltpu.VMEM((2, L, R, N), jnp.float32)],
        compiler_params=params(),
        cost_estimate=cost(12 * 2 * L * R * high.size, 4 * L * R * N * (8 + T)),
        name="second_step",
    )(
        band, table, thickness, wind_u, wind_v, tracers, up, down,
        jnp.broadcast_to(cutoff[:, None], (R, LANES)), jnp.asarray(high), jnp.asarray(low), *wait,
    )


def weight_sums(weight_ref, firsts, L, levels):
    total = jnp.float32(0.0)
    below = [jnp.float32(0.0) for _ in firsts]
    for k in range(levels):
        w = weight_ref[k]
        below = [b + jnp.where(k < first, w, 0.0) for b, first in zip(below, firsts)]
        total = total + w
    weights = [[weight_ref[first + i] for i in range(L)] for first in firsts]
    sums = []
    for start, row in zip(below, weights):
        sums.append([start])
        for w in row:
            sums[-1].append(sums[-1][-1] + w)
    return total, weights, sums


def source_levels(place, counts, thick, others):
    C, S = counts
    lev, sub = place
    spot = [lax.rem(lev - g // S + C, C) * S + lax.rem(sub - g % S + S, S) for g in range(len(thick))]
    group = [functools.reduce(jnp.add, levels) for levels in thick]
    mass = functools.reduce(jnp.add, group)
    base = jnp.zeros_like(mass)
    for s, other in enumerate(others, 1):
        mass = mass + other
        base = base + jnp.where(lev >= s, other, 0.0)
    sources = []
    for g, levels in enumerate(thick):
        low = base
        for other in range(len(thick)):
            if other != g:
                low = low + jnp.where(spot[other] < spot[g], group[other], 0.0)
        for m, value in enumerate(levels):
            sources.append((g, m, low, value))
            low = low + value
    return mass, sources


def covered(top, sources):
    return [jnp.minimum(jnp.maximum(top - low, 0.0), value) for _, _, low, value in sources]


def remap_kernel(C, S, G, steps, fields, compact, with_thickness, carried, place_ref, weight_ref, *refs):
    if carried:
        for source_ref, copy_ref in zip(refs[:carried], refs[len(refs) - carried :]):
            copy_ref[...] = source_ref[...]
        refs = refs[carried : len(refs) - carried]
    thick_refs, refs = refs[: G * S], refs[G * S :]
    field_refs, refs = refs[: G * S], refs[G * S :]
    other_refs, out_refs = refs[: (C - G) * S], refs[len(refs) - len(steps) - with_thickness :]
    _, L, R, N = field_refs[0].shape
    lev, sub = place_ref[0], place_ref[1]
    firsts = [(lax.rem(lev + s, C) * S + sub) * L for s in steps]
    weight_sum, weights, sums = weight_sums(weight_ref, firsts, L, C * S * L)

    def tile(r, rows, columns):
        at = slice(r, r + rows)
        thick = [[ref[0, m, at, columns] for m in range(L)] for ref in thick_refs]
        others = [
            functools.reduce(jnp.add, [ref[at, columns] for ref in other_refs[s * S : (s + 1) * S]])
            for s in range(C - G)
        ]
        mass, sources = source_levels((lev, sub), (C, S), thick, others)
        unit = mass / weight_sum
        for index, s in enumerate(steps):
            below = covered(unit * sums[index][0], sources)
            for i in range(L):
                upto = covered(unit * sums[index][i + 1], sources)
                part = [a - b for a, b in zip(upto, below)]
                below = upto
                target = unit * weights[index][i]
                scale = 1.0 / target
                for f, field in enumerate(fields):
                    terms = [field_refs[g][field, m, at, columns] * w for (g, m, _, _), w in zip(sources, part)]
                    total = functools.reduce(jnp.add, terms) * scale
                    if compact and s > 0:
                        lower, upper = max(r, 1), min(r + rows, R - 1)
                        start = (f * L + i) * (R - 2) - 1
                        out_refs[index][start + lower : start + upper, columns] = total[lower - r : upper - r]
                    else:
                        out_refs[index][f, i, at, columns] = total
                if with_thickness and s == 0:
                    out_refs[len(steps)][i, at, columns] = target

    rows = min(R, 8)
    for r in range(0, R, rows):

        def body(c, carry):
            tile(r, rows, pl.ds(pl.multiple_of(c * LANES, LANES), LANES))
            return carry

        lax.fori_loop(0, N // LANES, body, 0)


def remap_parts(counts, place, weights, thick, sources, others, fields, steps, compact=False, with_thickness=False, carry=(), wait=()):
    C, S = counts
    _, L, R, N = sources[0].shape
    F = len(fields)
    whole = jax.ShapeDtypeStruct((F, L, R, N), jnp.float32)
    inner = jax.ShapeDtypeStruct((F * L * (R - 2), N), jnp.float32)
    out_shape = [inner if compact and s > 0 else whole for s in steps]
    if with_thickness:
        out_shape = out_shape + [jax.ShapeDtypeStruct((L, R, N), jnp.float32)]
    out_shape = out_shape + [jax.ShapeDtypeStruct(a.shape, a.dtype) for a in carry]
    G = len(thick) // S
    return pl.pallas_call(
        functools.partial(remap_kernel, C, S, G, tuple(steps), tuple(fields), compact, with_thickness, len(carry)),
        in_specs=[SMEM] * 2 + [VMEM] * (len(carry) + len(thick) + len(sources) + len(others)) + after(wait),
        out_specs=[VMEM] * len(out_shape),
        out_shape=out_shape,
        compiler_params=params(),
        cost_estimate=cost(len(steps) * G * S * L * L * R * N * (5 + 2 * F), 4 * R * N * L * (F + 1) * (S * G + len(steps))),
        name="remap_parts",
    )(place, weights, *carry, *thick, *sources, *others, *wait)


def finish_kernel(C, S, chunks, place_ref, weight_ref, *refs):
    group_refs, refs = refs[:S], refs[S:]
    other_refs, refs = refs[: (C - 1) * S], refs[(C - 1) * S :]
    *arrived_refs, edge_ref, thick_edge_ref, out_ref, thick_out_ref = refs
    T, L, R, N = out_ref.shape
    lev, sub = place_ref[0], place_ref[1]
    weight_sum, weights, sums = weight_sums(weight_ref, [(lev * S + sub) * L], L, C * S * L)
    where = [(chunk, at) for chunk, count in enumerate(chunks) for at in range(count)]

    def tile(r, columns):
        at = slice(r, r + 8)
        thick = [[ref[0, m, at, columns] for m in range(L)] for ref in group_refs]
        others = [
            functools.reduce(jnp.add, [ref[at, columns] for ref in other_refs[s * S : (s + 1) * S]])
            for s in range(C - 1)
        ]
        mass, sources = source_levels((lev, sub), (C, S), thick, others)
        unit = mass / weight_sum
        below = covered(unit * sums[0][0], sources)
        lower, upper = max(r, 1), min(r + 8, R - 1)
        for i in range(L):
            upto = covered(unit * sums[0][i + 1], sources)
            part = [a - b for a, b in zip(upto, below)]
            below = upto
            target = unit * weights[0][i]
            thick_out_ref[i, at, columns] = target
            scale = 1.0 / target
            for f in range(T):
                terms = [group_refs[g][1 + f, m, at, columns] * w for (g, m, _, _), w in zip(sources, part)]
                total = (functools.reduce(jnp.add, terms) * scale)[lower - r : upper - r]
                chunk, place = where[f]
                start = (place * L + i) * (R - 2) - 1
                for s in range(C - 1):
                    total = total + arrived_refs[chunk * (C - 1) + s][start + lower : start + upper, columns]
                out_ref[f, i, lower:upper, columns] = total

    for r in range(0, R, 8):

        def body(c, carry):
            tile(r, pl.ds(pl.multiple_of(c * LANES, LANES), LANES))
            return carry

        lax.fori_loop(0, N // LANES, body, 0)
    for i in range(L):
        for row, j in ((0, 0), (R - 1, 1)):
            thick_out_ref[i, row : row + 1] = thick_edge_ref[i, j : j + 1]
            for f in range(T):
                out_ref[f, i, row : row + 1] = edge_ref[2 + f, i, j : j + 1]


def finish_tracers(counts, place, weights, group, others, arrived, edge, thick_edge):
    C, S = counts
    T = group[0].shape[0] - 1
    _, L, R, N = group[0].shape
    chunks = tuple(a[0].shape[0] // (L * (R - 2)) for a in arrived)
    flat = [a for chunk in arrived for a in chunk]
    operands = list(group) + list(others) + flat + [edge, thick_edge]
    return pl.pallas_call(
        functools.partial(finish_kernel, C, S, chunks),
        in_specs=[SMEM] * 2 + [VMEM] * len(operands),
        out_specs=[VMEM] * 2,
        out_shape=[
            jax.ShapeDtypeStruct((T, L, R, N), jnp.float32),
            jax.ShapeDtypeStruct((L, R, N), jnp.float32),
        ],
        compiler_params=params(),
        cost_estimate=cost(S * L * L * R * N * (5 + 2 * T), 4 * R * N * L * (T + 1) * (S + 2)),
        name="finish_tracers",
    )(place, weights, *operands)


def finish_winds_kernel(count, own_ref, edge_ref, *refs):
    arrived_refs, (u_ref, v_ref) = refs[:count], refs[-2:]
    _, L, R, N = own_ref.shape
    for f, out_ref in enumerate((u_ref, v_ref)):
        for i in range(L):
            start = (f * L + i) * (R - 2)
            total = own_ref[f, i, 1 : R - 1]
            for ref in arrived_refs:
                total = total + ref[start : start + R - 2]
            out_ref[i, 1 : R - 1] = total
            out_ref[i, 0:1] = edge_ref[f, i, 0:1]
            out_ref[i, R - 1 : R] = edge_ref[f, i, 1:2]


def finish_winds(own, arrived, edge, wait):
    shape = jax.ShapeDtypeStruct(own.shape[1:], jnp.float32)
    return pl.pallas_call(
        functools.partial(finish_winds_kernel, len(arrived)),
        in_specs=[VMEM] * (2 + len(arrived)) + after(wait),
        out_specs=[VMEM] * 2,
        out_shape=[shape] * 2,
        compiler_params=params(),
        cost_estimate=cost(own.size, 12 * own.size),
        name="finish_winds",
    )(own, edge, *arrived, *wait)


def shifted(value, lev_count, sub_count, s, t):
    if t == 0:
        return lax.ppermute(value, "lev", [(i, (i + s) % lev_count) for i in range(lev_count)])
    if s == 0:
        return lax.ppermute(value, "sub", [(i, (i + t) % sub_count) for i in range(sub_count)])
    pairs = [
        (i * sub_count + j, (i + s) % lev_count * sub_count + (j + t) % sub_count)
        for i in range(lev_count)
        for j in range(sub_count)
    ]
    return lax.ppermute(value, ("lev", "sub"), pairs)


def per_device(thickness, wind_u, wind_v, tracers, level_weights, cutoff):
    L, R, N = thickness.shape
    lat_count = lax.axis_size("lat")
    C, S = lax.axis_size("lev"), lax.axis_size("sub")
    lat_rows = R * lat_count
    send = functools.partial(shifted, lev_count=C, sub_count=S)

    T = tracers.shape[0]
    northward = [(i, i + 1) for i in range(lat_count - 1)]
    southward = [(j, i) for i, j in northward]
    band = lax.axis_index("lat").astype(jnp.int32).reshape(1)
    table = jnp.asarray(geometry_table(lat_rows, R))
    place = jnp.stack([lax.axis_index("lev"), lax.axis_index("sub")]).astype(jnp.int32)
    away = range(1, C)

    def with_others_of_chip(own):
        return [own] + [send(own, s=0, t=t) for t in range(1, S)]

    def sent(parts):
        return [send(part, s=s, t=0) for s, part in zip(away, parts)]

    remap = functools.partial(remap_parts, (C, S), place, level_weights)

    inner, own_sum, last, leading = inner_step(band, table, thickness, wind_u, wind_v, tracers)
    others = [send(own_sum, s=s, t=t) for s in away for t in range(S)]
    group = with_others_of_chip(inner)
    first_away = remap(group, group, others, range(1, 2), away, compact=True)
    *rest_away, last, leading = remap(
        group, group, others, range(2, 1 + T), away, compact=True, carry=(last, leading), wait=first_away[:1]
    )
    arrived = [sent(first_away), sent(rest_away)]

    up = lax.ppermute(last, "lat", northward)
    down = lax.ppermute(leading, "lat", southward)
    winds, edge = second_step(
        band, table, lat_rows, thickness, wind_u, wind_v, tracers, up, down, cutoff, [rest_away[0], *arrived[0][:1]]
    )
    edges = [edge] + [send(edge, s=s, t=0) for s in away]
    winds_own, *winds_away = remap(
        group, with_others_of_chip(winds), others, range(2), range(C), compact=True, wait=arrived[1][:1]
    )
    winds_arrived = sent(winds_away)
    edges = [a for own in edges for a in with_others_of_chip(own)]
    edge_out, thick_edge = remap(
        edges, edges, [], range(1, 3 + T), (0,), with_thickness=True, wait=winds_away[:1]
    )

    tracers_out, thickness_out = finish_tracers(
        (C, S), place, level_weights, group, others, arrived, edge_out, thick_edge
    )
    u_out, v_out = finish_winds(winds_own, winds_arrived, edge_out, [tracers_out])
    return thickness_out, u_out, v_out, tracers_out


def solution(mesh):
    placed = (
        P(("member", "lev", "sub"), "lat", None),
        P(("member", "lev", "sub"), "lat", None),
        P(("member", "lev", "sub"), "lat", None),
        P("member", ("lev", "sub"), "lat", None),
        P(),
        P("lat"),
    )
    return jax.shard_map(
        per_device,
        mesh=mesh,
        in_specs=placed,
        out_specs=(
            P(("member", "lev", "sub"), "lat", None),
            P(("member", "lev", "sub"), "lat", None),
            P(("member", "lev", "sub"), "lat", None),
            P("member", ("lev", "sub"), "lat", None),
        ),
        check_vma=False,
    )
```

```python
import functools

import jax
import jax.numpy as jnp
import ml_dtypes
import numpy as np
from jax import lax
from jax.experimental import pallas as pl
from jax.experimental.pallas import tpu as pltpu
from jax.sharding import PartitionSpec as P

LANES = 128
VMEM = pl.BlockSpec(memory_space=pltpu.VMEM)
SMEM = pl.BlockSpec(memory_space=pltpu.SMEM)


def params():
    return pltpu.CompilerParams(vmem_limit_bytes=48 * 1024 * 1024)


def cost(flops, bytes_accessed):
    return pl.CostEstimate(flops=int(flops), bytes_accessed=int(bytes_accessed), transcendentals=0)


def after(arrays):
    return [pl.BlockSpec(memory_space=pl.ANY)] * len(arrays)


def geometry_table(lat_rows, band_rows):
    bands = lat_rows // band_rows
    table = np.zeros((bands, band_rows + 8, LANES), np.float32)
    for band in range(bands):
        for j in range(band_rows + 1):
            row = band * band_rows + j
            south = np.sin(row * np.pi / lat_rows) if 0 < row < lat_rows else 0.0
            north = np.sin((row + 1) * np.pi / lat_rows) if row + 1 < lat_rows else 0.0
            table[band, j, 0] = south
            table[band, j, 1] = north
            table[band, j, 2] = 1.0 / np.sin((row + 0.5) * np.pi / lat_rows)
    return table


def east_of(value):
    return pltpu.roll(value, value.shape[1] - 1, 1)


def west_of(value):
    return pltpu.roll(value, 1, 1)


def row_ids(shape):
    return lax.broadcasted_iota(jnp.int32, shape, 0)


def north_of(value, beyond):
    rows = value.shape[0]
    return jnp.where(row_ids(value.shape) == rows - 1, beyond, pltpu.roll(value, rows - 1, 0))


def south_of(value, beyond):
    return jnp.where(row_ids(value.shape) == 0, beyond, pltpu.roll(value, 1, 0))


def fluxes(geo, thick, u, v, thick_s, v_s, thick_n):
    rows = thick.shape[0]
    east = u * jnp.where(u > 0, thick, east_of(thick))
    north = v * jnp.where(v > 0, thick, north_of(thick, thick_n)) * geo[0:rows, 1:2]
    below = v_s * jnp.where(v_s > 0, thick_s, thick[0:1]) * geo[0:1, 0:1]
    return east, north, below


def tracer_change(q, q_s, q_n, thick, u, v, v_s, east, north, below, inverse):
    t_east = east * jnp.where(u > 0, q, east_of(q))
    t_north = north * jnp.where(v > 0, q, north_of(q, q_n))
    t_below = below * jnp.where(v_s > 0, q_s, q[0:1])
    change = thick * q - (t_east - west_of(t_east))
    return change - (t_north - south_of(t_north, t_below)) * inverse


def inner_kernel(band_ref, table_ref, thick_ref, u_ref, v_ref, tracer_ref, out_ref, sum_ref, last_ref, leading_ref, near_ref, near_rest_ref):
    rows, width = thick_ref.shape[1:]
    geo = table_ref[band_ref[0]]
    thick, u, v = thick_ref[0], u_ref[0], v_ref[0]
    nothing = jnp.zeros((1, width), jnp.float32)
    east, north, below = fluxes(geo, thick, u, v, nothing, nothing, nothing)
    inverse = geo[0:rows, 2:3]
    new = thick - (east - west_of(east)) - (north - south_of(north, below)) * inverse
    def store(field, value):
        out_ref[field, 0] = value
        ref, at = (near_ref, field) if field < 2 else (near_rest_ref, field - 2)
        ref[at, 0, 0:1] = value[1:2]
        ref[at, 0, 1:2] = value[rows - 2 : rows - 1]

    store(0, new)
    last_ref[0, 0] = thick[rows - 1 : rows]
    last_ref[1, 0] = v[rows - 1 : rows]
    leading_ref[0, 0] = thick[0:1]
    leading_ref[1, 0] = thick[1:2]
    leading_ref[2, 0] = u[0:1]
    leading_ref[3, 0] = v[0:1]

    @pl.when(pl.program_id(0) == 0)
    def _():
        sum_ref[...] = new

    @pl.when(pl.program_id(0) > 0)
    def _():
        sum_ref[...] += new

    scale = 1.0 / new
    for c in range(tracer_ref.shape[0]):
        q = tracer_ref[c, 0]
        last_ref[2 + c, 0] = q[rows - 1 : rows]
        leading_ref[4 + c, 0] = q[0:1]
        change = tracer_change(q, nothing, nothing, thick, u, v, nothing, east, north, below, inverse)
        store(1 + c, change * scale)


def inner_step(band, table, thickness, wind_u, wind_v, tracers):
    L, R, N = thickness.shape
    T = tracers.shape[0]
    level = pl.BlockSpec((1, R, N), lambda k: (k, 0, 0))
    some = lambda n, rows: pl.BlockSpec((n, 1, rows, N), lambda k: (0, k, 0, 0))
    in_hbm = lambda x: pltpu.with_memory_space_constraint(x, pltpu.HBM)
    return pl.pallas_call(
        inner_kernel,
        grid=(L,),
        in_specs=[SMEM, pl.BlockSpec(table.shape, lambda k: (0, 0, 0)), level, level, level, some(T, R)],
        out_specs=[some(1 + T, R), pl.BlockSpec((R, N), lambda k: (0, 0)), some(2 + T, 1), some(4 + T, 1), some(2, 2), some(T - 1, 2)],
        out_shape=[
            jax.ShapeDtypeStruct((1 + T, L, R, N), jnp.float32),
            jax.ShapeDtypeStruct((R, N), jnp.float32),
            jax.ShapeDtypeStruct((2 + T, L, 1, N), jnp.float32),
            jax.ShapeDtypeStruct((4 + T, L, 1, N), jnp.float32),
            jax.ShapeDtypeStruct((2, L, 2, N), jnp.float32),
            jax.ShapeDtypeStruct((T - 1, L, 2, N), jnp.float32),
        ],
        compiler_params=params(),
        cost_estimate=cost(130 * L * R * N, 4 * L * R * N * (8 + 2 * T)),
        name="inner_step",
    )(band, in_hbm(table), in_hbm(thickness), in_hbm(wind_u), in_hbm(wind_v), in_hbm(tracers))


def filter_tables(N):
    A = N // LANES
    b = np.arange(LANES)[:, None]
    p = np.arange(LANES)[None, :]
    tables = []
    for q in range(A // 2 + 1):
        angle = 2.0 * np.pi * ((b * (A * p + q)) % N) / N
        c, s = np.cos(angle), np.sin(angle)
        tables.append(np.block([[c, -s], [s, c]]))
    table = np.stack(tables)
    high = table.astype(np.float32).astype(ml_dtypes.bfloat16)
    low = (table - high.astype(np.float64)).astype(np.float32).astype(ml_dtypes.bfloat16)
    return high, low


def split(value):
    high = value.astype(jnp.bfloat16)
    return high, (value - high.astype(jnp.float32)).astype(jnp.bfloat16)


def product(value, high, low, transposed):
    dims = (((1,), (1 if transposed else 0,)), ((), ()))
    dot = lambda x, y: lax.dot_general(x, y, dims, preferred_element_type=jnp.float32)
    v_high, v_low = split(value)
    return dot(v_high, high) + (dot(v_high, low) + dot(v_low, high))


def filter_rows(x, cutoff, high_ref, low_ref):
    A = len(x)
    N = A * LANES
    half = A // 2
    even = [x[a] + x[A - a] for a in range(1, half + 1)]
    odd = [x[a] - x[A - a] for a in range(1, half + 1)]
    angle = lambda q, a: 2.0 * np.pi * ((q * a) % A) / A
    p = lax.broadcasted_iota(jnp.int32, cutoff.shape, 1)
    real, imag = [], []
    for q in range(half + 1):
        re = x[0]
        for a in range(1, half + 1):
            re = re + (even[a - 1] if q == 0 else float(np.cos(angle(q, a))) * even[a - 1])
        if q == 0:
            high, low = high_ref[0, 0:LANES], low_ref[0, 0:LANES]
            spectrum = product(re, high, low, False)
        else:
            high, low = high_ref[q], low_ref[q]
            im = -float(np.sin(angle(q, 1))) * odd[0]
            for a in range(2, half + 1):
                im = im - float(np.sin(angle(q, a))) * odd[a - 1]
            spectrum = product(jnp.concatenate([re, im], axis=1), high, low, False)
        mode = A * p + q
        factor = 1.0 / N if q == 0 else 2.0 / N
        kept = jnp.where(jnp.minimum(mode, N - mode) <= cutoff, factor, 0.0)
        back = product(spectrum * jnp.concatenate([kept, kept], axis=1), high, low, True)
        real.append(back[:, :LANES])
        imag.append(back[:, LANES:])
    out = [None] * A
    out[0] = functools.reduce(jnp.add, real)
    for a in range(1, half + 1):
        even_part, odd_part = real[0], None
        for q in range(1, half + 1):
            even_part = even_part + float(np.cos(angle(q, a))) * real[q]
            term = float(np.sin(angle(q, a))) * imag[q]
            odd_part = term if odd_part is None else odd_part + term
        out[a] = even_part - odd_part
        out[A - a] = even_part + odd_part
    return out


def second_kernel(
    lat_rows, band_ref, table_ref, thick_ref, u_ref, v_ref, tracer_ref, up_ref, down_ref, cutoff_ref, high_ref, low_ref, *refs
):
    *wind_refs, edge_ref, new_wind = refs
    k = pl.program_id(0)
    _, L, rows, width = new_wind.shape
    geo = table_ref[band_ref[0]]
    thick, u, v = thick_ref[0], u_ref[0], v_ref[0]
    thick_s, v_s = up_ref[0, 0], up_ref[1, 0]
    thick_n, thick_nn, u_n, v_n = (down_ref[i, 0] for i in range(4))
    east, north, below = fluxes(geo, thick, u, v, thick_s, v_s, thick_n)
    inverse = geo[0:rows, 2:3]
    new = thick - (east - west_of(east)) - (north - south_of(north, below)) * inverse
    east_n = u_n * jnp.where(u_n > 0, thick_n, east_of(thick_n))
    north_n = v_n * jnp.where(v_n > 0, thick_n, thick_nn) * geo[rows : rows + 1, 1:2]
    new_n = (
        thick_n
        - (east_n - west_of(east_n))
        - (north_n - north[rows - 1 : rows]) * geo[rows : rows + 1, 2:3]
    )
    new_wind[0, k] = u - 0.05 * (east_of(new) - new)
    inside = band_ref[0] * rows + row_ids(new.shape) < lat_rows - 1
    new_wind[1, k] = jnp.where(inside, v - 0.05 * (north_of(new, new_n) - new), 0.0)

    def store_edges(field, level, value):
        edge_ref[field, level, 0:1] = value[0:1]
        edge_ref[field, level, 1:2] = value[rows - 1 : rows]

    store_edges(0, k, new)
    scale = 1.0 / new
    for c in range(tracer_ref.shape[0]):
        change = tracer_change(
            tracer_ref[c, 0], up_ref[2 + c, 0], down_ref[4 + c, 0], thick, u, v, v_s, east, north, below, inverse
        )
        store_edges(3 + c, k, change * scale)

    @pl.when(k == L - 1)
    def _():
        pieces = [
            new_wind[:, :, :, a * LANES : (a + 1) * LANES].reshape(2 * L * rows, LANES) for a in range(width // LANES)
        ]
        cutoff = jnp.broadcast_to(cutoff_ref[...][None], (2 * L, rows, LANES)).reshape(2 * L * rows, LANES)
        for a, piece in enumerate(filter_rows(pieces, cutoff, high_ref, low_ref)):
            piece = piece.reshape(2, L, rows, LANES)
            for f in range(2):
                wind_refs[f][0, :, :, a * LANES : (a + 1) * LANES] = piece[f]
        for f in range(2):
            for level in range(L):
                store_edges(1 + f, level, wind_refs[f][0, level])


def second_step(band, table, lat_rows, thickness, wind_u, wind_v, tracers, up, down, cutoff):
    L, R, N = thickness.shape
    T = tracers.shape[0]
    high, low = filter_tables(N)
    level = pl.BlockSpec((1, R, N), lambda k: (k, 0, 0))
    some = lambda n, rows: pl.BlockSpec((n, 1, rows, N), lambda k: (0, k, 0, 0))
    whole = lambda shape: pl.BlockSpec(shape, lambda k: (0,) * len(shape))
    return pl.pallas_call(
        functools.partial(second_kernel, lat_rows),
        grid=(L,),
        in_specs=[SMEM, whole(table.shape), level, level, level, some(T, R), some(2 + T, 1), some(4 + T, 1)]
        + [whole((R, LANES)), whole(high.shape), whole(low.shape)],
        out_specs=[whole((1, L, R, N)), whole((1, L, R, N)), whole((3 + T, L, 2, N))],
        out_shape=[
            jax.ShapeDtypeStruct((1, L, R, N), jnp.float32),
            jax.ShapeDtypeStruct((1, L, R, N), jnp.float32),
            jax.ShapeDtypeStruct((3 + T, L, 2, N), jnp.float32),
        ],
        scratch_shapes=[pltpu.VMEM((2, L, R, N), jnp.float32)],
        compiler_params=params(),
        cost_estimate=cost(12 * 2 * L * R * high.size, 4 * L * R * N * (8 + T)),
        name="second_step",
    )(
        band, table, thickness, wind_u, wind_v, tracers, up, down,
        jnp.broadcast_to(cutoff[:, None], (R, LANES)), jnp.asarray(high), jnp.asarray(low),
    )


def weight_sums(weight_ref, firsts, L, levels):
    total = jnp.float32(0.0)
    below = [jnp.float32(0.0) for _ in firsts]
    for k in range(levels):
        w = weight_ref[k]
        below = [b + jnp.where(k < first, w, 0.0) for b, first in zip(below, firsts)]
        total = total + w
    weights = [[weight_ref[first + i] for i in range(L)] for first in firsts]
    sums = []
    for start, row in zip(below, weights):
        sums.append([start])
        for w in row:
            sums[-1].append(sums[-1][-1] + w)
    return total, weights, sums


def source_levels(place, counts, thick, others):
    C, S = counts
    lev, sub = place
    spot = [lax.rem(lev - g // S + C, C) * S + lax.rem(sub - g % S + S, S) for g in range(len(thick))]
    group = [functools.reduce(jnp.add, levels) for levels in thick]
    mass = functools.reduce(jnp.add, group)
    base = jnp.zeros_like(mass)
    for s, other in enumerate(others, 1):
        mass = mass + other
        base = base + jnp.where(lev >= s, other, 0.0)
    sources = []
    for g, levels in enumerate(thick):
        low = base
        for other in range(len(thick)):
            if other != g:
                low = low + jnp.where(spot[other] < spot[g], group[other], 0.0)
        for m, value in enumerate(levels):
            sources.append((g, m, low, value))
            low = low + value
    return mass, sources


def covered(top, sources):
    return [jnp.minimum(jnp.maximum(top - low, 0.0), value) for _, _, low, value in sources]


def remap_rows(place, weight_ref, counts, steps, thick_refs, field_refs, other_refs, store):
    C, S = counts
    G = len(thick_refs) // S
    _, L, R, N = thick_refs[0].shape
    lev, sub = place
    firsts = [(lax.rem(lev + s, C) * S + sub) * L for s in steps]
    weight_sum, weights, sums = weight_sums(weight_ref, firsts, L, C * S * L)

    def tile(at, columns):
        thick = [[ref[0, m, at, columns] for m in range(L)] for ref in thick_refs]
        others = [
            functools.reduce(jnp.add, [ref[at, columns] for ref in other_refs[s * S : (s + 1) * S]])
            for s in range(C - G)
        ]
        mass, sources = source_levels(place, counts, thick, others)
        unit = mass / weight_sum
        for index, s in enumerate(steps):
            below = covered(unit * sums[index][0], sources)
            for i in range(L):
                upto = covered(unit * sums[index][i + 1], sources)
                part = [a - b for a, b in zip(upto, below)]
                below = upto
                target = unit * weights[index][i]
                scale = 1.0 / target
                means = []
                for refs in field_refs:
                    terms = [refs[g][0][refs[g][1], m, at, columns] * w for (g, m, _, _), w in zip(sources, part)]
                    means.append(functools.reduce(jnp.add, terms) * scale)
                store(s, i, at, columns, target, means)

    rows = min(R, 8)
    for r in range(0, R, rows):

        def body(c, carry):
            tile(slice(r, r + rows), pl.ds(pl.multiple_of(c * LANES, LANES), LANES))
            return carry

        lax.fori_loop(0, N // LANES, body, 0)


def inner_part(at, margin, rows):
    return max(at.start, margin), min(at.stop, rows - margin)


def remap_kernel(counts, steps, fields, margin, sizes, place_ref, weight_ref, *refs):
    C, S = counts
    thick_refs, refs = refs[:S], refs[S:]
    bundles = []
    for _ in range(sizes[0]):
        bundles.append(refs[:S])
        refs = refs[S:]
    other_refs, out_refs = refs[: (C - 1) * S], refs[len(refs) - len(steps) :]
    _, L, R, _ = thick_refs[0].shape
    field_refs = [[(ref, index) for ref in bundles[which]] for which, index in fields]

    def store(s, i, at, columns, target, means):
        out_ref = out_refs[steps.index(s)]
        for f, value in enumerate(means):
            if s == 0:
                out_ref[f, i, at, columns] = value
            else:
                lower, upper = inner_part(at, margin, R)
                start = (f * L + i) * (R - 2 * margin) - margin
                out_ref[start + lower : start + upper, columns] = value[lower - at.start : upper - at.start]

    remap_rows(
        (place_ref[0], place_ref[1]), weight_ref, counts, steps, thick_refs, field_refs, other_refs, store
    )


def remap_parts(counts, place, weights, thick, bundles, others, fields, steps, margin, wait=()):
    C, S = counts
    _, L, R, N = thick[0].shape
    F = len(fields)
    whole = jax.ShapeDtypeStruct((F, L, R, N), jnp.float32)
    inner = jax.ShapeDtypeStruct((F * L * (R - 2 * margin), N), jnp.float32)
    flat = [a for bundle in bundles for a in bundle]
    return pl.pallas_call(
        functools.partial(remap_kernel, counts, tuple(steps), tuple(fields), margin, (len(bundles),)),
        in_specs=[SMEM] * 2 + [VMEM] * (len(thick) + len(flat) + len(others)) + after(wait),
        out_specs=[VMEM] * len(steps),
        out_shape=[whole if s == 0 else inner for s in steps],
        compiler_params=params(),
        cost_estimate=cost(len(steps) * S * L * L * R * N * (5 + 2 * F), 4 * R * N * L * (F + 1) * (S + len(steps))),
        name="remap_parts",
    )(place, weights, *thick, *flat, *others, *wait)


def remap_edge_kernel(counts, near_fields, place_ref, weight_ref, *refs):
    G = counts[0] * counts[1]
    edge_refs, near_refs, rest_refs = refs[:G], refs[G : 2 * G], refs[2 * G : 3 * G]
    edge_out_ref, thick_out_ref, near_out_ref = refs[-3:]
    place = (place_ref[0], place_ref[1])

    def store_edge(s, i, at, columns, target, means):
        thick_out_ref[i, at, columns] = target
        for f, value in enumerate(means):
            edge_out_ref[f, i, at, columns] = value

    def store_near(s, i, at, columns, target, means):
        for f, value in enumerate(means):
            near_out_ref[f, i, at, columns] = value

    fields = [[(ref, f) for ref in edge_refs] for f in range(1, edge_refs[0].shape[0])]
    remap_rows(place, weight_ref, counts, (0,), edge_refs, fields, [], store_edge)
    bundles = (near_refs, rest_refs)
    fields = [[(ref, index) for ref in bundles[which]] for which, index in near_fields]
    remap_rows(place, weight_ref, counts, (0,), near_refs, fields, [], store_near)


def remap_edges(counts, place, weights, edges, near, near_rest, wait=()):
    F, L, R, N = edges[0].shape
    T = F - 3
    near_fields = tuple((0, 1) if f == 0 else (1, f - 1) for f in range(T))
    operands = [*edges, *near, *near_rest]
    return pl.pallas_call(
        functools.partial(remap_edge_kernel, counts, near_fields),
        in_specs=[SMEM] * 2 + [VMEM] * len(operands) + after(wait),
        out_specs=[VMEM] * 3,
        out_shape=[
            jax.ShapeDtypeStruct((F - 1, L, R, N), jnp.float32),
            jax.ShapeDtypeStruct((L, R, N), jnp.float32),
            jax.ShapeDtypeStruct((T, L, R, N), jnp.float32),
        ],
        compiler_params=params(),
        cost_estimate=cost(len(edges) * L * L * R * N * 40, 4 * R * N * L * len(operands) * F),
        name="remap_edges",
    )(place, weights, *operands, *wait)


def finish_kernel(counts, margin, place_ref, weight_ref, *refs):
    C, S = counts
    group_refs, refs = refs[:S], refs[S:]
    other_refs, refs = refs[: (C - 1) * S], refs[(C - 1) * S :]
    *arrived_refs, near_ref, edge_ref, thick_edge_ref, out_ref, thick_out_ref, token_ref = refs
    token_ref[...] = jnp.zeros_like(token_ref)
    T, L, R, _ = out_ref.shape

    def store(s, i, at, columns, target, means):
        thick_out_ref[i, at, columns] = target
        lower, upper = inner_part(at, margin, R)
        for f, value in enumerate(means):
            total = value[lower - at.start : upper - at.start]
            start = (f * L + i) * (R - 2 * margin) - margin
            for ref in arrived_refs:
                total = total + ref[start + lower : start + upper, columns]
            out_ref[f, i, lower:upper, columns] = total

    fields = [[(ref, 1 + f) for ref in group_refs] for f in range(T)]
    remap_rows((place_ref[0], place_ref[1]), weight_ref, counts, (0,), group_refs, fields, other_refs, store)
    for i in range(L):
        for row, j in ((0, 0), (R - 1, 1)):
            thick_out_ref[i, row : row + 1] = thick_edge_ref[i, j : j + 1]
            for f in range(T):
                out_ref[f, i, row : row + 1] = edge_ref[2 + f, i, j : j + 1]
        for row, j in ((1, 0), (R - 2, 1)):
            for f in range(T):
                out_ref[f, i, row : row + 1] = near_ref[f, i, j : j + 1]


def finish_tracers(counts, place, weights, group, others, arrived, near, edge, thick_edge):
    margin = 2
    C, S = counts
    T = group[0].shape[0] - 1
    _, L, R, N = group[0].shape
    operands = list(group) + list(others) + list(arrived) + [near, edge, thick_edge]
    return pl.pallas_call(
        functools.partial(finish_kernel, counts, margin),
        in_specs=[SMEM] * 2 + [VMEM] * len(operands),
        out_specs=[VMEM] * 3,
        out_shape=[
            jax.ShapeDtypeStruct((T, L, R, N), jnp.float32),
            jax.ShapeDtypeStruct((L, R, N), jnp.float32),
            jax.ShapeDtypeStruct((8, LANES), jnp.float32),
        ],
        compiler_params=params(),
        cost_estimate=cost(S * L * L * R * N * (5 + 2 * T), 4 * R * N * L * (T + 1) * (S + 2)),
        name="finish_tracers",
    )(place, weights, *operands)


def finish_winds_kernel(count, own_ref, edge_ref, *refs):
    arrived_refs, out_refs = refs[:count], refs[-2:]
    _, L, R, N = own_ref.shape
    for f, out_ref in enumerate(out_refs):
        for i in range(L):
            start = (f * L + i) * (R - 2)
            total = own_ref[f, i, 1 : R - 1]
            for ref in arrived_refs:
                total = total + ref[start : start + R - 2]
            out_ref[i, 1 : R - 1] = total
            out_ref[i, 0:1] = edge_ref[f, i, 0:1]
            out_ref[i, R - 1 : R] = edge_ref[f, i, 1:2]


def finish_winds(own, arrived, edge, wait):
    return pl.pallas_call(
        functools.partial(finish_winds_kernel, len(arrived)),
        in_specs=[VMEM] * (2 + len(arrived)) + after(wait),
        out_specs=[VMEM] * 2,
        out_shape=[jax.ShapeDtypeStruct(own.shape[1:], jnp.float32)] * 2,
        compiler_params=params(),
        cost_estimate=cost(own.size, 12 * own.size),
        name="finish_winds",
    )(own, edge, *arrived, *wait)


def hand_on_kernel(count, *refs):
    for source_ref, copy_ref in zip(refs[:count], refs[len(refs) - count :]):
        copy_ref[...] = source_ref[...]


def hand_on(arrays, wait):
    return pl.pallas_call(
        functools.partial(hand_on_kernel, len(arrays)),
        in_specs=[VMEM] * len(arrays) + after(wait),
        out_specs=[VMEM] * len(arrays),
        out_shape=[jax.ShapeDtypeStruct(a.shape, a.dtype) for a in arrays],
        compiler_params=params(),
        cost_estimate=cost(1e10, 1e9),
        name="hand_on",
    )(*arrays, *wait)


def shifted(value, lev_count, sub_count, s, t):
    if t == 0:
        return lax.ppermute(value, "lev", [(i, (i + s) % lev_count) for i in range(lev_count)])
    if s == 0:
        return lax.ppermute(value, "sub", [(i, (i + t) % sub_count) for i in range(sub_count)])
    pairs = [
        (i * sub_count + j, (i + s) % lev_count * sub_count + (j + t) % sub_count)
        for i in range(lev_count)
        for j in range(sub_count)
    ]
    return lax.ppermute(value, ("lev", "sub"), pairs)


def per_device(thickness, wind_u, wind_v, tracers, level_weights, cutoff):
    L, R, N = thickness.shape
    lat_count = lax.axis_size("lat")
    C, S = lax.axis_size("lev"), lax.axis_size("sub")
    lat_rows = R * lat_count
    send = functools.partial(shifted, lev_count=C, sub_count=S)

    T = tracers.shape[0]
    northward = [(i, i + 1) for i in range(lat_count - 1)]
    southward = [(j, i) for i, j in northward]
    band = lax.axis_index("lat").astype(jnp.int32).reshape(1)
    table = jnp.asarray(geometry_table(lat_rows, R))
    place = jnp.stack([lax.axis_index("lev"), lax.axis_index("sub")]).astype(jnp.int32)
    away = range(1, C)

    def with_others_of_chip(own):
        return [own] + [send(own, s=0, t=t) for t in range(1, S)]

    def sent(parts):
        return [send(part, s=s, t=0) for s, part in zip(away, parts)]

    remap = functools.partial(remap_parts, (C, S), place, level_weights)

    inner, own_sum, last, leading, near, near_rest = inner_step(band, table, thickness, wind_u, wind_v, tracers)
    others = [send(own_sum, s=s, t=t) for s in away for t in range(S)]
    group = with_others_of_chip(inner)
    near = [near] + [send(near, s=s, t=0) for s in away]
    near_rest = [near_rest] + [send(near_rest, s=s, t=0) for s in away]
    tracer_fields = [(0, 1 + c) for c in range(T)]
    away_parts = remap(group, [group], others, tracer_fields, away, 2)
    arrived = sent(away_parts)

    last, leading = hand_on((last, leading), [away_parts[0], *near[1:2], *near_rest[1:2]])
    up = lax.ppermute(last, "lat", northward)
    down = lax.ppermute(leading, "lat", southward)
    u, v, edge = second_step(band, table, lat_rows, thickness, wind_u, wind_v, tracers, up, down, cutoff)
    edges = [edge] + [send(edge, s=s, t=0) for s in away]
    winds = [with_others_of_chip(u), with_others_of_chip(v)]
    winds_own, *winds_away = remap(group, winds, others, [(0, 0), (1, 0)], range(C), 1, wait=arrived[:1])
    winds_arrived = sent(winds_away)
    near, near_rest, edges = (
        [a for own in sources for a in with_others_of_chip(own)] for sources in (near, near_rest, edges)
    )
    edge_out, thick_edge, near_out = remap_edges(
        (C, S), place, level_weights, edges, near, near_rest, wait=winds_away[:1]
    )

    tracers_out, thickness_out, token = finish_tracers(
        (C, S), place, level_weights, group, others, arrived, near_out, edge_out, thick_edge
    )
    u_out, v_out = finish_winds(winds_own, winds_arrived, edge_out, [token])
    return thickness_out, u_out, v_out, tracers_out


def solution(mesh):
    placed = (
        P(("member", "lev", "sub"), "lat", None),
        P(("member", "lev", "sub"), "lat", None),
        P(("member", "lev", "sub"), "lat", None),
        P("member", ("lev", "sub"), "lat", None),
        P(),
        P("lat"),
    )
    return jax.shard_map(
        per_device,
        mesh=mesh,
        in_specs=placed,
        out_specs=(
            P(("member", "lev", "sub"), "lat", None),
            P(("member", "lev", "sub"), "lat", None),
            P(("member", "lev", "sub"), "lat", None),
            P("member", ("lev", "sub"), "lat", None),
        ),
        check_vma=False,
    )
```

```python
import functools

import jax
import jax.numpy as jnp
import ml_dtypes
import numpy as np
from jax import lax
from jax.experimental import pallas as pl
from jax.experimental.pallas import tpu as pltpu
from jax.sharding import PartitionSpec as P

LANES = 128
VMEM = pl.BlockSpec(memory_space=pltpu.VMEM)
SMEM = pl.BlockSpec(memory_space=pltpu.SMEM)


def params():
    return pltpu.CompilerParams(vmem_limit_bytes=16 * 1024 * 1024)


def cost(flops, bytes_accessed):
    return pl.CostEstimate(flops=int(flops), bytes_accessed=int(bytes_accessed), transcendentals=0)


def after(arrays):
    return [pl.BlockSpec(memory_space=pl.ANY)] * len(arrays)


def geometry_table(lat_rows, band_rows):
    bands = lat_rows // band_rows
    table = np.zeros((bands, band_rows + 8, LANES), np.float32)
    for band in range(bands):
        for j in range(band_rows + 1):
            row = band * band_rows + j
            south = np.sin(row * np.pi / lat_rows) if 0 < row < lat_rows else 0.0
            north = np.sin((row + 1) * np.pi / lat_rows) if row + 1 < lat_rows else 0.0
            table[band, j, 0] = south
            table[band, j, 1] = north
            table[band, j, 2] = 1.0 / np.sin((row + 0.5) * np.pi / lat_rows)
    return table


def east_of(value):
    return pltpu.roll(value, value.shape[1] - 1, 1)


def west_of(value):
    return pltpu.roll(value, 1, 1)


def row_ids(shape):
    return lax.broadcasted_iota(jnp.int32, shape, 0)


def north_of(value, beyond):
    rows = value.shape[0]
    return jnp.where(row_ids(value.shape) == rows - 1, beyond, pltpu.roll(value, rows - 1, 0))


def south_of(value, beyond):
    return jnp.where(row_ids(value.shape) == 0, beyond, pltpu.roll(value, 1, 0))


def fluxes(geo, thick, u, v, thick_s, v_s, thick_n):
    rows = thick.shape[0]
    east = u * jnp.where(u > 0, thick, east_of(thick))
    north = v * jnp.where(v > 0, thick, north_of(thick, thick_n)) * geo[0:rows, 1:2]
    below = v_s * jnp.where(v_s > 0, thick_s, thick[0:1]) * geo[0:1, 0:1]
    return east, north, below


def tracer_change(q, q_s, q_n, thick, u, v, v_s, east, north, below, inverse):
    t_east = east * jnp.where(u > 0, q, east_of(q))
    t_north = north * jnp.where(v > 0, q, north_of(q, q_n))
    t_below = below * jnp.where(v_s > 0, q_s, q[0:1])
    change = thick * q - (t_east - west_of(t_east))
    return change - (t_north - south_of(t_north, t_below)) * inverse


def in_hbm(*arrays):
    return [pltpu.with_memory_space_constraint(a, pltpu.HBM) for a in arrays]


def first_kernel(band_ref, table_ref, thick_ref, u_ref, v_ref, new_ref, sum_ref):
    rows, width = thick_ref.shape[1:]
    geo = table_ref[band_ref[0]]
    thick, u, v = thick_ref[0], u_ref[0], v_ref[0]
    nothing = jnp.zeros((1, width), jnp.float32)
    east, north, below = fluxes(geo, thick, u, v, nothing, nothing, nothing)
    new = thick - (east - west_of(east)) - (north - south_of(north, below)) * geo[0:rows, 2:3]
    new_ref[0] = new

    @pl.when(pl.program_id(0) == 0)
    def _():
        sum_ref[...] = new

    @pl.when(pl.program_id(0) > 0)
    def _():
        sum_ref[...] += new


def first_step(band, table, thickness, wind_u, wind_v):
    L, R, N = thickness.shape
    level = pl.BlockSpec((1, R, N), lambda k: (k, 0, 0))
    return pl.pallas_call(
        first_kernel,
        grid=(L,),
        in_specs=[SMEM, pl.BlockSpec(table.shape, lambda k: (0, 0, 0)), level, level, level],
        out_specs=[level, pl.BlockSpec((R, N), lambda k: (0, 0))],
        out_shape=[jax.ShapeDtypeStruct((L, R, N), jnp.float32), jax.ShapeDtypeStruct((R, N), jnp.float32)],
        compiler_params=params(),
        cost_estimate=cost(40 * L * R * N, 4 * L * R * N * 5),
        name="first_step",
    )(band, *in_hbm(table, thickness, wind_u, wind_v))


def inner_kernel(band_ref, table_ref, thick_ref, u_ref, v_ref, new_ref, tracer_ref, *refs):
    out_ref, last_ref, leading_ref, near_ref, near_rest_ref = refs
    rows, width = thick_ref.shape[1:]
    geo = table_ref[band_ref[0]]
    thick, u, v, new = thick_ref[0], u_ref[0], v_ref[0], new_ref[0]
    nothing = jnp.zeros((1, width), jnp.float32)
    east, north, below = fluxes(geo, thick, u, v, nothing, nothing, nothing)
    inverse = geo[0:rows, 2:3]

    def store(field, value):
        out_ref[field, 0] = value
        ref, at = (near_ref, field) if field < 2 else (near_rest_ref, field - 2)
        ref[at, 0, 0:1] = value[1:2]
        ref[at, 0, 1:2] = value[rows - 2 : rows - 1]

    store(0, new)
    last_ref[0, 0] = thick[rows - 1 : rows]
    last_ref[1, 0] = v[rows - 1 : rows]
    leading_ref[0, 0] = thick[0:1]
    leading_ref[1, 0] = thick[1:2]
    leading_ref[2, 0] = u[0:1]
    leading_ref[3, 0] = v[0:1]
    scale = 1.0 / new
    for c in range(tracer_ref.shape[0]):
        q = tracer_ref[c, 0]
        last_ref[2 + c, 0] = q[rows - 1 : rows]
        leading_ref[4 + c, 0] = q[0:1]
        change = tracer_change(q, nothing, nothing, thick, u, v, nothing, east, north, below, inverse)
        store(1 + c, change * scale)


def inner_step(band, table, thickness, wind_u, wind_v, new, tracers):
    L, R, N = thickness.shape
    T = tracers.shape[0]
    level = pl.BlockSpec((1, R, N), lambda k: (k, 0, 0))
    some = lambda n, rows: pl.BlockSpec((n, 1, rows, N), lambda k: (0, k, 0, 0))
    shape = lambda n, rows: jax.ShapeDtypeStruct((n, L, rows, N), jnp.float32)
    return pl.pallas_call(
        inner_kernel,
        grid=(L,),
        in_specs=[SMEM, pl.BlockSpec(table.shape, lambda k: (0, 0, 0)), level, level, level, level, some(T, R)],
        out_specs=[some(1 + T, R), some(2 + T, 1), some(4 + T, 1), some(2, 2), some(T - 1, 2)],
        out_shape=[shape(1 + T, R), shape(2 + T, 1), shape(4 + T, 1), shape(2, 2), shape(T - 1, 2)],
        compiler_params=params(),
        cost_estimate=cost(130 * L * R * N, 4 * L * R * N * (8 + 2 * T)),
        name="inner_step",
    )(band, *in_hbm(table, thickness, wind_u, wind_v), new, *in_hbm(tracers))


def filter_tables(N):
    A = N // LANES
    b = np.arange(LANES)[:, None]
    p = np.arange(LANES)[None, :]
    tables = []
    for q in range(A // 2 + 1):
        angle = 2.0 * np.pi * ((b * (A * p + q)) % N) / N
        c, s = np.cos(angle), np.sin(angle)
        tables.append(np.block([[c, -s], [s, c]]))
    table = np.stack(tables)
    high = table.astype(np.float32).astype(ml_dtypes.bfloat16)
    low = (table - high.astype(np.float64)).astype(np.float32).astype(ml_dtypes.bfloat16)
    return high, low


def split(value):
    high = value.astype(jnp.bfloat16)
    return high, (value - high.astype(jnp.float32)).astype(jnp.bfloat16)


def product(value, high, low, transposed):
    dims = (((1,), (1 if transposed else 0,)), ((), ()))
    dot = lambda x, y: lax.dot_general(x, y, dims, preferred_element_type=jnp.float32)
    v_high, v_low = split(value)
    return dot(v_high, high) + (dot(v_high, low) + dot(v_low, high))


def filter_rows(x, cutoff, high_ref, low_ref):
    A = len(x)
    N = A * LANES
    half = A // 2
    even = [x[a] + x[A - a] for a in range(1, half + 1)]
    odd = [x[a] - x[A - a] for a in range(1, half + 1)]
    angle = lambda q, a: 2.0 * np.pi * ((q * a) % A) / A
    p = lax.broadcasted_iota(jnp.int32, cutoff.shape, 1)
    real, imag = [], []
    for q in range(half + 1):
        re = x[0]
        for a in range(1, half + 1):
            re = re + (even[a - 1] if q == 0 else float(np.cos(angle(q, a))) * even[a - 1])
        if q == 0:
            high, low = high_ref[0, 0:LANES], low_ref[0, 0:LANES]
            spectrum = product(re, high, low, False)
        else:
            high, low = high_ref[q], low_ref[q]
            im = -float(np.sin(angle(q, 1))) * odd[0]
            for a in range(2, half + 1):
                im = im - float(np.sin(angle(q, a))) * odd[a - 1]
            spectrum = product(jnp.concatenate([re, im], axis=1), high, low, False)
        mode = A * p + q
        factor = 1.0 / N if q == 0 else 2.0 / N
        kept = jnp.where(jnp.minimum(mode, N - mode) <= cutoff, factor, 0.0)
        back = product(spectrum * jnp.concatenate([kept, kept], axis=1), high, low, True)
        real.append(back[:, :LANES])
        imag.append(back[:, LANES:])
    out = [None] * A
    out[0] = functools.reduce(jnp.add, real)
    for a in range(1, half + 1):
        even_part, odd_part = real[0], None
        for q in range(1, half + 1):
            even_part = even_part + float(np.cos(angle(q, a))) * real[q]
            term = float(np.sin(angle(q, a))) * imag[q]
            odd_part = term if odd_part is None else odd_part + term
        out[a] = even_part - odd_part
        out[A - a] = even_part + odd_part
    return out


def second_kernel(
    lat_rows, band_ref, table_ref, thick_ref, u_ref, v_ref, tracer_ref, up_ref, down_ref, cutoff_ref, high_ref, low_ref, *refs
):
    *wind_refs, edge_ref, new_wind = refs
    k = pl.program_id(0)
    _, L, rows, width = new_wind.shape
    geo = table_ref[band_ref[0]]
    thick, u, v = thick_ref[0], u_ref[0], v_ref[0]
    thick_s, v_s = up_ref[0, 0], up_ref[1, 0]
    thick_n, thick_nn, u_n, v_n = (down_ref[i, 0] for i in range(4))
    east, north, below = fluxes(geo, thick, u, v, thick_s, v_s, thick_n)
    inverse = geo[0:rows, 2:3]
    new = thick - (east - west_of(east)) - (north - south_of(north, below)) * inverse
    east_n = u_n * jnp.where(u_n > 0, thick_n, east_of(thick_n))
    north_n = v_n * jnp.where(v_n > 0, thick_n, thick_nn) * geo[rows : rows + 1, 1:2]
    new_n = (
        thick_n
        - (east_n - west_of(east_n))
        - (north_n - north[rows - 1 : rows]) * geo[rows : rows + 1, 2:3]
    )
    new_wind[0, k] = u - 0.05 * (east_of(new) - new)
    inside = band_ref[0] * rows + row_ids(new.shape) < lat_rows - 1
    new_wind[1, k] = jnp.where(inside, v - 0.05 * (north_of(new, new_n) - new), 0.0)

    def store_edges(field, level, value):
        edge_ref[field, level, 0:1] = value[0:1]
        edge_ref[field, level, 1:2] = value[rows - 1 : rows]

    store_edges(0, k, new)
    scale = 1.0 / new
    for c in range(tracer_ref.shape[0]):
        change = tracer_change(
            tracer_ref[c, 0], up_ref[2 + c, 0], down_ref[4 + c, 0], thick, u, v, v_s, east, north, below, inverse
        )
        store_edges(3 + c, k, change * scale)

    @pl.when(k == L - 1)
    def _():
        pieces = [
            new_wind[:, :, :, a * LANES : (a + 1) * LANES].reshape(2 * L * rows, LANES) for a in range(width // LANES)
        ]
        cutoff = jnp.broadcast_to(cutoff_ref[...][None], (2 * L, rows, LANES)).reshape(2 * L * rows, LANES)
        for a, piece in enumerate(filter_rows(pieces, cutoff, high_ref, low_ref)):
            piece = piece.reshape(2, L, rows, LANES)
            for f in range(2):
                wind_refs[f][0, :, :, a * LANES : (a + 1) * LANES] = piece[f]
        for f in range(2):
            for level in range(L):
                store_edges(1 + f, level, wind_refs[f][0, level])


def second_step(band, table, lat_rows, thickness, wind_u, wind_v, tracers, up, down, cutoff):
    L, R, N = thickness.shape
    T = tracers.shape[0]
    high, low = filter_tables(N)
    level = pl.BlockSpec((1, R, N), lambda k: (k, 0, 0))
    some = lambda n, rows: pl.BlockSpec((n, 1, rows, N), lambda k: (0, k, 0, 0))
    whole = lambda shape: pl.BlockSpec(shape, lambda k: (0,) * len(shape))
    return pl.pallas_call(
        functools.partial(second_kernel, lat_rows),
        grid=(L,),
        in_specs=[SMEM, whole(table.shape), level, level, level, some(T, R), some(2 + T, 1), some(4 + T, 1)]
        + [whole((R, LANES)), whole(high.shape), whole(low.shape)],
        out_specs=[whole((1, L, R, N)), whole((1, L, R, N)), whole((3 + T, L, 2, N))],
        out_shape=[
            jax.ShapeDtypeStruct((1, L, R, N), jnp.float32),
            jax.ShapeDtypeStruct((1, L, R, N), jnp.float32),
            jax.ShapeDtypeStruct((3 + T, L, 2, N), jnp.float32),
        ],
        scratch_shapes=[pltpu.VMEM((2, L, R, N), jnp.float32)],
        compiler_params=params(),
        cost_estimate=cost(12 * 2 * L * R * high.size, 4 * L * R * N * (8 + T)),
        name="second_step",
    )(
        band, table, thickness, wind_u, wind_v, tracers, up, down,
        jnp.broadcast_to(cutoff[:, None], (R, LANES)), jnp.asarray(high), jnp.asarray(low),
    )


def mass_kernel(C, S, place_ref, new_ref, *refs):
    base_ref, mass_ref = refs[-2:]
    lev = place_ref[0]
    others_mass, base = None, None
    for s in range(1, C):
        other = functools.reduce(jnp.add, [ref[...] for ref in refs[(s - 1) * S : s * S]])
        below = jnp.where(lev >= s, other, 0.0)
        others_mass = other if others_mass is None else others_mass + other
        base = below if base is None else base + below
    base_ref[...] = base
    mass_ref[...] = others_mass


def other_chips(counts, place, new, others):
    return pl.pallas_call(
        functools.partial(mass_kernel, *counts),
        in_specs=[SMEM] + [VMEM] * (1 + len(others)),
        out_specs=[VMEM] * 2,
        out_shape=[jax.ShapeDtypeStruct(new.shape, jnp.float32)] * 2,
        compiler_params=params(),
        cost_estimate=cost(1e11, 1e9),
        name="other_chips",
    )(place, new, *others)


def weight_sums(weight_ref, firsts, L, levels):
    total = jnp.float32(0.0)
    below = [jnp.float32(0.0) for _ in firsts]
    for k in range(levels):
        w = weight_ref[k]
        below = [b + jnp.where(k < first, w, 0.0) for b, first in zip(below, firsts)]
        total = total + w
    weights = [[weight_ref[first + i] for i in range(L)] for first in firsts]
    sums = []
    for start, row in zip(below, weights):
        sums.append([start])
        for w in row:
            sums[-1].append(sums[-1][-1] + w)
    return total, weights, sums


def source_levels(place, counts, thick, others):
    C, S = counts
    lev, sub = place
    spot = [lax.rem(lev - g // S + C, C) * S + lax.rem(sub - g % S + S, S) for g in range(len(thick))]
    group = [functools.reduce(jnp.add, levels) for levels in thick]
    mass = functools.reduce(jnp.add, group)
    base = jnp.zeros_like(mass)
    if others:
        base, mass = others[0], mass + others[1]
    sources = []
    for g, levels in enumerate(thick):
        low = base
        for other in range(len(thick)):
            if other != g:
                low = low + jnp.where(spot[other] < spot[g], group[other], 0.0)
        for m, value in enumerate(levels):
            sources.append((g, m, low, value))
            low = low + value
    return mass, sources


def covered(top, sources):
    return [jnp.minimum(jnp.maximum(top - low, 0.0), value) for _, _, low, value in sources]


def remap_rows(place, weight_ref, counts, steps, thick_refs, field_refs, other_refs, store):
    C, S = counts
    _, L, R, N = thick_refs[0].shape
    lev, sub = place
    firsts = [(lax.rem(lev + s, C) * S + sub) * L for s in steps]
    weight_sum, weights, sums = weight_sums(weight_ref, firsts, L, C * S * L)

    def tile(at, columns):
        thick = [[ref[0, m, at, columns] for m in range(L)] for ref in thick_refs]
        others = [ref[at, columns] for ref in other_refs]
        mass, sources = source_levels(place, counts, thick, others)
        unit = mass / weight_sum
        for index, s in enumerate(steps):
            below = covered(unit * sums[index][0], sources)
            for i in range(L):
                upto = covered(unit * sums[index][i + 1], sources)
                part = [a - b for a, b in zip(upto, below)]
                below = upto
                target = unit * weights[index][i]
                scale = 1.0 / target
                means = []
                for refs in field_refs:
                    terms = [refs[g][0][refs[g][1], m, at, columns] * w for (g, m, _, _), w in zip(sources, part)]
                    means.append(functools.reduce(jnp.add, terms) * scale)
                store(s, i, at, columns, target, means)

    rows = min(R, 8)
    for r in range(0, R, rows):

        def body(c, carry):
            tile(slice(r, r + rows), pl.ds(pl.multiple_of(c * LANES, LANES), LANES))
            return carry

        lax.fori_loop(0, N // LANES, body, 0)


def inner_part(at, margin, rows):
    return max(at.start, margin), min(at.stop, rows - margin)


def remap_kernel(counts, steps, fields, margin, sizes, place_ref, weight_ref, *refs):
    C, S = counts
    thick_refs, refs = refs[:S], refs[S:]
    bundles = []
    for _ in range(sizes[0]):
        bundles.append(refs[:S])
        refs = refs[S:]
    other_refs, out_refs = refs[:2], refs[len(refs) - len(steps) :]
    _, L, R, _ = thick_refs[0].shape
    field_refs = [[(ref, index) for ref in bundles[which]] for which, index in fields]

    def store(s, i, at, columns, target, means):
        out_ref = out_refs[steps.index(s)]
        for f, value in enumerate(means):
            if s == 0:
                out_ref[f, i, at, columns] = value
            else:
                lower, upper = inner_part(at, margin, R)
                start = (f * L + i) * (R - 2 * margin) - margin
                out_ref[start + lower : start + upper, columns] = value[lower - at.start : upper - at.start]

    remap_rows(
        (place_ref[0], place_ref[1]), weight_ref, counts, steps, thick_refs, field_refs, other_refs, store
    )


def remap_parts(counts, place, weights, thick, bundles, others, fields, steps, margin, wait=()):
    C, S = counts
    _, L, R, N = thick[0].shape
    F = len(fields)
    whole = jax.ShapeDtypeStruct((F, L, R, N), jnp.float32)
    inner = jax.ShapeDtypeStruct((F * L * (R - 2 * margin), N), jnp.float32)
    flat = [a for bundle in bundles for a in bundle]
    return pl.pallas_call(
        functools.partial(remap_kernel, counts, tuple(steps), tuple(fields), margin, (len(bundles),)),
        in_specs=[SMEM] * 2 + [VMEM] * (len(thick) + len(flat) + len(others)) + after(wait),
        out_specs=[VMEM] * len(steps),
        out_shape=[whole if s == 0 else inner for s in steps],
        compiler_params=params(),
        cost_estimate=cost(len(steps) * S * L * L * R * N * (5 + 2 * F), 4 * R * N * L * (F + 1) * (S + len(steps))),
        name="remap_parts",
    )(place, weights, *thick, *flat, *others, *wait)


def remap_edge_kernel(counts, near_fields, place_ref, weight_ref, *refs):
    G = counts[0] * counts[1]
    edge_refs, near_refs, rest_refs = refs[:G], refs[G : 2 * G], refs[2 * G : 3 * G]
    edge_out_ref, thick_out_ref, near_out_ref = refs[-3:]
    place = (place_ref[0], place_ref[1])

    def store_edge(s, i, at, columns, target, means):
        thick_out_ref[i, at, columns] = target
        for f, value in enumerate(means):
            edge_out_ref[f, i, at, columns] = value

    def store_near(s, i, at, columns, target, means):
        for f, value in enumerate(means):
            near_out_ref[f, i, at, columns] = value

    fields = [[(ref, f) for ref in edge_refs] for f in range(1, edge_refs[0].shape[0])]
    remap_rows(place, weight_ref, counts, (0,), edge_refs, fields, [], store_edge)
    bundles = (near_refs, rest_refs)
    fields = [[(ref, index) for ref in bundles[which]] for which, index in near_fields]
    remap_rows(place, weight_ref, counts, (0,), near_refs, fields, [], store_near)


def remap_edges(counts, place, weights, edges, near, near_rest, wait=()):
    F, L, R, N = edges[0].shape
    T = F - 3
    near_fields = tuple((0, 1) if f == 0 else (1, f - 1) for f in range(T))
    operands = [*edges, *near, *near_rest]
    return pl.pallas_call(
        functools.partial(remap_edge_kernel, counts, near_fields),
        in_specs=[SMEM] * 2 + [VMEM] * len(operands) + after(wait),
        out_specs=[VMEM] * 3,
        out_shape=[
            jax.ShapeDtypeStruct((F - 1, L, R, N), jnp.float32),
            jax.ShapeDtypeStruct((L, R, N), jnp.float32),
            jax.ShapeDtypeStruct((T, L, R, N), jnp.float32),
        ],
        compiler_params=params(),
        cost_estimate=cost(len(edges) * L * L * R * N * 40, 4 * R * N * L * len(operands) * F),
        name="remap_edges",
    )(place, weights, *operands, *wait)


def finish_kernel(counts, margin, place_ref, weight_ref, *refs):
    C, S = counts
    group_refs, refs = refs[:S], refs[S:]
    other_refs, refs = refs[:2], refs[2:]
    *arrived_refs, near_ref, edge_ref, thick_edge_ref, out_ref, thick_out_ref, token_ref = refs
    token_ref[...] = jnp.zeros_like(token_ref)
    T, L, R, _ = out_ref.shape

    def store(s, i, at, columns, target, means):
        thick_out_ref[i, at, columns] = target
        lower, upper = inner_part(at, margin, R)
        for f, value in enumerate(means):
            total = value[lower - at.start : upper - at.start]
            start = (f * L + i) * (R - 2 * margin) - margin
            for ref in arrived_refs:
                total = total + ref[start + lower : start + upper, columns]
            out_ref[f, i, lower:upper, columns] = total

    fields = [[(ref, 1 + f) for ref in group_refs] for f in range(T)]
    remap_rows((place_ref[0], place_ref[1]), weight_ref, counts, (0,), group_refs, fields, other_refs, store)
    for i in range(L):
        for row, j in ((0, 0), (R - 1, 1)):
            thick_out_ref[i, row : row + 1] = thick_edge_ref[i, j : j + 1]
            for f in range(T):
                out_ref[f, i, row : row + 1] = edge_ref[2 + f, i, j : j + 1]
        for row, j in ((1, 0), (R - 2, 1)):
            for f in range(T):
                out_ref[f, i, row : row + 1] = near_ref[f, i, j : j + 1]


def finish_tracers(counts, place, weights, group, others, arrived, near, edge, thick_edge):
    margin = 2
    C, S = counts
    T = group[0].shape[0] - 1
    _, L, R, N = group[0].shape
    operands = list(group) + list(others) + list(arrived) + [near, edge, thick_edge]
    return pl.pallas_call(
        functools.partial(finish_kernel, counts, margin),
        in_specs=[SMEM] * 2 + [VMEM] * len(operands),
        out_specs=[VMEM] * 3,
        out_shape=[
            jax.ShapeDtypeStruct((T, L, R, N), jnp.float32),
            jax.ShapeDtypeStruct((L, R, N), jnp.float32),
            jax.ShapeDtypeStruct((8, LANES), jnp.float32),
        ],
        compiler_params=params(),
        cost_estimate=cost(S * L * L * R * N * (5 + 2 * T), 4 * R * N * L * (T + 1) * (S + 2)),
        name="finish_tracers",
    )(place, weights, *operands)


def finish_winds_kernel(count, own_ref, edge_ref, *refs):
    arrived_refs, out_refs = refs[:count], refs[-2:]
    _, L, R, N = own_ref.shape
    for f, out_ref in enumerate(out_refs):
        for i in range(L):
            start = (f * L + i) * (R - 2)
            total = own_ref[f, i, 1 : R - 1]
            for ref in arrived_refs:
                total = total + ref[start : start + R - 2]
            out_ref[i, 1 : R - 1] = total
            out_ref[i, 0:1] = edge_ref[f, i, 0:1]
            out_ref[i, R - 1 : R] = edge_ref[f, i, 1:2]


def finish_winds(own, arrived, edge, wait):
    return pl.pallas_call(
        functools.partial(finish_winds_kernel, len(arrived)),
        in_specs=[VMEM] * (2 + len(arrived)) + after(wait),
        out_specs=[VMEM] * 2,
        out_shape=[jax.ShapeDtypeStruct(own.shape[1:], jnp.float32)] * 2,
        compiler_params=params(),
        cost_estimate=cost(own.size, 12 * own.size),
        name="finish_winds",
    )(own, edge, *arrived, *wait)


def hand_on_kernel(count, *refs):
    for source_ref, copy_ref in zip(refs[:count], refs[len(refs) - count :]):
        copy_ref[...] = source_ref[...]


def hand_on(arrays, wait):
    return pl.pallas_call(
        functools.partial(hand_on_kernel, len(arrays)),
        in_specs=[VMEM] * len(arrays) + after(wait),
        out_specs=[VMEM] * len(arrays),
        out_shape=[jax.ShapeDtypeStruct(a.shape, a.dtype) for a in arrays],
        compiler_params=params(),
        cost_estimate=cost(1e10, 1e9),
        name="hand_on",
    )(*arrays, *wait)


def shifted(value, lev_count, sub_count, s, t):
    if t == 0:
        return lax.ppermute(value, "lev", [(i, (i + s) % lev_count) for i in range(lev_count)])
    if s == 0:
        return lax.ppermute(value, "sub", [(i, (i + t) % sub_count) for i in range(sub_count)])
    pairs = [
        (i * sub_count + j, (i + s) % lev_count * sub_count + (j + t) % sub_count)
        for i in range(lev_count)
        for j in range(sub_count)
    ]
    return lax.ppermute(value, ("lev", "sub"), pairs)


def per_device(thickness, wind_u, wind_v, tracers, level_weights, cutoff):
    L, R, N = thickness.shape
    lat_count = lax.axis_size("lat")
    C, S = lax.axis_size("lev"), lax.axis_size("sub")
    lat_rows = R * lat_count
    send = functools.partial(shifted, lev_count=C, sub_count=S)

    T = tracers.shape[0]
    northward = [(i, i + 1) for i in range(lat_count - 1)]
    southward = [(j, i) for i, j in northward]
    band = lax.axis_index("lat").astype(jnp.int32).reshape(1)
    table = jnp.asarray(geometry_table(lat_rows, R))
    place = jnp.stack([lax.axis_index("lev"), lax.axis_index("sub")]).astype(jnp.int32)
    away = range(1, C)

    def with_others_of_chip(own):
        return [own] + [send(own, s=0, t=t) for t in range(1, S)]

    def sent(parts):
        return [send(part, s=s, t=0) for s, part in zip(away, parts)]

    remap = functools.partial(remap_parts, (C, S), place, level_weights)

    new, own_sum = first_step(band, table, thickness, wind_u, wind_v)
    others = [send(own_sum, s=s, t=t) for s in away for t in range(S)]
    inner, last, leading, near, near_rest = inner_step(band, table, thickness, wind_u, wind_v, new, tracers)
    group = with_others_of_chip(inner)
    near = [near] + [send(near, s=s, t=0) for s in away]
    near_rest = [near_rest] + [send(near_rest, s=s, t=0) for s in away]
    others = other_chips((C, S), place, own_sum, others)
    tracer_fields = [(0, 1 + c) for c in range(T)]
    away_parts = remap(group, [group], others, tracer_fields, away, 2)
    arrived = sent(away_parts)

    last, leading = hand_on((last, leading), [away_parts[0], *near[1:2], *near_rest[1:2]])
    up = lax.ppermute(last, "lat", northward)
    down = lax.ppermute(leading, "lat", southward)
    u, v, edge = second_step(band, table, lat_rows, thickness, wind_u, wind_v, tracers, up, down, cutoff)
    edges = [edge] + [send(edge, s=s, t=0) for s in away]
    winds = [with_others_of_chip(u), with_others_of_chip(v)]
    winds_own, *winds_away = remap(group, winds, others, [(0, 0), (1, 0)], range(C), 1, wait=arrived[:1])
    winds_arrived = sent(winds_away)
    near, near_rest, edges = (
        [a for own in sources for a in with_others_of_chip(own)] for sources in (near, near_rest, edges)
    )
    edge_out, thick_edge, near_out = remap_edges(
        (C, S), place, level_weights, edges, near, near_rest, wait=winds_away[:1]
    )

    tracers_out, thickness_out, token = finish_tracers(
        (C, S), place, level_weights, group, others, arrived, near_out, edge_out, thick_edge
    )
    u_out, v_out = finish_winds(winds_own, winds_arrived, edge_out, [token])
    return thickness_out, u_out, v_out, tracers_out


def solution(mesh):
    placed = (
        P(("member", "lev", "sub"), "lat", None),
        P(("member", "lev", "sub"), "lat", None),
        P(("member", "lev", "sub"), "lat", None),
        P("member", ("lev", "sub"), "lat", None),
        P(),
        P("lat"),
    )
    return jax.shard_map(
        per_device,
        mesh=mesh,
        in_specs=placed,
        out_specs=(
            P(("member", "lev", "sub"), "lat", None),
            P(("member", "lev", "sub"), "lat", None),
            P(("member", "lev", "sub"), "lat", None),
            P("member", ("lev", "sub"), "lat", None),
        ),
        check_vma=False,
    )
```

```python
import functools

import jax
import jax.numpy as jnp
import ml_dtypes
import numpy as np
from jax import lax
from jax.experimental import pallas as pl
from jax.experimental.pallas import tpu as pltpu
from jax.sharding import PartitionSpec as P

LANES = 128
VMEM = pl.BlockSpec(memory_space=pltpu.VMEM)
SMEM = pl.BlockSpec(memory_space=pltpu.SMEM)


def params():
    return pltpu.CompilerParams(vmem_limit_bytes=16 * 1024 * 1024)


def cost(flops, bytes_accessed):
    return pl.CostEstimate(flops=int(flops), bytes_accessed=int(bytes_accessed), transcendentals=0)


def after(arrays):
    return [pl.BlockSpec(memory_space=pl.ANY)] * len(arrays)


def geometry_table(lat_rows, band_rows):
    bands = lat_rows // band_rows
    table = np.zeros((bands, band_rows + 8, LANES), np.float32)
    for band in range(bands):
        for j in range(band_rows + 1):
            row = band * band_rows + j
            south = np.sin(row * np.pi / lat_rows) if 0 < row < lat_rows else 0.0
            north = np.sin((row + 1) * np.pi / lat_rows) if row + 1 < lat_rows else 0.0
            table[band, j, 0] = south
            table[band, j, 1] = north
            table[band, j, 2] = 1.0 / np.sin((row + 0.5) * np.pi / lat_rows)
    return table


def east_of(value):
    return pltpu.roll(value, value.shape[1] - 1, 1)


def west_of(value):
    return pltpu.roll(value, 1, 1)


def row_ids(shape):
    return lax.broadcasted_iota(jnp.int32, shape, 0)


def north_of(value, beyond):
    rows = value.shape[0]
    return jnp.where(row_ids(value.shape) == rows - 1, beyond, pltpu.roll(value, rows - 1, 0))


def south_of(value, beyond):
    return jnp.where(row_ids(value.shape) == 0, beyond, pltpu.roll(value, 1, 0))


def fluxes(geo, thick, u, v, thick_s, v_s, thick_n):
    rows = thick.shape[0]
    east = u * jnp.where(u > 0, thick, east_of(thick))
    north = v * jnp.where(v > 0, thick, north_of(thick, thick_n)) * geo[0:rows, 1:2]
    below = v_s * jnp.where(v_s > 0, thick_s, thick[0:1]) * geo[0:1, 0:1]
    return east, north, below


def tracer_change(q, q_s, q_n, thick, u, v, v_s, east, north, below, inverse):
    t_east = east * jnp.where(u > 0, q, east_of(q))
    t_north = north * jnp.where(v > 0, q, north_of(q, q_n))
    t_below = below * jnp.where(v_s > 0, q_s, q[0:1])
    change = thick * q - (t_east - west_of(t_east))
    return change - (t_north - south_of(t_north, t_below)) * inverse


def inner_kernel(band_ref, table_hbm, thick_hbm, u_hbm, v_hbm, tracer_hbm, *refs):
    out_ref, sum_ref, last_ref, leading_ref, near_ref, near_rest_ref, geo_ref, wind_ref, tracer_ref, sems = refs
    T, L, rows, width = tracer_ref.shape

    def copies(k):
        return [
            pltpu.make_async_copy(thick_hbm.at[k], wind_ref.at[0, k], sems.at[0, k]),
            pltpu.make_async_copy(u_hbm.at[k], wind_ref.at[1, k], sems.at[1, k]),
            pltpu.make_async_copy(v_hbm.at[k], wind_ref.at[2, k], sems.at[2, k]),
        ] + [
            pltpu.make_async_copy(tracer_hbm.at[c, k], tracer_ref.at[c, k], sems.at[3 + c, k]) for c in range(T)
        ]

    table_copy = pltpu.make_async_copy(table_hbm.at[band_ref[0]], geo_ref, sems.at[3 + T, 0])
    table_copy.start()
    for k in range(L):
        for copy in copies(k):
            copy.start()
    table_copy.wait()
    geo = geo_ref[...]
    nothing = jnp.zeros((1, width), jnp.float32)
    inverse = geo[0:rows, 2:3]
    sum_ref[...] = jnp.zeros_like(sum_ref)

    def level(k, carry):
        for copy in copies(k):
            copy.wait()
        thick, u, v = wind_ref[0, k], wind_ref[1, k], wind_ref[2, k]
        east, north, below = fluxes(geo, thick, u, v, nothing, nothing, nothing)
        new = thick - (east - west_of(east)) - (north - south_of(north, below)) * inverse

        def store(field, value):
            out_ref[field, k] = value
            ref, at = (near_ref, field) if field < 2 else (near_rest_ref, field - 2)
            ref[at, k, 0:1] = value[1:2]
            ref[at, k, 1:2] = value[rows - 2 : rows - 1]

        store(0, new)
        sum_ref[...] += new
        last_ref[0, k] = thick[rows - 1 : rows]
        last_ref[1, k] = v[rows - 1 : rows]
        leading_ref[0, k] = thick[0:1]
        leading_ref[1, k] = thick[1:2]
        leading_ref[2, k] = u[0:1]
        leading_ref[3, k] = v[0:1]
        scale = 1.0 / new
        for c in range(T):
            q = tracer_ref[c, k]
            last_ref[2 + c, k] = q[rows - 1 : rows]
            leading_ref[4 + c, k] = q[0:1]
            change = tracer_change(q, nothing, nothing, thick, u, v, nothing, east, north, below, inverse)
            store(1 + c, change * scale)
        return carry

    lax.fori_loop(0, L, level, 0)


def inner_step(band, table, thickness, wind_u, wind_v, tracers):
    L, R, N = thickness.shape
    T = tracers.shape[0]
    shape = lambda n, rows: jax.ShapeDtypeStruct((n, L, rows, N), jnp.float32)
    in_hbm = lambda x: pltpu.with_memory_space_constraint(x, pltpu.HBM)
    out_shape = [
        shape(1 + T, R),
        jax.ShapeDtypeStruct((R, N), jnp.float32),
        shape(2 + T, 1),
        shape(4 + T, 1),
        shape(2, 2),
        shape(T - 1, 2),
    ]
    return pl.pallas_call(
        inner_kernel,
        in_specs=[SMEM] + after([table, thickness, wind_u, wind_v, tracers]),
        out_specs=[VMEM] * len(out_shape),
        out_shape=out_shape,
        scratch_shapes=[
            pltpu.VMEM(table.shape[1:], jnp.float32),
            pltpu.VMEM((3, L, R, N), jnp.float32),
            pltpu.VMEM((T, L, R, N), jnp.float32),
            pltpu.SemaphoreType.DMA((4 + T, L)),
        ],
        compiler_params=params(),
        cost_estimate=cost(130 * L * R * N, 4 * L * R * N * (8 + 2 * T)),
        name="inner_step",
    )(band, *[in_hbm(a) for a in (table, thickness, wind_u, wind_v, tracers)])


def filter_tables(N):
    A = N // LANES
    b = np.arange(LANES)[:, None]
    p = np.arange(LANES)[None, :]
    tables = []
    for q in range(A // 2 + 1):
        angle = 2.0 * np.pi * ((b * (A * p + q)) % N) / N
        c, s = np.cos(angle), np.sin(angle)
        tables.append(np.block([[c, -s], [s, c]]))
    table = np.stack(tables)
    high = table.astype(np.float32).astype(ml_dtypes.bfloat16)
    low = (table - high.astype(np.float64)).astype(np.float32).astype(ml_dtypes.bfloat16)
    return high, low


def split(value):
    high = value.astype(jnp.bfloat16)
    return high, (value - high.astype(jnp.float32)).astype(jnp.bfloat16)


def product(value, high, low, transposed):
    dims = (((1,), (1 if transposed else 0,)), ((), ()))
    dot = lambda x, y: lax.dot_general(x, y, dims, preferred_element_type=jnp.float32)
    v_high, v_low = split(value)
    return dot(v_high, high) + (dot(v_high, low) + dot(v_low, high))


def filter_rows(x, cutoff, high_ref, low_ref):
    A = len(x)
    N = A * LANES
    half = A // 2
    even = [x[a] + x[A - a] for a in range(1, half + 1)]
    odd = [x[a] - x[A - a] for a in range(1, half + 1)]
    angle = lambda q, a: 2.0 * np.pi * ((q * a) % A) / A
    p = lax.broadcasted_iota(jnp.int32, cutoff.shape, 1)
    real, imag = [], []
    for q in range(half + 1):
        re = x[0]
        for a in range(1, half + 1):
            re = re + (even[a - 1] if q == 0 else float(np.cos(angle(q, a))) * even[a - 1])
        if q == 0:
            high, low = high_ref[0, 0:LANES], low_ref[0, 0:LANES]
            spectrum = product(re, high, low, False)
        else:
            high, low = high_ref[q], low_ref[q]
            im = -float(np.sin(angle(q, 1))) * odd[0]
            for a in range(2, half + 1):
                im = im - float(np.sin(angle(q, a))) * odd[a - 1]
            spectrum = product(jnp.concatenate([re, im], axis=1), high, low, False)
        mode = A * p + q
        factor = 1.0 / N if q == 0 else 2.0 / N
        kept = jnp.where(jnp.minimum(mode, N - mode) <= cutoff, factor, 0.0)
        back = product(spectrum * jnp.concatenate([kept, kept], axis=1), high, low, True)
        real.append(back[:, :LANES])
        imag.append(back[:, LANES:])
    out = [None] * A
    out[0] = functools.reduce(jnp.add, real)
    for a in range(1, half + 1):
        even_part, odd_part = real[0], None
        for q in range(1, half + 1):
            even_part = even_part + float(np.cos(angle(q, a))) * real[q]
            term = float(np.sin(angle(q, a))) * imag[q]
            odd_part = term if odd_part is None else odd_part + term
        out[a] = even_part - odd_part
        out[A - a] = even_part + odd_part
    return out


def second_kernel(
    lat_rows, band_ref, table_ref, thick_ref, u_ref, v_ref, tracer_ref, up_ref, down_ref, cutoff_ref, high_ref, low_ref, *refs
):
    *wind_refs, edge_ref, new_wind = refs
    k = pl.program_id(0)
    _, L, rows, width = new_wind.shape
    geo = table_ref[band_ref[0]]
    thick, u, v = thick_ref[0], u_ref[0], v_ref[0]
    thick_s, v_s = up_ref[0, 0], up_ref[1, 0]
    thick_n, thick_nn, u_n, v_n = (down_ref[i, 0] for i in range(4))
    east, north, below = fluxes(geo, thick, u, v, thick_s, v_s, thick_n)
    inverse = geo[0:rows, 2:3]
    new = thick - (east - west_of(east)) - (north - south_of(north, below)) * inverse
    east_n = u_n * jnp.where(u_n > 0, thick_n, east_of(thick_n))
    north_n = v_n * jnp.where(v_n > 0, thick_n, thick_nn) * geo[rows : rows + 1, 1:2]
    new_n = (
        thick_n
        - (east_n - west_of(east_n))
        - (north_n - north[rows - 1 : rows]) * geo[rows : rows + 1, 2:3]
    )
    new_wind[0, k] = u - 0.05 * (east_of(new) - new)
    inside = band_ref[0] * rows + row_ids(new.shape) < lat_rows - 1
    new_wind[1, k] = jnp.where(inside, v - 0.05 * (north_of(new, new_n) - new), 0.0)

    def store_edges(field, level, value):
        edge_ref[field, level, 0:1] = value[0:1]
        edge_ref[field, level, 1:2] = value[rows - 1 : rows]

    store_edges(0, k, new)
    scale = 1.0 / new
    for c in range(tracer_ref.shape[0]):
        change = tracer_change(
            tracer_ref[c, 0], up_ref[2 + c, 0], down_ref[4 + c, 0], thick, u, v, v_s, east, north, below, inverse
        )
        store_edges(3 + c, k, change * scale)

    @pl.when(k == L - 1)
    def _():
        pieces = [
            new_wind[:, :, :, a * LANES : (a + 1) * LANES].reshape(2 * L * rows, LANES) for a in range(width // LANES)
        ]
        cutoff = jnp.broadcast_to(cutoff_ref[...][None], (2 * L, rows, LANES)).reshape(2 * L * rows, LANES)
        for a, piece in enumerate(filter_rows(pieces, cutoff, high_ref, low_ref)):
            piece = piece.reshape(2, L, rows, LANES)
            for f in range(2):
                wind_refs[f][0, :, :, a * LANES : (a + 1) * LANES] = piece[f]
        for f in range(2):
            for level in range(L):
                store_edges(1 + f, level, wind_refs[f][0, level])


def second_step(band, table, lat_rows, thickness, wind_u, wind_v, tracers, up, down, cutoff):
    L, R, N = thickness.shape
    T = tracers.shape[0]
    high, low = filter_tables(N)
    level = pl.BlockSpec((1, R, N), lambda k: (k, 0, 0))
    some = lambda n, rows: pl.BlockSpec((n, 1, rows, N), lambda k: (0, k, 0, 0))
    whole = lambda shape: pl.BlockSpec(shape, lambda k: (0,) * len(shape))
    return pl.pallas_call(
        functools.partial(second_kernel, lat_rows),
        grid=(L,),
        in_specs=[SMEM, whole(table.shape), level, level, level, some(T, R), some(2 + T, 1), some(4 + T, 1)]
        + [whole((R, LANES)), whole(high.shape), whole(low.shape)],
        out_specs=[whole((1, L, R, N)), whole((1, L, R, N)), whole((3 + T, L, 2, N))],
        out_shape=[
            jax.ShapeDtypeStruct((1, L, R, N), jnp.float32),
            jax.ShapeDtypeStruct((1, L, R, N), jnp.float32),
            jax.ShapeDtypeStruct((3 + T, L, 2, N), jnp.float32),
        ],
        scratch_shapes=[pltpu.VMEM((2, L, R, N), jnp.float32)],
        compiler_params=params(),
        cost_estimate=cost(12 * 2 * L * R * high.size, 4 * L * R * N * (8 + T)),
        name="second_step",
    )(
        band, table, thickness, wind_u, wind_v, tracers, up, down,
        jnp.broadcast_to(cutoff[:, None], (R, LANES)), jnp.asarray(high), jnp.asarray(low),
    )


def weight_sums(weight_ref, firsts, L, levels):
    total = jnp.float32(0.0)
    below = [jnp.float32(0.0) for _ in firsts]
    for k in range(levels):
        w = weight_ref[k]
        below = [b + jnp.where(k < first, w, 0.0) for b, first in zip(below, firsts)]
        total = total + w
    weights = [[weight_ref[first + i] for i in range(L)] for first in firsts]
    sums = []
    for start, row in zip(below, weights):
        sums.append([start])
        for w in row:
            sums[-1].append(sums[-1][-1] + w)
    return total, weights, sums


def source_levels(place, counts, thick, others):
    C, S = counts
    lev, sub = place
    spot = [lax.rem(lev - g // S + C, C) * S + lax.rem(sub - g % S + S, S) for g in range(len(thick))]
    group = [functools.reduce(jnp.add, levels) for levels in thick]
    mass = functools.reduce(jnp.add, group)
    base = jnp.zeros_like(mass)
    for s, other in enumerate(others, 1):
        mass = mass + other
        base = base + jnp.where(lev >= s, other, 0.0)
    sources = []
    for g, levels in enumerate(thick):
        low = base
        for other in range(len(thick)):
            if other != g:
                low = low + jnp.where(spot[other] < spot[g], group[other], 0.0)
        for m, value in enumerate(levels):
            sources.append((g, m, low, value))
            low = low + value
    return mass, sources


def covered(top, sources):
    return [jnp.minimum(jnp.maximum(top - low, 0.0), value) for _, _, low, value in sources]


def remap_rows(place, weight_ref, counts, steps, thick_refs, field_refs, other_refs, store):
    C, S = counts
    G = len(thick_refs) // S
    _, L, R, N = thick_refs[0].shape
    lev, sub = place
    firsts = [(lax.rem(lev + s, C) * S + sub) * L for s in steps]
    weight_sum, weights, sums = weight_sums(weight_ref, firsts, L, C * S * L)

    def tile(at, columns):
        thick = [[ref[0, m, at, columns] for m in range(L)] for ref in thick_refs]
        others = [
            functools.reduce(jnp.add, [ref[at, columns] for ref in other_refs[s * S : (s + 1) * S]])
            for s in range(C - G)
        ]
        mass, sources = source_levels(place, counts, thick, others)
        unit = mass / weight_sum
        for index, s in enumerate(steps):
            below = covered(unit * sums[index][0], sources)
            for i in range(L):
                upto = covered(unit * sums[index][i + 1], sources)
                part = [a - b for a, b in zip(upto, below)]
                below = upto
                target = unit * weights[index][i]
                scale = 1.0 / target
                means = []
                for refs in field_refs:
                    terms = [refs[g][0][refs[g][1], m, at, columns] * w for (g, m, _, _), w in zip(sources, part)]
                    means.append(functools.reduce(jnp.add, terms) * scale)
                store(s, i, at, columns, target, means)

    rows = min(R, 8)
    for r in range(0, R, rows):

        def body(c, carry):
            tile(slice(r, r + rows), pl.ds(pl.multiple_of(c * LANES, LANES), LANES))
            return carry

        lax.fori_loop(0, N // LANES, body, 0)


def inner_part(at, margin, rows):
    return max(at.start, margin), min(at.stop, rows - margin)


def remap_kernel(counts, steps, fields, margin, sizes, place_ref, weight_ref, *refs):
    C, S = counts
    thick_refs, refs = refs[:S], refs[S:]
    bundles = []
    for _ in range(sizes[0]):
        bundles.append(refs[:S])
        refs = refs[S:]
    other_refs, out_refs = refs[: (C - 1) * S], refs[len(refs) - len(steps) :]
    _, L, R, _ = thick_refs[0].shape
    field_refs = [[(ref, index) for ref in bundles[which]] for which, index in fields]

    def store(s, i, at, columns, target, means):
        out_ref = out_refs[steps.index(s)]
        for f, value in enumerate(means):
            if s == 0:
                out_ref[f, i, at, columns] = value
            else:
                lower, upper = inner_part(at, margin, R)
                start = (f * L + i) * (R - 2 * margin) - margin
                out_ref[start + lower : start + upper, columns] = value[lower - at.start : upper - at.start]

    remap_rows(
        (place_ref[0], place_ref[1]), weight_ref, counts, steps, thick_refs, field_refs, other_refs, store
    )


def remap_parts(counts, place, weights, thick, bundles, others, fields, steps, margin, wait=()):
    C, S = counts
    _, L, R, N = thick[0].shape
    F = len(fields)
    whole = jax.ShapeDtypeStruct((F, L, R, N), jnp.float32)
    inner = jax.ShapeDtypeStruct((F * L * (R - 2 * margin), N), jnp.float32)
    flat = [a for bundle in bundles for a in bundle]
    return pl.pallas_call(
        functools.partial(remap_kernel, counts, tuple(steps), tuple(fields), margin, (len(bundles),)),
        in_specs=[SMEM] * 2 + [VMEM] * (len(thick) + len(flat) + len(others)) + after(wait),
        out_specs=[VMEM] * len(steps),
        out_shape=[whole if s == 0 else inner for s in steps],
        compiler_params=params(),
        cost_estimate=cost(len(steps) * S * L * L * R * N * (5 + 2 * F), 4 * R * N * L * (F + 1) * (S + len(steps))),
        name="remap_parts",
    )(place, weights, *thick, *flat, *others, *wait)


def remap_edge_kernel(counts, near_fields, place_ref, weight_ref, *refs):
    G = counts[0] * counts[1]
    edge_refs, near_refs, rest_refs = refs[:G], refs[G : 2 * G], refs[2 * G : 3 * G]
    edge_out_ref, thick_out_ref, near_out_ref = refs[-3:]
    place = (place_ref[0], place_ref[1])

    def store_edge(s, i, at, columns, target, means):
        thick_out_ref[i, at, columns] = target
        for f, value in enumerate(means):
            edge_out_ref[f, i, at, columns] = value

    def store_near(s, i, at, columns, target, means):
        for f, value in enumerate(means):
            near_out_ref[f, i, at, columns] = value

    fields = [[(ref, f) for ref in edge_refs] for f in range(1, edge_refs[0].shape[0])]
    remap_rows(place, weight_ref, counts, (0,), edge_refs, fields, [], store_edge)
    bundles = (near_refs, rest_refs)
    fields = [[(ref, index) for ref in bundles[which]] for which, index in near_fields]
    remap_rows(place, weight_ref, counts, (0,), near_refs, fields, [], store_near)


def remap_edges(counts, place, weights, edges, near, near_rest, wait=()):
    F, L, R, N = edges[0].shape
    T = F - 3
    near_fields = tuple((0, 1) if f == 0 else (1, f - 1) for f in range(T))
    operands = [*edges, *near, *near_rest]
    return pl.pallas_call(
        functools.partial(remap_edge_kernel, counts, near_fields),
        in_specs=[SMEM] * 2 + [VMEM] * len(operands) + after(wait),
        out_specs=[VMEM] * 3,
        out_shape=[
            jax.ShapeDtypeStruct((F - 1, L, R, N), jnp.float32),
            jax.ShapeDtypeStruct((L, R, N), jnp.float32),
            jax.ShapeDtypeStruct((T, L, R, N), jnp.float32),
        ],
        compiler_params=params(),
        cost_estimate=cost(len(edges) * L * L * R * N * 40, 4 * R * N * L * len(operands) * F),
        name="remap_edges",
    )(place, weights, *operands, *wait)


def finish_kernel(counts, margin, place_ref, weight_ref, *refs):
    C, S = counts
    group_refs, refs = refs[:S], refs[S:]
    other_refs, refs = refs[: (C - 1) * S], refs[(C - 1) * S :]
    *arrived_refs, near_ref, edge_ref, thick_edge_ref, out_ref, thick_out_ref, token_ref = refs
    token_ref[...] = jnp.zeros_like(token_ref)
    T, L, R, _ = out_ref.shape

    def store(s, i, at, columns, target, means):
        thick_out_ref[i, at, columns] = target
        lower, upper = inner_part(at, margin, R)
        for f, value in enumerate(means):
            total = value[lower - at.start : upper - at.start]
            start = (f * L + i) * (R - 2 * margin) - margin
            for ref in arrived_refs:
                total = total + ref[start + lower : start + upper, columns]
            out_ref[f, i, lower:upper, columns] = total

    fields = [[(ref, 1 + f) for ref in group_refs] for f in range(T)]
    remap_rows((place_ref[0], place_ref[1]), weight_ref, counts, (0,), group_refs, fields, other_refs, store)
    for i in range(L):
        for row, j in ((0, 0), (R - 1, 1)):
            thick_out_ref[i, row : row + 1] = thick_edge_ref[i, j : j + 1]
            for f in range(T):
                out_ref[f, i, row : row + 1] = edge_ref[2 + f, i, j : j + 1]
        for row, j in ((1, 0), (R - 2, 1)):
            for f in range(T):
                out_ref[f, i, row : row + 1] = near_ref[f, i, j : j + 1]


def finish_tracers(counts, place, weights, group, others, arrived, near, edge, thick_edge):
    margin = 2
    C, S = counts
    T = group[0].shape[0] - 1
    _, L, R, N = group[0].shape
    operands = list(group) + list(others) + list(arrived) + [near, edge, thick_edge]
    return pl.pallas_call(
        functools.partial(finish_kernel, counts, margin),
        in_specs=[SMEM] * 2 + [VMEM] * len(operands),
        out_specs=[VMEM] * 3,
        out_shape=[
            jax.ShapeDtypeStruct((T, L, R, N), jnp.float32),
            jax.ShapeDtypeStruct((L, R, N), jnp.float32),
            jax.ShapeDtypeStruct((8, LANES), jnp.float32),
        ],
        compiler_params=params(),
        cost_estimate=cost(S * L * L * R * N * (5 + 2 * T), 4 * R * N * L * (T + 1) * (S + 2)),
        name="finish_tracers",
    )(place, weights, *operands)


def finish_winds_kernel(count, own_ref, edge_ref, *refs):
    arrived_refs, out_refs = refs[:count], refs[-2:]
    _, L, R, N = own_ref.shape
    for f, out_ref in enumerate(out_refs):
        for i in range(L):
            start = (f * L + i) * (R - 2)
            total = own_ref[f, i, 1 : R - 1]
            for ref in arrived_refs:
                total = total + ref[start : start + R - 2]
            out_ref[i, 1 : R - 1] = total
            out_ref[i, 0:1] = edge_ref[f, i, 0:1]
            out_ref[i, R - 1 : R] = edge_ref[f, i, 1:2]


def finish_winds(own, arrived, edge, wait):
    return pl.pallas_call(
        functools.partial(finish_winds_kernel, len(arrived)),
        in_specs=[VMEM] * (2 + len(arrived)) + after(wait),
        out_specs=[VMEM] * 2,
        out_shape=[jax.ShapeDtypeStruct(own.shape[1:], jnp.float32)] * 2,
        compiler_params=params(),
        cost_estimate=cost(own.size, 12 * own.size),
        name="finish_winds",
    )(own, edge, *arrived, *wait)


def hand_on_kernel(count, *refs):
    for source_ref, copy_ref in zip(refs[:count], refs[len(refs) - count :]):
        copy_ref[...] = source_ref[...]


def hand_on(arrays, wait):
    return pl.pallas_call(
        functools.partial(hand_on_kernel, len(arrays)),
        in_specs=[VMEM] * len(arrays) + after(wait),
        out_specs=[VMEM] * len(arrays),
        out_shape=[jax.ShapeDtypeStruct(a.shape, a.dtype) for a in arrays],
        compiler_params=params(),
        cost_estimate=cost(1e10, 1e9),
        name="hand_on",
    )(*arrays, *wait)


def shifted(value, lev_count, sub_count, s, t):
    if t == 0:
        return lax.ppermute(value, "lev", [(i, (i + s) % lev_count) for i in range(lev_count)])
    if s == 0:
        return lax.ppermute(value, "sub", [(i, (i + t) % sub_count) for i in range(sub_count)])
    pairs = [
        (i * sub_count + j, (i + s) % lev_count * sub_count + (j + t) % sub_count)
        for i in range(lev_count)
        for j in range(sub_count)
    ]
    return lax.ppermute(value, ("lev", "sub"), pairs)


def per_device(thickness, wind_u, wind_v, tracers, level_weights, cutoff):
    L, R, N = thickness.shape
    lat_count = lax.axis_size("lat")
    C, S = lax.axis_size("lev"), lax.axis_size("sub")
    lat_rows = R * lat_count
    send = functools.partial(shifted, lev_count=C, sub_count=S)

    T = tracers.shape[0]
    northward = [(i, i + 1) for i in range(lat_count - 1)]
    southward = [(j, i) for i, j in northward]
    band = lax.axis_index("lat").astype(jnp.int32).reshape(1)
    table = jnp.asarray(geometry_table(lat_rows, R))
    place = jnp.stack([lax.axis_index("lev"), lax.axis_index("sub")]).astype(jnp.int32)
    away = range(1, C)

    def with_others_of_chip(own):
        return [own] + [send(own, s=0, t=t) for t in range(1, S)]

    def sent(parts):
        return [send(part, s=s, t=0) for s, part in zip(away, parts)]

    remap = functools.partial(remap_parts, (C, S), place, level_weights)

    inner, own_sum, last, leading, near, near_rest = inner_step(band, table, thickness, wind_u, wind_v, tracers)
    others = [send(own_sum, s=s, t=t) for s in away for t in range(S)]
    group = with_others_of_chip(inner)
    near = [near] + [send(near, s=s, t=0) for s in away]
    near_rest = [near_rest] + [send(near_rest, s=s, t=0) for s in away]
    tracer_fields = [(0, 1 + c) for c in range(T)]
    away_parts = remap(group, [group], others, tracer_fields, away, 2)
    arrived = sent(away_parts)

    last, leading = hand_on((last, leading), [away_parts[0], *near[1:2], *near_rest[1:2]])
    up = lax.ppermute(last, "lat", northward)
    down = lax.ppermute(leading, "lat", southward)
    u, v, edge = second_step(band, table, lat_rows, thickness, wind_u, wind_v, tracers, up, down, cutoff)
    edges = [edge] + [send(edge, s=s, t=0) for s in away]
    winds = [with_others_of_chip(u), with_others_of_chip(v)]
    winds_own, *winds_away = remap(group, winds, others, [(0, 0), (1, 0)], range(C), 1, wait=arrived[:1])
    winds_arrived = sent(winds_away)
    near, near_rest, edges = (
        [a for own in sources for a in with_others_of_chip(own)] for sources in (near, near_rest, edges)
    )
    edge_out, thick_edge, near_out = remap_edges(
        (C, S), place, level_weights, edges, near, near_rest, wait=winds_away[:1]
    )

    tracers_out, thickness_out, token = finish_tracers(
        (C, S), place, level_weights, group, others, arrived, near_out, edge_out, thick_edge
    )
    u_out, v_out = finish_winds(winds_own, winds_arrived, edge_out, [token])
    return thickness_out, u_out, v_out, tracers_out


def solution(mesh):
    placed = (
        P(("member", "lev", "sub"), "lat", None),
        P(("member", "lev", "sub"), "lat", None),
        P(("member", "lev", "sub"), "lat", None),
        P("member", ("lev", "sub"), "lat", None),
        P(),
        P("lat"),
    )
    return jax.shard_map(
        per_device,
        mesh=mesh,
        in_specs=placed,
        out_specs=(
            P(("member", "lev", "sub"), "lat", None),
            P(("member", "lev", "sub"), "lat", None),
            P(("member", "lev", "sub"), "lat", None),
            P("member", ("lev", "sub"), "lat", None),
        ),
        check_vma=False,
    )
```

```python
import functools

import jax
import jax.numpy as jnp
import ml_dtypes
import numpy as np
from jax import lax
from jax.experimental import pallas as pl
from jax.experimental.pallas import tpu as pltpu
from jax.sharding import PartitionSpec as P

LANES = 128
VMEM = pl.BlockSpec(memory_space=pltpu.VMEM)
SMEM = pl.BlockSpec(memory_space=pltpu.SMEM)


def params():
    return pltpu.CompilerParams(vmem_limit_bytes=16 * 1024 * 1024)


def cost(flops, bytes_accessed):
    return pl.CostEstimate(flops=int(flops), bytes_accessed=int(bytes_accessed), transcendentals=0)


def after(arrays):
    return [pl.BlockSpec(memory_space=pl.ANY)] * len(arrays)


def geometry_table(lat_rows, band_rows):
    bands = lat_rows // band_rows
    table = np.zeros((bands, band_rows + 8, LANES), np.float32)
    for band in range(bands):
        for j in range(band_rows + 1):
            row = band * band_rows + j
            south = np.sin(row * np.pi / lat_rows) if 0 < row < lat_rows else 0.0
            north = np.sin((row + 1) * np.pi / lat_rows) if row + 1 < lat_rows else 0.0
            table[band, j, 0] = south
            table[band, j, 1] = north
            table[band, j, 2] = 1.0 / np.sin((row + 0.5) * np.pi / lat_rows)
    return table


def east_of(value):
    return pltpu.roll(value, value.shape[1] - 1, 1)


def west_of(value):
    return pltpu.roll(value, 1, 1)


def row_ids(shape):
    return lax.broadcasted_iota(jnp.int32, shape, 0)


def north_of(value, beyond):
    rows = value.shape[0]
    return jnp.where(row_ids(value.shape) == rows - 1, beyond, pltpu.roll(value, rows - 1, 0))


def south_of(value, beyond):
    return jnp.where(row_ids(value.shape) == 0, beyond, pltpu.roll(value, 1, 0))


def fluxes(geo, thick, u, v, thick_s, v_s, thick_n):
    rows = thick.shape[0]
    east = u * jnp.where(u > 0, thick, east_of(thick))
    north = v * jnp.where(v > 0, thick, north_of(thick, thick_n)) * geo[0:rows, 1:2]
    below = v_s * jnp.where(v_s > 0, thick_s, thick[0:1]) * geo[0:1, 0:1]
    return east, north, below


def tracer_change(q, q_s, q_n, thick, u, v, v_s, east, north, below, inverse):
    t_east = east * jnp.where(u > 0, q, east_of(q))
    t_north = north * jnp.where(v > 0, q, north_of(q, q_n))
    t_below = below * jnp.where(v_s > 0, q_s, q[0:1])
    change = thick * q - (t_east - west_of(t_east))
    return change - (t_north - south_of(t_north, t_below)) * inverse


def inner_kernel(band_ref, table_hbm, thick_hbm, u_hbm, v_hbm, tracer_hbm, *refs):
    out_ref, sum_ref, near_ref, near_rest_ref, geo_ref, wind_ref, tracer_ref, sems = refs
    T, L, rows, width = tracer_ref.shape

    def copies(k):
        return [
            pltpu.make_async_copy(thick_hbm.at[k], wind_ref.at[0, k], sems.at[0, k]),
            pltpu.make_async_copy(u_hbm.at[k], wind_ref.at[1, k], sems.at[1, k]),
            pltpu.make_async_copy(v_hbm.at[k], wind_ref.at[2, k], sems.at[2, k]),
        ] + [
            pltpu.make_async_copy(tracer_hbm.at[c, k], tracer_ref.at[c, k], sems.at[3 + c, k]) for c in range(T)
        ]

    table_copy = pltpu.make_async_copy(table_hbm.at[band_ref[0]], geo_ref, sems.at[3 + T, 0])
    table_copy.start()
    for k in range(L):
        for copy in copies(k):
            copy.start()
    table_copy.wait()
    geo = geo_ref[...]
    nothing = jnp.zeros((1, width), jnp.float32)
    inverse = geo[0:rows, 2:3]
    sum_ref[...] = jnp.zeros_like(sum_ref)

    def level(k, carry):
        for copy in copies(k):
            copy.wait()
        thick, u, v = wind_ref[0, k], wind_ref[1, k], wind_ref[2, k]
        east, north, below = fluxes(geo, thick, u, v, nothing, nothing, nothing)
        new = thick - (east - west_of(east)) - (north - south_of(north, below)) * inverse

        def store(field, value):
            out_ref[field, k] = value
            ref, at = (near_ref, field) if field < 2 else (near_rest_ref, field - 2)
            ref[at, k, 0:1] = value[1:2]
            ref[at, k, 1:2] = value[rows - 2 : rows - 1]

        store(0, new)
        sum_ref[...] += new
        scale = 1.0 / new
        for c in range(T):
            q = tracer_ref[c, k]
            change = tracer_change(q, nothing, nothing, thick, u, v, nothing, east, north, below, inverse)
            store(1 + c, change * scale)
        return carry

    lax.fori_loop(0, L, level, 0)


def inner_step(band, table, thickness, wind_u, wind_v, tracers):
    L, R, N = thickness.shape
    T = tracers.shape[0]
    shape = lambda n, rows: jax.ShapeDtypeStruct((n, L, rows, N), jnp.float32)
    in_hbm = lambda x: pltpu.with_memory_space_constraint(x, pltpu.HBM)
    out_shape = [
        shape(1 + T, R),
        jax.ShapeDtypeStruct((R, N), jnp.float32),
        shape(2, 2),
        shape(T - 1, 2),
    ]
    return pl.pallas_call(
        inner_kernel,
        in_specs=[SMEM] + after([table, thickness, wind_u, wind_v, tracers]),
        out_specs=[VMEM] * len(out_shape),
        out_shape=out_shape,
        scratch_shapes=[
            pltpu.VMEM(table.shape[1:], jnp.float32),
            pltpu.VMEM((3, L, R, N), jnp.float32),
            pltpu.VMEM((T, L, R, N), jnp.float32),
            pltpu.SemaphoreType.DMA((4 + T, L)),
        ],
        compiler_params=params(),
        cost_estimate=cost(130 * L * R * N, 4 * L * R * N * (8 + 2 * T)),
        name="inner_step",
    )(band, *[in_hbm(a) for a in (table, thickness, wind_u, wind_v, tracers)])


def filter_tables(N):
    A = N // LANES
    b = np.arange(LANES)[:, None]
    p = np.arange(LANES)[None, :]
    tables = []
    for q in range(A // 2 + 1):
        angle = 2.0 * np.pi * ((b * (A * p + q)) % N) / N
        c, s = np.cos(angle), np.sin(angle)
        tables.append(np.block([[c, -s], [s, c]]))
    table = np.stack(tables)
    high = table.astype(np.float32).astype(ml_dtypes.bfloat16)
    low = (table - high.astype(np.float64)).astype(np.float32).astype(ml_dtypes.bfloat16)
    return high, low


def split(value):
    high = value.astype(jnp.bfloat16)
    return high, (value - high.astype(jnp.float32)).astype(jnp.bfloat16)


def product(value, high, low, transposed):
    dims = (((1,), (1 if transposed else 0,)), ((), ()))
    dot = lambda x, y: lax.dot_general(x, y, dims, preferred_element_type=jnp.float32)
    v_high, v_low = split(value)
    return dot(v_high, high) + (dot(v_high, low) + dot(v_low, high))


def filter_rows(x, cutoff, high_ref, low_ref):
    A = len(x)
    N = A * LANES
    half = A // 2
    even = [x[a] + x[A - a] for a in range(1, half + 1)]
    odd = [x[a] - x[A - a] for a in range(1, half + 1)]
    angle = lambda q, a: 2.0 * np.pi * ((q * a) % A) / A
    p = lax.broadcasted_iota(jnp.int32, cutoff.shape, 1)
    real, imag = [], []
    for q in range(half + 1):
        re = x[0]
        for a in range(1, half + 1):
            re = re + (even[a - 1] if q == 0 else float(np.cos(angle(q, a))) * even[a - 1])
        if q == 0:
            high, low = high_ref[0, 0:LANES], low_ref[0, 0:LANES]
            spectrum = product(re, high, low, False)
        else:
            high, low = high_ref[q], low_ref[q]
            im = -float(np.sin(angle(q, 1))) * odd[0]
            for a in range(2, half + 1):
                im = im - float(np.sin(angle(q, a))) * odd[a - 1]
            spectrum = product(jnp.concatenate([re, im], axis=1), high, low, False)
        mode = A * p + q
        factor = 1.0 / N if q == 0 else 2.0 / N
        kept = jnp.where(jnp.minimum(mode, N - mode) <= cutoff, factor, 0.0)
        back = product(spectrum * jnp.concatenate([kept, kept], axis=1), high, low, True)
        real.append(back[:, :LANES])
        imag.append(back[:, LANES:])
    out = [None] * A
    out[0] = functools.reduce(jnp.add, real)
    for a in range(1, half + 1):
        even_part, odd_part = real[0], None
        for q in range(1, half + 1):
            even_part = even_part + float(np.cos(angle(q, a))) * real[q]
            term = float(np.sin(angle(q, a))) * imag[q]
            odd_part = term if odd_part is None else odd_part + term
        out[a] = even_part - odd_part
        out[A - a] = even_part + odd_part
    return out


def second_kernel(
    lat_rows, band_ref, table_ref, thick_ref, u_ref, v_ref, tracer_ref, up_ref, down_ref, cutoff_ref, high_ref, low_ref, *refs
):
    *wind_refs, edge_ref, new_wind = refs
    k = pl.program_id(0)
    _, L, rows, width = new_wind.shape
    geo = table_ref[band_ref[0]]
    thick, u, v = thick_ref[0], u_ref[0], v_ref[0]
    thick_s, v_s = up_ref[0, 0], up_ref[1, 0]
    thick_n, thick_nn, u_n, v_n = (down_ref[i, 0] for i in range(4))
    east, north, below = fluxes(geo, thick, u, v, thick_s, v_s, thick_n)
    inverse = geo[0:rows, 2:3]
    new = thick - (east - west_of(east)) - (north - south_of(north, below)) * inverse
    east_n = u_n * jnp.where(u_n > 0, thick_n, east_of(thick_n))
    north_n = v_n * jnp.where(v_n > 0, thick_n, thick_nn) * geo[rows : rows + 1, 1:2]
    new_n = (
        thick_n
        - (east_n - west_of(east_n))
        - (north_n - north[rows - 1 : rows]) * geo[rows : rows + 1, 2:3]
    )
    new_wind[0, k] = u - 0.05 * (east_of(new) - new)
    inside = band_ref[0] * rows + row_ids(new.shape) < lat_rows - 1
    new_wind[1, k] = jnp.where(inside, v - 0.05 * (north_of(new, new_n) - new), 0.0)

    def store_edges(field, level, value):
        edge_ref[field, level, 0:1] = value[0:1]
        edge_ref[field, level, 1:2] = value[rows - 1 : rows]

    store_edges(0, k, new)
    scale = 1.0 / new
    for c in range(tracer_ref.shape[0]):
        change = tracer_change(
            tracer_ref[c, 0], up_ref[2 + c, 0], down_ref[4 + c, 0], thick, u, v, v_s, east, north, below, inverse
        )
        store_edges(3 + c, k, change * scale)

    @pl.when(k == L - 1)
    def _():
        pieces = [
            new_wind[:, :, :, a * LANES : (a + 1) * LANES].reshape(2 * L * rows, LANES) for a in range(width // LANES)
        ]
        cutoff = jnp.broadcast_to(cutoff_ref[...][None], (2 * L, rows, LANES)).reshape(2 * L * rows, LANES)
        for a, piece in enumerate(filter_rows(pieces, cutoff, high_ref, low_ref)):
            piece = piece.reshape(2, L, rows, LANES)
            for f in range(2):
                wind_refs[f][0, :, :, a * LANES : (a + 1) * LANES] = piece[f]
        for f in range(2):
            for level in range(L):
                store_edges(1 + f, level, wind_refs[f][0, level])


def second_step(band, table, lat_rows, thickness, wind_u, wind_v, tracers, up, down, cutoff):
    L, R, N = thickness.shape
    T = tracers.shape[0]
    high, low = filter_tables(N)
    level = pl.BlockSpec((1, R, N), lambda k: (k, 0, 0))
    some = lambda n, rows: pl.BlockSpec((n, 1, rows, N), lambda k: (0, k, 0, 0))
    whole = lambda shape: pl.BlockSpec(shape, lambda k: (0,) * len(shape))
    return pl.pallas_call(
        functools.partial(second_kernel, lat_rows),
        grid=(L,),
        in_specs=[SMEM, whole(table.shape), level, level, level, some(T, R), some(2 + T, 1), some(4 + T, 1)]
        + [whole((R, LANES)), whole(high.shape), whole(low.shape)],
        out_specs=[whole((1, L, R, N)), whole((1, L, R, N)), whole((3 + T, L, 2, N))],
        out_shape=[
            jax.ShapeDtypeStruct((1, L, R, N), jnp.float32),
            jax.ShapeDtypeStruct((1, L, R, N), jnp.float32),
            jax.ShapeDtypeStruct((3 + T, L, 2, N), jnp.float32),
        ],
        scratch_shapes=[pltpu.VMEM((2, L, R, N), jnp.float32)],
        compiler_params=params(),
        cost_estimate=cost(12 * 2 * L * R * high.size, 4 * L * R * N * (8 + T)),
        name="second_step",
    )(
        band, table, thickness, wind_u, wind_v, tracers, up, down,
        jnp.broadcast_to(cutoff[:, None], (R, LANES)), jnp.asarray(high), jnp.asarray(low),
    )


def weight_sums(weight_ref, firsts, L, levels):
    total = jnp.float32(0.0)
    below = [jnp.float32(0.0) for _ in firsts]
    for k in range(levels):
        w = weight_ref[k]
        below = [b + jnp.where(k < first, w, 0.0) for b, first in zip(below, firsts)]
        total = total + w
    weights = [[weight_ref[first + i] for i in range(L)] for first in firsts]
    sums = []
    for start, row in zip(below, weights):
        sums.append([start])
        for w in row:
            sums[-1].append(sums[-1][-1] + w)
    return total, weights, sums


def source_levels(place, counts, thick, others):
    C, S = counts
    lev, sub = place
    spot = [lax.rem(lev - g // S + C, C) * S + lax.rem(sub - g % S + S, S) for g in range(len(thick))]
    group = [functools.reduce(jnp.add, levels) for levels in thick]
    mass = functools.reduce(jnp.add, group)
    base = jnp.zeros_like(mass)
    for s, other in enumerate(others, 1):
        mass = mass + other
        base = base + jnp.where(lev >= s, other, 0.0)
    sources = []
    for g, levels in enumerate(thick):
        low = base
        for other in range(len(thick)):
            if other != g:
                low = low + jnp.where(spot[other] < spot[g], group[other], 0.0)
        for m, value in enumerate(levels):
            sources.append((g, m, low, value))
            low = low + value
    return mass, sources


def covered(top, sources):
    return [jnp.minimum(jnp.maximum(top - low, 0.0), value) for _, _, low, value in sources]


def remap_rows(place, weight_ref, counts, steps, thick_refs, field_refs, other_refs, store):
    C, S = counts
    G = len(thick_refs) // S
    _, L, R, N = thick_refs[0].shape
    lev, sub = place
    firsts = [(lax.rem(lev + s, C) * S + sub) * L for s in steps]
    weight_sum, weights, sums = weight_sums(weight_ref, firsts, L, C * S * L)

    def tile(at, columns):
        thick = [[ref[0, m, at, columns] for m in range(L)] for ref in thick_refs]
        others = [
            functools.reduce(jnp.add, [ref[at, columns] for ref in other_refs[s * S : (s + 1) * S]])
            for s in range(C - G)
        ]
        mass, sources = source_levels(place, counts, thick, others)
        unit = mass / weight_sum
        for index, s in enumerate(steps):
            below = covered(unit * sums[index][0], sources)
            for i in range(L):
                upto = covered(unit * sums[index][i + 1], sources)
                part = [a - b for a, b in zip(upto, below)]
                below = upto
                target = unit * weights[index][i]
                scale = 1.0 / target
                means = []
                for refs in field_refs:
                    terms = [refs[g][0][refs[g][1], m, at, columns] * w for (g, m, _, _), w in zip(sources, part)]
                    means.append(functools.reduce(jnp.add, terms) * scale)
                store(s, i, at, columns, target, means)

    rows = min(R, 8)
    for r in range(0, R, rows):

        def body(c, carry):
            tile(slice(r, r + rows), pl.ds(pl.multiple_of(c * LANES, LANES), LANES))
            return carry

        lax.fori_loop(0, N // LANES, body, 0)


def inner_part(at, margin, rows):
    return max(at.start, margin), min(at.stop, rows - margin)


def remap_kernel(counts, steps, fields, margin, sizes, place_ref, weight_ref, *refs):
    C, S = counts
    thick_refs, refs = refs[:S], refs[S:]
    bundles = []
    for _ in range(sizes[0]):
        bundles.append(refs[:S])
        refs = refs[S:]
    other_refs, out_refs = refs[: (C - 1) * S], refs[len(refs) - len(steps) :]
    _, L, R, _ = thick_refs[0].shape
    field_refs = [[(ref, index) for ref in bundles[which]] for which, index in fields]

    def store(s, i, at, columns, target, means):
        out_ref = out_refs[steps.index(s)]
        for f, value in enumerate(means):
            if s == 0:
                out_ref[f, i, at, columns] = value
            else:
                lower, upper = inner_part(at, margin, R)
                start = (f * L + i) * (R - 2 * margin) - margin
                out_ref[start + lower : start + upper, columns] = value[lower - at.start : upper - at.start]

    remap_rows(
        (place_ref[0], place_ref[1]), weight_ref, counts, steps, thick_refs, field_refs, other_refs, store
    )


def remap_parts(counts, place, weights, thick, bundles, others, fields, steps, margin, wait=()):
    C, S = counts
    _, L, R, N = thick[0].shape
    F = len(fields)
    whole = jax.ShapeDtypeStruct((F, L, R, N), jnp.float32)
    inner = jax.ShapeDtypeStruct((F * L * (R - 2 * margin), N), jnp.float32)
    flat = [a for bundle in bundles for a in bundle]
    return pl.pallas_call(
        functools.partial(remap_kernel, counts, tuple(steps), tuple(fields), margin, (len(bundles),)),
        in_specs=[SMEM] * 2 + [VMEM] * (len(thick) + len(flat) + len(others)) + after(wait),
        out_specs=[VMEM] * len(steps),
        out_shape=[whole if s == 0 else inner for s in steps],
        compiler_params=params(),
        cost_estimate=cost(len(steps) * S * L * L * R * N * (5 + 2 * F), 4 * R * N * L * (F + 1) * (S + len(steps))),
        name="remap_parts",
    )(place, weights, *thick, *flat, *others, *wait)


def remap_edge_kernel(counts, near_fields, place_ref, weight_ref, *refs):
    G = counts[0] * counts[1]
    edge_refs, near_refs, rest_refs = refs[:G], refs[G : 2 * G], refs[2 * G : 3 * G]
    edge_out_ref, thick_out_ref, near_out_ref = refs[-3:]
    place = (place_ref[0], place_ref[1])

    def store_edge(s, i, at, columns, target, means):
        thick_out_ref[i, at, columns] = target
        for f, value in enumerate(means):
            edge_out_ref[f, i, at, columns] = value

    def store_near(s, i, at, columns, target, means):
        for f, value in enumerate(means):
            near_out_ref[f, i, at, columns] = value

    fields = [[(ref, f) for ref in edge_refs] for f in range(1, edge_refs[0].shape[0])]
    remap_rows(place, weight_ref, counts, (0,), edge_refs, fields, [], store_edge)
    bundles = (near_refs, rest_refs)
    fields = [[(ref, index) for ref in bundles[which]] for which, index in near_fields]
    remap_rows(place, weight_ref, counts, (0,), near_refs, fields, [], store_near)


def remap_edges(counts, place, weights, edges, near, near_rest, wait=()):
    F, L, R, N = edges[0].shape
    T = F - 3
    near_fields = tuple((0, 1) if f == 0 else (1, f - 1) for f in range(T))
    operands = [*edges, *near, *near_rest]
    return pl.pallas_call(
        functools.partial(remap_edge_kernel, counts, near_fields),
        in_specs=[SMEM] * 2 + [VMEM] * len(operands) + after(wait),
        out_specs=[VMEM] * 3,
        out_shape=[
            jax.ShapeDtypeStruct((F - 1, L, R, N), jnp.float32),
            jax.ShapeDtypeStruct((L, R, N), jnp.float32),
            jax.ShapeDtypeStruct((T, L, R, N), jnp.float32),
        ],
        compiler_params=params(),
        cost_estimate=cost(len(edges) * L * L * R * N * 40, 4 * R * N * L * len(operands) * F),
        name="remap_edges",
    )(place, weights, *operands, *wait)


def finish_kernel(counts, margin, place_ref, weight_ref, *refs):
    C, S = counts
    group_refs, refs = refs[:S], refs[S:]
    other_refs, refs = refs[: (C - 1) * S], refs[(C - 1) * S :]
    *arrived_refs, near_ref, edge_ref, thick_edge_ref, out_ref, thick_out_ref, token_ref = refs
    token_ref[...] = jnp.zeros_like(token_ref)
    T, L, R, _ = out_ref.shape

    def store(s, i, at, columns, target, means):
        thick_out_ref[i, at, columns] = target
        lower, upper = inner_part(at, margin, R)
        for f, value in enumerate(means):
            total = value[lower - at.start : upper - at.start]
            start = (f * L + i) * (R - 2 * margin) - margin
            for ref in arrived_refs:
                total = total + ref[start + lower : start + upper, columns]
            out_ref[f, i, lower:upper, columns] = total

    fields = [[(ref, 1 + f) for ref in group_refs] for f in range(T)]
    remap_rows((place_ref[0], place_ref[1]), weight_ref, counts, (0,), group_refs, fields, other_refs, store)
    for i in range(L):
        for row, j in ((0, 0), (R - 1, 1)):
            thick_out_ref[i, row : row + 1] = thick_edge_ref[i, j : j + 1]
            for f in range(T):
                out_ref[f, i, row : row + 1] = edge_ref[2 + f, i, j : j + 1]
        for row, j in ((1, 0), (R - 2, 1)):
            for f in range(T):
                out_ref[f, i, row : row + 1] = near_ref[f, i, j : j + 1]


def finish_tracers(counts, place, weights, group, others, arrived, near, edge, thick_edge):
    margin = 2
    C, S = counts
    T = group[0].shape[0] - 1
    _, L, R, N = group[0].shape
    operands = list(group) + list(others) + list(arrived) + [near, edge, thick_edge]
    return pl.pallas_call(
        functools.partial(finish_kernel, counts, margin),
        in_specs=[SMEM] * 2 + [VMEM] * len(operands),
        out_specs=[VMEM] * 3,
        out_shape=[
            jax.ShapeDtypeStruct((T, L, R, N), jnp.float32),
            jax.ShapeDtypeStruct((L, R, N), jnp.float32),
            jax.ShapeDtypeStruct((8, LANES), jnp.float32),
        ],
        compiler_params=params(),
        cost_estimate=cost(S * L * L * R * N * (5 + 2 * T), 4 * R * N * L * (T + 1) * (S + 2)),
        name="finish_tracers",
    )(place, weights, *operands)


def finish_winds_kernel(count, own_ref, edge_ref, *refs):
    arrived_refs, out_refs = refs[:count], refs[-2:]
    _, L, R, N = own_ref.shape
    for f, out_ref in enumerate(out_refs):
        for i in range(L):
            start = (f * L + i) * (R - 2)
            total = own_ref[f, i, 1 : R - 1]
            for ref in arrived_refs:
                total = total + ref[start : start + R - 2]
            out_ref[i, 1 : R - 1] = total
            out_ref[i, 0:1] = edge_ref[f, i, 0:1]
            out_ref[i, R - 1 : R] = edge_ref[f, i, 1:2]


def finish_winds(own, arrived, edge, wait):
    return pl.pallas_call(
        functools.partial(finish_winds_kernel, len(arrived)),
        in_specs=[VMEM] * (2 + len(arrived)) + after(wait),
        out_specs=[VMEM] * 2,
        out_shape=[jax.ShapeDtypeStruct(own.shape[1:], jnp.float32)] * 2,
        compiler_params=params(),
        cost_estimate=cost(own.size, 12 * own.size),
        name="finish_winds",
    )(own, edge, *arrived, *wait)


def edge_kernel(thick_hbm, u_hbm, v_hbm, tracer_hbm, *refs):
    last_ref, leading_ref, top_ref, low_ref, tracer_ref, sems = refs[-6:]
    T, L, R, _ = tracer_hbm.shape
    top = pl.ds(R - 8, 8)
    copies = [
        pltpu.make_async_copy(thick_hbm.at[:, top], top_ref.at[0], sems.at[0]),
        pltpu.make_async_copy(v_hbm.at[:, top], top_ref.at[1], sems.at[1]),
        pltpu.make_async_copy(thick_hbm.at[:, pl.ds(0, 8)], low_ref.at[0], sems.at[2]),
        pltpu.make_async_copy(u_hbm.at[:, pl.ds(0, 8)], low_ref.at[1], sems.at[3]),
        pltpu.make_async_copy(v_hbm.at[:, pl.ds(0, 8)], low_ref.at[2], sems.at[4]),
        pltpu.make_async_copy(tracer_hbm.at[:, :, top], tracer_ref.at[0], sems.at[5]),
        pltpu.make_async_copy(tracer_hbm.at[:, :, pl.ds(0, 8)], tracer_ref.at[1], sems.at[6]),
    ]
    for copy in copies:
        copy.start()
    for copy in copies:
        copy.wait()
    last_ref[0:2] = top_ref[:, :, 7:8]
    last_ref[2 : 2 + T] = tracer_ref[0, :, :, 7:8]
    leading_ref[0] = low_ref[0, :, 0:1]
    leading_ref[1] = low_ref[0, :, 1:2]
    leading_ref[2:4] = low_ref[1:3, :, 0:1]
    leading_ref[4 : 4 + T] = tracer_ref[1, :, :, 0:1]


def edge_rows(thickness, wind_u, wind_v, tracers, wait):
    L, R, N = thickness.shape
    T = tracers.shape[0]
    operands = [pltpu.with_memory_space_constraint(a, pltpu.HBM) for a in (thickness, wind_u, wind_v, tracers)]
    return pl.pallas_call(
        edge_kernel,
        in_specs=after(operands) + after(wait),
        out_specs=[VMEM] * 2,
        out_shape=[
            jax.ShapeDtypeStruct((2 + T, L, 1, N), jnp.float32),
            jax.ShapeDtypeStruct((4 + T, L, 1, N), jnp.float32),
        ],
        scratch_shapes=[
            pltpu.VMEM((2, L, 8, N), jnp.float32),
            pltpu.VMEM((3, L, 8, N), jnp.float32),
            pltpu.VMEM((2, T, L, 8, N), jnp.float32),
            pltpu.SemaphoreType.DMA((7,)),
        ],
        compiler_params=params(),
        cost_estimate=cost(1e10, 1e9),
        name="edge_rows",
    )(*operands, *wait)


def shifted(value, lev_count, sub_count, s, t):
    if t == 0:
        return lax.ppermute(value, "lev", [(i, (i + s) % lev_count) for i in range(lev_count)])
    if s == 0:
        return lax.ppermute(value, "sub", [(i, (i + t) % sub_count) for i in range(sub_count)])
    pairs = [
        (i * sub_count + j, (i + s) % lev_count * sub_count + (j + t) % sub_count)
        for i in range(lev_count)
        for j in range(sub_count)
    ]
    return lax.ppermute(value, ("lev", "sub"), pairs)


def per_device(thickness, wind_u, wind_v, tracers, level_weights, cutoff):
    L, R, N = thickness.shape
    lat_count = lax.axis_size("lat")
    C, S = lax.axis_size("lev"), lax.axis_size("sub")
    lat_rows = R * lat_count
    send = functools.partial(shifted, lev_count=C, sub_count=S)

    T = tracers.shape[0]
    northward = [(i, i + 1) for i in range(lat_count - 1)]
    southward = [(j, i) for i, j in northward]
    band = lax.axis_index("lat").astype(jnp.int32).reshape(1)
    table = jnp.asarray(geometry_table(lat_rows, R))
    place = jnp.stack([lax.axis_index("lev"), lax.axis_index("sub")]).astype(jnp.int32)
    away = range(1, C)

    def with_others_of_chip(own):
        return [own] + [send(own, s=0, t=t) for t in range(1, S)]

    def sent(parts):
        return [send(part, s=s, t=0) for s, part in zip(away, parts)]

    remap = functools.partial(remap_parts, (C, S), place, level_weights)

    inner, own_sum, near, near_rest = inner_step(band, table, thickness, wind_u, wind_v, tracers)
    others = [send(own_sum, s=s, t=t) for s in away for t in range(S)]
    group = with_others_of_chip(inner)
    near = [near] + [send(near, s=s, t=0) for s in away]
    near_rest = [near_rest] + [send(near_rest, s=s, t=0) for s in away]
    tracer_fields = [(0, 1 + c) for c in range(T)]
    away_parts = remap(group, [group], others, tracer_fields, away, 2)
    arrived = sent(away_parts)

    last, leading = edge_rows(
        thickness, wind_u, wind_v, tracers, [away_parts[0], *near[1:2], *near_rest[1:2]]
    )
    up = lax.ppermute(last, "lat", northward)
    down = lax.ppermute(leading, "lat", southward)
    u, v, edge = second_step(band, table, lat_rows, thickness, wind_u, wind_v, tracers, up, down, cutoff)
    edges = [edge] + [send(edge, s=s, t=0) for s in away]
    winds = [with_others_of_chip(u), with_others_of_chip(v)]
    winds_own, *winds_away = remap(group, winds, others, [(0, 0), (1, 0)], range(C), 1, wait=arrived[:1])
    winds_arrived = sent(winds_away)
    near, near_rest, edges = (
        [a for own in sources for a in with_others_of_chip(own)] for sources in (near, near_rest, edges)
    )
    edge_out, thick_edge, near_out = remap_edges(
        (C, S), place, level_weights, edges, near, near_rest, wait=winds_away[:1]
    )

    tracers_out, thickness_out, token = finish_tracers(
        (C, S), place, level_weights, group, others, arrived, near_out, edge_out, thick_edge
    )
    u_out, v_out = finish_winds(winds_own, winds_arrived, edge_out, [token])
    return thickness_out, u_out, v_out, tracers_out


def solution(mesh):
    placed = (
        P(("member", "lev", "sub"), "lat", None),
        P(("member", "lev", "sub"), "lat", None),
        P(("member", "lev", "sub"), "lat", None),
        P("member", ("lev", "sub"), "lat", None),
        P(),
        P("lat"),
    )
    return jax.shard_map(
        per_device,
        mesh=mesh,
        in_specs=placed,
        out_specs=(
            P(("member", "lev", "sub"), "lat", None),
            P(("member", "lev", "sub"), "lat", None),
            P(("member", "lev", "sub"), "lat", None),
            P("member", ("lev", "sub"), "lat", None),
        ),
        check_vma=False,
    )
```

```python
import functools

import jax
import jax.numpy as jnp
import ml_dtypes
import numpy as np
from jax import lax
from jax.experimental import pallas as pl
from jax.experimental.pallas import tpu as pltpu
from jax.sharding import PartitionSpec as P

LANES = 128
VMEM = pl.BlockSpec(memory_space=pltpu.VMEM)
SMEM = pl.BlockSpec(memory_space=pltpu.SMEM)


def params():
    return pltpu.CompilerParams(vmem_limit_bytes=16 * 1024 * 1024)


def cost(flops, bytes_accessed):
    return pl.CostEstimate(flops=int(flops), bytes_accessed=int(bytes_accessed), transcendentals=0)


def after(arrays):
    return [pl.BlockSpec(memory_space=pl.ANY)] * len(arrays)


def geometry_table(lat_rows, band_rows):
    bands = lat_rows // band_rows
    table = np.zeros((bands, band_rows + 8, LANES), np.float32)
    for band in range(bands):
        for j in range(band_rows + 1):
            row = band * band_rows + j
            south = np.sin(row * np.pi / lat_rows) if 0 < row < lat_rows else 0.0
            north = np.sin((row + 1) * np.pi / lat_rows) if row + 1 < lat_rows else 0.0
            table[band, j, 0] = south
            table[band, j, 1] = north
            table[band, j, 2] = 1.0 / np.sin((row + 0.5) * np.pi / lat_rows)
    return table


def east_of(value):
    return pltpu.roll(value, value.shape[1] - 1, 1)


def west_of(value):
    return pltpu.roll(value, 1, 1)


def row_ids(shape):
    return lax.broadcasted_iota(jnp.int32, shape, 0)


def north_of(value, beyond):
    rows = value.shape[0]
    rolled = pltpu.roll(value, rows - 1, 0)
    return rolled if beyond is None else jnp.where(row_ids(value.shape) == rows - 1, beyond, rolled)


def south_of(value, beyond):
    rolled = pltpu.roll(value, 1, 0)
    return rolled if beyond is None else jnp.where(row_ids(value.shape) == 0, beyond, rolled)


def fluxes(geo, thick, u, v, thick_s, v_s, thick_n):
    rows = thick.shape[0]
    east = u * jnp.where(u > 0, thick, east_of(thick))
    north = v * jnp.where(v > 0, thick, north_of(thick, thick_n)) * geo[0:rows, 1:2]
    below = None if v_s is None else v_s * jnp.where(v_s > 0, thick_s, thick[0:1]) * geo[0:1, 0:1]
    return east, north, below


def tracer_change(q, q_s, q_n, thick, u, v, v_s, east, north, below, inverse):
    t_east = east * jnp.where(u > 0, q, east_of(q))
    t_north = north * jnp.where(v > 0, q, north_of(q, q_n))
    t_below = None if v_s is None else below * jnp.where(v_s > 0, q_s, q[0:1])
    change = thick * q - (t_east - west_of(t_east))
    return change - (t_north - south_of(t_north, t_below)) * inverse


def first_kernel(band_ref, table_hbm, thick_hbm, u_hbm, v_hbm, tracer_hbm, *refs):
    new_ref, sum_ref, thick_ref, u_ref, v_ref, tracer_ref, geo_ref, sems = refs
    L, rows, _ = thick_ref.shape
    table_copy = pltpu.make_async_copy(table_hbm.at[band_ref[0]], geo_ref, sems.at[3, 0])
    table_copy.start()
    pairs = ((thick_hbm, thick_ref), (u_hbm, u_ref), (v_hbm, v_ref))

    def copies(k):
        return [pltpu.make_async_copy(a.at[k], b.at[k], sems.at[i, k]) for i, (a, b) in enumerate(pairs)]

    for k in range(L):
        for copy in copies(k):
            copy.start()
    tracer_copy = pltpu.make_async_copy(tracer_hbm, tracer_ref, sems.at[3, 1])
    tracer_copy.start()
    table_copy.wait()
    geo = geo_ref[...]
    sum_ref[...] = jnp.zeros_like(sum_ref)

    def level(k, carry):
        for copy in copies(k):
            copy.wait()
        thick, u, v = thick_ref[k], u_ref[k], v_ref[k]
        east, north, _ = fluxes(geo, thick, u, v, None, None, None)
        new = thick - (east - west_of(east)) - (north - south_of(north, None)) * geo[0:rows, 2:3]
        new_ref[k] = new
        sum_ref[...] += new
        return carry

    lax.fori_loop(0, L, level, 0)
    tracer_copy.wait()


def first_step(band, table, thickness, wind_u, wind_v, tracers):
    L, R, N = thickness.shape
    arguments = (thickness, wind_u, wind_v, tracers)
    operands = [pltpu.with_memory_space_constraint(a, pltpu.HBM) for a in (table, *arguments)]
    shapes = [(L, R, N), (R, N)] + [a.shape for a in arguments]
    return pl.pallas_call(
        first_kernel,
        in_specs=[SMEM] + after(operands),
        out_specs=[VMEM] * len(shapes),
        out_shape=[jax.ShapeDtypeStruct(shape, jnp.float32) for shape in shapes],
        scratch_shapes=[pltpu.VMEM(table.shape[1:], jnp.float32), pltpu.SemaphoreType.DMA((4, max(L, 2)))],
        compiler_params=params(),
        cost_estimate=cost(40 * L * R * N, 4 * L * R * N * (7 + 2 * tracers.shape[0])),
        name="first_step",
    )(band, *operands)


def inner_kernel(band_ref, table_ref, new_ref, thick_ref, u_ref, v_ref, tracer_ref, out_ref, near_ref, near_rest_ref):
    T, L, rows, _ = tracer_ref.shape
    geo = table_ref[band_ref[0]]
    inverse = geo[0:rows, 2:3]

    def level(k, carry):
        thick, u, v, new = thick_ref[k], u_ref[k], v_ref[k], new_ref[k]
        east, north, _ = fluxes(geo, thick, u, v, None, None, None)

        def store(field, value):
            out_ref[field, k] = value
            ref, at = (near_ref, field) if field < 2 else (near_rest_ref, field - 2)
            ref[at, k, 0:1] = value[1:2]
            ref[at, k, 1:2] = value[rows - 2 : rows - 1]

        store(0, new)
        scale = 1.0 / new
        for c in range(T):
            change = tracer_change(
                tracer_ref[c, k], None, None, thick, u, v, None, east, north, None, inverse
            )
            store(1 + c, change * scale)
        return carry

    lax.fori_loop(0, L, level, 0)


def inner_step(band, table, new, thickness, wind_u, wind_v, tracers):
    L, R, N = thickness.shape
    T = tracers.shape[0]
    shape = lambda n, rows: jax.ShapeDtypeStruct((n, L, rows, N), jnp.float32)
    return pl.pallas_call(
        inner_kernel,
        in_specs=[SMEM] + [VMEM] * 6,
        out_specs=[VMEM] * 3,
        out_shape=[shape(1 + T, R), shape(2, 2), shape(T - 1, 2)],
        compiler_params=params(),
        cost_estimate=cost(130 * L * R * N, 4 * L * R * N * (8 + 2 * T)),
        name="inner_step",
    )(band, table, new, thickness, wind_u, wind_v, tracers)


def filter_tables(N):
    A = N // LANES
    b = np.arange(LANES)[:, None]
    p = np.arange(LANES)[None, :]
    tables = []
    for q in range(A // 2 + 1):
        angle = 2.0 * np.pi * ((b * (A * p + q)) % N) / N
        c, s = np.cos(angle), np.sin(angle)
        tables.append(np.block([[c, -s], [s, c]]))
    table = np.stack(tables)
    high = table.astype(np.float32).astype(ml_dtypes.bfloat16)
    low = (table - high.astype(np.float64)).astype(np.float32).astype(ml_dtypes.bfloat16)
    return high, low


def split(value):
    high = value.astype(jnp.bfloat16)
    return high, (value - high.astype(jnp.float32)).astype(jnp.bfloat16)


def product(value, high, low, transposed):
    dims = (((1,), (1 if transposed else 0,)), ((), ()))
    dot = lambda x, y: lax.dot_general(x, y, dims, preferred_element_type=jnp.float32)
    v_high, v_low = split(value)
    return dot(v_high, high) + (dot(v_high, low) + dot(v_low, high))


def filter_rows(x, cutoff, high_ref, low_ref):
    A = len(x)
    N = A * LANES
    half = A // 2
    even = [x[a] + x[A - a] for a in range(1, half + 1)]
    odd = [x[a] - x[A - a] for a in range(1, half + 1)]
    angle = lambda q, a: 2.0 * np.pi * ((q * a) % A) / A
    p = lax.broadcasted_iota(jnp.int32, cutoff.shape, 1)
    real, imag = [], []
    for q in range(half + 1):
        re = x[0]
        for a in range(1, half + 1):
            re = re + (even[a - 1] if q == 0 else float(np.cos(angle(q, a))) * even[a - 1])
        if q == 0:
            high, low = high_ref[0, 0:LANES], low_ref[0, 0:LANES]
            spectrum = product(re, high, low, False)
        else:
            high, low = high_ref[q], low_ref[q]
            im = -float(np.sin(angle(q, 1))) * odd[0]
            for a in range(2, half + 1):
                im = im - float(np.sin(angle(q, a))) * odd[a - 1]
            spectrum = product(jnp.concatenate([re, im], axis=1), high, low, False)
        mode = A * p + q
        factor = 1.0 / N if q == 0 else 2.0 / N
        kept = jnp.where(jnp.minimum(mode, N - mode) <= cutoff, factor, 0.0)
        back = product(spectrum * jnp.concatenate([kept, kept], axis=1), high, low, True)
        real.append(back[:, :LANES])
        imag.append(back[:, LANES:])
    out = [None] * A
    out[0] = functools.reduce(jnp.add, real)
    for a in range(1, half + 1):
        even_part, odd_part = real[0], None
        for q in range(1, half + 1):
            even_part = even_part + float(np.cos(angle(q, a))) * real[q]
            term = float(np.sin(angle(q, a))) * imag[q]
            odd_part = term if odd_part is None else odd_part + term
        out[a] = even_part - odd_part
        out[A - a] = even_part + odd_part
    return out


def second_kernel(
    lat_rows, band_ref, table_ref, thick_ref, u_ref, v_ref, tracer_ref, up_ref, down_ref, cutoff_ref, high_ref, low_ref, *refs
):
    *wind_refs, edge_ref, new_wind = refs
    k = pl.program_id(0)
    _, L, rows, width = new_wind.shape
    geo = table_ref[band_ref[0]]
    thick, u, v = thick_ref[0], u_ref[0], v_ref[0]
    thick_s, v_s = up_ref[0, 0], up_ref[1, 0]
    thick_n, thick_nn, u_n, v_n = (down_ref[i, 0] for i in range(4))
    east, north, below = fluxes(geo, thick, u, v, thick_s, v_s, thick_n)
    inverse = geo[0:rows, 2:3]
    new = thick - (east - west_of(east)) - (north - south_of(north, below)) * inverse
    east_n = u_n * jnp.where(u_n > 0, thick_n, east_of(thick_n))
    north_n = v_n * jnp.where(v_n > 0, thick_n, thick_nn) * geo[rows : rows + 1, 1:2]
    new_n = (
        thick_n
        - (east_n - west_of(east_n))
        - (north_n - north[rows - 1 : rows]) * geo[rows : rows + 1, 2:3]
    )
    new_wind[0, k] = u - 0.05 * (east_of(new) - new)
    inside = band_ref[0] * rows + row_ids(new.shape) < lat_rows - 1
    new_wind[1, k] = jnp.where(inside, v - 0.05 * (north_of(new, new_n) - new), 0.0)

    def store_edges(field, level, value):
        edge_ref[field, level, 0:1] = value[0:1]
        edge_ref[field, level, 1:2] = value[rows - 1 : rows]

    store_edges(0, k, new)
    scale = 1.0 / new
    for c in range(tracer_ref.shape[0]):
        change = tracer_change(
            tracer_ref[c, 0], up_ref[2 + c, 0], down_ref[4 + c, 0], thick, u, v, v_s, east, north, below, inverse
        )
        store_edges(3 + c, k, change * scale)

    @pl.when(k == L - 1)
    def _():
        pieces = [
            new_wind[:, :, :, a * LANES : (a + 1) * LANES].reshape(2 * L * rows, LANES) for a in range(width // LANES)
        ]
        cutoff = jnp.broadcast_to(cutoff_ref[...][None], (2 * L, rows, LANES)).reshape(2 * L * rows, LANES)
        for a, piece in enumerate(filter_rows(pieces, cutoff, high_ref, low_ref)):
            piece = piece.reshape(2, L, rows, LANES)
            for f in range(2):
                wind_refs[f][0, :, :, a * LANES : (a + 1) * LANES] = piece[f]
        for f in range(2):
            for level in range(L):
                store_edges(1 + f, level, wind_refs[f][0, level])


def second_step(band, table, lat_rows, thickness, wind_u, wind_v, tracers, up, down, cutoff):
    L, R, N = thickness.shape
    T = tracers.shape[0]
    high, low = filter_tables(N)
    level = pl.BlockSpec((1, R, N), lambda k: (k, 0, 0))
    some = lambda n, rows: pl.BlockSpec((n, 1, rows, N), lambda k: (0, k, 0, 0))
    whole = lambda shape: pl.BlockSpec(shape, lambda k: (0,) * len(shape))
    return pl.pallas_call(
        functools.partial(second_kernel, lat_rows),
        grid=(L,),
        in_specs=[SMEM, whole(table.shape), level, level, level, some(T, R), some(2 + T, 1), some(4 + T, 1)]
        + [whole((R, LANES)), whole(high.shape), whole(low.shape)],
        out_specs=[whole((1, L, R, N)), whole((1, L, R, N)), whole((3 + T, L, 2, N))],
        out_shape=[
            jax.ShapeDtypeStruct((1, L, R, N), jnp.float32),
            jax.ShapeDtypeStruct((1, L, R, N), jnp.float32),
            jax.ShapeDtypeStruct((3 + T, L, 2, N), jnp.float32),
        ],
        scratch_shapes=[pltpu.VMEM((2, L, R, N), jnp.float32)],
        compiler_params=params(),
        cost_estimate=cost(12 * 2 * L * R * high.size, 4 * L * R * N * (8 + T)),
        name="second_step",
    )(
        band, table, thickness, wind_u, wind_v, tracers, up, down,
        jnp.broadcast_to(cutoff[:, None], (R, LANES)), jnp.asarray(high), jnp.asarray(low),
    )


def mass_kernel(C, S, place_ref, new_ref, *refs):
    base_ref, mass_ref = refs[-2:]
    lev = place_ref[0]
    others_mass, base = None, None
    for s in range(1, C):
        other = functools.reduce(jnp.add, [ref[...] for ref in refs[(s - 1) * S : s * S]])
        below = jnp.where(lev >= s, other, 0.0)
        others_mass = other if others_mass is None else others_mass + other
        base = below if base is None else base + below
    base_ref[...] = base
    mass_ref[...] = others_mass


def other_chips(counts, place, new, others):
    return pl.pallas_call(
        functools.partial(mass_kernel, *counts),
        in_specs=[SMEM] + [VMEM] * (1 + len(others)),
        out_specs=[VMEM] * 2,
        out_shape=[jax.ShapeDtypeStruct(new.shape, jnp.float32)] * 2,
        compiler_params=params(),
        cost_estimate=cost(1e11, 1e9),
        name="other_chips",
    )(place, new, *others)


def weight_sums(weight_ref, firsts, L, levels):
    total = jnp.float32(0.0)
    below = [jnp.float32(0.0) for _ in firsts]
    for k in range(levels):
        w = weight_ref[k]
        below = [b + jnp.where(k < first, w, 0.0) for b, first in zip(below, firsts)]
        total = total + w
    weights = [[weight_ref[first + i] for i in range(L)] for first in firsts]
    sums = []
    for start, row in zip(below, weights):
        sums.append([start])
        for w in row:
            sums[-1].append(sums[-1][-1] + w)
    return total, weights, sums


def source_levels(place, counts, thick, others):
    C, S = counts
    lev, sub = place
    spot = [lax.rem(lev - g // S + C, C) * S + lax.rem(sub - g % S + S, S) for g in range(len(thick))]
    group = [functools.reduce(jnp.add, levels) for levels in thick]
    mass = functools.reduce(jnp.add, group)
    base = jnp.zeros_like(mass)
    if others:
        base, mass = others[0], mass + others[1]
    sources = []
    for g, levels in enumerate(thick):
        low = base
        for other in range(len(thick)):
            if other != g:
                low = low + jnp.where(spot[other] < spot[g], group[other], 0.0)
        for m, value in enumerate(levels):
            sources.append((g, m, low, value))
            low = low + value
    return mass, sources


def covered(top, sources):
    return [jnp.minimum(jnp.maximum(top - low, 0.0), value) for _, _, low, value in sources]


def remap_rows(place, weight_ref, counts, steps, thick_refs, field_refs, other_refs, store):
    C, S = counts
    _, L, R, N = thick_refs[0].shape
    lev, sub = place
    firsts = [(lax.rem(lev + s, C) * S + sub) * L for s in steps]
    weight_sum, weights, sums = weight_sums(weight_ref, firsts, L, C * S * L)

    def tile(at, columns):
        thick = [[ref[0, m, at, columns] for m in range(L)] for ref in thick_refs]
        others = [ref[at, columns] for ref in other_refs]
        mass, sources = source_levels(place, counts, thick, others)
        unit = mass / weight_sum
        for index, s in enumerate(steps):
            below = covered(unit * sums[index][0], sources)
            for i in range(L):
                upto = covered(unit * sums[index][i + 1], sources)
                part = [a - b for a, b in zip(upto, below)]
                below = upto
                target = unit * weights[index][i]
                scale = 1.0 / target
                means = []
                for refs in field_refs:
                    terms = [refs[g][0][refs[g][1], m, at, columns] * w for (g, m, _, _), w in zip(sources, part)]
                    means.append(functools.reduce(jnp.add, terms) * scale)
                store(s, i, at, columns, target, means)

    rows = min(R, 8)
    for r in range(0, R, rows):

        def body(c, carry):
            tile(slice(r, r + rows), pl.ds(pl.multiple_of(c * LANES, LANES), LANES))
            return carry

        lax.fori_loop(0, N // LANES, body, 0)


def inner_part(at, margin, rows):
    return max(at.start, margin), min(at.stop, rows - margin)


def remap_kernel(counts, steps, fields, margin, sizes, place_ref, weight_ref, *refs):
    C, S = counts
    thick_refs, refs = refs[:S], refs[S:]
    bundles = []
    for _ in range(sizes[0]):
        bundles.append(refs[:S])
        refs = refs[S:]
    other_refs, out_refs = refs[:2], refs[len(refs) - len(steps) :]
    _, L, R, _ = thick_refs[0].shape
    field_refs = [[(ref, index) for ref in bundles[which]] for which, index in fields]

    def store(s, i, at, columns, target, means):
        out_ref = out_refs[steps.index(s)]
        for f, value in enumerate(means):
            if s == 0:
                out_ref[f, i, at, columns] = value
            else:
                lower, upper = inner_part(at, margin, R)
                start = (f * L + i) * (R - 2 * margin) - margin
                out_ref[start + lower : start + upper, columns] = value[lower - at.start : upper - at.start]

    remap_rows(
        (place_ref[0], place_ref[1]), weight_ref, counts, steps, thick_refs, field_refs, other_refs, store
    )


def remap_parts(counts, place, weights, thick, bundles, others, fields, steps, margin, wait=()):
    C, S = counts
    _, L, R, N = thick[0].shape
    F = len(fields)
    whole = jax.ShapeDtypeStruct((F, L, R, N), jnp.float32)
    inner = jax.ShapeDtypeStruct((F * L * (R - 2 * margin), N), jnp.float32)
    flat = [a for bundle in bundles for a in bundle]
    return pl.pallas_call(
        functools.partial(remap_kernel, counts, tuple(steps), tuple(fields), margin, (len(bundles),)),
        in_specs=[SMEM] * 2 + [VMEM] * (len(thick) + len(flat) + len(others)) + after(wait),
        out_specs=[VMEM] * len(steps),
        out_shape=[whole if s == 0 else inner for s in steps],
        compiler_params=params(),
        cost_estimate=cost(len(steps) * S * L * L * R * N * (5 + 2 * F), 4 * R * N * L * (F + 1) * (S + len(steps))),
        name="remap_parts",
    )(place, weights, *thick, *flat, *others, *wait)


def remap_edge_kernel(counts, near_fields, place_ref, weight_ref, *refs):
    G = counts[0] * counts[1]
    edge_refs, near_refs, rest_refs = refs[:G], refs[G : 2 * G], refs[2 * G : 3 * G]
    edge_out_ref, thick_out_ref, near_out_ref = refs[-3:]
    place = (place_ref[0], place_ref[1])

    def store_edge(s, i, at, columns, target, means):
        thick_out_ref[i, at, columns] = target
        for f, value in enumerate(means):
            edge_out_ref[f, i, at, columns] = value

    def store_near(s, i, at, columns, target, means):
        for f, value in enumerate(means):
            near_out_ref[f, i, at, columns] = value

    fields = [[(ref, f) for ref in edge_refs] for f in range(1, edge_refs[0].shape[0])]
    remap_rows(place, weight_ref, counts, (0,), edge_refs, fields, [], store_edge)
    bundles = (near_refs, rest_refs)
    fields = [[(ref, index) for ref in bundles[which]] for which, index in near_fields]
    remap_rows(place, weight_ref, counts, (0,), near_refs, fields, [], store_near)


def remap_edges(counts, place, weights, edges, near, near_rest, wait=()):
    F, L, R, N = edges[0].shape
    T = F - 3
    near_fields = tuple((0, 1) if f == 0 else (1, f - 1) for f in range(T))
    operands = [*edges, *near, *near_rest]
    return pl.pallas_call(
        functools.partial(remap_edge_kernel, counts, near_fields),
        in_specs=[SMEM] * 2 + [VMEM] * len(operands) + after(wait),
        out_specs=[VMEM] * 3,
        out_shape=[
            jax.ShapeDtypeStruct((F - 1, L, R, N), jnp.float32),
            jax.ShapeDtypeStruct((L, R, N), jnp.float32),
            jax.ShapeDtypeStruct((T, L, R, N), jnp.float32),
        ],
        compiler_params=params(),
        cost_estimate=cost(len(edges) * L * L * R * N * 40, 4 * R * N * L * len(operands) * F),
        name="remap_edges",
    )(place, weights, *operands, *wait)


def finish_kernel(counts, margin, place_ref, weight_ref, *refs):
    C, S = counts
    group_refs, refs = refs[:S], refs[S:]
    other_refs, refs = refs[:2], refs[2:]
    *arrived_refs, near_ref, edge_ref, thick_edge_ref, out_ref, thick_out_ref, token_ref = refs
    token_ref[...] = jnp.zeros_like(token_ref)
    T, L, R, _ = out_ref.shape

    def store(s, i, at, columns, target, means):
        thick_out_ref[i, at, columns] = target
        lower, upper = inner_part(at, margin, R)
        for f, value in enumerate(means):
            total = value[lower - at.start : upper - at.start]
            start = (f * L + i) * (R - 2 * margin) - margin
            for ref in arrived_refs:
                total = total + ref[start + lower : start + upper, columns]
            out_ref[f, i, lower:upper, columns] = total

    fields = [[(ref, 1 + f) for ref in group_refs] for f in range(T)]
    remap_rows((place_ref[0], place_ref[1]), weight_ref, counts, (0,), group_refs, fields, other_refs, store)
    for i in range(L):
        for row, j in ((0, 0), (R - 1, 1)):
            thick_out_ref[i, row : row + 1] = thick_edge_ref[i, j : j + 1]
            for f in range(T):
                out_ref[f, i, row : row + 1] = edge_ref[2 + f, i, j : j + 1]
        for row, j in ((1, 0), (R - 2, 1)):
            for f in range(T):
                out_ref[f, i, row : row + 1] = near_ref[f, i, j : j + 1]


def finish_tracers(counts, place, weights, group, others, arrived, near, edge, thick_edge):
    margin = 2
    C, S = counts
    T = group[0].shape[0] - 1
    _, L, R, N = group[0].shape
    operands = list(group) + list(others) + list(arrived) + [near, edge, thick_edge]
    return pl.pallas_call(
        functools.partial(finish_kernel, counts, margin),
        in_specs=[SMEM] * 2 + [VMEM] * len(operands),
        out_specs=[VMEM] * 3,
        out_shape=[
            jax.ShapeDtypeStruct((T, L, R, N), jnp.float32),
            jax.ShapeDtypeStruct((L, R, N), jnp.float32),
            jax.ShapeDtypeStruct((8, LANES), jnp.float32),
        ],
        compiler_params=params(),
        cost_estimate=cost(S * L * L * R * N * (5 + 2 * T), 4 * R * N * L * (T + 1) * (S + 2)),
        name="finish_tracers",
    )(place, weights, *operands)


def finish_winds_kernel(count, own_ref, edge_ref, *refs):
    arrived_refs, out_refs = refs[:count], refs[-2:]
    _, L, R, N = own_ref.shape
    for f, out_ref in enumerate(out_refs):
        for i in range(L):
            start = (f * L + i) * (R - 2)
            total = own_ref[f, i, 1 : R - 1]
            for ref in arrived_refs:
                total = total + ref[start : start + R - 2]
            out_ref[i, 1 : R - 1] = total
            out_ref[i, 0:1] = edge_ref[f, i, 0:1]
            out_ref[i, R - 1 : R] = edge_ref[f, i, 1:2]


def finish_winds(own, arrived, edge, wait):
    return pl.pallas_call(
        functools.partial(finish_winds_kernel, len(arrived)),
        in_specs=[VMEM] * (2 + len(arrived)) + after(wait),
        out_specs=[VMEM] * 2,
        out_shape=[jax.ShapeDtypeStruct(own.shape[1:], jnp.float32)] * 2,
        compiler_params=params(),
        cost_estimate=cost(own.size, 12 * own.size),
        name="finish_winds",
    )(own, edge, *arrived, *wait)


def edge_kernel(thick_hbm, u_hbm, v_hbm, tracer_hbm, *refs):
    last_ref, leading_ref, top_ref, low_ref, tracer_ref, sems = refs[-6:]
    T, L, R, _ = tracer_hbm.shape
    top = pl.ds(R - 8, 8)
    copies = [
        pltpu.make_async_copy(thick_hbm.at[:, top], top_ref.at[0], sems.at[0]),
        pltpu.make_async_copy(v_hbm.at[:, top], top_ref.at[1], sems.at[1]),
        pltpu.make_async_copy(thick_hbm.at[:, pl.ds(0, 8)], low_ref.at[0], sems.at[2]),
        pltpu.make_async_copy(u_hbm.at[:, pl.ds(0, 8)], low_ref.at[1], sems.at[3]),
        pltpu.make_async_copy(v_hbm.at[:, pl.ds(0, 8)], low_ref.at[2], sems.at[4]),
        pltpu.make_async_copy(tracer_hbm.at[:, :, top], tracer_ref.at[0], sems.at[5]),
        pltpu.make_async_copy(tracer_hbm.at[:, :, pl.ds(0, 8)], tracer_ref.at[1], sems.at[6]),
    ]
    for copy in copies:
        copy.start()
    for copy in copies:
        copy.wait()
    last_ref[0:2] = top_ref[:, :, 7:8]
    last_ref[2 : 2 + T] = tracer_ref[0, :, :, 7:8]
    leading_ref[0] = low_ref[0, :, 0:1]
    leading_ref[1] = low_ref[0, :, 1:2]
    leading_ref[2:4] = low_ref[1:3, :, 0:1]
    leading_ref[4 : 4 + T] = tracer_ref[1, :, :, 0:1]


def edge_rows(thickness, wind_u, wind_v, tracers, wait):
    L, R, N = thickness.shape
    T = tracers.shape[0]
    operands = [pltpu.with_memory_space_constraint(a, pltpu.HBM) for a in (thickness, wind_u, wind_v, tracers)]
    return pl.pallas_call(
        edge_kernel,
        in_specs=after(operands) + after(wait),
        out_specs=[VMEM] * 2,
        out_shape=[
            jax.ShapeDtypeStruct((2 + T, L, 1, N), jnp.float32),
            jax.ShapeDtypeStruct((4 + T, L, 1, N), jnp.float32),
        ],
        scratch_shapes=[
            pltpu.VMEM((2, L, 8, N), jnp.float32),
            pltpu.VMEM((3, L, 8, N), jnp.float32),
            pltpu.VMEM((2, T, L, 8, N), jnp.float32),
            pltpu.SemaphoreType.DMA((7,)),
        ],
        compiler_params=params(),
        cost_estimate=cost(1e10, 1e9),
        name="edge_rows",
    )(*operands, *wait)


def shifted(value, lev_count, sub_count, s, t):
    if t == 0:
        return lax.ppermute(value, "lev", [(i, (i + s) % lev_count) for i in range(lev_count)])
    if s == 0:
        return lax.ppermute(value, "sub", [(i, (i + t) % sub_count) for i in range(sub_count)])
    pairs = [
        (i * sub_count + j, (i + s) % lev_count * sub_count + (j + t) % sub_count)
        for i in range(lev_count)
        for j in range(sub_count)
    ]
    return lax.ppermute(value, ("lev", "sub"), pairs)


def per_device(thickness, wind_u, wind_v, tracers, level_weights, cutoff):
    L, R, N = thickness.shape
    lat_count = lax.axis_size("lat")
    C, S = lax.axis_size("lev"), lax.axis_size("sub")
    lat_rows = R * lat_count
    send = functools.partial(shifted, lev_count=C, sub_count=S)

    T = tracers.shape[0]
    northward = [(i, i + 1) for i in range(lat_count - 1)]
    southward = [(j, i) for i, j in northward]
    band = lax.axis_index("lat").astype(jnp.int32).reshape(1)
    table = jnp.asarray(geometry_table(lat_rows, R))
    place = jnp.stack([lax.axis_index("lev"), lax.axis_index("sub")]).astype(jnp.int32)
    away = range(1, C)

    def with_others_of_chip(own):
        return [own] + [send(own, s=0, t=t) for t in range(1, S)]

    def sent(parts):
        return [send(part, s=s, t=0) for s, part in zip(away, parts)]

    remap = functools.partial(remap_parts, (C, S), place, level_weights)

    new, own_sum, *arguments = first_step(band, table, thickness, wind_u, wind_v, tracers)
    others = [send(own_sum, s=s, t=t) for s in away for t in range(S)]
    inner, near, near_rest = inner_step(band, table, new, *arguments)
    group = with_others_of_chip(inner)
    near = [near] + [send(near, s=s, t=0) for s in away]
    near_rest = [near_rest] + [send(near_rest, s=s, t=0) for s in away]
    others = other_chips((C, S), place, own_sum, others)
    tracer_fields = [(0, 1 + c) for c in range(T)]
    away_parts = remap(group, [group], others, tracer_fields, away, 2)
    arrived = sent(away_parts)

    last, leading = edge_rows(
        thickness, wind_u, wind_v, tracers, [away_parts[0], *near[1:2], *near_rest[1:2]]
    )
    up = lax.ppermute(last, "lat", northward)
    down = lax.ppermute(leading, "lat", southward)
    u, v, edge = second_step(band, table, lat_rows, thickness, wind_u, wind_v, tracers, up, down, cutoff)
    edges = [edge] + [send(edge, s=s, t=0) for s in away]
    winds = [with_others_of_chip(u), with_others_of_chip(v)]
    winds_own, *winds_away = remap(group, winds, others, [(0, 0), (1, 0)], range(C), 1, wait=arrived[:1])
    winds_arrived = sent(winds_away)
    near, near_rest, edges = (
        [a for own in sources for a in with_others_of_chip(own)] for sources in (near, near_rest, edges)
    )
    edge_out, thick_edge, near_out = remap_edges(
        (C, S), place, level_weights, edges, near, near_rest, wait=winds_away[:1]
    )

    tracers_out, thickness_out, token = finish_tracers(
        (C, S), place, level_weights, group, others, arrived, near_out, edge_out, thick_edge
    )
    u_out, v_out = finish_winds(winds_own, winds_arrived, edge_out, [token])
    return thickness_out, u_out, v_out, tracers_out


def solution(mesh):
    placed = (
        P(("member", "lev", "sub"), "lat", None),
        P(("member", "lev", "sub"), "lat", None),
        P(("member", "lev", "sub"), "lat", None),
        P("member", ("lev", "sub"), "lat", None),
        P(),
        P("lat"),
    )
    return jax.shard_map(
        per_device,
        mesh=mesh,
        in_specs=placed,
        out_specs=(
            P(("member", "lev", "sub"), "lat", None),
            P(("member", "lev", "sub"), "lat", None),
            P(("member", "lev", "sub"), "lat", None),
            P("member", ("lev", "sub"), "lat", None),
        ),
        check_vma=False,
    )
```

```python
import functools

import jax
import jax.numpy as jnp
import ml_dtypes
import numpy as np
from jax import lax
from jax.experimental import pallas as pl
from jax.experimental.pallas import tpu as pltpu
from jax.sharding import PartitionSpec as P

LANES = 128
VMEM = pl.BlockSpec(memory_space=pltpu.VMEM)


def params():
    return pltpu.CompilerParams(vmem_limit_bytes=16 * 1024 * 1024)


def cost(flops, bytes_accessed):
    return pl.CostEstimate(flops=int(flops), bytes_accessed=int(bytes_accessed), transcendentals=0)


def after(arrays):
    return [pl.BlockSpec(memory_space=pl.ANY)] * len(arrays)


def geometry_table(lat_rows, band_rows):
    bands = lat_rows // band_rows
    table = np.zeros((bands, band_rows + 8, LANES), np.float32)
    for band in range(bands):
        for j in range(band_rows + 1):
            row = band * band_rows + j
            south = np.sin(row * np.pi / lat_rows) if 0 < row < lat_rows else 0.0
            north = np.sin((row + 1) * np.pi / lat_rows) if row + 1 < lat_rows else 0.0
            table[band, j, 0] = south
            table[band, j, 1] = north
            table[band, j, 2] = 1.0 / np.sin((row + 0.5) * np.pi / lat_rows)
    return table


def east_of(value):
    return pltpu.roll(value, value.shape[1] - 1, 1)


def west_of(value):
    return pltpu.roll(value, 1, 1)


def row_ids(shape):
    return lax.broadcasted_iota(jnp.int32, shape, 0)


def north_of(value, beyond):
    rows = value.shape[0]
    rolled = pltpu.roll(value, rows - 1, 0)
    return rolled if beyond is None else jnp.where(row_ids(value.shape) == rows - 1, beyond, rolled)


def south_of(value, beyond):
    rolled = pltpu.roll(value, 1, 0)
    return rolled if beyond is None else jnp.where(row_ids(value.shape) == 0, beyond, rolled)


def fluxes(geo, thick, u, v, thick_s, v_s, thick_n):
    rows = thick.shape[0]
    east = u * jnp.where(u > 0, thick, east_of(thick))
    north = v * jnp.where(v > 0, thick, north_of(thick, thick_n)) * geo[0:rows, 1:2]
    below = None if v_s is None else v_s * jnp.where(v_s > 0, thick_s, thick[0:1]) * geo[0:1, 0:1]
    return east, north, below


def tracer_change(q, q_s, q_n, thick, u, v, v_s, east, north, below, inverse):
    t_east = east * jnp.where(u > 0, q, east_of(q))
    t_north = north * jnp.where(v > 0, q, north_of(q, q_n))
    t_below = None if v_s is None else below * jnp.where(v_s > 0, q_s, q[0:1])
    change = thick * q - (t_east - west_of(t_east))
    return change - (t_north - south_of(t_north, t_below)) * inverse


def first_kernel(table_hbm, thick_hbm, u_hbm, v_hbm, tracer_hbm, *refs):
    new_ref, sum_ref, thick_ref, u_ref, v_ref, tracer_ref, geo_ref, sems = refs
    L, rows, _ = thick_ref.shape
    table_copy = pltpu.make_async_copy(table_hbm.at[lax.axis_index("lat")], geo_ref, sems.at[3, 0])
    table_copy.start()
    pairs = ((thick_hbm, thick_ref), (u_hbm, u_ref), (v_hbm, v_ref))

    def copies(k):
        return [pltpu.make_async_copy(a.at[k], b.at[k], sems.at[i, k]) for i, (a, b) in enumerate(pairs)]

    for k in range(L):
        for copy in copies(k):
            copy.start()
    tracer_copy = pltpu.make_async_copy(tracer_hbm, tracer_ref, sems.at[3, 1])
    tracer_copy.start()
    table_copy.wait()
    geo = geo_ref[...]
    sum_ref[...] = jnp.zeros_like(sum_ref)

    def level(k, carry):
        for copy in copies(k):
            copy.wait()
        thick, u, v = thick_ref[k], u_ref[k], v_ref[k]
        east, north, _ = fluxes(geo, thick, u, v, None, None, None)
        new = thick - (east - west_of(east)) - (north - south_of(north, None)) * geo[0:rows, 2:3]
        new_ref[k] = new
        sum_ref[...] += new
        return carry

    lax.fori_loop(0, L, level, 0)
    tracer_copy.wait()


def first_step(table, thickness, wind_u, wind_v, tracers):
    L, R, N = thickness.shape
    arguments = (thickness, wind_u, wind_v, tracers)
    operands = [pltpu.with_memory_space_constraint(a, pltpu.HBM) for a in (table, *arguments)]
    shapes = [(L, R, N), (R, N)] + [a.shape for a in arguments]
    return pl.pallas_call(
        first_kernel,
        in_specs=after(operands),
        out_specs=[VMEM] * len(shapes),
        out_shape=[jax.ShapeDtypeStruct(shape, jnp.float32) for shape in shapes],
        scratch_shapes=[pltpu.VMEM(table.shape[1:], jnp.float32), pltpu.SemaphoreType.DMA((4, max(L, 2)))],
        compiler_params=params(),
        cost_estimate=cost(40 * L * R * N, 4 * L * R * N * (7 + 2 * tracers.shape[0])),
        name="first_step",
    )(*operands)


def inner_kernel(table_ref, new_ref, thick_ref, u_ref, v_ref, tracer_ref, out_ref, near_ref, near_rest_ref):
    T, L, rows, _ = tracer_ref.shape
    geo = table_ref[lax.axis_index("lat")]
    inverse = geo[0:rows, 2:3]

    def level(k, carry):
        thick, u, v, new = thick_ref[k], u_ref[k], v_ref[k], new_ref[k]
        east, north, _ = fluxes(geo, thick, u, v, None, None, None)

        def store(field, value):
            out_ref[field, k] = value
            ref, at = (near_ref, field) if field < 2 else (near_rest_ref, field - 2)
            ref[at, k, 0:1] = value[1:2]
            ref[at, k, 1:2] = value[rows - 2 : rows - 1]

        store(0, new)
        scale = 1.0 / new
        for c in range(T):
            change = tracer_change(
                tracer_ref[c, k], None, None, thick, u, v, None, east, north, None, inverse
            )
            store(1 + c, change * scale)
        return carry

    lax.fori_loop(0, L, level, 0)


def inner_step(table, new, thickness, wind_u, wind_v, tracers):
    L, R, N = thickness.shape
    T = tracers.shape[0]
    shape = lambda n, rows: jax.ShapeDtypeStruct((n, L, rows, N), jnp.float32)
    return pl.pallas_call(
        inner_kernel,
        in_specs=[VMEM] * 6,
        out_specs=[VMEM] * 3,
        out_shape=[shape(1 + T, R), shape(2, 2), shape(T - 1, 2)],
        compiler_params=params(),
        cost_estimate=cost(130 * L * R * N, 4 * L * R * N * (8 + 2 * T)),
        name="inner_step",
    )(table, new, thickness, wind_u, wind_v, tracers)


def filter_tables(N):
    A = N // LANES
    b = np.arange(LANES)[:, None]
    p = np.arange(LANES)[None, :]
    tables = []
    for q in range(A // 2 + 1):
        angle = 2.0 * np.pi * ((b * (A * p + q)) % N) / N
        c, s = np.cos(angle), np.sin(angle)
        tables.append(np.block([[c, -s], [s, c]]))
    table = np.stack(tables)
    high = table.astype(np.float32).astype(ml_dtypes.bfloat16)
    low = (table - high.astype(np.float64)).astype(np.float32).astype(ml_dtypes.bfloat16)
    return high, low


def split(value):
    high = value.astype(jnp.bfloat16)
    return high, (value - high.astype(jnp.float32)).astype(jnp.bfloat16)


def product(value, high, low, transposed):
    dims = (((1,), (1 if transposed else 0,)), ((), ()))
    dot = lambda x, y: lax.dot_general(x, y, dims, preferred_element_type=jnp.float32)
    v_high, v_low = split(value)
    return dot(v_high, high) + (dot(v_high, low) + dot(v_low, high))


def filter_rows(x, cutoff, high_ref, low_ref):
    A = len(x)
    N = A * LANES
    half = A // 2
    even = [x[a] + x[A - a] for a in range(1, half + 1)]
    odd = [x[a] - x[A - a] for a in range(1, half + 1)]
    angle = lambda q, a: 2.0 * np.pi * ((q * a) % A) / A
    p = lax.broadcasted_iota(jnp.int32, cutoff.shape, 1)
    real, imag = [], []
    for q in range(half + 1):
        re = x[0]
        for a in range(1, half + 1):
            re = re + (even[a - 1] if q == 0 else float(np.cos(angle(q, a))) * even[a - 1])
        if q == 0:
            high, low = high_ref[0, 0:LANES], low_ref[0, 0:LANES]
            spectrum = product(re, high, low, False)
        else:
            high, low = high_ref[q], low_ref[q]
            im = -float(np.sin(angle(q, 1))) * odd[0]
            for a in range(2, half + 1):
                im = im - float(np.sin(angle(q, a))) * odd[a - 1]
            spectrum = product(jnp.concatenate([re, im], axis=1), high, low, False)
        mode = A * p + q
        factor = 1.0 / N if q == 0 else 2.0 / N
        kept = jnp.where(jnp.minimum(mode, N - mode) <= cutoff, factor, 0.0)
        back = product(spectrum * jnp.concatenate([kept, kept], axis=1), high, low, True)
        real.append(back[:, :LANES])
        imag.append(back[:, LANES:])
    out = [None] * A
    out[0] = functools.reduce(jnp.add, real)
    for a in range(1, half + 1):
        even_part, odd_part = real[0], None
        for q in range(1, half + 1):
            even_part = even_part + float(np.cos(angle(q, a))) * real[q]
            term = float(np.sin(angle(q, a))) * imag[q]
            odd_part = term if odd_part is None else odd_part + term
        out[a] = even_part - odd_part
        out[A - a] = even_part + odd_part
    return out


def second_kernel(
    lat_rows, table_ref, thick_ref, u_ref, v_ref, tracer_ref, up_ref, down_ref, cutoff_ref, high_ref, low_ref, *refs
):
    *wind_refs, edge_ref, new_wind = refs
    k = pl.program_id(0)
    _, L, rows, width = new_wind.shape
    band = lax.axis_index("lat")
    geo = table_ref[band]
    thick, u, v = thick_ref[0], u_ref[0], v_ref[0]
    thick_s, v_s = up_ref[0, 0], up_ref[1, 0]
    thick_n, thick_nn, u_n, v_n = (down_ref[i, 0] for i in range(4))
    east, north, below = fluxes(geo, thick, u, v, thick_s, v_s, thick_n)
    inverse = geo[0:rows, 2:3]
    new = thick - (east - west_of(east)) - (north - south_of(north, below)) * inverse
    east_n = u_n * jnp.where(u_n > 0, thick_n, east_of(thick_n))
    north_n = v_n * jnp.where(v_n > 0, thick_n, thick_nn) * geo[rows : rows + 1, 1:2]
    new_n = (
        thick_n
        - (east_n - west_of(east_n))
        - (north_n - north[rows - 1 : rows]) * geo[rows : rows + 1, 2:3]
    )
    new_wind[0, k] = u - 0.05 * (east_of(new) - new)
    inside = band * rows + row_ids(new.shape) < lat_rows - 1
    new_wind[1, k] = jnp.where(inside, v - 0.05 * (north_of(new, new_n) - new), 0.0)

    def store_edges(field, level, value):
        edge_ref[field, level, 0:1] = value[0:1]
        edge_ref[field, level, 1:2] = value[rows - 1 : rows]

    store_edges(0, k, new)
    scale = 1.0 / new
    for c in range(tracer_ref.shape[0]):
        change = tracer_change(
            tracer_ref[c, 0], up_ref[2 + c, 0], down_ref[4 + c, 0], thick, u, v, v_s, east, north, below, inverse
        )
        store_edges(3 + c, k, change * scale)

    @pl.when(k == L - 1)
    def _():
        pieces = [
            new_wind[:, :, :, a * LANES : (a + 1) * LANES].reshape(2 * L * rows, LANES) for a in range(width // LANES)
        ]
        cutoff = jnp.broadcast_to(cutoff_ref[...][None], (2 * L, rows, LANES)).reshape(2 * L * rows, LANES)
        for a, piece in enumerate(filter_rows(pieces, cutoff, high_ref, low_ref)):
            piece = piece.reshape(2, L, rows, LANES)
            for f in range(2):
                wind_refs[f][0, :, :, a * LANES : (a + 1) * LANES] = piece[f]
        for f in range(2):
            for level in range(L):
                store_edges(1 + f, level, wind_refs[f][0, level])


def second_step(table, lat_rows, thickness, wind_u, wind_v, tracers, up, down, cutoff):
    L, R, N = thickness.shape
    T = tracers.shape[0]
    high, low = filter_tables(N)
    level = pl.BlockSpec((1, R, N), lambda k: (k, 0, 0))
    some = lambda n, rows: pl.BlockSpec((n, 1, rows, N), lambda k: (0, k, 0, 0))
    whole = lambda shape: pl.BlockSpec(shape, lambda k: (0,) * len(shape))
    return pl.pallas_call(
        functools.partial(second_kernel, lat_rows),
        grid=(L,),
        in_specs=[whole(table.shape), level, level, level, some(T, R), some(2 + T, 1), some(4 + T, 1)]
        + [whole((R, LANES)), whole(high.shape), whole(low.shape)],
        out_specs=[whole((1, L, R, N)), whole((1, L, R, N)), whole((3 + T, L, 2, N))],
        out_shape=[
            jax.ShapeDtypeStruct((1, L, R, N), jnp.float32),
            jax.ShapeDtypeStruct((1, L, R, N), jnp.float32),
            jax.ShapeDtypeStruct((3 + T, L, 2, N), jnp.float32),
        ],
        scratch_shapes=[pltpu.VMEM((2, L, R, N), jnp.float32)],
        compiler_params=params(),
        cost_estimate=cost(12 * 2 * L * R * high.size, 4 * L * R * N * (8 + T)),
        name="second_step",
    )(
        table, thickness, wind_u, wind_v, tracers, up, down,
        jnp.broadcast_to(cutoff[:, None], (R, LANES)), jnp.asarray(high), jnp.asarray(low),
    )


def mass_kernel(C, S, *refs):
    base_ref, mass_ref = refs[-2:]
    lev = lax.axis_index("lev")
    others_mass, base = None, None
    for s in range(1, C):
        other = functools.reduce(jnp.add, [ref[...] for ref in refs[(s - 1) * S : s * S]])
        below = jnp.where(lev >= s, other, 0.0)
        others_mass = other if others_mass is None else others_mass + other
        base = below if base is None else base + below
    base_ref[...] = base
    mass_ref[...] = others_mass


def other_chips(counts, others):
    return pl.pallas_call(
        functools.partial(mass_kernel, *counts),
        in_specs=[VMEM] * len(others),
        out_specs=[VMEM] * 2,
        out_shape=[jax.ShapeDtypeStruct(others[0].shape, jnp.float32)] * 2,
        compiler_params=params(),
        cost_estimate=cost(1e11, 1e9),
        name="other_chips",
    )(*others)


def add_weights(weight_ref, sum_ref):
    total = jnp.zeros(weight_ref.shape[1:], jnp.float32)
    for k in range(weight_ref.shape[0]):
        sum_ref[k] = total
        total = total + weight_ref[k]
    sum_ref[weight_ref.shape[0]] = total
    return total


def source_levels(place, counts, thick, others):
    C, S = counts
    lev, sub = place
    spot = [lax.rem(lev - g // S + C, C) * S + lax.rem(sub - g % S + S, S) for g in range(len(thick))]
    group = [functools.reduce(jnp.add, levels) for levels in thick]
    mass = functools.reduce(jnp.add, group)
    base = jnp.zeros_like(mass)
    if others:
        base, mass = others[0], mass + others[1]
    sources = []
    for g, levels in enumerate(thick):
        low = base
        for other in range(len(thick)):
            if other != g:
                low = low + jnp.where(spot[other] < spot[g], group[other], 0.0)
        for m, value in enumerate(levels):
            sources.append((g, m, low, value))
            low = low + value
    return mass, sources


def covered(top, sources):
    return [jnp.minimum(jnp.maximum(top - low, 0.0), value) for _, _, low, value in sources]


def remap_rows(weight_ref, sum_ref, counts, steps, thick_refs, field_refs, other_refs, store):
    C, S = counts
    _, L, R, N = thick_refs[0].shape
    rows = min(R, 8)
    place = lev, sub = lax.axis_index("lev"), lax.axis_index("sub")
    firsts = [(lax.rem(lev + s, C) * S + sub) * L for s in steps]
    weight_sum = add_weights(weight_ref, sum_ref)[0:rows]

    def tile(at, columns):
        thick = [[ref[0, m, at, columns] for m in range(L)] for ref in thick_refs]
        others = [ref[at, columns] for ref in other_refs]
        mass, sources = source_levels(place, counts, thick, others)
        unit = mass / weight_sum
        for index, s in enumerate(steps):
            below = covered(unit * sum_ref[firsts[index], 0:rows], sources)
            for i in range(L):
                upto = covered(unit * sum_ref[firsts[index] + i + 1, 0:rows], sources)
                part = [a - b for a, b in zip(upto, below)]
                below = upto
                target = unit * weight_ref[firsts[index] + i, 0:rows]
                scale = 1.0 / target
                means = []
                for refs in field_refs:
                    terms = [refs[g][0][refs[g][1], m, at, columns] * w for (g, m, _, _), w in zip(sources, part)]
                    means.append(functools.reduce(jnp.add, terms) * scale)
                store(s, i, at, columns, target, means)

    for r in range(0, R, rows):

        def body(c, carry):
            tile(slice(r, r + rows), pl.ds(pl.multiple_of(c * LANES, LANES), LANES))
            return carry

        lax.fori_loop(0, N // LANES, body, 0)


def inner_part(at, margin, rows):
    return max(at.start, margin), min(at.stop, rows - margin)


def remap_kernel(counts, steps, fields, margin, with_thickness, sizes, weight_ref, *refs):
    *refs, sum_ref = refs
    C, S = counts
    thick_refs, refs = refs[:S], refs[S:]
    bundles = []
    for _ in range(sizes[0]):
        bundles.append(refs[:S])
        refs = refs[S:]
    other_refs, out_refs = refs[:2], refs[len(refs) - len(steps) - with_thickness :]
    _, L, R, _ = thick_refs[0].shape
    thick_out_ref = out_refs[-1]
    field_refs = [[(ref, index) for ref in bundles[which]] for which, index in fields]

    def store(s, i, at, columns, target, means):
        out_ref = out_refs[steps.index(s)]
        if with_thickness and s == 0:
            thick_out_ref[i, at, columns] = target
        for f, value in enumerate(means):
            if s == 0:
                out_ref[f, i, at, columns] = value
            else:
                lower, upper = inner_part(at, margin, R)
                start = (f * L + i) * (R - 2 * margin) - margin
                out_ref[start + lower : start + upper, columns] = value[lower - at.start : upper - at.start]

    remap_rows(
        weight_ref, sum_ref, counts, steps, thick_refs, field_refs, other_refs, store
    )


def remap_parts(counts, weights, thick, bundles, others, fields, steps, margin, with_thickness=False, wait=()):
    C, S = counts
    _, L, R, N = thick[0].shape
    F = len(fields)
    whole = jax.ShapeDtypeStruct((F, L, R, N), jnp.float32)
    inner = jax.ShapeDtypeStruct((F * L * (R - 2 * margin), N), jnp.float32)
    flat = [a for bundle in bundles for a in bundle]
    out_shape = [whole if s == 0 else inner for s in steps]
    if with_thickness:
        out_shape.append(jax.ShapeDtypeStruct((L, R, N), jnp.float32))
    return pl.pallas_call(
        functools.partial(remap_kernel, counts, tuple(steps), tuple(fields), margin, with_thickness, (len(bundles),)),
        in_specs=[VMEM] * (1 + len(thick) + len(flat) + len(others)) + after(wait),
        out_specs=[VMEM] * len(out_shape),
        out_shape=out_shape,
        scratch_shapes=[pltpu.VMEM((weights.shape[0] + 1, 8, LANES), jnp.float32)],
        compiler_params=params(),
        cost_estimate=cost(len(steps) * S * L * L * R * N * (5 + 2 * F), 4 * R * N * L * (F + 1) * (S + len(steps))),
        name="remap_parts",
    )(weights, *thick, *flat, *others, *wait)


def remap_edge_kernel(counts, near_fields, weight_ref, *refs):
    *refs, sum_ref = refs
    G = counts[0] * counts[1]
    edge_refs, near_refs, rest_refs = refs[:G], refs[G : 2 * G], refs[2 * G : 3 * G]
    edge_out_ref, thick_out_ref, near_out_ref = refs[-3:]

    def store_edge(s, i, at, columns, target, means):
        thick_out_ref[i, at, columns] = target
        for f, value in enumerate(means):
            edge_out_ref[f, i, at, columns] = value

    def store_near(s, i, at, columns, target, means):
        for f, value in enumerate(means):
            near_out_ref[f, i, at, columns] = value

    fields = [[(ref, f) for ref in edge_refs] for f in range(1, edge_refs[0].shape[0])]
    remap_rows(weight_ref, sum_ref, counts, (0,), edge_refs, fields, [], store_edge)
    bundles = (near_refs, rest_refs)
    fields = [[(ref, index) for ref in bundles[which]] for which, index in near_fields]
    remap_rows(weight_ref, sum_ref, counts, (0,), near_refs, fields, [], store_near)


def remap_edges(counts, weights, edges, near, near_rest, wait=()):
    F, L, R, N = edges[0].shape
    T = F - 3
    near_fields = tuple((0, 1) if f == 0 else (1, f - 1) for f in range(T))
    operands = [*edges, *near, *near_rest]
    return pl.pallas_call(
        functools.partial(remap_edge_kernel, counts, near_fields),
        in_specs=[VMEM] * (1 + len(operands)) + after(wait),
        out_specs=[VMEM] * 3,
        out_shape=[
            jax.ShapeDtypeStruct((F - 1, L, R, N), jnp.float32),
            jax.ShapeDtypeStruct((L, R, N), jnp.float32),
            jax.ShapeDtypeStruct((T, L, R, N), jnp.float32),
        ],
        scratch_shapes=[pltpu.VMEM((weights.shape[0] + 1, 8, LANES), jnp.float32)],
        compiler_params=params(),
        cost_estimate=cost(len(edges) * L * L * R * N * 40, 4 * R * N * L * len(operands) * F),
        name="remap_edges",
    )(weights, *operands, *wait)


def finish_kernel(margin, own_ref, near_ref, edge_ref, thick_ref, thick_edge_ref, *refs):
    *arrived_refs, out_ref, thick_out_ref, token_ref = refs
    token_ref[...] = jnp.zeros_like(token_ref)
    T, L, R, _ = out_ref.shape
    thick_out_ref[...] = thick_ref[...]
    for i in range(L):
        for row, j in ((0, 0), (R - 1, 1)):
            thick_out_ref[i, row : row + 1] = thick_edge_ref[i, j : j + 1]
    for f in range(T):
        for i in range(L):
            start = (f * L + i) * (R - 2 * margin)
            total = own_ref[f, i, margin : R - margin]
            for ref in arrived_refs:
                total = total + ref[start : start + R - 2 * margin]
            out_ref[f, i, margin : R - margin] = total
            for row, j in ((0, 0), (R - 1, 1)):
                out_ref[f, i, row : row + 1] = edge_ref[2 + f, i, j : j + 1]
            for row, j in ((1, 0), (R - 2, 1)):
                out_ref[f, i, row : row + 1] = near_ref[f, i, j : j + 1]


def finish_tracers(own, near, edge, thick, thick_edge, arrived):
    return pl.pallas_call(
        functools.partial(finish_kernel, 2),
        in_specs=[VMEM] * (5 + len(arrived)),
        out_specs=[VMEM] * 3,
        out_shape=[
            jax.ShapeDtypeStruct(own.shape, jnp.float32),
            jax.ShapeDtypeStruct(thick.shape, jnp.float32),
            jax.ShapeDtypeStruct((8, LANES), jnp.float32),
        ],
        compiler_params=params(),
        cost_estimate=cost(2 * own.size, 12 * own.size),
        name="finish_tracers",
    )(own, near, edge, thick, thick_edge, *arrived)


def finish_winds_kernel(count, own_ref, edge_ref, *refs):
    arrived_refs, out_refs = refs[:count], refs[-2:]
    _, L, R, N = own_ref.shape
    for f, out_ref in enumerate(out_refs):
        for i in range(L):
            start = (f * L + i) * (R - 2)
            total = own_ref[f, i, 1 : R - 1]
            for ref in arrived_refs:
                total = total + ref[start : start + R - 2]
            out_ref[i, 1 : R - 1] = total
            out_ref[i, 0:1] = edge_ref[f, i, 0:1]
            out_ref[i, R - 1 : R] = edge_ref[f, i, 1:2]


def finish_winds(own, arrived, edge, wait):
    return pl.pallas_call(
        functools.partial(finish_winds_kernel, len(arrived)),
        in_specs=[VMEM] * (2 + len(arrived)) + after(wait),
        out_specs=[VMEM] * 2,
        out_shape=[jax.ShapeDtypeStruct(own.shape[1:], jnp.float32)] * 2,
        compiler_params=params(),
        cost_estimate=cost(own.size, 12 * own.size),
        name="finish_winds",
    )(own, edge, *arrived, *wait)


def edge_kernel(thick_hbm, u_hbm, v_hbm, tracer_hbm, *refs):
    last_ref, leading_ref, top_ref, low_ref, tracer_ref, sems = refs[-6:]
    T, L, R, _ = tracer_hbm.shape
    top = pl.ds(R - 8, 8)
    copies = [
        pltpu.make_async_copy(thick_hbm.at[:, top], top_ref.at[0], sems.at[0]),
        pltpu.make_async_copy(v_hbm.at[:, top], top_ref.at[1], sems.at[1]),
        pltpu.make_async_copy(thick_hbm.at[:, pl.ds(0, 8)], low_ref.at[0], sems.at[2]),
        pltpu.make_async_copy(u_hbm.at[:, pl.ds(0, 8)], low_ref.at[1], sems.at[3]),
        pltpu.make_async_copy(v_hbm.at[:, pl.ds(0, 8)], low_ref.at[2], sems.at[4]),
        pltpu.make_async_copy(tracer_hbm.at[:, :, top], tracer_ref.at[0], sems.at[5]),
        pltpu.make_async_copy(tracer_hbm.at[:, :, pl.ds(0, 8)], tracer_ref.at[1], sems.at[6]),
    ]
    for copy in copies:
        copy.start()
    for copy in copies:
        copy.wait()
    last_ref[0:2] = top_ref[:, :, 7:8]
    last_ref[2 : 2 + T] = tracer_ref[0, :, :, 7:8]
    leading_ref[0] = low_ref[0, :, 0:1]
    leading_ref[1] = low_ref[0, :, 1:2]
    leading_ref[2:4] = low_ref[1:3, :, 0:1]
    leading_ref[4 : 4 + T] = tracer_ref[1, :, :, 0:1]


def edge_rows(thickness, wind_u, wind_v, tracers, wait):
    L, R, N = thickness.shape
    T = tracers.shape[0]
    operands = [pltpu.with_memory_space_constraint(a, pltpu.HBM) for a in (thickness, wind_u, wind_v, tracers)]
    return pl.pallas_call(
        edge_kernel,
        in_specs=after(operands) + after(wait),
        out_specs=[VMEM] * 2,
        out_shape=[
            jax.ShapeDtypeStruct((2 + T, L, 1, N), jnp.float32),
            jax.ShapeDtypeStruct((4 + T, L, 1, N), jnp.float32),
        ],
        scratch_shapes=[
            pltpu.VMEM((2, L, 8, N), jnp.float32),
            pltpu.VMEM((3, L, 8, N), jnp.float32),
            pltpu.VMEM((2, T, L, 8, N), jnp.float32),
            pltpu.SemaphoreType.DMA((7,)),
        ],
        compiler_params=params(),
        cost_estimate=cost(1e10, 1e9),
        name="edge_rows",
    )(*operands, *wait)


def shifted(value, lev_count, sub_count, s, t):
    if t == 0:
        return lax.ppermute(value, "lev", [(i, (i + s) % lev_count) for i in range(lev_count)])
    if s == 0:
        return lax.ppermute(value, "sub", [(i, (i + t) % sub_count) for i in range(sub_count)])
    pairs = [
        (i * sub_count + j, (i + s) % lev_count * sub_count + (j + t) % sub_count)
        for i in range(lev_count)
        for j in range(sub_count)
    ]
    return lax.ppermute(value, ("lev", "sub"), pairs)


def per_device(thickness, wind_u, wind_v, tracers, level_weights, cutoff):
    L, R, N = thickness.shape
    lat_count = lax.axis_size("lat")
    C, S = lax.axis_size("lev"), lax.axis_size("sub")
    lat_rows = R * lat_count
    send = functools.partial(shifted, lev_count=C, sub_count=S)

    T = tracers.shape[0]
    northward = [(i, i + 1) for i in range(lat_count - 1)]
    southward = [(j, i) for i, j in northward]
    table = jnp.asarray(geometry_table(lat_rows, R))
    weights = jnp.broadcast_to(level_weights[:, None, None], (level_weights.shape[0], 8, LANES))
    away = range(1, C)

    def with_others_of_chip(own):
        return [own] + [send(own, s=0, t=t) for t in range(1, S)]

    def sent(parts):
        return [send(part, s=s, t=0) for s, part in zip(away, parts)]

    remap = functools.partial(remap_parts, (C, S), weights)

    new, own_sum, *arguments = first_step(table, thickness, wind_u, wind_v, tracers)
    others = [send(own_sum, s=s, t=t) for s in away for t in range(S)]
    inner, near, near_rest = inner_step(table, new, *arguments)
    group = with_others_of_chip(inner)
    near = [near] + [send(near, s=s, t=0) for s in away]
    near_rest = [near_rest] + [send(near_rest, s=s, t=0) for s in away]
    others = other_chips((C, S), others)
    tracer_fields = [(0, 1 + c) for c in range(T)]
    away_parts = remap(group, [group], others, tracer_fields, away, 2)
    arrived = sent(away_parts)

    last, leading = edge_rows(
        thickness, wind_u, wind_v, tracers, [away_parts[0], *near[1:2], *near_rest[1:2]]
    )
    up = lax.ppermute(last, "lat", northward)
    down = lax.ppermute(leading, "lat", southward)
    u, v, edge = second_step(table, lat_rows, thickness, wind_u, wind_v, tracers, up, down, cutoff)
    edges = [edge] + [send(edge, s=s, t=0) for s in away]
    winds = [with_others_of_chip(u), with_others_of_chip(v)]
    tracers_own, thick_inner = remap(group, [group], others, tracer_fields, (0,), 0, with_thickness=True, wait=[edge])
    winds_own, *winds_away = remap(
        group, winds, others, [(0, 0), (1, 0)], range(C), 1, wait=[tracers_own, *arrived[:1]]
    )
    winds_arrived = sent(winds_away)
    near, near_rest, edges = (
        [a for own in sources for a in with_others_of_chip(own)] for sources in (near, near_rest, edges)
    )
    edge_out, thick_edge, near_out = remap_edges(
        (C, S), weights, edges, near, near_rest, wait=winds_away[:1]
    )

    tracers_out, thickness_out, token = finish_tracers(
        tracers_own, near_out, edge_out, thick_inner, thick_edge, arrived
    )
    u_out, v_out = finish_winds(winds_own, winds_arrived, edge_out, [token])
    return thickness_out, u_out, v_out, tracers_out


def solution(mesh):
    placed = (
        P(("member", "lev", "sub"), "lat", None),
        P(("member", "lev", "sub"), "lat", None),
        P(("member", "lev", "sub"), "lat", None),
        P("member", ("lev", "sub"), "lat", None),
        P(),
        P("lat"),
    )
    return jax.shard_map(
        per_device,
        mesh=mesh,
        in_specs=placed,
        out_specs=(
            P(("member", "lev", "sub"), "lat", None),
            P(("member", "lev", "sub"), "lat", None),
            P(("member", "lev", "sub"), "lat", None),
            P("member", ("lev", "sub"), "lat", None),
        ),
        check_vma=False,
    )
```

```python
import functools

import jax
import jax.numpy as jnp
import ml_dtypes
import numpy as np
from jax import lax
from jax.experimental import pallas as pl
from jax.experimental.pallas import tpu as pltpu
from jax.sharding import PartitionSpec as P

LANES = 128
VMEM = pl.BlockSpec(memory_space=pltpu.VMEM)


def params():
    return pltpu.CompilerParams(vmem_limit_bytes=16 * 1024 * 1024)


def cost(flops, bytes_accessed):
    return pl.CostEstimate(flops=int(flops), bytes_accessed=int(bytes_accessed), transcendentals=0)


def after(arrays):
    return [pl.BlockSpec(memory_space=pl.ANY)] * len(arrays)


def geometry_table(lat_rows, band_rows):
    bands = lat_rows // band_rows
    table = np.zeros((bands, band_rows + 8, LANES), np.float32)
    for band in range(bands):
        for j in range(band_rows + 1):
            row = band * band_rows + j
            south = np.sin(row * np.pi / lat_rows) if 0 < row < lat_rows else 0.0
            north = np.sin((row + 1) * np.pi / lat_rows) if row + 1 < lat_rows else 0.0
            table[band, j, 0] = south
            table[band, j, 1] = north
            table[band, j, 2] = 1.0 / np.sin((row + 0.5) * np.pi / lat_rows)
    return table


def east_of(value):
    return pltpu.roll(value, value.shape[1] - 1, 1)


def west_of(value):
    return pltpu.roll(value, 1, 1)


def row_ids(shape):
    return lax.broadcasted_iota(jnp.int32, shape, 0)


def north_of(value, beyond):
    rows = value.shape[0]
    rolled = pltpu.roll(value, rows - 1, 0)
    return rolled if beyond is None else jnp.where(row_ids(value.shape) == rows - 1, beyond, rolled)


def south_of(value, beyond):
    rolled = pltpu.roll(value, 1, 0)
    return rolled if beyond is None else jnp.where(row_ids(value.shape) == 0, beyond, rolled)


def fluxes(geo, thick, u, v, thick_s, v_s, thick_n):
    rows = thick.shape[0]
    east = u * jnp.where(u > 0, thick, east_of(thick))
    north = v * jnp.where(v > 0, thick, north_of(thick, thick_n)) * geo[0:rows, 1:2]
    below = None if v_s is None else v_s * jnp.where(v_s > 0, thick_s, thick[0:1]) * geo[0:1, 0:1]
    return east, north, below


def tracer_change(q, q_s, q_n, thick, u, v, v_s, east, north, below, inverse):
    t_east = east * jnp.where(u > 0, q, east_of(q))
    t_north = north * jnp.where(v > 0, q, north_of(q, q_n))
    t_below = None if v_s is None else below * jnp.where(v_s > 0, q_s, q[0:1])
    change = thick * q - (t_east - west_of(t_east))
    return change - (t_north - south_of(t_north, t_below)) * inverse


def first_kernel(table_hbm, thick_hbm, u_hbm, v_hbm, tracer_hbm, *refs):
    new_ref, sum_ref, near_ref, thick_ref, u_ref, v_ref, tracer_ref, geo_ref, sems = refs
    L, rows, _ = thick_ref.shape
    table_copy = pltpu.make_async_copy(table_hbm.at[lax.axis_index("lat")], geo_ref, sems.at[3, 0])
    table_copy.start()
    pairs = ((thick_hbm, thick_ref), (u_hbm, u_ref), (v_hbm, v_ref))

    def copies(k):
        return [pltpu.make_async_copy(a.at[k], b.at[k], sems.at[i, k]) for i, (a, b) in enumerate(pairs)]

    for k in range(L):
        for copy in copies(k):
            copy.start()
    tracer_copy = pltpu.make_async_copy(tracer_hbm, tracer_ref, sems.at[3, 1])
    tracer_copy.start()
    table_copy.wait()
    geo = geo_ref[...]
    sum_ref[...] = jnp.zeros_like(sum_ref)

    def level(k, carry):
        for copy in copies(k):
            copy.wait()
        thick, u, v = thick_ref[k], u_ref[k], v_ref[k]
        east, north, _ = fluxes(geo, thick, u, v, None, None, None)
        new = thick - (east - west_of(east)) - (north - south_of(north, None)) * geo[0:rows, 2:3]
        new_ref[k] = new
        near_ref[0, k, 0:1] = new[1:2]
        near_ref[0, k, 1:2] = new[rows - 2 : rows - 1]
        sum_ref[...] += new
        return carry

    lax.fori_loop(0, L, level, 0)
    tracer_copy.wait()


def first_step(table, thickness, wind_u, wind_v, tracers):
    L, R, N = thickness.shape
    arguments = (thickness, wind_u, wind_v, tracers)
    operands = [pltpu.with_memory_space_constraint(a, pltpu.HBM) for a in (table, *arguments)]
    shapes = [(L, R, N), (R, N), (1, L, 2, N)] + [a.shape for a in arguments]
    return pl.pallas_call(
        first_kernel,
        in_specs=after(operands),
        out_specs=[VMEM] * len(shapes),
        out_shape=[jax.ShapeDtypeStruct(shape, jnp.float32) for shape in shapes],
        scratch_shapes=[pltpu.VMEM(table.shape[1:], jnp.float32), pltpu.SemaphoreType.DMA((4, max(L, 2)))],
        compiler_params=params(),
        cost_estimate=cost(40 * L * R * N, 4 * L * R * N * (7 + 2 * tracers.shape[0])),
        name="first_step",
    )(*operands)


def inner_kernel(table_ref, new_ref, thick_ref, u_ref, v_ref, tracer_ref, out_ref, near_ref, near_rest_ref):
    T, L, rows, _ = tracer_ref.shape
    geo = table_ref[lax.axis_index("lat")]
    inverse = geo[0:rows, 2:3]

    def level(k, carry):
        thick, u, v, new = thick_ref[k], u_ref[k], v_ref[k], new_ref[k]
        east, north, _ = fluxes(geo, thick, u, v, None, None, None)

        out_ref[0, k] = new
        scale = 1.0 / new
        for c in range(T):
            change = tracer_change(
                tracer_ref[c, k], None, None, thick, u, v, None, east, north, None, inverse
            )
            value = change * scale
            out_ref[1 + c, k] = value
            ref, at = (near_ref, c) if c < T // 2 else (near_rest_ref, c - T // 2)
            ref[at, k, 0:1] = value[1:2]
            ref[at, k, 1:2] = value[rows - 2 : rows - 1]
        return carry

    lax.fori_loop(0, L, level, 0)


def inner_step(table, new, thickness, wind_u, wind_v, tracers):
    L, R, N = thickness.shape
    T = tracers.shape[0]
    shape = lambda n, rows: jax.ShapeDtypeStruct((n, L, rows, N), jnp.float32)
    return pl.pallas_call(
        inner_kernel,
        in_specs=[VMEM] * 6,
        out_specs=[VMEM] * 3,
        out_shape=[shape(1 + T, R), shape(T // 2, 2), shape(T - T // 2, 2)],
        compiler_params=params(),
        cost_estimate=cost(130 * L * R * N, 4 * L * R * N * (8 + 2 * T)),
        name="inner_step",
    )(table, new, thickness, wind_u, wind_v, tracers)


def filter_tables(N):
    A = N // LANES
    b = np.arange(LANES)[:, None]
    p = np.arange(LANES)[None, :]
    tables = []
    for q in range(A // 2 + 1):
        angle = 2.0 * np.pi * ((b * (A * p + q)) % N) / N
        c, s = np.cos(angle), np.sin(angle)
        tables.append(np.block([[c, -s], [s, c]]))
    table = np.stack(tables)
    high = table.astype(np.float32).astype(ml_dtypes.bfloat16)
    low = (table - high.astype(np.float64)).astype(np.float32).astype(ml_dtypes.bfloat16)
    return high, low


def split(value):
    high = value.astype(jnp.bfloat16)
    return high, (value - high.astype(jnp.float32)).astype(jnp.bfloat16)


def product(value, high, low, transposed):
    dims = (((1,), (1 if transposed else 0,)), ((), ()))
    dot = lambda x, y: lax.dot_general(x, y, dims, preferred_element_type=jnp.float32)
    v_high, v_low = split(value)
    return dot(v_high, high) + (dot(v_high, low) + dot(v_low, high))


def filter_rows(x, cutoff, high_ref, low_ref):
    A = len(x)
    N = A * LANES
    half = A // 2
    even = [x[a] + x[A - a] for a in range(1, half + 1)]
    odd = [x[a] - x[A - a] for a in range(1, half + 1)]
    angle = lambda q, a: 2.0 * np.pi * ((q * a) % A) / A
    p = lax.broadcasted_iota(jnp.int32, cutoff.shape, 1)
    real, imag = [], []
    for q in range(half + 1):
        re = x[0]
        for a in range(1, half + 1):
            re = re + (even[a - 1] if q == 0 else float(np.cos(angle(q, a))) * even[a - 1])
        if q == 0:
            high, low = high_ref[0, 0:LANES], low_ref[0, 0:LANES]
            spectrum = product(re, high, low, False)
        else:
            high, low = high_ref[q], low_ref[q]
            im = -float(np.sin(angle(q, 1))) * odd[0]
            for a in range(2, half + 1):
                im = im - float(np.sin(angle(q, a))) * odd[a - 1]
            spectrum = product(jnp.concatenate([re, im], axis=1), high, low, False)
        mode = A * p + q
        factor = 1.0 / N if q == 0 else 2.0 / N
        kept = jnp.where(jnp.minimum(mode, N - mode) <= cutoff, factor, 0.0)
        back = product(spectrum * jnp.concatenate([kept, kept], axis=1), high, low, True)
        real.append(back[:, :LANES])
        imag.append(back[:, LANES:])
    out = [None] * A
    out[0] = functools.reduce(jnp.add, real)
    for a in range(1, half + 1):
        even_part, odd_part = real[0], None
        for q in range(1, half + 1):
            even_part = even_part + float(np.cos(angle(q, a))) * real[q]
            term = float(np.sin(angle(q, a))) * imag[q]
            odd_part = term if odd_part is None else odd_part + term
        out[a] = even_part - odd_part
        out[A - a] = even_part + odd_part
    return out


def second_kernel(
    lat_rows, table_ref, thick_ref, u_ref, v_ref, tracer_ref, up_ref, down_ref, cutoff_ref, high_ref, low_ref, *refs
):
    *wind_refs, edge_ref, new_wind = refs
    k = pl.program_id(0)
    _, L, rows, width = new_wind.shape
    band = lax.axis_index("lat")
    geo = table_ref[band]
    thick, u, v = thick_ref[0], u_ref[0], v_ref[0]
    thick_s, v_s = up_ref[0, 0], up_ref[1, 0]
    thick_n, thick_nn, u_n, v_n = (down_ref[i, 0] for i in range(4))
    east, north, below = fluxes(geo, thick, u, v, thick_s, v_s, thick_n)
    inverse = geo[0:rows, 2:3]
    new = thick - (east - west_of(east)) - (north - south_of(north, below)) * inverse
    east_n = u_n * jnp.where(u_n > 0, thick_n, east_of(thick_n))
    north_n = v_n * jnp.where(v_n > 0, thick_n, thick_nn) * geo[rows : rows + 1, 1:2]
    new_n = (
        thick_n
        - (east_n - west_of(east_n))
        - (north_n - north[rows - 1 : rows]) * geo[rows : rows + 1, 2:3]
    )
    new_wind[0, k] = u - 0.05 * (east_of(new) - new)
    inside = band * rows + row_ids(new.shape) < lat_rows - 1
    new_wind[1, k] = jnp.where(inside, v - 0.05 * (north_of(new, new_n) - new), 0.0)

    def store_edges(field, level, value):
        edge_ref[field, level, 0:1] = value[0:1]
        edge_ref[field, level, 1:2] = value[rows - 1 : rows]

    store_edges(0, k, new)
    scale = 1.0 / new
    for c in range(tracer_ref.shape[0]):
        change = tracer_change(
            tracer_ref[c, 0], up_ref[2 + c, 0], down_ref[4 + c, 0], thick, u, v, v_s, east, north, below, inverse
        )
        store_edges(3 + c, k, change * scale)

    @pl.when(k == L - 1)
    def _():
        pieces = [
            new_wind[:, :, :, a * LANES : (a + 1) * LANES].reshape(2 * L * rows, LANES) for a in range(width // LANES)
        ]
        cutoff = jnp.broadcast_to(cutoff_ref[...][None], (2 * L, rows, LANES)).reshape(2 * L * rows, LANES)
        for a, piece in enumerate(filter_rows(pieces, cutoff, high_ref, low_ref)):
            piece = piece.reshape(2, L, rows, LANES)
            for f in range(2):
                wind_refs[f][0, :, :, a * LANES : (a + 1) * LANES] = piece[f]
        for f in range(2):
            for level in range(L):
                store_edges(1 + f, level, wind_refs[f][0, level])


def second_step(table, lat_rows, thickness, wind_u, wind_v, tracers, up, down, cutoff):
    L, R, N = thickness.shape
    T = tracers.shape[0]
    high, low = filter_tables(N)
    level = pl.BlockSpec((1, R, N), lambda k: (k, 0, 0))
    some = lambda n, rows: pl.BlockSpec((n, 1, rows, N), lambda k: (0, k, 0, 0))
    whole = lambda shape: pl.BlockSpec(shape, lambda k: (0,) * len(shape))
    return pl.pallas_call(
        functools.partial(second_kernel, lat_rows),
        grid=(L,),
        in_specs=[whole(table.shape), level, level, level, some(T, R), some(2 + T, 1), some(4 + T, 1)]
        + [whole((R, LANES)), whole(high.shape), whole(low.shape)],
        out_specs=[whole((1, L, R, N)), whole((1, L, R, N)), whole((3 + T, L, 2, N))],
        out_shape=[
            jax.ShapeDtypeStruct((1, L, R, N), jnp.float32),
            jax.ShapeDtypeStruct((1, L, R, N), jnp.float32),
            jax.ShapeDtypeStruct((3 + T, L, 2, N), jnp.float32),
        ],
        scratch_shapes=[pltpu.VMEM((2, L, R, N), jnp.float32)],
        compiler_params=params(),
        cost_estimate=cost(12 * 2 * L * R * high.size, 4 * L * R * N * (8 + T)),
        name="second_step",
    )(
        table, thickness, wind_u, wind_v, tracers, up, down,
        jnp.broadcast_to(cutoff[:, None], (R, LANES)), jnp.asarray(high), jnp.asarray(low),
    )


def mass_kernel(C, S, *refs):
    base_ref, mass_ref = refs[-2:]
    lev = lax.axis_index("lev")
    others_mass, base = None, None
    for s in range(1, C):
        other = functools.reduce(jnp.add, [ref[...] for ref in refs[(s - 1) * S : s * S]])
        below = jnp.where(lev >= s, other, 0.0)
        others_mass = other if others_mass is None else others_mass + other
        base = below if base is None else base + below
    base_ref[...] = base
    mass_ref[...] = others_mass


def other_chips(counts, others, wait):
    return pl.pallas_call(
        functools.partial(mass_kernel, *counts),
        in_specs=[VMEM] * len(others) + after(wait),
        out_specs=[VMEM] * 2,
        out_shape=[jax.ShapeDtypeStruct(others[0].shape, jnp.float32)] * 2,
        compiler_params=params(),
        cost_estimate=cost(1e11, 1e9),
        name="other_chips",
    )(*others, *wait)


def add_weights(weight_ref, sum_ref):
    total = jnp.zeros(weight_ref.shape[1:], jnp.float32)
    for k in range(weight_ref.shape[0]):
        sum_ref[k] = total
        total = total + weight_ref[k]
    sum_ref[weight_ref.shape[0]] = total
    return total


def source_levels(place, counts, thick, others):
    C, S = counts
    lev, sub = place
    spot = [lax.rem(lev - g // S + C, C) * S + lax.rem(sub - g % S + S, S) for g in range(len(thick))]
    group = [functools.reduce(jnp.add, levels) for levels in thick]
    mass = functools.reduce(jnp.add, group)
    base = jnp.zeros_like(mass)
    if others:
        base, mass = others[0], mass + others[1]
    sources = []
    for g, levels in enumerate(thick):
        low = base
        for other in range(len(thick)):
            if other != g:
                low = low + jnp.where(spot[other] < spot[g], group[other], 0.0)
        for m, value in enumerate(levels):
            sources.append((g, m, low, value))
            low = low + value
    return mass, sources


def covered(top, sources):
    return [jnp.minimum(jnp.maximum(top - low, 0.0), value) for _, _, low, value in sources]


def remap_rows(weight_ref, sum_ref, counts, steps, thick_refs, field_refs, other_refs, store):
    C, S = counts
    _, L, R, N = thick_refs[0].shape
    rows = min(R, 8)
    place = lev, sub = lax.axis_index("lev"), lax.axis_index("sub")
    firsts = [(lax.rem(lev + s, C) * S + sub) * L for s in steps]
    weight_sum = add_weights(weight_ref, sum_ref)[0:rows]

    def tile(at, columns):
        thick = [[ref[0, m, at, columns] for m in range(L)] for ref in thick_refs]
        others = [ref[at, columns] for ref in other_refs]
        mass, sources = source_levels(place, counts, thick, others)
        unit = mass / weight_sum
        for index, s in enumerate(steps):
            below = covered(unit * sum_ref[firsts[index], 0:rows], sources)
            for i in range(L):
                upto = covered(unit * sum_ref[firsts[index] + i + 1, 0:rows], sources)
                part = [a - b for a, b in zip(upto, below)]
                below = upto
                target = unit * weight_ref[firsts[index] + i, 0:rows]
                scale = 1.0 / target
                means = []
                for refs in field_refs:
                    terms = [refs[g][0][refs[g][1], m, at, columns] * w for (g, m, _, _), w in zip(sources, part)]
                    means.append(functools.reduce(jnp.add, terms) * scale)
                store(s, i, at, columns, target, means)

    for r in range(0, R, rows):

        def body(c, carry):
            tile(slice(r, r + rows), pl.ds(pl.multiple_of(c * LANES, LANES), LANES))
            return carry

        lax.fori_loop(0, N // LANES, body, 0)


def inner_part(at, margin, rows):
    return max(at.start, margin), min(at.stop, rows - margin)


def remap_kernel(counts, steps, fields, margin, with_thickness, sizes, weight_ref, *refs):
    *refs, sum_ref = refs
    C, S = counts
    thick_refs, refs = refs[:S], refs[S:]
    bundles = []
    for _ in range(sizes[0]):
        bundles.append(refs[:S])
        refs = refs[S:]
    other_refs, out_refs = refs[:2], refs[len(refs) - len(steps) - with_thickness :]
    _, L, R, _ = thick_refs[0].shape
    thick_out_ref = out_refs[-1]
    field_refs = [[(ref, index) for ref in bundles[which]] for which, index in fields]

    def store(s, i, at, columns, target, means):
        out_ref = out_refs[steps.index(s)]
        if with_thickness and s == 0:
            thick_out_ref[i, at, columns] = target
        for f, value in enumerate(means):
            if s == 0:
                out_ref[f, i, at, columns] = value
            else:
                lower, upper = inner_part(at, margin, R)
                start = (f * L + i) * (R - 2 * margin) - margin
                out_ref[start + lower : start + upper, columns] = value[lower - at.start : upper - at.start]

    remap_rows(
        weight_ref, sum_ref, counts, steps, thick_refs, field_refs, other_refs, store
    )


def remap_parts(counts, weights, thick, bundles, others, fields, steps, margin, with_thickness=False, wait=()):
    C, S = counts
    _, L, R, N = thick[0].shape
    F = len(fields)
    whole = jax.ShapeDtypeStruct((F, L, R, N), jnp.float32)
    inner = jax.ShapeDtypeStruct((F * L * (R - 2 * margin), N), jnp.float32)
    flat = [a for bundle in bundles for a in bundle]
    out_shape = [whole if s == 0 else inner for s in steps]
    if with_thickness:
        out_shape.append(jax.ShapeDtypeStruct((L, R, N), jnp.float32))
    return pl.pallas_call(
        functools.partial(remap_kernel, counts, tuple(steps), tuple(fields), margin, with_thickness, (len(bundles),)),
        in_specs=[VMEM] * (1 + len(thick) + len(flat) + len(others)) + after(wait),
        out_specs=[VMEM] * len(out_shape),
        out_shape=out_shape,
        scratch_shapes=[pltpu.VMEM((weights.shape[0] + 1, 8, LANES), jnp.float32)],
        compiler_params=params(),
        cost_estimate=cost(len(steps) * S * L * L * R * N * (5 + 2 * F), 4 * R * N * L * (F + 1) * (S + len(steps))),
        name="remap_parts",
    )(weights, *thick, *flat, *others, *wait)


def remap_edge_kernel(counts, near_fields, weight_ref, *refs):
    *refs, sum_ref = refs
    G = counts[0] * counts[1]
    edge_refs, near_refs = refs[:G], refs[G : 2 * G]
    bundles = (refs[2 * G : 3 * G], refs[3 * G : 4 * G])
    edge_out_ref, thick_out_ref, near_out_ref = refs[-3:]

    def store_edge(s, i, at, columns, target, means):
        thick_out_ref[i, at, columns] = target
        for f, value in enumerate(means):
            edge_out_ref[f, i, at, columns] = value

    def store_near(s, i, at, columns, target, means):
        for f, value in enumerate(means):
            near_out_ref[f, i, at, columns] = value

    fields = [[(ref, f) for ref in edge_refs] for f in range(1, edge_refs[0].shape[0])]
    remap_rows(weight_ref, sum_ref, counts, (0,), edge_refs, fields, [], store_edge)
    fields = [[(ref, index) for ref in bundles[which]] for which, index in near_fields]
    remap_rows(weight_ref, sum_ref, counts, (0,), near_refs, fields, [], store_near)


def remap_edges(counts, weights, edges, near_new, near, near_rest, wait=()):
    F, L, R, N = edges[0].shape
    T = F - 3
    near_fields = tuple((0, f) if f < T // 2 else (1, f - T // 2) for f in range(T))
    operands = [*edges, *near_new, *near, *near_rest]
    return pl.pallas_call(
        functools.partial(remap_edge_kernel, counts, near_fields),
        in_specs=[VMEM] * (1 + len(operands)) + after(wait),
        out_specs=[VMEM] * 3,
        out_shape=[
            jax.ShapeDtypeStruct((F - 1, L, R, N), jnp.float32),
            jax.ShapeDtypeStruct((L, R, N), jnp.float32),
            jax.ShapeDtypeStruct((T, L, R, N), jnp.float32),
        ],
        scratch_shapes=[pltpu.VMEM((weights.shape[0] + 1, 8, LANES), jnp.float32)],
        compiler_params=params(),
        cost_estimate=cost(len(edges) * L * L * R * N * 40, 4 * R * N * L * len(operands) * F),
        name="remap_edges",
    )(weights, *operands, *wait)


def finish_kernel(margin, own_ref, near_ref, edge_ref, thick_ref, thick_edge_ref, *refs):
    *arrived_refs, out_ref, thick_out_ref, token_ref = refs
    token_ref[...] = jnp.zeros_like(token_ref)
    T, L, R, _ = out_ref.shape
    thick_out_ref[...] = thick_ref[...]
    for i in range(L):
        for row, j in ((0, 0), (R - 1, 1)):
            thick_out_ref[i, row : row + 1] = thick_edge_ref[i, j : j + 1]
    for f in range(T):
        for i in range(L):
            start = (f * L + i) * (R - 2 * margin)
            total = own_ref[f, i, margin : R - margin]
            for ref in arrived_refs:
                total = total + ref[start : start + R - 2 * margin]
            out_ref[f, i, margin : R - margin] = total
            for row, j in ((0, 0), (R - 1, 1)):
                out_ref[f, i, row : row + 1] = edge_ref[2 + f, i, j : j + 1]
            for row, j in ((1, 0), (R - 2, 1)):
                out_ref[f, i, row : row + 1] = near_ref[f, i, j : j + 1]


def finish_tracers(own, near, edge, thick, thick_edge, arrived):
    return pl.pallas_call(
        functools.partial(finish_kernel, 2),
        in_specs=[VMEM] * (5 + len(arrived)),
        out_specs=[VMEM] * 3,
        out_shape=[
            jax.ShapeDtypeStruct(own.shape, jnp.float32),
            jax.ShapeDtypeStruct(thick.shape, jnp.float32),
            jax.ShapeDtypeStruct((8, LANES), jnp.float32),
        ],
        compiler_params=params(),
        cost_estimate=cost(2 * own.size, 12 * own.size),
        name="finish_tracers",
    )(own, near, edge, thick, thick_edge, *arrived)


def finish_winds_kernel(count, own_ref, edge_ref, *refs):
    arrived_refs, (*out_refs, result_ref, sems) = refs[:count], refs[len(refs) - 4 :]
    _, L, R, _ = own_ref.shape
    copies = []
    for f, out_ref in enumerate(out_refs):
        for i in range(L):
            start = (f * L + i) * (R - 2)
            total = own_ref[f, i, 1 : R - 1]
            for ref in arrived_refs:
                total = total + ref[start : start + R - 2]
            result_ref[f, i, 1 : R - 1] = total
            result_ref[f, i, 0:1] = edge_ref[f, i, 0:1]
            result_ref[f, i, R - 1 : R] = edge_ref[f, i, 1:2]
            copies.append(pltpu.make_async_copy(result_ref.at[f, i], out_ref.at[i], sems.at[f, i]))
            copies[-1].start()
    for copy in copies:
        copy.wait()


def finish_winds(own, arrived, edge, wait):
    F, L = own.shape[:2]
    return pl.pallas_call(
        functools.partial(finish_winds_kernel, len(arrived)),
        in_specs=[VMEM] * (2 + len(arrived)) + after(wait),
        out_specs=[pl.BlockSpec(memory_space=pl.ANY)] * F,
        out_shape=[jax.ShapeDtypeStruct(own.shape[1:], jnp.float32)] * F,
        scratch_shapes=[pltpu.VMEM(own.shape, jnp.float32), pltpu.SemaphoreType.DMA((F, L))],
        compiler_params=params(),
        cost_estimate=cost(own.size, 12 * own.size),
        name="finish_winds",
    )(own, edge, *arrived, *wait)


def edge_kernel(thick_hbm, u_hbm, v_hbm, tracer_hbm, *refs):
    last_ref, leading_ref, top_ref, low_ref, tracer_ref, sems = refs[-6:]
    T, L, R, _ = tracer_hbm.shape
    top = pl.ds(R - 8, 8)
    copies = [
        pltpu.make_async_copy(thick_hbm.at[:, top], top_ref.at[0], sems.at[0]),
        pltpu.make_async_copy(v_hbm.at[:, top], top_ref.at[1], sems.at[1]),
        pltpu.make_async_copy(thick_hbm.at[:, pl.ds(0, 8)], low_ref.at[0], sems.at[2]),
        pltpu.make_async_copy(u_hbm.at[:, pl.ds(0, 8)], low_ref.at[1], sems.at[3]),
        pltpu.make_async_copy(v_hbm.at[:, pl.ds(0, 8)], low_ref.at[2], sems.at[4]),
        pltpu.make_async_copy(tracer_hbm.at[:, :, top], tracer_ref.at[0], sems.at[5]),
        pltpu.make_async_copy(tracer_hbm.at[:, :, pl.ds(0, 8)], tracer_ref.at[1], sems.at[6]),
    ]
    for copy in copies:
        copy.start()
    for copy in copies:
        copy.wait()
    last_ref[0:2] = top_ref[:, :, 7:8]
    last_ref[2 : 2 + T] = tracer_ref[0, :, :, 7:8]
    leading_ref[0] = low_ref[0, :, 0:1]
    leading_ref[1] = low_ref[0, :, 1:2]
    leading_ref[2:4] = low_ref[1:3, :, 0:1]
    leading_ref[4 : 4 + T] = tracer_ref[1, :, :, 0:1]


def edge_rows(thickness, wind_u, wind_v, tracers, wait):
    L, R, N = thickness.shape
    T = tracers.shape[0]
    operands = [pltpu.with_memory_space_constraint(a, pltpu.HBM) for a in (thickness, wind_u, wind_v, tracers)]
    return pl.pallas_call(
        edge_kernel,
        in_specs=after(operands) + after(wait),
        out_specs=[VMEM] * 2,
        out_shape=[
            jax.ShapeDtypeStruct((2 + T, L, 1, N), jnp.float32),
            jax.ShapeDtypeStruct((4 + T, L, 1, N), jnp.float32),
        ],
        scratch_shapes=[
            pltpu.VMEM((2, L, 8, N), jnp.float32),
            pltpu.VMEM((3, L, 8, N), jnp.float32),
            pltpu.VMEM((2, T, L, 8, N), jnp.float32),
            pltpu.SemaphoreType.DMA((7,)),
        ],
        compiler_params=params(),
        cost_estimate=cost(1e10, 1e9),
        name="edge_rows",
    )(*operands, *wait)


def shifted(value, lev_count, sub_count, s, t):
    if t == 0:
        return lax.ppermute(value, "lev", [(i, (i + s) % lev_count) for i in range(lev_count)])
    if s == 0:
        return lax.ppermute(value, "sub", [(i, (i + t) % sub_count) for i in range(sub_count)])
    pairs = [
        (i * sub_count + j, (i + s) % lev_count * sub_count + (j + t) % sub_count)
        for i in range(lev_count)
        for j in range(sub_count)
    ]
    return lax.ppermute(value, ("lev", "sub"), pairs)


def per_device(thickness, wind_u, wind_v, tracers, level_weights, cutoff):
    L, R, N = thickness.shape
    lat_count = lax.axis_size("lat")
    C, S = lax.axis_size("lev"), lax.axis_size("sub")
    lat_rows = R * lat_count
    send = functools.partial(shifted, lev_count=C, sub_count=S)

    T = tracers.shape[0]
    northward = [(i, i + 1) for i in range(lat_count - 1)]
    southward = [(j, i) for i, j in northward]
    table = jnp.asarray(geometry_table(lat_rows, R))
    weights = jnp.broadcast_to(level_weights[:, None, None], (level_weights.shape[0], 8, LANES))
    away = range(1, C)

    def with_others_of_chip(own):
        return [own] + [send(own, s=0, t=t) for t in range(1, S)]

    def sent(parts):
        return [send(part, s=s, t=0) for s, part in zip(away, parts)]

    remap = functools.partial(remap_parts, (C, S), weights)

    new, own_sum, near_new, *arguments = first_step(table, thickness, wind_u, wind_v, tracers)
    others = [send(own_sum, s=s, t=t) for s in away for t in range(S)]
    near_new = [near_new] + [send(near_new, s=s, t=0) for s in away]
    inner, near, near_rest = inner_step(table, new, *arguments)
    group = with_others_of_chip(inner)
    near = [near] + [send(near, s=s, t=0) for s in away]
    near_rest = [near_rest] + [send(near_rest, s=s, t=0) for s in away]
    others = other_chips((C, S), others, near_new[1:2])
    tracer_fields = [(0, 1 + c) for c in range(T)]
    away_parts = remap(group, [group], others, tracer_fields, away, 2)
    arrived = sent(away_parts)

    last, leading = edge_rows(
        thickness, wind_u, wind_v, tracers, [away_parts[0], *near[1:2], *near_rest[1:2]]
    )
    up = lax.ppermute(last, "lat", northward)
    down = lax.ppermute(leading, "lat", southward)
    u, v, edge = second_step(table, lat_rows, thickness, wind_u, wind_v, tracers, up, down, cutoff)
    edges = [edge] + [send(edge, s=s, t=0) for s in away]
    winds = [with_others_of_chip(u), with_others_of_chip(v)]
    tracers_own, thick_inner = remap(group, [group], others, tracer_fields, (0,), 0, with_thickness=True, wait=[edge])
    winds_own, *winds_away = remap(
        group, winds, others, [(0, 0), (1, 0)], range(C), 1, wait=[tracers_own, *arrived[:1]]
    )
    winds_arrived = sent(winds_away)
    near_new, near, near_rest, edges = (
        [a for own in sources for a in with_others_of_chip(own)] for sources in (near_new, near, near_rest, edges)
    )
    edge_out, thick_edge, near_out = remap_edges(
        (C, S), weights, edges, near_new, near, near_rest, wait=winds_away[:1]
    )

    tracers_out, thickness_out, token = finish_tracers(
        tracers_own, near_out, edge_out, thick_inner, thick_edge, arrived
    )
    u_out, v_out = finish_winds(winds_own, winds_arrived, edge_out, [token])
    return thickness_out, u_out, v_out, tracers_out


def solution(mesh):
    placed = (
        P(("member", "lev", "sub"), "lat", None),
        P(("member", "lev", "sub"), "lat", None),
        P(("member", "lev", "sub"), "lat", None),
        P("member", ("lev", "sub"), "lat", None),
        P(),
        P("lat"),
    )
    return jax.shard_map(
        per_device,
        mesh=mesh,
        in_specs=placed,
        out_specs=(
            P(("member", "lev", "sub"), "lat", None),
            P(("member", "lev", "sub"), "lat", None),
            P(("member", "lev", "sub"), "lat", None),
            P("member", ("lev", "sub"), "lat", None),
        ),
        check_vma=False,
    )
```

```python
import functools

import jax
import jax.numpy as jnp
import ml_dtypes
import numpy as np
from jax import lax
from jax.experimental import pallas as pl
from jax.experimental.pallas import tpu as pltpu
from jax.sharding import PartitionSpec as P

LANES = 128
VMEM = pl.BlockSpec(memory_space=pltpu.VMEM)


def params():
    return pltpu.CompilerParams(vmem_limit_bytes=16 * 1024 * 1024)


def cost(flops, bytes_accessed):
    return pl.CostEstimate(flops=int(flops), bytes_accessed=int(bytes_accessed), transcendentals=0)


def after(arrays):
    return [pl.BlockSpec(memory_space=pl.ANY)] * len(arrays)


def near_rows(rows):
    return (1, 2, rows - 2), (3, 2)


def geometry_table(lat_rows, band_rows):
    bands = lat_rows // band_rows
    table = np.zeros((bands, band_rows + 8, LANES), np.float32)
    for band in range(bands):
        for j in range(band_rows + 1):
            row = band * band_rows + j
            south = np.sin(row * np.pi / lat_rows) if 0 < row < lat_rows else 0.0
            north = np.sin((row + 1) * np.pi / lat_rows) if row + 1 < lat_rows else 0.0
            table[band, j, 0] = south
            table[band, j, 1] = north
            table[band, j, 2] = 1.0 / np.sin((row + 0.5) * np.pi / lat_rows)
    return table


def east_of(value):
    return pltpu.roll(value, value.shape[1] - 1, 1)


def west_of(value):
    return pltpu.roll(value, 1, 1)


def row_ids(shape):
    return lax.broadcasted_iota(jnp.int32, shape, 0)


def north_of(value, beyond):
    rows = value.shape[0]
    rolled = pltpu.roll(value, rows - 1, 0)
    return rolled if beyond is None else jnp.where(row_ids(value.shape) == rows - 1, beyond, rolled)


def south_of(value, beyond):
    rolled = pltpu.roll(value, 1, 0)
    return rolled if beyond is None else jnp.where(row_ids(value.shape) == 0, beyond, rolled)


def fluxes(geo, thick, u, v, thick_s, v_s, thick_n):
    rows = thick.shape[0]
    east = u * jnp.where(u > 0, thick, east_of(thick))
    north = v * jnp.where(v > 0, thick, north_of(thick, thick_n)) * geo[0:rows, 1:2]
    below = None if v_s is None else v_s * jnp.where(v_s > 0, thick_s, thick[0:1]) * geo[0:1, 0:1]
    return east, north, below


def tracer_change(q, q_s, q_n, thick, u, v, v_s, east, north, below, inverse):
    t_east = east * jnp.where(u > 0, q, east_of(q))
    t_north = north * jnp.where(v > 0, q, north_of(q, q_n))
    t_below = None if v_s is None else below * jnp.where(v_s > 0, q_s, q[0:1])
    change = thick * q - (t_east - west_of(t_east))
    return change - (t_north - south_of(t_north, t_below)) * inverse


def first_kernel(table_hbm, thick_hbm, u_hbm, v_hbm, tracer_hbm, *refs):
    new_ref, sum_ref, both_ref, near_ref, thick_ref, u_ref, v_ref, tracer_ref, geo_ref, sems = refs
    L, rows, _ = thick_ref.shape
    near, _ = near_rows(rows)
    table_copy = pltpu.make_async_copy(table_hbm.at[lax.axis_index("lat")], geo_ref, sems.at[3, 0])
    table_copy.start()
    pairs = ((thick_hbm, thick_ref), (u_hbm, u_ref), (v_hbm, v_ref))

    def copies(k):
        return [pltpu.make_async_copy(a.at[k], b.at[k], sems.at[i, k]) for i, (a, b) in enumerate(pairs)]

    for k in range(L):
        for copy in copies(k):
            copy.start()
    tracer_copy = pltpu.make_async_copy(tracer_hbm, tracer_ref, sems.at[3, 1])
    tracer_copy.start()
    table_copy.wait()
    geo = geo_ref[...]
    sum_ref[...] = jnp.zeros_like(sum_ref)

    def level(k, carry):
        for copy in copies(k):
            copy.wait()
        thick, u, v = thick_ref[k], u_ref[k], v_ref[k]
        east, north, _ = fluxes(geo, thick, u, v, None, None, None)
        new = thick - (east - west_of(east)) - (north - south_of(north, None)) * geo[0:rows, 2:3]
        new_ref[k] = new
        for j, row in enumerate(near):
            near_ref[0, k, j : j + 1] = new[row : row + 1]
        sum_ref[...] += new
        return carry

    lax.fori_loop(0, L, level, 0)
    both_ref[0:rows] = sum_ref[...]
    for k in range(L):
        at = rows + k * len(near)
        both_ref[at : at + len(near)] = near_ref[0, k]
    tracer_copy.wait()


def first_step(table, thickness, wind_u, wind_v, tracers):
    L, R, N = thickness.shape
    arguments = (thickness, wind_u, wind_v, tracers)
    operands = [pltpu.with_memory_space_constraint(a, pltpu.HBM) for a in (table, *arguments)]
    near = len(near_rows(R)[0])
    shapes = [(L, R, N), (R, N), (-(-(R + L * near) // 8) * 8, N), (1, L, near, N)] + [a.shape for a in arguments]
    return pl.pallas_call(
        first_kernel,
        in_specs=after(operands),
        out_specs=[VMEM] * len(shapes),
        out_shape=[jax.ShapeDtypeStruct(shape, jnp.float32) for shape in shapes],
        scratch_shapes=[pltpu.VMEM(table.shape[1:], jnp.float32), pltpu.SemaphoreType.DMA((4, max(L, 2)))],
        compiler_params=params(),
        cost_estimate=cost(40 * L * R * N, 4 * L * R * N * (7 + 2 * tracers.shape[0])),
        name="first_step",
    )(*operands)


def inner_kernel(table_ref, new_ref, thick_ref, u_ref, v_ref, tracer_ref, out_ref, near_ref, near_rest_ref):
    T, L, rows, _ = tracer_ref.shape
    near, _ = near_rows(rows)
    geo = table_ref[lax.axis_index("lat")]
    inverse = geo[0:rows, 2:3]

    def level(k, carry):
        thick, u, v, new = thick_ref[k], u_ref[k], v_ref[k], new_ref[k]
        east, north, _ = fluxes(geo, thick, u, v, None, None, None)

        out_ref[0, k] = new
        scale = 1.0 / new
        for c in range(T):
            change = tracer_change(
                tracer_ref[c, k], None, None, thick, u, v, None, east, north, None, inverse
            )
            value = change * scale
            out_ref[1 + c, k] = value
            ref, at = (near_ref, c) if c < T // 2 else (near_rest_ref, c - T // 2)
            for j, row in enumerate(near):
                ref[pl.ds((at * L + k) * len(near) + j, 1)] = value[row : row + 1]
        return carry

    lax.fori_loop(0, L, level, 0)


def inner_step(table, new, thickness, wind_u, wind_v, tracers):
    L, R, N = thickness.shape
    T = tracers.shape[0]
    rows = lambda n: jax.ShapeDtypeStruct((n * L * len(near_rows(R)[0]), N), jnp.float32)
    shape = lambda n, rows: jax.ShapeDtypeStruct((n, L, rows, N), jnp.float32)
    return pl.pallas_call(
        inner_kernel,
        in_specs=[VMEM] * 6,
        out_specs=[VMEM] * 3,
        out_shape=[shape(1 + T, R), rows(T // 2), rows(T - T // 2)],
        compiler_params=params(),
        cost_estimate=cost(130 * L * R * N, 4 * L * R * N * (8 + 2 * T)),
        name="inner_step",
    )(table, new, thickness, wind_u, wind_v, tracers)


def filter_tables(N):
    A = N // LANES
    b = np.arange(LANES)[:, None]
    p = np.arange(LANES)[None, :]
    tables = []
    for q in range(A // 2 + 1):
        angle = 2.0 * np.pi * ((b * (A * p + q)) % N) / N
        c, s = np.cos(angle), np.sin(angle)
        tables.append(np.block([[c, -s], [s, c]]))
    table = np.stack(tables)
    high = table.astype(np.float32).astype(ml_dtypes.bfloat16)
    low = (table - high.astype(np.float64)).astype(np.float32).astype(ml_dtypes.bfloat16)
    return high, low


def split(value):
    high = value.astype(jnp.bfloat16)
    return high, (value - high.astype(jnp.float32)).astype(jnp.bfloat16)


def product(value, high, low, transposed):
    dims = (((1,), (1 if transposed else 0,)), ((), ()))
    dot = lambda x, y: lax.dot_general(x, y, dims, preferred_element_type=jnp.float32)
    v_high, v_low = split(value)
    return dot(v_high, high) + (dot(v_high, low) + dot(v_low, high))


def filter_rows(x, cutoff, high_ref, low_ref):
    A = len(x)
    N = A * LANES
    half = A // 2
    even = [x[a] + x[A - a] for a in range(1, half + 1)]
    odd = [x[a] - x[A - a] for a in range(1, half + 1)]
    angle = lambda q, a: 2.0 * np.pi * ((q * a) % A) / A
    p = lax.broadcasted_iota(jnp.int32, cutoff.shape, 1)
    real, imag = [], []
    for q in range(half + 1):
        re = x[0]
        for a in range(1, half + 1):
            re = re + (even[a - 1] if q == 0 else float(np.cos(angle(q, a))) * even[a - 1])
        if q == 0:
            high, low = high_ref[0, 0:LANES], low_ref[0, 0:LANES]
            spectrum = product(re, high, low, False)
        else:
            high, low = high_ref[q], low_ref[q]
            im = -float(np.sin(angle(q, 1))) * odd[0]
            for a in range(2, half + 1):
                im = im - float(np.sin(angle(q, a))) * odd[a - 1]
            spectrum = product(jnp.concatenate([re, im], axis=1), high, low, False)
        mode = A * p + q
        factor = 1.0 / N if q == 0 else 2.0 / N
        kept = jnp.where(jnp.minimum(mode, N - mode) <= cutoff, factor, 0.0)
        back = product(spectrum * jnp.concatenate([kept, kept], axis=1), high, low, True)
        real.append(back[:, :LANES])
        imag.append(back[:, LANES:])
    out = [None] * A
    out[0] = functools.reduce(jnp.add, real)
    for a in range(1, half + 1):
        even_part, odd_part = real[0], None
        for q in range(1, half + 1):
            even_part = even_part + float(np.cos(angle(q, a))) * real[q]
            term = float(np.sin(angle(q, a))) * imag[q]
            odd_part = term if odd_part is None else odd_part + term
        out[a] = even_part - odd_part
        out[A - a] = even_part + odd_part
    return out


def second_kernel(
    lat_rows, table_ref, thick_ref, u_ref, v_ref, tracer_ref, up_ref, down_ref, cutoff_ref, high_ref, low_ref, *refs
):
    *wind_refs, edge_ref, new_wind = refs
    k = pl.program_id(0)
    _, L, rows, width = new_wind.shape
    band = lax.axis_index("lat")
    geo = table_ref[band]
    thick, u, v = thick_ref[0], u_ref[0], v_ref[0]
    thick_s, v_s = up_ref[0, 0], up_ref[1, 0]
    thick_n, thick_nn, u_n, v_n = (down_ref[i, 0] for i in range(4))
    east, north, below = fluxes(geo, thick, u, v, thick_s, v_s, thick_n)
    inverse = geo[0:rows, 2:3]
    new = thick - (east - west_of(east)) - (north - south_of(north, below)) * inverse
    east_n = u_n * jnp.where(u_n > 0, thick_n, east_of(thick_n))
    north_n = v_n * jnp.where(v_n > 0, thick_n, thick_nn) * geo[rows : rows + 1, 1:2]
    new_n = (
        thick_n
        - (east_n - west_of(east_n))
        - (north_n - north[rows - 1 : rows]) * geo[rows : rows + 1, 2:3]
    )
    new_wind[0, k] = u - 0.05 * (east_of(new) - new)
    inside = band * rows + row_ids(new.shape) < lat_rows - 1
    new_wind[1, k] = jnp.where(inside, v - 0.05 * (north_of(new, new_n) - new), 0.0)

    def store_edges(field, level, value):
        edge_ref[field, level, 0:1] = value[0:1]
        edge_ref[field, level, 1:2] = value[rows - 1 : rows]

    store_edges(0, k, new)
    scale = 1.0 / new
    for c in range(tracer_ref.shape[0]):
        change = tracer_change(
            tracer_ref[c, 0], up_ref[2 + c, 0], down_ref[4 + c, 0], thick, u, v, v_s, east, north, below, inverse
        )
        store_edges(3 + c, k, change * scale)

    @pl.when(k == L - 1)
    def _():
        pieces = [
            new_wind[:, :, :, a * LANES : (a + 1) * LANES].reshape(2 * L * rows, LANES) for a in range(width // LANES)
        ]
        cutoff = jnp.broadcast_to(cutoff_ref[...][None], (2 * L, rows, LANES)).reshape(2 * L * rows, LANES)
        for a, piece in enumerate(filter_rows(pieces, cutoff, high_ref, low_ref)):
            piece = piece.reshape(2, L, rows, LANES)
            for f in range(2):
                wind_refs[f][0, :, :, a * LANES : (a + 1) * LANES] = piece[f]
        for f in range(2):
            for level in range(L):
                store_edges(1 + f, level, wind_refs[f][0, level])


def second_step(table, lat_rows, thickness, wind_u, wind_v, tracers, up, down, cutoff):
    L, R, N = thickness.shape
    T = tracers.shape[0]
    high, low = filter_tables(N)
    level = pl.BlockSpec((1, R, N), lambda k: (k, 0, 0))
    some = lambda n, rows: pl.BlockSpec((n, 1, rows, N), lambda k: (0, k, 0, 0))
    whole = lambda shape: pl.BlockSpec(shape, lambda k: (0,) * len(shape))
    return pl.pallas_call(
        functools.partial(second_kernel, lat_rows),
        grid=(L,),
        in_specs=[whole(table.shape), level, level, level, some(T, R), some(2 + T, 1), some(4 + T, 1)]
        + [whole((R, LANES)), whole(high.shape), whole(low.shape)],
        out_specs=[whole((1, L, R, N)), whole((1, L, R, N)), whole((3 + T, L, 2, N))],
        out_shape=[
            jax.ShapeDtypeStruct((1, L, R, N), jnp.float32),
            jax.ShapeDtypeStruct((1, L, R, N), jnp.float32),
            jax.ShapeDtypeStruct((3 + T, L, 2, N), jnp.float32),
        ],
        scratch_shapes=[pltpu.VMEM((2, L, R, N), jnp.float32)],
        compiler_params=params(),
        cost_estimate=cost(12 * 2 * L * R * high.size, 4 * L * R * N * (8 + T)),
        name="second_step",
    )(
        table, thickness, wind_u, wind_v, tracers, up, down,
        jnp.broadcast_to(cutoff[:, None], (R, LANES)), jnp.asarray(high), jnp.asarray(low),
    )


def mass_kernel(C, S, *refs):
    other_refs, (base_ref, mass_ref, *near_refs) = refs[: (C - 1) * S], refs[(C - 1) * S :]
    rows = base_ref.shape[0]
    lev = lax.axis_index("lev")
    others_mass, base = None, None
    for s in range(1, C):
        first, *rest = other_refs[(s - 1) * S : s * S]
        other = functools.reduce(jnp.add, [first[0:rows]] + [ref[...] for ref in rest])
        below = jnp.where(lev >= s, other, 0.0)
        others_mass = other if others_mass is None else others_mass + other
        base = below if base is None else base + below
        _, L, near, _ = near_refs[s - 1].shape
        for k in range(L):
            near_refs[s - 1][0, k] = first[rows + k * near : rows + (k + 1) * near]
    base_ref[...] = base
    mass_ref[...] = others_mass


def other_chips(counts, others, levels):
    C, S = counts
    R, N = others[1].shape
    near = len(near_rows(R)[0])
    return pl.pallas_call(
        functools.partial(mass_kernel, C, S),
        in_specs=[VMEM] * len(others),
        out_specs=[VMEM] * (1 + C),
        out_shape=[jax.ShapeDtypeStruct((R, N), jnp.float32)] * 2
        + [jax.ShapeDtypeStruct((1, levels, near, N), jnp.float32)] * (C - 1),
        compiler_params=params(),
        cost_estimate=cost(1e11, 1e9),
        name="other_chips",
    )(*others)


def add_weights(weight_ref, sum_ref):
    total = jnp.zeros(weight_ref.shape[1:], jnp.float32)
    for k in range(weight_ref.shape[0]):
        sum_ref[k] = total
        total = total + weight_ref[k]
    sum_ref[weight_ref.shape[0]] = total
    return total


def source_levels(place, counts, thick, others):
    C, S = counts
    lev, sub = place
    spot = [lax.rem(lev - g // S + C, C) * S + lax.rem(sub - g % S + S, S) for g in range(len(thick))]
    group = [functools.reduce(jnp.add, levels) for levels in thick]
    mass = functools.reduce(jnp.add, group)
    base = jnp.zeros_like(mass)
    if others:
        base, mass = others[0], mass + others[1]
    sources = []
    for g, levels in enumerate(thick):
        low = base
        for other in range(len(thick)):
            if other != g:
                low = low + jnp.where(spot[other] < spot[g], group[other], 0.0)
        for m, value in enumerate(levels):
            sources.append((g, m, low, value))
            low = low + value
    return mass, sources


def covered(top, sources):
    return [jnp.minimum(jnp.maximum(top - low, 0.0), value) for _, _, low, value in sources]


def level_of(ref, index):
    return lambda m, at, columns: ref[index, m, at, columns]


def packed_level_of(ref, index, L, rows):
    return lambda m, at, columns: ref[(index * L + m) * rows : (index * L + m + 1) * rows, columns]


def remap_rows(weight_ref, sum_ref, counts, steps, thick_refs, field_refs, other_refs, store):
    C, S = counts
    _, L, R, N = thick_refs[0].shape
    rows = min(R, 8)
    place = lev, sub = lax.axis_index("lev"), lax.axis_index("sub")
    firsts = [(lax.rem(lev + s, C) * S + sub) * L for s in steps]
    weight_sum = add_weights(weight_ref, sum_ref)[0:rows]

    def tile(at, columns):
        thick = [[ref[0, m, at, columns] for m in range(L)] for ref in thick_refs]
        others = [ref[at, columns] for ref in other_refs]
        mass, sources = source_levels(place, counts, thick, others)
        unit = mass / weight_sum
        for index, s in enumerate(steps):
            below = covered(unit * sum_ref[firsts[index], 0:rows], sources)
            for i in range(L):
                upto = covered(unit * sum_ref[firsts[index] + i + 1, 0:rows], sources)
                part = [a - b for a, b in zip(upto, below)]
                below = upto
                target = unit * weight_ref[firsts[index] + i, 0:rows]
                scale = 1.0 / target
                means = []
                for refs in field_refs:
                    terms = [refs[g](m, at, columns) * w for (g, m, _, _), w in zip(sources, part)]
                    means.append(functools.reduce(jnp.add, terms) * scale)
                store(s, i, at, columns, target, means)

    for r in range(0, R, rows):

        def body(c, carry):
            tile(slice(r, r + rows), pl.ds(pl.multiple_of(c * LANES, LANES), LANES))
            return carry

        lax.fori_loop(0, N // LANES, body, 0)


def inner_part(at, margin, rows):
    return max(at.start, margin[0]), min(at.stop, rows - margin[1])


def remap_kernel(counts, steps, fields, margin, with_thickness, sizes, weight_ref, *refs):
    *refs, sum_ref = refs
    C, S = counts
    thick_refs, refs = refs[:S], refs[S:]
    bundles = []
    for _ in range(sizes[0]):
        bundles.append(refs[:S])
        refs = refs[S:]
    other_refs, out_refs = refs[:2], refs[len(refs) - len(steps) - with_thickness :]
    _, L, R, _ = thick_refs[0].shape
    thick_out_ref = out_refs[-1]
    field_refs = [[level_of(ref, index) for ref in bundles[which]] for which, index in fields]

    def store(s, i, at, columns, target, means):
        out_ref = out_refs[steps.index(s)]
        if with_thickness and s == 0:
            thick_out_ref[i, at, columns] = target
        for f, value in enumerate(means):
            if s == 0:
                out_ref[f, i, at, columns] = value
            else:
                lower, upper = inner_part(at, margin, R)
                start = (f * L + i) * (R - sum(margin)) - margin[0]
                out_ref[start + lower : start + upper, columns] = value[lower - at.start : upper - at.start]

    remap_rows(
        weight_ref, sum_ref, counts, steps, thick_refs, field_refs, other_refs, store
    )


def remap_parts(counts, weights, thick, bundles, others, fields, steps, margin, with_thickness=False, wait=()):
    C, S = counts
    _, L, R, N = thick[0].shape
    F = len(fields)
    whole = jax.ShapeDtypeStruct((F, L, R, N), jnp.float32)
    inner = jax.ShapeDtypeStruct((F * L * (R - sum(margin)), N), jnp.float32)
    flat = [a for bundle in bundles for a in bundle]
    out_shape = [whole if s == 0 else inner for s in steps]
    if with_thickness:
        out_shape.append(jax.ShapeDtypeStruct((L, R, N), jnp.float32))
    return pl.pallas_call(
        functools.partial(remap_kernel, counts, tuple(steps), tuple(fields), margin, with_thickness, (len(bundles),)),
        in_specs=[VMEM] * (1 + len(thick) + len(flat) + len(others)) + after(wait),
        out_specs=[VMEM] * len(out_shape),
        out_shape=out_shape,
        scratch_shapes=[pltpu.VMEM((weights.shape[0] + 1, 8, LANES), jnp.float32)],
        compiler_params=params(),
        cost_estimate=cost(len(steps) * S * L * L * R * N * (5 + 2 * F), 4 * R * N * L * (F + 1) * (S + len(steps))),
        name="remap_parts",
    )(weights, *thick, *flat, *others, *wait)


def remap_edge_kernel(counts, near_fields, weight_ref, *refs):
    *refs, sum_ref = refs
    G = counts[0] * counts[1]
    edge_refs, near_refs = refs[:G], refs[G : 2 * G]
    bundles = (refs[2 * G : 3 * G], refs[3 * G : 4 * G])
    edge_out_ref, thick_out_ref, near_out_ref = refs[-3:]

    def store_edge(s, i, at, columns, target, means):
        thick_out_ref[i, at, columns] = target
        for f, value in enumerate(means):
            edge_out_ref[f, i, at, columns] = value

    def store_near(s, i, at, columns, target, means):
        for f, value in enumerate(means):
            near_out_ref[f, i, at, columns] = value

    fields = [[level_of(ref, f) for ref in edge_refs] for f in range(1, edge_refs[0].shape[0])]
    remap_rows(weight_ref, sum_ref, counts, (0,), edge_refs, fields, [], store_edge)
    _, L, R, _ = near_refs[0].shape
    fields = [[packed_level_of(ref, index, L, R) for ref in bundles[which]] for which, index in near_fields]
    remap_rows(weight_ref, sum_ref, counts, (0,), near_refs, fields, [], store_near)


def remap_edges(counts, weights, edges, near_new, near, near_rest, wait=()):
    F, L, R, N = edges[0].shape
    T = F - 3
    near_fields = tuple((0, f) if f < T // 2 else (1, f - T // 2) for f in range(T))
    operands = [*edges, *near_new, *near, *near_rest]
    return pl.pallas_call(
        functools.partial(remap_edge_kernel, counts, near_fields),
        in_specs=[VMEM] * (1 + len(operands)) + after(wait),
        out_specs=[VMEM] * 3,
        out_shape=[
            jax.ShapeDtypeStruct((F - 1, L, R, N), jnp.float32),
            jax.ShapeDtypeStruct((L, R, N), jnp.float32),
            jax.ShapeDtypeStruct((T, *near_new[0].shape[1:]), jnp.float32),
        ],
        scratch_shapes=[pltpu.VMEM((weights.shape[0] + 1, 8, LANES), jnp.float32)],
        compiler_params=params(),
        cost_estimate=cost(len(edges) * L * L * R * N * 40, 4 * R * N * L * len(operands) * F),
        name="remap_edges",
    )(weights, *operands, *wait)


def finish_kernel(margin, own_ref, near_ref, edge_ref, thick_ref, thick_edge_ref, *refs):
    *arrived_refs, out_ref, thick_out_ref, token_ref = refs
    token_ref[...] = jnp.zeros_like(token_ref)
    T, L, R, _ = out_ref.shape
    thick_out_ref[...] = thick_ref[...]
    for i in range(L):
        for row, j in ((0, 0), (R - 1, 1)):
            thick_out_ref[i, row : row + 1] = thick_edge_ref[i, j : j + 1]
    for f in range(T):
        for i in range(L):
            start, first, end = (f * L + i) * (R - sum(margin)), margin[0], R - margin[1]
            total = own_ref[f, i, first:end]
            for ref in arrived_refs:
                total = total + ref[start : start + end - first]
            out_ref[f, i, first:end] = total
            for row, j in ((0, 0), (R - 1, 1)):
                out_ref[f, i, row : row + 1] = edge_ref[2 + f, i, j : j + 1]
            for j, row in enumerate(near_rows(R)[0]):
                out_ref[f, i, row : row + 1] = near_ref[f, i, j : j + 1]


def finish_tracers(own, near, edge, thick, thick_edge, arrived):
    return pl.pallas_call(
        functools.partial(finish_kernel, near_rows(own.shape[2])[1]),
        in_specs=[VMEM] * (5 + len(arrived)),
        out_specs=[VMEM] * 3,
        out_shape=[
            jax.ShapeDtypeStruct(own.shape, jnp.float32),
            jax.ShapeDtypeStruct(thick.shape, jnp.float32),
            jax.ShapeDtypeStruct((8, LANES), jnp.float32),
        ],
        compiler_params=params(),
        cost_estimate=cost(2 * own.size, 12 * own.size),
        name="finish_tracers",
    )(own, near, edge, thick, thick_edge, *arrived)


def finish_winds_kernel(count, own_ref, edge_ref, *refs):
    arrived_refs, out_refs = refs[:count], refs[-2:]
    _, L, R, N = own_ref.shape
    for f, out_ref in enumerate(out_refs):
        for i in range(L):
            start = (f * L + i) * (R - 2)
            total = own_ref[f, i, 1 : R - 1]
            for ref in arrived_refs:
                total = total + ref[start : start + R - 2]
            out_ref[i, 1 : R - 1] = total
            out_ref[i, 0:1] = edge_ref[f, i, 0:1]
            out_ref[i, R - 1 : R] = edge_ref[f, i, 1:2]


def finish_winds(own, arrived, edge, wait):
    return pl.pallas_call(
        functools.partial(finish_winds_kernel, len(arrived)),
        in_specs=[VMEM] * (2 + len(arrived)) + after(wait),
        out_specs=[VMEM] * 2,
        out_shape=[jax.ShapeDtypeStruct(own.shape[1:], jnp.float32)] * 2,
        compiler_params=params(),
        cost_estimate=cost(own.size, 12 * own.size),
        name="finish_winds",
    )(own, edge, *arrived, *wait)


def edge_kernel(thick_hbm, u_hbm, v_hbm, tracer_hbm, *refs):
    last_ref, leading_ref, top_ref, low_ref, tracer_ref, sems = refs[-6:]
    T, L, R, _ = tracer_hbm.shape
    top = pl.ds(R - 8, 8)
    copies = [
        pltpu.make_async_copy(thick_hbm.at[:, top], top_ref.at[0], sems.at[0]),
        pltpu.make_async_copy(v_hbm.at[:, top], top_ref.at[1], sems.at[1]),
        pltpu.make_async_copy(thick_hbm.at[:, pl.ds(0, 8)], low_ref.at[0], sems.at[2]),
        pltpu.make_async_copy(u_hbm.at[:, pl.ds(0, 8)], low_ref.at[1], sems.at[3]),
        pltpu.make_async_copy(v_hbm.at[:, pl.ds(0, 8)], low_ref.at[2], sems.at[4]),
        pltpu.make_async_copy(tracer_hbm.at[:, :, top], tracer_ref.at[0], sems.at[5]),
        pltpu.make_async_copy(tracer_hbm.at[:, :, pl.ds(0, 8)], tracer_ref.at[1], sems.at[6]),
    ]
    for copy in copies:
        copy.start()
    for copy in copies:
        copy.wait()
    last_ref[0:2] = top_ref[:, :, 7:8]
    last_ref[2 : 2 + T] = tracer_ref[0, :, :, 7:8]
    leading_ref[0] = low_ref[0, :, 0:1]
    leading_ref[1] = low_ref[0, :, 1:2]
    leading_ref[2:4] = low_ref[1:3, :, 0:1]
    leading_ref[4 : 4 + T] = tracer_ref[1, :, :, 0:1]


def edge_rows(thickness, wind_u, wind_v, tracers, wait):
    L, R, N = thickness.shape
    T = tracers.shape[0]
    operands = [pltpu.with_memory_space_constraint(a, pltpu.HBM) for a in (thickness, wind_u, wind_v, tracers)]
    return pl.pallas_call(
        edge_kernel,
        in_specs=after(operands) + after(wait),
        out_specs=[VMEM] * 2,
        out_shape=[
            jax.ShapeDtypeStruct((2 + T, L, 1, N), jnp.float32),
            jax.ShapeDtypeStruct((4 + T, L, 1, N), jnp.float32),
        ],
        scratch_shapes=[
            pltpu.VMEM((2, L, 8, N), jnp.float32),
            pltpu.VMEM((3, L, 8, N), jnp.float32),
            pltpu.VMEM((2, T, L, 8, N), jnp.float32),
            pltpu.SemaphoreType.DMA((7,)),
        ],
        compiler_params=params(),
        cost_estimate=cost(1e10, 1e9),
        name="edge_rows",
    )(*operands, *wait)


def shifted(value, lev_count, sub_count, s, t):
    if t == 0:
        return lax.ppermute(value, "lev", [(i, (i + s) % lev_count) for i in range(lev_count)])
    if s == 0:
        return lax.ppermute(value, "sub", [(i, (i + t) % sub_count) for i in range(sub_count)])
    pairs = [
        (i * sub_count + j, (i + s) % lev_count * sub_count + (j + t) % sub_count)
        for i in range(lev_count)
        for j in range(sub_count)
    ]
    return lax.ppermute(value, ("lev", "sub"), pairs)


def per_device(thickness, wind_u, wind_v, tracers, level_weights, cutoff):
    L, R, N = thickness.shape
    lat_count = lax.axis_size("lat")
    C, S = lax.axis_size("lev"), lax.axis_size("sub")
    lat_rows = R * lat_count
    send = functools.partial(shifted, lev_count=C, sub_count=S)

    T = tracers.shape[0]
    northward = [(i, i + 1) for i in range(lat_count - 1)]
    southward = [(j, i) for i, j in northward]
    table = jnp.asarray(geometry_table(lat_rows, R))
    weights = jnp.broadcast_to(level_weights[:, None, None], (level_weights.shape[0], 8, LANES))
    away = range(1, C)

    def with_others_of_chip(own):
        return [own] + [send(own, s=0, t=t) for t in range(1, S)]

    def sent(parts):
        return [send(part, s=s, t=0) for s, part in zip(away, parts)]

    remap = functools.partial(remap_parts, (C, S), weights)

    new, own_sum, own_both, near_new, *arguments = first_step(table, thickness, wind_u, wind_v, tracers)
    others = [send(own_sum if t else own_both, s=s, t=t) for s in away for t in range(S)]
    inner, near, near_rest = inner_step(table, new, *arguments)
    group = with_others_of_chip(inner)
    near = [near] + [send(near, s=s, t=0) for s in away]
    near_rest = [near_rest] + [send(near_rest, s=s, t=0) for s in away]
    base, rest_mass, *near_arrived = other_chips((C, S), others, L)
    others = [base, rest_mass]
    near_new = [near_new, *near_arrived]
    tracer_fields = [(0, 1 + c) for c in range(T)]
    away_parts = remap(group, [group], others, tracer_fields, away, near_rows(R)[1])
    arrived = sent(away_parts)

    last, leading = edge_rows(
        thickness, wind_u, wind_v, tracers, [away_parts[0], *near[1:2], *near_rest[1:2]]
    )
    up = lax.ppermute(last, "lat", northward)
    down = lax.ppermute(leading, "lat", southward)
    u, v, edge = second_step(table, lat_rows, thickness, wind_u, wind_v, tracers, up, down, cutoff)
    edges = [edge] + [send(edge, s=s, t=0) for s in away]
    winds = [with_others_of_chip(u), with_others_of_chip(v)]
    tracers_own, thick_inner = remap(group, [group], others, tracer_fields, (0,), (0, 0), with_thickness=True, wait=[edge])
    winds_own, *winds_away = remap(
        group, winds, others, [(0, 0), (1, 0)], range(C), (1, 1), wait=[tracers_own, *arrived[:1]]
    )
    winds_arrived = sent(winds_away)
    near_new, near, near_rest, edges = (
        [a for own in sources for a in with_others_of_chip(own)] for sources in (near_new, near, near_rest, edges)
    )
    edge_out, thick_edge, near_out = remap_edges(
        (C, S), weights, edges, near_new, near, near_rest, wait=winds_away[:1]
    )

    tracers_out, thickness_out, token = finish_tracers(
        tracers_own, near_out, edge_out, thick_inner, thick_edge, arrived
    )
    u_out, v_out = finish_winds(winds_own, winds_arrived, edge_out, [token])
    return thickness_out, u_out, v_out, tracers_out


def solution(mesh):
    placed = (
        P(("member", "lev", "sub"), "lat", None),
        P(("member", "lev", "sub"), "lat", None),
        P(("member", "lev", "sub"), "lat", None),
        P("member", ("lev", "sub"), "lat", None),
        P(),
        P("lat"),
    )
    return jax.shard_map(
        per_device,
        mesh=mesh,
        in_specs=placed,
        out_specs=(
            P(("member", "lev", "sub"), "lat", None),
            P(("member", "lev", "sub"), "lat", None),
            P(("member", "lev", "sub"), "lat", None),
            P("member", ("lev", "sub"), "lat", None),
        ),
        check_vma=False,
    )
```

```python
import functools

import jax
import jax.numpy as jnp
import ml_dtypes
import numpy as np
from jax import lax
from jax.experimental import pallas as pl
from jax.experimental.pallas import tpu as pltpu
from jax.sharding import PartitionSpec as P

LANES = 128
VMEM = pl.BlockSpec(memory_space=pltpu.VMEM)


def params():
    return pltpu.CompilerParams(vmem_limit_bytes=16 * 1024 * 1024)


def cost(flops, bytes_accessed):
    return pl.CostEstimate(flops=int(flops), bytes_accessed=int(bytes_accessed), transcendentals=0)


def after(arrays):
    return [pl.BlockSpec(memory_space=pl.ANY)] * len(arrays)


def near_rows(rows):
    return (1, 2, rows - 3, rows - 2), (3, 3)


def geometry_table(lat_rows, band_rows):
    bands = lat_rows // band_rows
    table = np.zeros((bands, band_rows + 8, LANES), np.float32)
    for band in range(bands):
        for j in range(band_rows + 1):
            row = band * band_rows + j
            south = np.sin(row * np.pi / lat_rows) if 0 < row < lat_rows else 0.0
            north = np.sin((row + 1) * np.pi / lat_rows) if row + 1 < lat_rows else 0.0
            table[band, j, 0] = south
            table[band, j, 1] = north
            table[band, j, 2] = 1.0 / np.sin((row + 0.5) * np.pi / lat_rows)
    return table


def east_of(value):
    return pltpu.roll(value, value.shape[1] - 1, 1)


def west_of(value):
    return pltpu.roll(value, 1, 1)


def row_ids(shape):
    return lax.broadcasted_iota(jnp.int32, shape, 0)


def north_of(value, beyond):
    rows = value.shape[0]
    rolled = pltpu.roll(value, rows - 1, 0)
    return rolled if beyond is None else jnp.where(row_ids(value.shape) == rows - 1, beyond, rolled)


def south_of(value, beyond):
    rolled = pltpu.roll(value, 1, 0)
    return rolled if beyond is None else jnp.where(row_ids(value.shape) == 0, beyond, rolled)


def fluxes(geo, thick, u, v, thick_s, v_s, thick_n):
    rows = thick.shape[0]
    east = u * jnp.where(u > 0, thick, east_of(thick))
    north = v * jnp.where(v > 0, thick, north_of(thick, thick_n)) * geo[0:rows, 1:2]
    below = None if v_s is None else v_s * jnp.where(v_s > 0, thick_s, thick[0:1]) * geo[0:1, 0:1]
    return east, north, below


def tracer_change(q, q_s, q_n, thick, u, v, v_s, east, north, below, inverse):
    t_east = east * jnp.where(u > 0, q, east_of(q))
    t_north = north * jnp.where(v > 0, q, north_of(q, q_n))
    t_below = None if v_s is None else below * jnp.where(v_s > 0, q_s, q[0:1])
    change = thick * q - (t_east - west_of(t_east))
    return change - (t_north - south_of(t_north, t_below)) * inverse


def first_kernel(table_hbm, thick_hbm, u_hbm, v_hbm, tracer_hbm, *refs):
    new_ref, both_ref, near_ref, thick_ref, u_ref, v_ref, tracer_ref, geo_ref, sems = refs
    L, rows, _ = thick_ref.shape
    near, _ = near_rows(rows)
    table_copy = pltpu.make_async_copy(table_hbm.at[lax.axis_index("lat")], geo_ref, sems.at[3, 0])
    table_copy.start()
    pairs = ((thick_hbm, thick_ref), (u_hbm, u_ref), (v_hbm, v_ref))

    def copies(k):
        return [pltpu.make_async_copy(a.at[k], b.at[k], sems.at[i, k]) for i, (a, b) in enumerate(pairs)]

    for k in range(L):
        for copy in copies(k):
            copy.start()
    tracer_copy = pltpu.make_async_copy(tracer_hbm, tracer_ref, sems.at[3, 1])
    tracer_copy.start()
    table_copy.wait()
    geo = geo_ref[...]
    both_ref[...] = jnp.zeros_like(both_ref)

    def level(k, carry):
        for copy in copies(k):
            copy.wait()
        thick, u, v = thick_ref[k], u_ref[k], v_ref[k]
        east, north, _ = fluxes(geo, thick, u, v, None, None, None)
        new = thick - (east - west_of(east)) - (north - south_of(north, None)) * geo[0:rows, 2:3]
        new_ref[k] = new
        for j, row in enumerate(near):
            near_ref[0, k, j : j + 1] = new[row : row + 1]
        both_ref[0:rows] += new
        return carry

    lax.fori_loop(0, L, level, 0)
    for k in range(L):
        at = rows + k * len(near)
        both_ref[at : at + len(near)] = near_ref[0, k]
    tracer_copy.wait()


def first_step(table, thickness, wind_u, wind_v, tracers):
    L, R, N = thickness.shape
    arguments = (thickness, wind_u, wind_v, tracers)
    operands = [pltpu.with_memory_space_constraint(a, pltpu.HBM) for a in (table, *arguments)]
    near = len(near_rows(R)[0])
    shapes = [(L, R, N), (-(-(R + L * near) // 8) * 8, N), (1, L, near, N)] + [a.shape for a in arguments]
    return pl.pallas_call(
        first_kernel,
        in_specs=after(operands),
        out_specs=[VMEM] * len(shapes),
        out_shape=[jax.ShapeDtypeStruct(shape, jnp.float32) for shape in shapes],
        scratch_shapes=[pltpu.VMEM(table.shape[1:], jnp.float32), pltpu.SemaphoreType.DMA((4, max(L, 2)))],
        compiler_params=params(),
        cost_estimate=cost(40 * L * R * N, 4 * L * R * N * (7 + 2 * tracers.shape[0])),
        name="first_step",
    )(*operands)


def inner_kernel(table_ref, new_ref, thick_ref, u_ref, v_ref, tracer_ref, out_ref, near_ref, near_rest_ref):
    T, L, rows, _ = tracer_ref.shape
    near, _ = near_rows(rows)
    geo = table_ref[lax.axis_index("lat")]
    inverse = geo[0:rows, 2:3]

    def level(k, carry):
        thick, u, v, new = thick_ref[k], u_ref[k], v_ref[k], new_ref[k]
        east, north, _ = fluxes(geo, thick, u, v, None, None, None)

        out_ref[0, k] = new
        scale = 1.0 / new
        for c in range(T):
            change = tracer_change(
                tracer_ref[c, k], None, None, thick, u, v, None, east, north, None, inverse
            )
            value = change * scale
            out_ref[1 + c, k] = value
            ref, at = (near_ref, c) if c < T // 2 else (near_rest_ref, c - T // 2)
            for j, row in enumerate(near):
                ref[pl.ds((at * L + k) * len(near) + j, 1)] = value[row : row + 1]
        return carry

    lax.fori_loop(0, L, level, 0)


def inner_step(table, new, thickness, wind_u, wind_v, tracers):
    L, R, N = thickness.shape
    T = tracers.shape[0]
    rows = lambda n: jax.ShapeDtypeStruct((n * L * len(near_rows(R)[0]), N), jnp.float32)
    shape = lambda n, rows: jax.ShapeDtypeStruct((n, L, rows, N), jnp.float32)
    return pl.pallas_call(
        inner_kernel,
        in_specs=[VMEM] * 6,
        out_specs=[VMEM] * 3,
        out_shape=[shape(1 + T, R), rows(T // 2), rows(T - T // 2)],
        compiler_params=params(),
        cost_estimate=cost(130 * L * R * N, 4 * L * R * N * (8 + 2 * T)),
        name="inner_step",
    )(table, new, thickness, wind_u, wind_v, tracers)


def filter_tables(N):
    A = N // LANES
    b = np.arange(LANES)[:, None]
    p = np.arange(LANES)[None, :]
    tables = []
    for q in range(A // 2 + 1):
        angle = 2.0 * np.pi * ((b * (A * p + q)) % N) / N
        c, s = np.cos(angle), np.sin(angle)
        tables.append(np.block([[c, -s], [s, c]]))
    table = np.stack(tables)
    high = table.astype(np.float32).astype(ml_dtypes.bfloat16)
    low = (table - high.astype(np.float64)).astype(np.float32).astype(ml_dtypes.bfloat16)
    return high, low


def split(value):
    high = value.astype(jnp.bfloat16)
    return high, (value - high.astype(jnp.float32)).astype(jnp.bfloat16)


def product(value, high, low, transposed):
    dims = (((1,), (1 if transposed else 0,)), ((), ()))
    dot = lambda x, y: lax.dot_general(x, y, dims, preferred_element_type=jnp.float32)
    v_high, v_low = split(value)
    return dot(v_high, high) + (dot(v_high, low) + dot(v_low, high))


def filter_rows(x, cutoff, high_ref, low_ref):
    A = len(x)
    N = A * LANES
    half = A // 2
    even = [x[a] + x[A - a] for a in range(1, half + 1)]
    odd = [x[a] - x[A - a] for a in range(1, half + 1)]
    angle = lambda q, a: 2.0 * np.pi * ((q * a) % A) / A
    p = lax.broadcasted_iota(jnp.int32, cutoff.shape, 1)
    real, imag = [], []
    for q in range(half + 1):
        re = x[0]
        for a in range(1, half + 1):
            re = re + (even[a - 1] if q == 0 else float(np.cos(angle(q, a))) * even[a - 1])
        if q == 0:
            high, low = high_ref[0, 0:LANES], low_ref[0, 0:LANES]
            spectrum = product(re, high, low, False)
        else:
            high, low = high_ref[q], low_ref[q]
            im = -float(np.sin(angle(q, 1))) * odd[0]
            for a in range(2, half + 1):
                im = im - float(np.sin(angle(q, a))) * odd[a - 1]
            spectrum = product(jnp.concatenate([re, im], axis=1), high, low, False)
        mode = A * p + q
        factor = 1.0 / N if q == 0 else 2.0 / N
        kept = jnp.where(jnp.minimum(mode, N - mode) <= cutoff, factor, 0.0)
        back = product(spectrum * jnp.concatenate([kept, kept], axis=1), high, low, True)
        real.append(back[:, :LANES])
        imag.append(back[:, LANES:])
    out = [None] * A
    out[0] = functools.reduce(jnp.add, real)
    for a in range(1, half + 1):
        even_part, odd_part = real[0], None
        for q in range(1, half + 1):
            even_part = even_part + float(np.cos(angle(q, a))) * real[q]
            term = float(np.sin(angle(q, a))) * imag[q]
            odd_part = term if odd_part is None else odd_part + term
        out[a] = even_part - odd_part
        out[A - a] = even_part + odd_part
    return out


def second_kernel(
    lat_rows, table_ref, thick_ref, u_ref, v_ref, tracer_ref, up_ref, down_ref, cutoff_ref, high_ref, low_ref, *refs
):
    *wind_refs, edge_ref, new_wind = refs
    k = pl.program_id(0)
    _, L, rows, width = new_wind.shape
    band = lax.axis_index("lat")
    geo = table_ref[band]
    thick, u, v = thick_ref[0], u_ref[0], v_ref[0]
    thick_s, v_s = up_ref[0, 0], up_ref[1, 0]
    thick_n, thick_nn, u_n, v_n = (down_ref[i, 0] for i in range(4))
    east, north, below = fluxes(geo, thick, u, v, thick_s, v_s, thick_n)
    inverse = geo[0:rows, 2:3]
    new = thick - (east - west_of(east)) - (north - south_of(north, below)) * inverse
    east_n = u_n * jnp.where(u_n > 0, thick_n, east_of(thick_n))
    north_n = v_n * jnp.where(v_n > 0, thick_n, thick_nn) * geo[rows : rows + 1, 1:2]
    new_n = (
        thick_n
        - (east_n - west_of(east_n))
        - (north_n - north[rows - 1 : rows]) * geo[rows : rows + 1, 2:3]
    )
    new_wind[0, k] = u - 0.05 * (east_of(new) - new)
    inside = band * rows + row_ids(new.shape) < lat_rows - 1
    new_wind[1, k] = jnp.where(inside, v - 0.05 * (north_of(new, new_n) - new), 0.0)

    def store_edges(field, level, value):
        edge_ref[field, level, 0:1] = value[0:1]
        edge_ref[field, level, 1:2] = value[rows - 1 : rows]

    store_edges(0, k, new)
    scale = 1.0 / new
    for c in range(tracer_ref.shape[0]):
        change = tracer_change(
            tracer_ref[c, 0], up_ref[2 + c, 0], down_ref[4 + c, 0], thick, u, v, v_s, east, north, below, inverse
        )
        store_edges(3 + c, k, change * scale)

    @pl.when(k == L - 1)
    def _():
        pieces = [
            new_wind[:, :, :, a * LANES : (a + 1) * LANES].reshape(2 * L * rows, LANES) for a in range(width // LANES)
        ]
        cutoff = jnp.broadcast_to(cutoff_ref[...][None], (2 * L, rows, LANES)).reshape(2 * L * rows, LANES)
        for a, piece in enumerate(filter_rows(pieces, cutoff, high_ref, low_ref)):
            piece = piece.reshape(2, L, rows, LANES)
            for f in range(2):
                wind_refs[f][0, :, :, a * LANES : (a + 1) * LANES] = piece[f]
        for f in range(2):
            for level in range(L):
                store_edges(1 + f, level, wind_refs[f][0, level])


def second_step(table, lat_rows, thickness, wind_u, wind_v, tracers, up, down, cutoff):
    L, R, N = thickness.shape
    T = tracers.shape[0]
    high, low = filter_tables(N)
    level = pl.BlockSpec((1, R, N), lambda k: (k, 0, 0))
    some = lambda n, rows: pl.BlockSpec((n, 1, rows, N), lambda k: (0, k, 0, 0))
    whole = lambda shape: pl.BlockSpec(shape, lambda k: (0,) * len(shape))
    return pl.pallas_call(
        functools.partial(second_kernel, lat_rows),
        grid=(L,),
        in_specs=[whole(table.shape), level, level, level, some(T, R), some(2 + T, 1), some(4 + T, 1)]
        + [whole((R, LANES)), whole(high.shape), whole(low.shape)],
        out_specs=[whole((1, L, R, N)), whole((1, L, R, N)), whole((3 + T, L, 2, N))],
        out_shape=[
            jax.ShapeDtypeStruct((1, L, R, N), jnp.float32),
            jax.ShapeDtypeStruct((1, L, R, N), jnp.float32),
            jax.ShapeDtypeStruct((3 + T, L, 2, N), jnp.float32),
        ],
        scratch_shapes=[pltpu.VMEM((2, L, R, N), jnp.float32)],
        compiler_params=params(),
        cost_estimate=cost(12 * 2 * L * R * high.size, 4 * L * R * N * (8 + T)),
        name="second_step",
    )(
        table, thickness, wind_u, wind_v, tracers, up, down,
        jnp.broadcast_to(cutoff[:, None], (R, LANES)), jnp.asarray(high), jnp.asarray(low),
    )


def part_kernel(both_ref, *refs):
    sum_ref, near_ref = refs[-2:]
    rows = sum_ref.shape[0]
    sum_ref[...] = both_ref[0:rows]
    _, L, near, _ = near_ref.shape
    for k in range(L):
        near_ref[0, k] = both_ref[rows + k * near : rows + (k + 1) * near]


def part(both, shape, wait):
    L, R, N = shape
    return pl.pallas_call(
        part_kernel,
        in_specs=[VMEM] + after(wait),
        out_specs=[VMEM] * 2,
        out_shape=[
            jax.ShapeDtypeStruct((R, N), jnp.float32),
            jax.ShapeDtypeStruct((1, L, len(near_rows(R)[0]), N), jnp.float32),
        ],
        compiler_params=params(),
        cost_estimate=cost(1e11, 1e9),
        name="part",
    )(both, *wait)


def mass_kernel(C, S, *refs):
    other_refs, (base_ref, mass_ref) = refs[: (C - 1) * S], refs[(C - 1) * S :]
    lev = lax.axis_index("lev")
    others_mass, base = None, None
    for s in range(1, C):
        other = functools.reduce(jnp.add, [ref[...] for ref in other_refs[(s - 1) * S : s * S]])
        below = jnp.where(lev >= s, other, 0.0)
        others_mass = other if others_mass is None else others_mass + other
        base = below if base is None else base + below
    base_ref[...] = base
    mass_ref[...] = others_mass


def other_chips(counts, others):
    return pl.pallas_call(
        functools.partial(mass_kernel, *counts),
        in_specs=[VMEM] * len(others),
        out_specs=[VMEM] * 2,
        out_shape=[jax.ShapeDtypeStruct(others[0].shape, jnp.float32)] * 2,
        compiler_params=params(),
        cost_estimate=cost(1, 1),
        name="other_chips",
    )(*others)


def add_weights(weight_ref, sum_ref):
    total = jnp.zeros(weight_ref.shape[1:], jnp.float32)
    for k in range(weight_ref.shape[0]):
        sum_ref[k] = total
        total = total + weight_ref[k]
    sum_ref[weight_ref.shape[0]] = total
    return total


def source_levels(place, counts, thick, others):
    C, S = counts
    lev, sub = place
    spot = [lax.rem(lev - g // S + C, C) * S + lax.rem(sub - g % S + S, S) for g in range(len(thick))]
    group = [functools.reduce(jnp.add, levels) for levels in thick]
    mass = functools.reduce(jnp.add, group)
    base = jnp.zeros_like(mass)
    if others:
        base, mass = others[0], mass + others[1]
    sources = []
    for g, levels in enumerate(thick):
        low = base
        for other in range(len(thick)):
            if other != g:
                low = low + jnp.where(spot[other] < spot[g], group[other], 0.0)
        for m, value in enumerate(levels):
            sources.append((g, m, low, value))
            low = low + value
    return mass, sources


def covered(top, sources):
    return [jnp.minimum(jnp.maximum(top - low, 0.0), value) for _, _, low, value in sources]


def level_of(ref, index):
    return lambda m, at, columns: ref[index, m, at, columns]


def packed_level_of(ref, index, L, rows):
    return lambda m, at, columns: ref[(index * L + m) * rows : (index * L + m + 1) * rows, columns]


def remap_rows(weight_ref, sum_ref, counts, steps, thick_refs, field_refs, other_refs, store):
    C, S = counts
    _, L, R, N = thick_refs[0].shape
    rows = min(R, 8)
    place = lev, sub = lax.axis_index("lev"), lax.axis_index("sub")
    firsts = [(lax.rem(lev + s, C) * S + sub) * L for s in steps]
    weight_sum = add_weights(weight_ref, sum_ref)[0:rows]

    def tile(at, columns):
        thick = [[ref[0, m, at, columns] for m in range(L)] for ref in thick_refs]
        others = [ref[at, columns] for ref in other_refs]
        mass, sources = source_levels(place, counts, thick, others)
        unit = mass / weight_sum
        for index, s in enumerate(steps):
            below = covered(unit * sum_ref[firsts[index], 0:rows], sources)
            for i in range(L):
                upto = covered(unit * sum_ref[firsts[index] + i + 1, 0:rows], sources)
                part = [a - b for a, b in zip(upto, below)]
                below = upto
                target = unit * weight_ref[firsts[index] + i, 0:rows]
                scale = 1.0 / target
                means = []
                for refs in field_refs:
                    terms = [refs[g](m, at, columns) * w for (g, m, _, _), w in zip(sources, part)]
                    means.append(functools.reduce(jnp.add, terms) * scale)
                store(s, i, at, columns, target, means)

    for r in range(0, R, rows):

        def body(c, carry):
            tile(slice(r, r + rows), pl.ds(pl.multiple_of(c * LANES, LANES), LANES))
            return carry

        lax.fori_loop(0, N // LANES, body, 0)


def inner_part(at, margin, rows):
    return max(at.start, margin[0]), min(at.stop, rows - margin[1])


def remap_kernel(counts, steps, fields, margin, with_thickness, sizes, weight_ref, *refs):
    *refs, sum_ref = refs
    C, S = counts
    thick_refs, refs = refs[:S], refs[S:]
    bundles = []
    for _ in range(sizes[0]):
        bundles.append(refs[:S])
        refs = refs[S:]
    other_refs, out_refs = refs[:2], refs[len(refs) - len(steps) - with_thickness :]
    _, L, R, _ = thick_refs[0].shape
    thick_out_ref = out_refs[-1]
    field_refs = [[level_of(ref, index) for ref in bundles[which]] for which, index in fields]

    def store(s, i, at, columns, target, means):
        out_ref = out_refs[steps.index(s)]
        if with_thickness and s == 0:
            thick_out_ref[i, at, columns] = target
        for f, value in enumerate(means):
            if s == 0:
                out_ref[f, i, at, columns] = value
            else:
                lower, upper = inner_part(at, margin, R)
                start = (f * L + i) * (R - sum(margin)) - margin[0]
                out_ref[start + lower : start + upper, columns] = value[lower - at.start : upper - at.start]

    remap_rows(
        weight_ref, sum_ref, counts, steps, thick_refs, field_refs, other_refs, store
    )


def remap_parts(counts, weights, thick, bundles, others, fields, steps, margin, with_thickness=False, wait=()):
    C, S = counts
    _, L, R, N = thick[0].shape
    F = len(fields)
    whole = jax.ShapeDtypeStruct((F, L, R, N), jnp.float32)
    inner = jax.ShapeDtypeStruct((F * L * (R - sum(margin)), N), jnp.float32)
    flat = [a for bundle in bundles for a in bundle]
    out_shape = [whole if s == 0 else inner for s in steps]
    if with_thickness:
        out_shape.append(jax.ShapeDtypeStruct((L, R, N), jnp.float32))
    return pl.pallas_call(
        functools.partial(remap_kernel, counts, tuple(steps), tuple(fields), margin, with_thickness, (len(bundles),)),
        in_specs=[VMEM] * (1 + len(thick) + len(flat) + len(others)) + after(wait),
        out_specs=[VMEM] * len(out_shape),
        out_shape=out_shape,
        scratch_shapes=[pltpu.VMEM((weights.shape[0] + 1, 8, LANES), jnp.float32)],
        compiler_params=params(),
        cost_estimate=cost(len(steps) * S * L * L * R * N * (5 + 2 * F), 4 * R * N * L * (F + 1) * (S + len(steps))),
        name="remap_parts",
    )(weights, *thick, *flat, *others, *wait)


def remap_edge_kernel(counts, near_fields, weight_ref, *refs):
    *refs, sum_ref = refs
    G = counts[0] * counts[1]
    edge_refs, near_refs = refs[:G], refs[G : 2 * G]
    bundles = (refs[2 * G : 3 * G], refs[3 * G : 4 * G])
    edge_out_ref, thick_out_ref, near_out_ref = refs[-3:]

    def store_edge(s, i, at, columns, target, means):
        thick_out_ref[i, at, columns] = target
        for f, value in enumerate(means):
            edge_out_ref[f, i, at, columns] = value

    def store_near(s, i, at, columns, target, means):
        for f, value in enumerate(means):
            near_out_ref[f, i, at, columns] = value

    fields = [[level_of(ref, f) for ref in edge_refs] for f in range(1, edge_refs[0].shape[0])]
    remap_rows(weight_ref, sum_ref, counts, (0,), edge_refs, fields, [], store_edge)
    _, L, R, _ = near_refs[0].shape
    fields = [[packed_level_of(ref, index, L, R) for ref in bundles[which]] for which, index in near_fields]
    remap_rows(weight_ref, sum_ref, counts, (0,), near_refs, fields, [], store_near)


def remap_edges(counts, weights, edges, near_new, near, near_rest, wait=()):
    F, L, R, N = edges[0].shape
    T = F - 3
    near_fields = tuple((0, f) if f < T // 2 else (1, f - T // 2) for f in range(T))
    operands = [*edges, *near_new, *near, *near_rest]
    return pl.pallas_call(
        functools.partial(remap_edge_kernel, counts, near_fields),
        in_specs=[VMEM] * (1 + len(operands)) + after(wait),
        out_specs=[VMEM] * 3,
        out_shape=[
            jax.ShapeDtypeStruct((F - 1, L, R, N), jnp.float32),
            jax.ShapeDtypeStruct((L, R, N), jnp.float32),
            jax.ShapeDtypeStruct((T, *near_new[0].shape[1:]), jnp.float32),
        ],
        scratch_shapes=[pltpu.VMEM((weights.shape[0] + 1, 8, LANES), jnp.float32)],
        compiler_params=params(),
        cost_estimate=cost(len(edges) * L * L * R * N * 40, 4 * R * N * L * len(operands) * F),
        name="remap_edges",
    )(weights, *operands, *wait)


def finish_kernel(margin, own_ref, near_ref, edge_ref, thick_ref, thick_edge_ref, *refs):
    *arrived_refs, out_ref, thick_out_ref, token_ref = refs
    token_ref[...] = jnp.zeros_like(token_ref)
    T, L, R, _ = out_ref.shape
    thick_out_ref[...] = thick_ref[...]
    for i in range(L):
        for row, j in ((0, 0), (R - 1, 1)):
            thick_out_ref[i, row : row + 1] = thick_edge_ref[i, j : j + 1]
    for f in range(T):
        for i in range(L):
            start, first, end = (f * L + i) * (R - sum(margin)), margin[0], R - margin[1]
            total = own_ref[f, i, first:end]
            for ref in arrived_refs:
                total = total + ref[start : start + end - first]
            out_ref[f, i, first:end] = total
            for row, j in ((0, 0), (R - 1, 1)):
                out_ref[f, i, row : row + 1] = edge_ref[2 + f, i, j : j + 1]
            for j, row in enumerate(near_rows(R)[0]):
                out_ref[f, i, row : row + 1] = near_ref[f, i, j : j + 1]


def finish_tracers(own, near, edge, thick, thick_edge, arrived):
    return pl.pallas_call(
        functools.partial(finish_kernel, near_rows(own.shape[2])[1]),
        in_specs=[VMEM] * (5 + len(arrived)),
        out_specs=[VMEM] * 3,
        out_shape=[
            jax.ShapeDtypeStruct(own.shape, jnp.float32),
            jax.ShapeDtypeStruct(thick.shape, jnp.float32),
            jax.ShapeDtypeStruct((8, LANES), jnp.float32),
        ],
        compiler_params=params(),
        cost_estimate=cost(2 * own.size, 12 * own.size),
        name="finish_tracers",
    )(own, near, edge, thick, thick_edge, *arrived)


def finish_winds_kernel(count, own_ref, edge_ref, *refs):
    arrived_refs, out_refs = refs[:count], refs[-2:]
    _, L, R, N = own_ref.shape
    for f, out_ref in enumerate(out_refs):
        for i in range(L):
            start = (f * L + i) * (R - 2)
            total = own_ref[f, i, 1 : R - 1]
            for ref in arrived_refs:
                total = total + ref[start : start + R - 2]
            out_ref[i, 1 : R - 1] = total
            out_ref[i, 0:1] = edge_ref[f, i, 0:1]
            out_ref[i, R - 1 : R] = edge_ref[f, i, 1:2]


def finish_winds(own, arrived, edge, wait):
    return pl.pallas_call(
        functools.partial(finish_winds_kernel, len(arrived)),
        in_specs=[VMEM] * (2 + len(arrived)) + after(wait),
        out_specs=[VMEM] * 2,
        out_shape=[jax.ShapeDtypeStruct(own.shape[1:], jnp.float32)] * 2,
        compiler_params=params(),
        cost_estimate=cost(own.size, 12 * own.size),
        name="finish_winds",
    )(own, edge, *arrived, *wait)


def edge_kernel(thick_hbm, u_hbm, v_hbm, tracer_hbm, *refs):
    last_ref, leading_ref, top_ref, low_ref, tracer_ref, sems = refs[-6:]
    T, L, R, _ = tracer_hbm.shape
    top = pl.ds(R - 8, 8)
    copies = [
        pltpu.make_async_copy(thick_hbm.at[:, top], top_ref.at[0], sems.at[0]),
        pltpu.make_async_copy(v_hbm.at[:, top], top_ref.at[1], sems.at[1]),
        pltpu.make_async_copy(thick_hbm.at[:, pl.ds(0, 8)], low_ref.at[0], sems.at[2]),
        pltpu.make_async_copy(u_hbm.at[:, pl.ds(0, 8)], low_ref.at[1], sems.at[3]),
        pltpu.make_async_copy(v_hbm.at[:, pl.ds(0, 8)], low_ref.at[2], sems.at[4]),
        pltpu.make_async_copy(tracer_hbm.at[:, :, top], tracer_ref.at[0], sems.at[5]),
        pltpu.make_async_copy(tracer_hbm.at[:, :, pl.ds(0, 8)], tracer_ref.at[1], sems.at[6]),
    ]
    for copy in copies:
        copy.start()
    for copy in copies:
        copy.wait()
    last_ref[0:2] = top_ref[:, :, 7:8]
    last_ref[2 : 2 + T] = tracer_ref[0, :, :, 7:8]
    leading_ref[0] = low_ref[0, :, 0:1]
    leading_ref[1] = low_ref[0, :, 1:2]
    leading_ref[2:4] = low_ref[1:3, :, 0:1]
    leading_ref[4 : 4 + T] = tracer_ref[1, :, :, 0:1]


def edge_rows(thickness, wind_u, wind_v, tracers, wait):
    L, R, N = thickness.shape
    T = tracers.shape[0]
    operands = [pltpu.with_memory_space_constraint(a, pltpu.HBM) for a in (thickness, wind_u, wind_v, tracers)]
    return pl.pallas_call(
        edge_kernel,
        in_specs=after(operands) + after(wait),
        out_specs=[VMEM] * 2,
        out_shape=[
            jax.ShapeDtypeStruct((2 + T, L, 1, N), jnp.float32),
            jax.ShapeDtypeStruct((4 + T, L, 1, N), jnp.float32),
        ],
        scratch_shapes=[
            pltpu.VMEM((2, L, 8, N), jnp.float32),
            pltpu.VMEM((3, L, 8, N), jnp.float32),
            pltpu.VMEM((2, T, L, 8, N), jnp.float32),
            pltpu.SemaphoreType.DMA((7,)),
        ],
        compiler_params=params(),
        cost_estimate=cost(1e10, 1e9),
        name="edge_rows",
    )(*operands, *wait)


def shifted(value, lev_count, sub_count, s, t):
    if t == 0:
        return lax.ppermute(value, "lev", [(i, (i + s) % lev_count) for i in range(lev_count)])
    if s == 0:
        return lax.ppermute(value, "sub", [(i, (i + t) % sub_count) for i in range(sub_count)])
    pairs = [
        (i * sub_count + j, (i + s) % lev_count * sub_count + (j + t) % sub_count)
        for i in range(lev_count)
        for j in range(sub_count)
    ]
    return lax.ppermute(value, ("lev", "sub"), pairs)


def per_device(thickness, wind_u, wind_v, tracers, level_weights, cutoff):
    L, R, N = thickness.shape
    lat_count = lax.axis_size("lat")
    C, S = lax.axis_size("lev"), lax.axis_size("sub")
    lat_rows = R * lat_count
    send = functools.partial(shifted, lev_count=C, sub_count=S)

    T = tracers.shape[0]
    northward = [(i, i + 1) for i in range(lat_count - 1)]
    southward = [(j, i) for i, j in northward]
    table = jnp.asarray(geometry_table(lat_rows, R))
    weights = jnp.broadcast_to(level_weights[:, None, None], (level_weights.shape[0], 8, LANES))
    away = range(1, C)

    def with_others_of_chip(own):
        return [own] + [send(own, s=0, t=t) for t in range(1, S)]

    def sent(parts):
        return [send(part, s=s, t=0) for s, part in zip(away, parts)]

    remap = functools.partial(remap_parts, (C, S), weights)

    new, both, near_new, *arguments = first_step(table, thickness, wind_u, wind_v, tracers)
    both = [send(both, s=s, t=0) for s in away]
    inner, near, near_rest = inner_step(table, new, *arguments)
    group = with_others_of_chip(inner)
    near = [near] + [send(near, s=s, t=0) for s in away]
    near_rest = [near_rest] + [send(near_rest, s=s, t=0) for s in away]
    parted = [part(each, (L, R, N), [near[0]]) for each in both]
    near_new = [near_new] + [each[1] for each in parted]
    others = other_chips((C, S), [a for each in parted for a in with_others_of_chip(each[0])])
    tracer_fields = [(0, 1 + c) for c in range(T)]
    away_parts = remap(group, [group], others, tracer_fields, away, near_rows(R)[1])
    arrived = sent(away_parts)

    last, leading = edge_rows(
        thickness, wind_u, wind_v, tracers, [away_parts[0], *near[1:2], *near_rest[1:2]]
    )
    up = lax.ppermute(last, "lat", northward)
    down = lax.ppermute(leading, "lat", southward)
    u, v, edge = second_step(table, lat_rows, thickness, wind_u, wind_v, tracers, up, down, cutoff)
    edges = [edge] + [send(edge, s=s, t=0) for s in away]
    winds = [with_others_of_chip(u), with_others_of_chip(v)]
    tracers_own, thick_inner = remap(group, [group], others, tracer_fields, (0,), (0, 0), with_thickness=True, wait=[edge])
    winds_own, *winds_away = remap(
        group, winds, others, [(0, 0), (1, 0)], range(C), (1, 1), wait=[tracers_own, *arrived[:1]]
    )
    winds_arrived = sent(winds_away)
    near_new, near, near_rest, edges = (
        [a for own in sources for a in with_others_of_chip(own)] for sources in (near_new, near, near_rest, edges)
    )
    edge_out, thick_edge, near_out = remap_edges(
        (C, S), weights, edges, near_new, near, near_rest, wait=winds_away[:1]
    )

    tracers_out, thickness_out, token = finish_tracers(
        tracers_own, near_out, edge_out, thick_inner, thick_edge, arrived
    )
    u_out, v_out = finish_winds(winds_own, winds_arrived, edge_out, [token])
    return thickness_out, u_out, v_out, tracers_out


def solution(mesh):
    placed = (
        P(("member", "lev", "sub"), "lat", None),
        P(("member", "lev", "sub"), "lat", None),
        P(("member", "lev", "sub"), "lat", None),
        P("member", ("lev", "sub"), "lat", None),
        P(),
        P("lat"),
    )
    return jax.shard_map(
        per_device,
        mesh=mesh,
        in_specs=placed,
        out_specs=(
            P(("member", "lev", "sub"), "lat", None),
            P(("member", "lev", "sub"), "lat", None),
            P(("member", "lev", "sub"), "lat", None),
            P("member", ("lev", "sub"), "lat", None),
        ),
        check_vma=False,
    )
```

```python
import functools

import jax
import jax.numpy as jnp
import ml_dtypes
import numpy as np
from jax import lax
from jax.experimental import pallas as pl
from jax.experimental.pallas import tpu as pltpu
from jax.sharding import PartitionSpec as P

LANES = 128
VMEM = pl.BlockSpec(memory_space=pltpu.VMEM)


def params():
    return pltpu.CompilerParams(vmem_limit_bytes=16 * 1024 * 1024)


def cost(flops, bytes_accessed):
    return pl.CostEstimate(flops=int(flops), bytes_accessed=int(bytes_accessed), transcendentals=0)


def after(arrays):
    return [pl.BlockSpec(memory_space=pl.ANY)] * len(arrays)


def near_rows(rows):
    return (1, 2, rows - 2), (3, 2)


def geometry_table(lat_rows, band_rows):
    bands = lat_rows // band_rows
    table = np.zeros((bands, band_rows + 8, LANES), np.float32)
    for band in range(bands):
        for j in range(band_rows + 1):
            row = band * band_rows + j
            south = np.sin(row * np.pi / lat_rows) if 0 < row < lat_rows else 0.0
            north = np.sin((row + 1) * np.pi / lat_rows) if row + 1 < lat_rows else 0.0
            table[band, j, 0] = south
            table[band, j, 1] = north
            table[band, j, 2] = 1.0 / np.sin((row + 0.5) * np.pi / lat_rows)
    return table


def east_of(value):
    return pltpu.roll(value, value.shape[1] - 1, 1)


def west_of(value):
    return pltpu.roll(value, 1, 1)


def row_ids(shape):
    return lax.broadcasted_iota(jnp.int32, shape, 0)


def north_of(value, beyond):
    rows = value.shape[0]
    rolled = pltpu.roll(value, rows - 1, 0)
    return rolled if beyond is None else jnp.where(row_ids(value.shape) == rows - 1, beyond, rolled)


def south_of(value, beyond):
    rolled = pltpu.roll(value, 1, 0)
    return rolled if beyond is None else jnp.where(row_ids(value.shape) == 0, beyond, rolled)


def fluxes(geo, thick, u, v, thick_s, v_s, thick_n):
    rows = thick.shape[0]
    east = u * jnp.where(u > 0, thick, east_of(thick))
    north = v * jnp.where(v > 0, thick, north_of(thick, thick_n)) * geo[0:rows, 1:2]
    below = None if v_s is None else v_s * jnp.where(v_s > 0, thick_s, thick[0:1]) * geo[0:1, 0:1]
    return east, north, below


def tracer_change(q, q_s, q_n, thick, u, v, v_s, east, north, below, inverse):
    t_east = east * jnp.where(u > 0, q, east_of(q))
    t_north = north * jnp.where(v > 0, q, north_of(q, q_n))
    t_below = None if v_s is None else below * jnp.where(v_s > 0, q_s, q[0:1])
    change = thick * q - (t_east - west_of(t_east))
    return change - (t_north - south_of(t_north, t_below)) * inverse


def first_kernel(table_hbm, thick_hbm, u_hbm, v_hbm, tracer_hbm, *refs):
    new_ref, both_ref, near_ref, thick_ref, u_ref, v_ref, tracer_ref, geo_ref, sems = refs
    L, rows, _ = thick_ref.shape
    near, _ = near_rows(rows)
    table_copy = pltpu.make_async_copy(table_hbm.at[lax.axis_index("lat")], geo_ref, sems.at[3, 0])
    table_copy.start()
    pairs = ((thick_hbm, thick_ref), (u_hbm, u_ref), (v_hbm, v_ref))

    def copies(k):
        return [pltpu.make_async_copy(a.at[k], b.at[k], sems.at[i, k]) for i, (a, b) in enumerate(pairs)]

    for k in range(L):
        for copy in copies(k):
            copy.start()
    tracer_copy = pltpu.make_async_copy(tracer_hbm, tracer_ref, sems.at[3, 1])
    tracer_copy.start()
    table_copy.wait()
    geo = geo_ref[...]
    both_ref[...] = jnp.zeros_like(both_ref)

    def level(k, carry):
        for copy in copies(k):
            copy.wait()
        thick, u, v = thick_ref[k], u_ref[k], v_ref[k]
        east, north, _ = fluxes(geo, thick, u, v, None, None, None)
        new = thick - (east - west_of(east)) - (north - south_of(north, None)) * geo[0:rows, 2:3]
        new_ref[k] = new
        for j, row in enumerate(near):
            near_ref[0, k, j : j + 1] = new[row : row + 1]
        both_ref[0:rows] += new
        return carry

    lax.fori_loop(0, L, level, 0)
    for k in range(L):
        at = rows + k * len(near)
        both_ref[at : at + len(near)] = near_ref[0, k]
    tracer_copy.wait()


def first_step(table, thickness, wind_u, wind_v, tracers):
    L, R, N = thickness.shape
    arguments = (thickness, wind_u, wind_v, tracers)
    operands = [pltpu.with_memory_space_constraint(a, pltpu.HBM) for a in (table, *arguments)]
    near = len(near_rows(R)[0])
    shapes = [(L, R, N), (-(-(R + L * near) // 8) * 8, N), (1, L, near, N)] + [a.shape for a in arguments]
    return pl.pallas_call(
        first_kernel,
        in_specs=after(operands),
        out_specs=[VMEM] * len(shapes),
        out_shape=[jax.ShapeDtypeStruct(shape, jnp.float32) for shape in shapes],
        scratch_shapes=[pltpu.VMEM(table.shape[1:], jnp.float32), pltpu.SemaphoreType.DMA((4, max(L, 2)))],
        compiler_params=params(),
        cost_estimate=cost(40 * L * R * N, 4 * L * R * N * (7 + 2 * tracers.shape[0])),
        name="first_step",
    )(*operands)


def inner_kernel(table_ref, new_ref, thick_ref, u_ref, v_ref, tracer_ref, out_ref, near_ref, near_rest_ref):
    T, L, rows, _ = tracer_ref.shape
    near, _ = near_rows(rows)
    geo = table_ref[lax.axis_index("lat")]
    inverse = geo[0:rows, 2:3]

    def level(k, carry):
        thick, u, v, new = thick_ref[k], u_ref[k], v_ref[k], new_ref[k]
        east, north, _ = fluxes(geo, thick, u, v, None, None, None)

        out_ref[0, k] = new
        scale = 1.0 / new
        for c in range(T):
            change = tracer_change(
                tracer_ref[c, k], None, None, thick, u, v, None, east, north, None, inverse
            )
            value = change * scale
            out_ref[1 + c, k] = value
            ref, at = (near_ref, c) if c < T // 2 else (near_rest_ref, c - T // 2)
            for j, row in enumerate(near):
                ref[pl.ds((at * L + k) * len(near) + j, 1)] = value[row : row + 1]
        return carry

    lax.fori_loop(0, L, level, 0)


def inner_step(table, new, thickness, wind_u, wind_v, tracers):
    L, R, N = thickness.shape
    T = tracers.shape[0]
    rows = lambda n: jax.ShapeDtypeStruct((n * L * len(near_rows(R)[0]), N), jnp.float32)
    shape = lambda n, rows: jax.ShapeDtypeStruct((n, L, rows, N), jnp.float32)
    return pl.pallas_call(
        inner_kernel,
        in_specs=[VMEM] * 6,
        out_specs=[VMEM] * 3,
        out_shape=[shape(1 + T, R), rows(T // 2), rows(T - T // 2)],
        compiler_params=params(),
        cost_estimate=cost(130 * L * R * N, 4 * L * R * N * (8 + 2 * T)),
        name="inner_step",
    )(table, new, thickness, wind_u, wind_v, tracers)


def filter_tables(N):
    A = N // LANES
    b = np.arange(LANES)[:, None]
    p = np.arange(LANES)[None, :]
    tables = []
    for q in range(A // 2 + 1):
        angle = 2.0 * np.pi * ((b * (A * p + q)) % N) / N
        c, s = np.cos(angle), np.sin(angle)
        tables.append(np.block([[c, -s], [s, c]]))
    table = np.stack(tables)
    high = table.astype(np.float32).astype(ml_dtypes.bfloat16)
    low = (table - high.astype(np.float64)).astype(np.float32).astype(ml_dtypes.bfloat16)
    return high, low


def split(value):
    high = value.astype(jnp.bfloat16)
    return high, (value - high.astype(jnp.float32)).astype(jnp.bfloat16)


def product(value, high, low, transposed):
    dims = (((1,), (1 if transposed else 0,)), ((), ()))
    dot = lambda x, y: lax.dot_general(x, y, dims, preferred_element_type=jnp.float32)
    v_high, v_low = split(value)
    return dot(v_high, high) + (dot(v_high, low) + dot(v_low, high))


def filter_rows(x, cutoff, high_ref, low_ref):
    A = len(x)
    N = A * LANES
    half = A // 2
    even = [x[a] + x[A - a] for a in range(1, half + 1)]
    odd = [x[a] - x[A - a] for a in range(1, half + 1)]
    angle = lambda q, a: 2.0 * np.pi * ((q * a) % A) / A
    p = lax.broadcasted_iota(jnp.int32, cutoff.shape, 1)
    real, imag = [], []
    for q in range(half + 1):
        re = x[0]
        for a in range(1, half + 1):
            re = re + (even[a - 1] if q == 0 else float(np.cos(angle(q, a))) * even[a - 1])
        if q == 0:
            high, low = high_ref[0, 0:LANES], low_ref[0, 0:LANES]
            spectrum = product(re, high, low, False)
        else:
            high, low = high_ref[q], low_ref[q]
            im = -float(np.sin(angle(q, 1))) * odd[0]
            for a in range(2, half + 1):
                im = im - float(np.sin(angle(q, a))) * odd[a - 1]
            spectrum = product(jnp.concatenate([re, im], axis=1), high, low, False)
        mode = A * p + q
        factor = 1.0 / N if q == 0 else 2.0 / N
        kept = jnp.where(jnp.minimum(mode, N - mode) <= cutoff, factor, 0.0)
        back = product(spectrum * jnp.concatenate([kept, kept], axis=1), high, low, True)
        real.append(back[:, :LANES])
        imag.append(back[:, LANES:])
    out = [None] * A
    out[0] = functools.reduce(jnp.add, real)
    for a in range(1, half + 1):
        even_part, odd_part = real[0], None
        for q in range(1, half + 1):
            even_part = even_part + float(np.cos(angle(q, a))) * real[q]
            term = float(np.sin(angle(q, a))) * imag[q]
            odd_part = term if odd_part is None else odd_part + term
        out[a] = even_part - odd_part
        out[A - a] = even_part + odd_part
    return out


def second_kernel(
    lat_rows, table_ref, thick_ref, u_ref, v_ref, tracer_ref, up_ref, down_ref, cutoff_ref, high_ref, low_ref, *refs
):
    *wind_refs, edge_ref, new_wind = refs
    k = pl.program_id(0)
    _, L, rows, width = new_wind.shape
    band = lax.axis_index("lat")
    geo = table_ref[band]
    thick, u, v = thick_ref[0], u_ref[0], v_ref[0]
    thick_s, v_s = up_ref[0, 0], up_ref[1, 0]
    thick_n, thick_nn, u_n, v_n = (down_ref[i, 0] for i in range(4))
    east, north, below = fluxes(geo, thick, u, v, thick_s, v_s, thick_n)
    inverse = geo[0:rows, 2:3]
    new = thick - (east - west_of(east)) - (north - south_of(north, below)) * inverse
    east_n = u_n * jnp.where(u_n > 0, thick_n, east_of(thick_n))
    north_n = v_n * jnp.where(v_n > 0, thick_n, thick_nn) * geo[rows : rows + 1, 1:2]
    new_n = (
        thick_n
        - (east_n - west_of(east_n))
        - (north_n - north[rows - 1 : rows]) * geo[rows : rows + 1, 2:3]
    )
    new_wind[0, k] = u - 0.05 * (east_of(new) - new)
    inside = band * rows + row_ids(new.shape) < lat_rows - 1
    new_wind[1, k] = jnp.where(inside, v - 0.05 * (north_of(new, new_n) - new), 0.0)

    def store_edges(field, level, value):
        edge_ref[field, level, 0:1] = value[0:1]
        edge_ref[field, level, 1:2] = value[rows - 1 : rows]

    store_edges(0, k, new)
    scale = 1.0 / new
    for c in range(tracer_ref.shape[0]):
        change = tracer_change(
            tracer_ref[c, 0], up_ref[2 + c, 0], down_ref[4 + c, 0], thick, u, v, v_s, east, north, below, inverse
        )
        store_edges(3 + c, k, change * scale)

    @pl.when(k == L - 1)
    def _():
        pieces = [
            new_wind[:, :, :, a * LANES : (a + 1) * LANES].reshape(2 * L * rows, LANES) for a in range(width // LANES)
        ]
        cutoff = jnp.broadcast_to(cutoff_ref[...][None], (2 * L, rows, LANES)).reshape(2 * L * rows, LANES)
        for a, piece in enumerate(filter_rows(pieces, cutoff, high_ref, low_ref)):
            piece = piece.reshape(2, L, rows, LANES)
            for f in range(2):
                wind_refs[f][0, :, :, a * LANES : (a + 1) * LANES] = piece[f]
        for f in range(2):
            for level in range(L):
                store_edges(1 + f, level, wind_refs[f][0, level])


def second_step(table, lat_rows, thickness, wind_u, wind_v, tracers, up, down, cutoff):
    L, R, N = thickness.shape
    T = tracers.shape[0]
    high, low = filter_tables(N)
    level = pl.BlockSpec((1, R, N), lambda k: (k, 0, 0))
    some = lambda n, rows: pl.BlockSpec((n, 1, rows, N), lambda k: (0, k, 0, 0))
    whole = lambda shape: pl.BlockSpec(shape, lambda k: (0,) * len(shape))
    return pl.pallas_call(
        functools.partial(second_kernel, lat_rows),
        grid=(L,),
        in_specs=[whole(table.shape), level, level, level, some(T, R), some(2 + T, 1), some(4 + T, 1)]
        + [whole((R, LANES)), whole(high.shape), whole(low.shape)],
        out_specs=[whole((1, L, R, N)), whole((1, L, R, N)), whole((3 + T, L, 2, N))],
        out_shape=[
            jax.ShapeDtypeStruct((1, L, R, N), jnp.float32),
            jax.ShapeDtypeStruct((1, L, R, N), jnp.float32),
            jax.ShapeDtypeStruct((3 + T, L, 2, N), jnp.float32),
        ],
        scratch_shapes=[pltpu.VMEM((2, L, R, N), jnp.float32)],
        compiler_params=params(),
        cost_estimate=cost(12 * 2 * L * R * high.size, 4 * L * R * N * (8 + T)),
        name="second_step",
    )(
        table, thickness, wind_u, wind_v, tracers, up, down,
        jnp.broadcast_to(cutoff[:, None], (R, LANES)), jnp.asarray(high), jnp.asarray(low),
    )


def part_kernel(both_ref, *refs):
    sum_ref, near_ref = refs[-2:]
    rows = sum_ref.shape[0]
    sum_ref[...] = both_ref[0:rows]
    _, L, near, _ = near_ref.shape
    for k in range(L):
        near_ref[0, k] = both_ref[rows + k * near : rows + (k + 1) * near]


def part(both, shape, wait):
    L, R, N = shape
    return pl.pallas_call(
        part_kernel,
        in_specs=[VMEM] + after(wait),
        out_specs=[VMEM] * 2,
        out_shape=[
            jax.ShapeDtypeStruct((R, N), jnp.float32),
            jax.ShapeDtypeStruct((1, L, len(near_rows(R)[0]), N), jnp.float32),
        ],
        compiler_params=params(),
        cost_estimate=cost(1e11, 1e9),
        name="part",
    )(both, *wait)


def mass_kernel(C, S, *refs):
    other_refs, (base_ref, mass_ref) = refs[: (C - 1) * S], refs[(C - 1) * S :]
    lev = lax.axis_index("lev")
    others_mass, base = None, None
    for s in range(1, C):
        other = functools.reduce(jnp.add, [ref[...] for ref in other_refs[(s - 1) * S : s * S]])
        below = jnp.where(lev >= s, other, 0.0)
        others_mass = other if others_mass is None else others_mass + other
        base = below if base is None else base + below
    base_ref[...] = base
    mass_ref[...] = others_mass


def other_chips(counts, others):
    return pl.pallas_call(
        functools.partial(mass_kernel, *counts),
        in_specs=[VMEM] * len(others),
        out_specs=[VMEM] * 2,
        out_shape=[jax.ShapeDtypeStruct(others[0].shape, jnp.float32)] * 2,
        compiler_params=params(),
        cost_estimate=cost(1, 1),
        name="other_chips",
    )(*others)


def add_weights(weight_ref, sum_ref):
    total = jnp.zeros(weight_ref.shape[1:], jnp.float32)
    for k in range(weight_ref.shape[0]):
        sum_ref[k] = total
        total = total + weight_ref[k]
    sum_ref[weight_ref.shape[0]] = total
    return total


def source_levels(place, counts, thick, others):
    C, S = counts
    lev, sub = place
    spot = [lax.rem(lev - g // S + C, C) * S + lax.rem(sub - g % S + S, S) for g in range(len(thick))]
    group = [functools.reduce(jnp.add, levels) for levels in thick]
    mass = functools.reduce(jnp.add, group)
    base = jnp.zeros_like(mass)
    if others:
        base, mass = others[0], mass + others[1]
    sources = []
    for g, levels in enumerate(thick):
        low = base
        for other in range(len(thick)):
            if other != g:
                low = low + jnp.where(spot[other] < spot[g], group[other], 0.0)
        for m, value in enumerate(levels):
            sources.append((g, m, low, value))
            low = low + value
    return mass, sources


def covered(top, sources):
    return [jnp.minimum(jnp.maximum(top - low, 0.0), value) for _, _, low, value in sources]


def level_of(ref, index):
    return lambda m, at, columns: ref[index, m, at, columns]


def packed_level_of(ref, index, L, rows):
    return lambda m, at, columns: ref[(index * L + m) * rows : (index * L + m + 1) * rows, columns]


def remap_rows(weight_ref, sum_ref, counts, steps, thick_refs, field_refs, other_refs, store):
    C, S = counts
    _, L, R, N = thick_refs[0].shape
    rows = min(R, 8)
    place = lev, sub = lax.axis_index("lev"), lax.axis_index("sub")
    firsts = [(lax.rem(lev + s, C) * S + sub) * L for s in steps]
    weight_sum = add_weights(weight_ref, sum_ref)[0:rows]

    def tile(at, columns):
        thick = [[ref[0, m, at, columns] for m in range(L)] for ref in thick_refs]
        others = [ref[at, columns] for ref in other_refs]
        mass, sources = source_levels(place, counts, thick, others)
        unit = mass / weight_sum
        for index, s in enumerate(steps):
            below = covered(unit * sum_ref[firsts[index], 0:rows], sources)
            for i in range(L):
                upto = covered(unit * sum_ref[firsts[index] + i + 1, 0:rows], sources)
                part = [a - b for a, b in zip(upto, below)]
                below = upto
                target = unit * weight_ref[firsts[index] + i, 0:rows]
                scale = 1.0 / target
                means = []
                for refs in field_refs:
                    terms = [refs[g](m, at, columns) * w for (g, m, _, _), w in zip(sources, part)]
                    means.append(functools.reduce(jnp.add, terms) * scale)
                store(s, i, at, columns, target, means)

    for r in range(0, R, rows):

        def body(c, carry):
            tile(slice(r, r + rows), pl.ds(pl.multiple_of(c * LANES, LANES), LANES))
            return carry

        lax.fori_loop(0, N // LANES, body, 0)


def inner_part(at, margin, rows):
    return max(at.start, margin[0]), min(at.stop, rows - margin[1])


def remap_kernel(counts, steps, fields, margin, with_thickness, sizes, weight_ref, *refs):
    *refs, sum_ref = refs
    C, S = counts
    thick_refs, refs = refs[:S], refs[S:]
    bundles = []
    for _ in range(sizes[0]):
        bundles.append(refs[:S])
        refs = refs[S:]
    other_refs, out_refs = refs[:2], refs[len(refs) - len(steps) - with_thickness :]
    _, L, R, _ = thick_refs[0].shape
    thick_out_ref = out_refs[-1]
    field_refs = [[level_of(ref, index) for ref in bundles[which]] for which, index in fields]

    def store(s, i, at, columns, target, means):
        out_ref = out_refs[steps.index(s)]
        if with_thickness and s == 0:
            thick_out_ref[i, at, columns] = target
        for f, value in enumerate(means):
            if s == 0:
                out_ref[f, i, at, columns] = value
            else:
                lower, upper = inner_part(at, margin, R)
                start = (f * L + i) * (R - sum(margin)) - margin[0]
                out_ref[start + lower : start + upper, columns] = value[lower - at.start : upper - at.start]

    remap_rows(
        weight_ref, sum_ref, counts, steps, thick_refs, field_refs, other_refs, store
    )


def remap_parts(counts, weights, thick, bundles, others, fields, steps, margin, with_thickness=False, wait=()):
    C, S = counts
    _, L, R, N = thick[0].shape
    F = len(fields)
    whole = jax.ShapeDtypeStruct((F, L, R, N), jnp.float32)
    inner = jax.ShapeDtypeStruct((F * L * (R - sum(margin)), N), jnp.float32)
    flat = [a for bundle in bundles for a in bundle]
    out_shape = [whole if s == 0 else inner for s in steps]
    if with_thickness:
        out_shape.append(jax.ShapeDtypeStruct((L, R, N), jnp.float32))
    return pl.pallas_call(
        functools.partial(remap_kernel, counts, tuple(steps), tuple(fields), margin, with_thickness, (len(bundles),)),
        in_specs=[VMEM] * (1 + len(thick) + len(flat) + len(others)) + after(wait),
        out_specs=[VMEM] * len(out_shape),
        out_shape=out_shape,
        scratch_shapes=[pltpu.VMEM((weights.shape[0] + 1, 8, LANES), jnp.float32)],
        compiler_params=params(),
        cost_estimate=cost(len(steps) * S * L * L * R * N * (5 + 2 * F), 4 * R * N * L * (F + 1) * (S + len(steps))),
        name="remap_parts",
    )(weights, *thick, *flat, *others, *wait)


def remap_edge_kernel(counts, near_fields, weight_ref, *refs):
    *refs, sum_ref = refs
    G = counts[0] * counts[1]
    edge_refs, near_refs = refs[:G], refs[G : 2 * G]
    bundles = (refs[2 * G : 3 * G], refs[3 * G : 4 * G])
    edge_out_ref, thick_out_ref, near_out_ref = refs[-3:]

    def store_edge(s, i, at, columns, target, means):
        thick_out_ref[i, at, columns] = target
        for f, value in enumerate(means):
            edge_out_ref[f, i, at, columns] = value

    def store_near(s, i, at, columns, target, means):
        for f, value in enumerate(means):
            near_out_ref[f, i, at, columns] = value

    fields = [[level_of(ref, f) for ref in edge_refs] for f in range(1, edge_refs[0].shape[0])]
    remap_rows(weight_ref, sum_ref, counts, (0,), edge_refs, fields, [], store_edge)
    _, L, R, _ = near_refs[0].shape
    fields = [[packed_level_of(ref, index, L, R) for ref in bundles[which]] for which, index in near_fields]
    remap_rows(weight_ref, sum_ref, counts, (0,), near_refs, fields, [], store_near)


def remap_edges(counts, weights, edges, near_new, near, near_rest, wait=()):
    F, L, R, N = edges[0].shape
    T = F - 3
    near_fields = tuple((0, f) if f < T // 2 else (1, f - T // 2) for f in range(T))
    operands = [*edges, *near_new, *near, *near_rest]
    return pl.pallas_call(
        functools.partial(remap_edge_kernel, counts, near_fields),
        in_specs=[VMEM] * (1 + len(operands)) + after(wait),
        out_specs=[VMEM] * 3,
        out_shape=[
            jax.ShapeDtypeStruct((F - 1, L, R, N), jnp.float32),
            jax.ShapeDtypeStruct((L, R, N), jnp.float32),
            jax.ShapeDtypeStruct((T, *near_new[0].shape[1:]), jnp.float32),
        ],
        scratch_shapes=[pltpu.VMEM((weights.shape[0] + 1, 8, LANES), jnp.float32)],
        compiler_params=params(),
        cost_estimate=cost(len(edges) * L * L * R * N * 40, 4 * R * N * L * len(operands) * F),
        name="remap_edges",
    )(weights, *operands, *wait)


def finish_kernel(margin, own_ref, near_ref, edge_ref, thick_ref, thick_edge_ref, *refs):
    *arrived_refs, out_ref, thick_out_ref, token_ref = refs
    token_ref[...] = jnp.zeros_like(token_ref)
    T, L, R, _ = out_ref.shape
    thick_out_ref[...] = thick_ref[...]
    for i in range(L):
        for row, j in ((0, 0), (R - 1, 1)):
            thick_out_ref[i, row : row + 1] = thick_edge_ref[i, j : j + 1]
    for f in range(T):
        for i in range(L):
            start, first, end = (f * L + i) * (R - sum(margin)), margin[0], R - margin[1]
            total = own_ref[f, i, first:end]
            for ref in arrived_refs:
                total = total + ref[start : start + end - first]
            out_ref[f, i, first:end] = total
            for row, j in ((0, 0), (R - 1, 1)):
                out_ref[f, i, row : row + 1] = edge_ref[2 + f, i, j : j + 1]
            for j, row in enumerate(near_rows(R)[0]):
                out_ref[f, i, row : row + 1] = near_ref[f, i, j : j + 1]


def finish_tracers(own, near, edge, thick, thick_edge, arrived):
    return pl.pallas_call(
        functools.partial(finish_kernel, near_rows(own.shape[2])[1]),
        in_specs=[VMEM] * (5 + len(arrived)),
        out_specs=[VMEM] * 3,
        out_shape=[
            jax.ShapeDtypeStruct(own.shape, jnp.float32),
            jax.ShapeDtypeStruct(thick.shape, jnp.float32),
            jax.ShapeDtypeStruct((8, LANES), jnp.float32),
        ],
        compiler_params=params(),
        cost_estimate=cost(2 * own.size, 12 * own.size),
        name="finish_tracers",
    )(own, near, edge, thick, thick_edge, *arrived)


def finish_winds_kernel(count, own_ref, edge_ref, *refs):
    arrived_refs, out_refs = refs[:count], refs[-2:]
    _, L, R, N = own_ref.shape
    for f, out_ref in enumerate(out_refs):
        for i in range(L):
            start = (f * L + i) * (R - 2)
            total = own_ref[f, i, 1 : R - 1]
            for ref in arrived_refs:
                total = total + ref[start : start + R - 2]
            out_ref[i, 1 : R - 1] = total
            out_ref[i, 0:1] = edge_ref[f, i, 0:1]
            out_ref[i, R - 1 : R] = edge_ref[f, i, 1:2]


def finish_winds(own, arrived, edge, wait):
    return pl.pallas_call(
        functools.partial(finish_winds_kernel, len(arrived)),
        in_specs=[VMEM] * (2 + len(arrived)) + after(wait),
        out_specs=[VMEM] * 2,
        out_shape=[jax.ShapeDtypeStruct(own.shape[1:], jnp.float32)] * 2,
        compiler_params=params(),
        cost_estimate=cost(own.size, 12 * own.size),
        name="finish_winds",
    )(own, edge, *arrived, *wait)


def edge_kernel(thick_hbm, u_hbm, v_hbm, tracer_hbm, *refs):
    last_ref, leading_ref, top_ref, low_ref, tracer_ref, sems = refs[-6:]
    T, L, R, _ = tracer_hbm.shape
    top = pl.ds(R - 8, 8)
    copies = [
        pltpu.make_async_copy(thick_hbm.at[:, top], top_ref.at[0], sems.at[0]),
        pltpu.make_async_copy(v_hbm.at[:, top], top_ref.at[1], sems.at[1]),
        pltpu.make_async_copy(thick_hbm.at[:, pl.ds(0, 8)], low_ref.at[0], sems.at[2]),
        pltpu.make_async_copy(u_hbm.at[:, pl.ds(0, 8)], low_ref.at[1], sems.at[3]),
        pltpu.make_async_copy(v_hbm.at[:, pl.ds(0, 8)], low_ref.at[2], sems.at[4]),
        pltpu.make_async_copy(tracer_hbm.at[:, :, top], tracer_ref.at[0], sems.at[5]),
        pltpu.make_async_copy(tracer_hbm.at[:, :, pl.ds(0, 8)], tracer_ref.at[1], sems.at[6]),
    ]
    for copy in copies:
        copy.start()
    for copy in copies:
        copy.wait()
    last_ref[0:2] = top_ref[:, :, 7:8]
    last_ref[2 : 2 + T] = tracer_ref[0, :, :, 7:8]
    leading_ref[0] = low_ref[0, :, 0:1]
    leading_ref[1] = low_ref[0, :, 1:2]
    leading_ref[2:4] = low_ref[1:3, :, 0:1]
    leading_ref[4 : 4 + T] = tracer_ref[1, :, :, 0:1]


def edge_rows(thickness, wind_u, wind_v, tracers, wait):
    L, R, N = thickness.shape
    T = tracers.shape[0]
    operands = [pltpu.with_memory_space_constraint(a, pltpu.HBM) for a in (thickness, wind_u, wind_v, tracers)]
    return pl.pallas_call(
        edge_kernel,
        in_specs=after(operands) + after(wait),
        out_specs=[VMEM] * 2,
        out_shape=[
            jax.ShapeDtypeStruct((2 + T, L, 1, N), jnp.float32),
            jax.ShapeDtypeStruct((4 + T, L, 1, N), jnp.float32),
        ],
        scratch_shapes=[
            pltpu.VMEM((2, L, 8, N), jnp.float32),
            pltpu.VMEM((3, L, 8, N), jnp.float32),
            pltpu.VMEM((2, T, L, 8, N), jnp.float32),
            pltpu.SemaphoreType.DMA((7,)),
        ],
        compiler_params=params(),
        cost_estimate=cost(1e10, 1e9),
        name="edge_rows",
    )(*operands, *wait)


def shifted(value, lev_count, sub_count, s, t):
    if t == 0:
        return lax.ppermute(value, "lev", [(i, (i + s) % lev_count) for i in range(lev_count)])
    if s == 0:
        return lax.ppermute(value, "sub", [(i, (i + t) % sub_count) for i in range(sub_count)])
    pairs = [
        (i * sub_count + j, (i + s) % lev_count * sub_count + (j + t) % sub_count)
        for i in range(lev_count)
        for j in range(sub_count)
    ]
    return lax.ppermute(value, ("lev", "sub"), pairs)


def per_device(thickness, wind_u, wind_v, tracers, level_weights, cutoff):
    L, R, N = thickness.shape
    lat_count = lax.axis_size("lat")
    C, S = lax.axis_size("lev"), lax.axis_size("sub")
    lat_rows = R * lat_count
    send = functools.partial(shifted, lev_count=C, sub_count=S)

    T = tracers.shape[0]
    northward = [(i, i + 1) for i in range(lat_count - 1)]
    southward = [(j, i) for i, j in northward]
    table = jnp.asarray(geometry_table(lat_rows, R))
    weights = jnp.broadcast_to(level_weights[:, None, None], (level_weights.shape[0], 8, LANES))
    away = range(1, C)

    def with_others_of_chip(own):
        return [own] + [send(own, s=0, t=t) for t in range(1, S)]

    def sent(parts):
        return [send(part, s=s, t=0) for s, part in zip(away, parts)]

    remap = functools.partial(remap_parts, (C, S), weights)

    new, both, near_new, *arguments = first_step(table, thickness, wind_u, wind_v, tracers)
    both = [send(both, s=s, t=0) for s in away]
    inner, near, near_rest = inner_step(table, new, *arguments)
    group = with_others_of_chip(inner)
    near = [near] + [send(near, s=s, t=0) for s in away]
    near_rest = [near_rest] + [send(near_rest, s=s, t=0) for s in away]
    parted = [part(each, (L, R, N), [near[0]]) for each in both]
    near_new = [near_new] + [each[1] for each in parted]
    others = other_chips((C, S), [a for each in parted for a in with_others_of_chip(each[0])])
    tracer_fields = [(0, 1 + c) for c in range(T)]
    away_parts = remap(group, [group], others, tracer_fields, away, near_rows(R)[1])
    arrived = sent(away_parts)

    last, leading = edge_rows(
        thickness, wind_u, wind_v, tracers, [away_parts[0], *near[1:2], *near_rest[1:2]]
    )
    up = lax.ppermute(last, "lat", northward)
    down = lax.ppermute(leading, "lat", southward)
    u, v, edge = second_step(table, lat_rows, thickness, wind_u, wind_v, tracers, up, down, cutoff)
    edges = [edge] + [send(edge, s=s, t=0) for s in away]
    winds = [with_others_of_chip(u), with_others_of_chip(v)]
    tracers_own, thick_inner = remap(group, [group], others, tracer_fields, (0,), (0, 0), with_thickness=True, wait=[edge])
    winds_own, *winds_away = remap(
        group, winds, others, [(0, 0), (1, 0)], range(C), (1, 1), wait=[tracers_own, *arrived[:1]]
    )
    winds_arrived = sent(winds_away)
    near_new, near, near_rest, edges = (
        [a for own in sources for a in with_others_of_chip(own)] for sources in (near_new, near, near_rest, edges)
    )
    edge_out, thick_edge, near_out = remap_edges(
        (C, S), weights, edges, near_new, near, near_rest, wait=winds_away[:1]
    )

    tracers_out, thickness_out, token = finish_tracers(
        tracers_own, near_out, edge_out, thick_inner, thick_edge, arrived
    )
    u_out, v_out = finish_winds(winds_own, winds_arrived, edge_out, [token])
    return thickness_out, u_out, v_out, tracers_out


def solution(mesh):
    placed = (
        P(("member", "lev", "sub"), "lat", None),
        P(("member", "lev", "sub"), "lat", None),
        P(("member", "lev", "sub"), "lat", None),
        P("member", ("lev", "sub"), "lat", None),
        P(),
        P("lat"),
    )
    return jax.shard_map(
        per_device,
        mesh=mesh,
        in_specs=placed,
        out_specs=(
            P(("member", "lev", "sub"), "lat", None),
            P(("member", "lev", "sub"), "lat", None),
            P(("member", "lev", "sub"), "lat", None),
            P("member", ("lev", "sub"), "lat", None),
        ),
        check_vma=False,
    )
```

```python
import functools

import jax
import jax.numpy as jnp
import ml_dtypes
import numpy as np
from jax import lax
from jax.experimental import pallas as pl
from jax.experimental.pallas import tpu as pltpu
from jax.sharding import PartitionSpec as P

LANES = 128
VMEM = pl.BlockSpec(memory_space=pltpu.VMEM)


def params():
    return pltpu.CompilerParams(vmem_limit_bytes=16 * 1024 * 1024)


def cost(flops, bytes_accessed):
    return pl.CostEstimate(flops=int(flops), bytes_accessed=int(bytes_accessed), transcendentals=0)


def after(arrays):
    return [pl.BlockSpec(memory_space=pl.ANY)] * len(arrays)


def near_rows(rows):
    return (1, 2, rows - 2), (3, 2)


def geometry_table(lat_rows, band_rows):
    bands = lat_rows // band_rows
    table = np.zeros((bands, band_rows + 8, LANES), np.float32)
    for band in range(bands):
        for j in range(band_rows + 1):
            row = band * band_rows + j
            south = np.sin(row * np.pi / lat_rows) if 0 < row < lat_rows else 0.0
            north = np.sin((row + 1) * np.pi / lat_rows) if row + 1 < lat_rows else 0.0
            table[band, j, 0] = south
            table[band, j, 1] = north
            table[band, j, 2] = 1.0 / np.sin((row + 0.5) * np.pi / lat_rows)
    return table


def east_of(value):
    return pltpu.roll(value, value.shape[1] - 1, 1)


def west_of(value):
    return pltpu.roll(value, 1, 1)


def row_ids(shape):
    return lax.broadcasted_iota(jnp.int32, shape, 0)


def north_of(value, beyond):
    rows = value.shape[0]
    rolled = pltpu.roll(value, rows - 1, 0)
    return rolled if beyond is None else jnp.where(row_ids(value.shape) == rows - 1, beyond, rolled)


def south_of(value, beyond):
    rolled = pltpu.roll(value, 1, 0)
    return rolled if beyond is None else jnp.where(row_ids(value.shape) == 0, beyond, rolled)


def fluxes(geo, thick, u, v, thick_s, v_s, thick_n):
    rows = thick.shape[0]
    east = u * jnp.where(u > 0, thick, east_of(thick))
    north = v * jnp.where(v > 0, thick, north_of(thick, thick_n)) * geo[0:rows, 1:2]
    below = None if v_s is None else v_s * jnp.where(v_s > 0, thick_s, thick[0:1]) * geo[0:1, 0:1]
    return east, north, below


def tracer_change(q, q_s, q_n, thick, u, v, v_s, east, north, below, inverse):
    t_east = east * jnp.where(u > 0, q, east_of(q))
    t_north = north * jnp.where(v > 0, q, north_of(q, q_n))
    t_below = None if v_s is None else below * jnp.where(v_s > 0, q_s, q[0:1])
    change = thick * q - (t_east - west_of(t_east))
    return change - (t_north - south_of(t_north, t_below)) * inverse


def packed_at(rows, levels, width):
    near = len(near_rows(rows)[0])
    size = rows - 2 + levels * near
    for a in range(width // LANES):
        yield a, a * size, [a * size + rows - 2 + k * near for k in range(levels)]


def first_kernel(table_hbm, thick_hbm, u_hbm, v_hbm, tracer_hbm, *refs):
    new_ref, both_ref, near_ref, thick_ref, u_ref, v_ref, tracer_ref, sum_ref, geo_ref, sems = refs
    L, rows, _ = thick_ref.shape
    near, _ = near_rows(rows)
    table_copy = pltpu.make_async_copy(table_hbm.at[lax.axis_index("lat")], geo_ref, sems.at[3, 0])
    table_copy.start()
    pairs = ((thick_hbm, thick_ref), (u_hbm, u_ref), (v_hbm, v_ref))

    def copies(k):
        return [pltpu.make_async_copy(a.at[k], b.at[k], sems.at[i, k]) for i, (a, b) in enumerate(pairs)]

    for k in range(L):
        for copy in copies(k):
            copy.start()
    tracer_copy = pltpu.make_async_copy(tracer_hbm, tracer_ref, sems.at[3, 1])
    tracer_copy.start()
    table_copy.wait()
    geo = geo_ref[...]
    sum_ref[...] = jnp.zeros_like(sum_ref)

    def level(k, carry):
        for copy in copies(k):
            copy.wait()
        thick, u, v = thick_ref[k], u_ref[k], v_ref[k]
        east, north, _ = fluxes(geo, thick, u, v, None, None, None)
        new = thick - (east - west_of(east)) - (north - south_of(north, None)) * geo[0:rows, 2:3]
        new_ref[k] = new
        for j, row in enumerate(near):
            near_ref[0, k, j : j + 1] = new[row : row + 1]
        sum_ref[...] += new
        return carry

    lax.fori_loop(0, L, level, 0)
    for a, at, each in packed_at(rows, L, thick_ref.shape[2]):
        lanes = slice(a * LANES, (a + 1) * LANES)
        both_ref[at : at + rows - 2] = sum_ref[1 : rows - 1, lanes]
        for k in range(L):
            both_ref[each[k] : each[k] + len(near)] = near_ref[0, k, :, lanes]
    tracer_copy.wait()


def first_step(table, thickness, wind_u, wind_v, tracers):
    L, R, N = thickness.shape
    arguments = (thickness, wind_u, wind_v, tracers)
    operands = [pltpu.with_memory_space_constraint(a, pltpu.HBM) for a in (table, *arguments)]
    near = len(near_rows(R)[0])
    shapes = [(L, R, N), ((R - 2 + L * near) * N // LANES, LANES), (1, L, near, N)] + [a.shape for a in arguments]
    return pl.pallas_call(
        first_kernel,
        in_specs=after(operands),
        out_specs=[VMEM] * len(shapes),
        out_shape=[jax.ShapeDtypeStruct(shape, jnp.float32) for shape in shapes],
        scratch_shapes=[
            pltpu.VMEM((R, N), jnp.float32),
            pltpu.VMEM(table.shape[1:], jnp.float32),
            pltpu.SemaphoreType.DMA((4, max(L, 2))),
        ],
        compiler_params=params(),
        cost_estimate=cost(40 * L * R * N, 4 * L * R * N * (7 + 2 * tracers.shape[0])),
        name="first_step",
    )(*operands)


def inner_kernel(table_ref, new_ref, thick_ref, u_ref, v_ref, tracer_ref, out_ref, near_ref, near_rest_ref):
    T, L, rows, _ = tracer_ref.shape
    near, _ = near_rows(rows)
    geo = table_ref[lax.axis_index("lat")]
    inverse = geo[0:rows, 2:3]

    def level(k, carry):
        thick, u, v, new = thick_ref[k], u_ref[k], v_ref[k], new_ref[k]
        east, north, _ = fluxes(geo, thick, u, v, None, None, None)

        out_ref[0, k] = new
        scale = 1.0 / new
        for c in range(T):
            change = tracer_change(
                tracer_ref[c, k], None, None, thick, u, v, None, east, north, None, inverse
            )
            value = change * scale
            out_ref[1 + c, k] = value
            ref, at = (near_ref, c) if c < T // 2 else (near_rest_ref, c - T // 2)
            for j, row in enumerate(near):
                ref[pl.ds((at * L + k) * len(near) + j, 1)] = value[row : row + 1]
        return carry

    lax.fori_loop(0, L, level, 0)


def inner_step(table, new, thickness, wind_u, wind_v, tracers):
    L, R, N = thickness.shape
    T = tracers.shape[0]
    rows = lambda n: jax.ShapeDtypeStruct((n * L * len(near_rows(R)[0]), N), jnp.float32)
    shape = lambda n, rows: jax.ShapeDtypeStruct((n, L, rows, N), jnp.float32)
    return pl.pallas_call(
        inner_kernel,
        in_specs=[VMEM] * 6,
        out_specs=[VMEM] * 3,
        out_shape=[shape(1 + T, R), rows(T // 2), rows(T - T // 2)],
        compiler_params=params(),
        cost_estimate=cost(130 * L * R * N, 4 * L * R * N * (8 + 2 * T)),
        name="inner_step",
    )(table, new, thickness, wind_u, wind_v, tracers)


def filter_tables(N):
    A = N // LANES
    b = np.arange(LANES)[:, None]
    p = np.arange(LANES)[None, :]
    tables = []
    for q in range(A // 2 + 1):
        angle = 2.0 * np.pi * ((b * (A * p + q)) % N) / N
        c, s = np.cos(angle), np.sin(angle)
        tables.append(np.block([[c, -s], [s, c]]))
    table = np.stack(tables)
    high = table.astype(np.float32).astype(ml_dtypes.bfloat16)
    low = (table - high.astype(np.float64)).astype(np.float32).astype(ml_dtypes.bfloat16)
    return high, low


def split(value):
    high = value.astype(jnp.bfloat16)
    return high, (value - high.astype(jnp.float32)).astype(jnp.bfloat16)


def product(value, high, low, transposed):
    dims = (((1,), (1 if transposed else 0,)), ((), ()))
    dot = lambda x, y: lax.dot_general(x, y, dims, preferred_element_type=jnp.float32)
    v_high, v_low = split(value)
    return dot(v_high, high) + (dot(v_high, low) + dot(v_low, high))


def filter_rows(x, cutoff, high_ref, low_ref):
    A = len(x)
    N = A * LANES
    half = A // 2
    even = [x[a] + x[A - a] for a in range(1, half + 1)]
    odd = [x[a] - x[A - a] for a in range(1, half + 1)]
    angle = lambda q, a: 2.0 * np.pi * ((q * a) % A) / A
    p = lax.broadcasted_iota(jnp.int32, cutoff.shape, 1)
    real, imag = [], []
    for q in range(half + 1):
        re = x[0]
        for a in range(1, half + 1):
            re = re + (even[a - 1] if q == 0 else float(np.cos(angle(q, a))) * even[a - 1])
        if q == 0:
            high, low = high_ref[0, 0:LANES], low_ref[0, 0:LANES]
            spectrum = product(re, high, low, False)
        else:
            high, low = high_ref[q], low_ref[q]
            im = -float(np.sin(angle(q, 1))) * odd[0]
            for a in range(2, half + 1):
                im = im - float(np.sin(angle(q, a))) * odd[a - 1]
            spectrum = product(jnp.concatenate([re, im], axis=1), high, low, False)
        mode = A * p + q
        factor = 1.0 / N if q == 0 else 2.0 / N
        kept = jnp.where(jnp.minimum(mode, N - mode) <= cutoff, factor, 0.0)
        back = product(spectrum * jnp.concatenate([kept, kept], axis=1), high, low, True)
        real.append(back[:, :LANES])
        imag.append(back[:, LANES:])
    out = [None] * A
    out[0] = functools.reduce(jnp.add, real)
    for a in range(1, half + 1):
        even_part, odd_part = real[0], None
        for q in range(1, half + 1):
            even_part = even_part + float(np.cos(angle(q, a))) * real[q]
            term = float(np.sin(angle(q, a))) * imag[q]
            odd_part = term if odd_part is None else odd_part + term
        out[a] = even_part - odd_part
        out[A - a] = even_part + odd_part
    return out


def second_kernel(
    lat_rows, table_ref, thick_ref, u_ref, v_ref, tracer_ref, up_ref, down_ref, cutoff_ref, high_ref, low_ref, *refs
):
    *wind_refs, edge_ref, new_wind = refs
    k = pl.program_id(0)
    _, L, rows, width = new_wind.shape
    band = lax.axis_index("lat")
    geo = table_ref[band]
    thick, u, v = thick_ref[0], u_ref[0], v_ref[0]
    thick_s, v_s = up_ref[0, 0], up_ref[1, 0]
    thick_n, thick_nn, u_n, v_n = (down_ref[i, 0] for i in range(4))
    east, north, below = fluxes(geo, thick, u, v, thick_s, v_s, thick_n)
    inverse = geo[0:rows, 2:3]
    new = thick - (east - west_of(east)) - (north - south_of(north, below)) * inverse
    east_n = u_n * jnp.where(u_n > 0, thick_n, east_of(thick_n))
    north_n = v_n * jnp.where(v_n > 0, thick_n, thick_nn) * geo[rows : rows + 1, 1:2]
    new_n = (
        thick_n
        - (east_n - west_of(east_n))
        - (north_n - north[rows - 1 : rows]) * geo[rows : rows + 1, 2:3]
    )
    new_wind[0, k] = u - 0.05 * (east_of(new) - new)
    inside = band * rows + row_ids(new.shape) < lat_rows - 1
    new_wind[1, k] = jnp.where(inside, v - 0.05 * (north_of(new, new_n) - new), 0.0)

    def store_edges(field, level, value):
        edge_ref[field, level, 0:1] = value[0:1]
        edge_ref[field, level, 1:2] = value[rows - 1 : rows]

    store_edges(0, k, new)
    scale = 1.0 / new
    for c in range(tracer_ref.shape[0]):
        change = tracer_change(
            tracer_ref[c, 0], up_ref[2 + c, 0], down_ref[4 + c, 0], thick, u, v, v_s, east, north, below, inverse
        )
        store_edges(3 + c, k, change * scale)

    @pl.when(k == L - 1)
    def _():
        pieces = [
            new_wind[:, :, :, a * LANES : (a + 1) * LANES].reshape(2 * L * rows, LANES) for a in range(width // LANES)
        ]
        cutoff = jnp.broadcast_to(cutoff_ref[...][None], (2 * L, rows, LANES)).reshape(2 * L * rows, LANES)
        for a, piece in enumerate(filter_rows(pieces, cutoff, high_ref, low_ref)):
            piece = piece.reshape(2, L, rows, LANES)
            for f in range(2):
                wind_refs[f][0, :, :, a * LANES : (a + 1) * LANES] = piece[f]
        for f in range(2):
            for level in range(L):
                store_edges(1 + f, level, wind_refs[f][0, level])


def second_step(table, lat_rows, thickness, wind_u, wind_v, tracers, up, down, cutoff):
    L, R, N = thickness.shape
    T = tracers.shape[0]
    high, low = filter_tables(N)
    level = pl.BlockSpec((1, R, N), lambda k: (k, 0, 0))
    some = lambda n, rows: pl.BlockSpec((n, 1, rows, N), lambda k: (0, k, 0, 0))
    whole = lambda shape: pl.BlockSpec(shape, lambda k: (0,) * len(shape))
    return pl.pallas_call(
        functools.partial(second_kernel, lat_rows),
        grid=(L,),
        in_specs=[whole(table.shape), level, level, level, some(T, R), some(2 + T, 1), some(4 + T, 1)]
        + [whole((R, LANES)), whole(high.shape), whole(low.shape)],
        out_specs=[whole((1, L, R, N)), whole((1, L, R, N)), whole((3 + T, L, 2, N))],
        out_shape=[
            jax.ShapeDtypeStruct((1, L, R, N), jnp.float32),
            jax.ShapeDtypeStruct((1, L, R, N), jnp.float32),
            jax.ShapeDtypeStruct((3 + T, L, 2, N), jnp.float32),
        ],
        scratch_shapes=[pltpu.VMEM((2, L, R, N), jnp.float32)],
        compiler_params=params(),
        cost_estimate=cost(12 * 2 * L * R * high.size, 4 * L * R * N * (8 + T)),
        name="second_step",
    )(
        table, thickness, wind_u, wind_v, tracers, up, down,
        jnp.broadcast_to(cutoff[:, None], (R, LANES)), jnp.asarray(high), jnp.asarray(low),
    )


def part_kernel(both_ref, *refs):
    sum_ref, near_ref = refs[-2:]
    rows, width = sum_ref.shape
    _, L, near, _ = near_ref.shape
    sum_ref[...] = jnp.zeros_like(sum_ref)
    for a, at, each in packed_at(rows, L, width):
        lanes = slice(a * LANES, (a + 1) * LANES)
        sum_ref[1 : rows - 1, lanes] = both_ref[at : at + rows - 2]
        for k in range(L):
            near_ref[0, k, :, lanes] = both_ref[each[k] : each[k] + near]


def part(both, shape, wait):
    L, R, N = shape
    return pl.pallas_call(
        part_kernel,
        in_specs=[VMEM] + after(wait),
        out_specs=[VMEM] * 2,
        out_shape=[
            jax.ShapeDtypeStruct((R, N), jnp.float32),
            jax.ShapeDtypeStruct((1, L, len(near_rows(R)[0]), N), jnp.float32),
        ],
        compiler_params=params(),
        cost_estimate=cost(1e11, 1e9),
        name="part",
    )(both, *wait)


def mass_kernel(C, S, *refs):
    other_refs, (base_ref, mass_ref) = refs[: (C - 1) * S], refs[(C - 1) * S :]
    lev = lax.axis_index("lev")
    others_mass, base = None, None
    for s in range(1, C):
        other = functools.reduce(jnp.add, [ref[...] for ref in other_refs[(s - 1) * S : s * S]])
        below = jnp.where(lev >= s, other, 0.0)
        others_mass = other if others_mass is None else others_mass + other
        base = below if base is None else base + below
    base_ref[...] = base
    mass_ref[...] = others_mass


def other_chips(counts, others):
    return pl.pallas_call(
        functools.partial(mass_kernel, *counts),
        in_specs=[VMEM] * len(others),
        out_specs=[VMEM] * 2,
        out_shape=[jax.ShapeDtypeStruct(others[0].shape, jnp.float32)] * 2,
        compiler_params=params(),
        cost_estimate=cost(1, 1),
        name="other_chips",
    )(*others)


def add_weights(weight_ref, sum_ref):
    total = jnp.zeros(weight_ref.shape[1:], jnp.float32)
    for k in range(weight_ref.shape[0]):
        sum_ref[k] = total
        total = total + weight_ref[k]
    sum_ref[weight_ref.shape[0]] = total
    return total


def source_levels(place, counts, thick, others):
    C, S = counts
    lev, sub = place
    spot = [lax.rem(lev - g // S + C, C) * S + lax.rem(sub - g % S + S, S) for g in range(len(thick))]
    group = [functools.reduce(jnp.add, levels) for levels in thick]
    mass = functools.reduce(jnp.add, group)
    base = jnp.zeros_like(mass)
    if others:
        base, mass = others[0], mass + others[1]
    sources = []
    for g, levels in enumerate(thick):
        low = base
        for other in range(len(thick)):
            if other != g:
                low = low + jnp.where(spot[other] < spot[g], group[other], 0.0)
        for m, value in enumerate(levels):
            sources.append((g, m, low, value))
            low = low + value
    return mass, sources


def covered(top, sources):
    return [jnp.minimum(jnp.maximum(top - low, 0.0), value) for _, _, low, value in sources]


def level_of(ref, index):
    return lambda m, at, columns: ref[index, m, at, columns]


def packed_level_of(ref, index, L, rows):
    return lambda m, at, columns: ref[(index * L + m) * rows : (index * L + m + 1) * rows, columns]


def remap_rows(weight_ref, sum_ref, counts, steps, thick_refs, field_refs, other_refs, store):
    C, S = counts
    _, L, R, N = thick_refs[0].shape
    rows = min(R, 8)
    place = lev, sub = lax.axis_index("lev"), lax.axis_index("sub")
    firsts = [(lax.rem(lev + s, C) * S + sub) * L for s in steps]
    weight_sum = add_weights(weight_ref, sum_ref)[0:rows]

    def tile(at, columns):
        thick = [[ref[0, m, at, columns] for m in range(L)] for ref in thick_refs]
        others = [ref[at, columns] for ref in other_refs]
        mass, sources = source_levels(place, counts, thick, others)
        unit = mass / weight_sum
        for index, s in enumerate(steps):
            below = covered(unit * sum_ref[firsts[index], 0:rows], sources)
            for i in range(L):
                upto = covered(unit * sum_ref[firsts[index] + i + 1, 0:rows], sources)
                part = [a - b for a, b in zip(upto, below)]
                below = upto
                target = unit * weight_ref[firsts[index] + i, 0:rows]
                scale = 1.0 / target
                means = []
                for refs in field_refs:
                    terms = [refs[g](m, at, columns) * w for (g, m, _, _), w in zip(sources, part)]
                    means.append(functools.reduce(jnp.add, terms) * scale)
                store(s, i, at, columns, target, means)

    for r in range(0, R, rows):

        def body(c, carry):
            tile(slice(r, r + rows), pl.ds(pl.multiple_of(c * LANES, LANES), LANES))
            return carry

        lax.fori_loop(0, N // LANES, body, 0)


def inner_part(at, margin, rows):
    return max(at.start, margin[0]), min(at.stop, rows - margin[1])


def remap_kernel(counts, steps, fields, margin, cut, with_thickness, sizes, weight_ref, *refs):
    *refs, sum_ref = refs
    C, S = counts
    thick_refs, refs = refs[:S], refs[S:]
    bundles = []
    for _ in range(sizes[0]):
        bundles.append(refs[:S])
        refs = refs[S:]
    other_refs, out_refs = refs[:2], refs[len(refs) - sum(2 if cut and s > 0 else 1 for s in steps) - with_thickness :]
    _, L, R, _ = thick_refs[0].shape
    thick_out_ref = out_refs[-1]
    field_refs = [[level_of(ref, index) for ref in bundles[which]] for which, index in fields]

    def store(s, i, at, columns, target, means):
        at_out = sum(2 if cut and s > 0 else 1 for s in steps[: steps.index(s)])
        if with_thickness and s == 0:
            thick_out_ref[i, at, columns] = target
        for f, value in enumerate(means):
            if s == 0:
                out_refs[at_out][f, i, at, columns] = value
            else:
                lower, upper = inner_part(at, margin, R)
                group = f * L + i
                late = cut > 0 and group >= cut
                out_ref = out_refs[at_out + late]
                start = (group - cut * late) * (R - sum(margin)) - margin[0]
                out_ref[start + lower : start + upper, columns] = value[lower - at.start : upper - at.start]

    remap_rows(
        weight_ref, sum_ref, counts, steps, thick_refs, field_refs, other_refs, store
    )


def remap_parts(counts, weights, thick, bundles, others, fields, steps, margin, cut=0, with_thickness=False, wait=()):
    C, S = counts
    _, L, R, N = thick[0].shape
    F = len(fields)
    whole = jax.ShapeDtypeStruct((F, L, R, N), jnp.float32)
    inner = [
        jax.ShapeDtypeStruct((n * (R - sum(margin)), N), jnp.float32) for n in ((cut, F * L - cut) if cut else (F * L,))
    ]
    flat = [a for bundle in bundles for a in bundle]
    out_shape = [a for s in steps for a in ([whole] if s == 0 else inner)]
    if with_thickness:
        out_shape.append(jax.ShapeDtypeStruct((L, R, N), jnp.float32))
    return pl.pallas_call(
        functools.partial(remap_kernel, counts, tuple(steps), tuple(fields), margin, cut, with_thickness, (len(bundles),)),
        in_specs=[VMEM] * (1 + len(thick) + len(flat) + len(others)) + after(wait),
        out_specs=[VMEM] * len(out_shape),
        out_shape=out_shape,
        scratch_shapes=[pltpu.VMEM((weights.shape[0] + 1, 8, LANES), jnp.float32)],
        compiler_params=params(),
        cost_estimate=cost(len(steps) * S * L * L * R * N * (5 + 2 * F), 4 * R * N * L * (F + 1) * (S + len(steps))),
        name="remap_parts",
    )(weights, *thick, *flat, *others, *wait)


def remap_edge_kernel(counts, weight_ref, *refs):
    *refs, sum_ref = refs
    edge_refs = refs[: counts[0] * counts[1]]
    edge_out_ref, thick_out_ref = refs[-2:]

    def store(s, i, at, columns, target, means):
        thick_out_ref[i, at, columns] = target
        for f, value in enumerate(means):
            edge_out_ref[f, i, at, columns] = value

    fields = [[level_of(ref, f) for ref in edge_refs] for f in range(1, edge_refs[0].shape[0])]
    remap_rows(weight_ref, sum_ref, counts, (0,), edge_refs, fields, [], store)


def remap_edges(counts, weights, edges, wait=()):
    F, L, R, N = edges[0].shape
    return pl.pallas_call(
        functools.partial(remap_edge_kernel, counts),
        in_specs=[VMEM] * (1 + len(edges)) + after(wait),
        out_specs=[VMEM] * 2,
        out_shape=[
            jax.ShapeDtypeStruct((F - 1, L, R, N), jnp.float32),
            jax.ShapeDtypeStruct((L, R, N), jnp.float32),
        ],
        scratch_shapes=[pltpu.VMEM((weights.shape[0] + 1, 8, LANES), jnp.float32)],
        compiler_params=params(),
        cost_estimate=cost(len(edges) * L * L * R * N * 20, 4 * R * N * L * len(edges) * F),
        name="remap_edges",
    )(weights, *edges, *wait)


def remap_near_kernel(counts, weight_ref, *refs):
    *refs, near_out_ref, sum_ref = refs
    G = counts[0] * counts[1]
    near_refs, bundles = refs[:G], (refs[G : 2 * G], refs[2 * G : 3 * G])
    T, L, R, _ = near_out_ref.shape

    def store(s, i, at, columns, target, means):
        for f, value in enumerate(means):
            near_out_ref[f, i, at, columns] = value

    fields = [[packed_level_of(ref, f % (T // 2), L, R) for ref in bundles[f // (T // 2)]] for f in range(T)]
    remap_rows(weight_ref, sum_ref, counts, (0,), near_refs, fields, [], store)


def remap_near(counts, weights, total, near_new, near, near_rest, wait=()):
    _, L, R, N = near_new[0].shape
    operands = [*near_new, *near, *near_rest]
    return pl.pallas_call(
        functools.partial(remap_near_kernel, counts),
        in_specs=[VMEM] * (1 + len(operands)) + after(wait),
        out_specs=VMEM,
        out_shape=jax.ShapeDtypeStruct((total, L, R, N), jnp.float32),
        scratch_shapes=[pltpu.VMEM((weights.shape[0] + 1, 8, LANES), jnp.float32)],
        compiler_params=params(),
        cost_estimate=cost(len(near) * L * L * R * N * 20, 4 * R * N * L * len(near) * (1 + total)),
        name="remap_near",
    )(weights, *operands, *wait)


def finish_kernel(margin, own_ref, near_ref, edge_ref, thick_ref, thick_edge_ref, *refs):
    *arrived_refs, out_ref, thick_out_ref, token_ref = refs
    token_ref[...] = jnp.zeros_like(token_ref)
    T, L, R, _ = out_ref.shape
    thick_out_ref[...] = thick_ref[...]
    for i in range(L):
        for row, j in ((0, 0), (R - 1, 1)):
            thick_out_ref[i, row : row + 1] = thick_edge_ref[i, j : j + 1]
    for f in range(T):
        for i in range(L):
            start, first, end = (f * L + i) * (R - sum(margin)), margin[0], R - margin[1]
            total = own_ref[f, i, first:end]
            for ref in arrived_refs:
                total = total + ref[start : start + end - first]
            out_ref[f, i, first:end] = total
            for row, j in ((0, 0), (R - 1, 1)):
                out_ref[f, i, row : row + 1] = edge_ref[2 + f, i, j : j + 1]
            for j, row in enumerate(near_rows(R)[0]):
                out_ref[f, i, row : row + 1] = near_ref[f, i, j : j + 1]


def finish_tracers(own, near, edge, thick, thick_edge, arrived):
    return pl.pallas_call(
        functools.partial(finish_kernel, near_rows(own.shape[2])[1]),
        in_specs=[VMEM] * (5 + len(arrived)),
        out_specs=[VMEM] * 3,
        out_shape=[
            jax.ShapeDtypeStruct(own.shape, jnp.float32),
            jax.ShapeDtypeStruct(thick.shape, jnp.float32),
            jax.ShapeDtypeStruct((8, LANES), jnp.float32),
        ],
        compiler_params=params(),
        cost_estimate=cost(2 * own.size, 12 * own.size),
        name="finish_tracers",
    )(own, near, edge, thick, thick_edge, *arrived)


def finish_level(own_ref, edge_ref, arrived_refs, result, f, i, start):
    R = own_ref.shape[2]
    total = own_ref[f, i, 1 : R - 1]
    for ref in arrived_refs:
        total = total + ref[start : start + R - 2]
    result[1 : R - 1] = total
    result[0:1] = edge_ref[f, i, 0:1]
    result[R - 1 : R] = edge_ref[f, i, 1:2]


def finish_winds_kernel(count, cut, own_ref, edge_ref, *refs):
    arrived_refs, (*out_refs, result_ref, sems) = refs[:count], refs[len(refs) - 4 :]
    _, L, R, _ = own_ref.shape
    copies = []
    for f, out_ref in enumerate(out_refs):
        for i in range(L):
            if f * L + i < cut:
                finish_level(own_ref, edge_ref, arrived_refs, result_ref.at[f, i], f, i, (f * L + i) * (R - 2))
                copies.append(pltpu.make_async_copy(result_ref.at[f, i], out_ref.at[i], sems.at[f, i]))
                copies[-1].start()
    for copy in copies:
        copy.wait()


def finish_winds(own, arrived, edge, cut, wait):
    F, L = own.shape[:2]
    return pl.pallas_call(
        functools.partial(finish_winds_kernel, len(arrived), cut),
        in_specs=[VMEM] * (2 + len(arrived)) + after(wait),
        out_specs=[pl.BlockSpec(memory_space=pl.ANY)] * F,
        out_shape=[jax.ShapeDtypeStruct(own.shape[1:], jnp.float32)] * F,
        scratch_shapes=[pltpu.VMEM(own.shape, jnp.float32), pltpu.SemaphoreType.DMA((F, L))],
        compiler_params=params(),
        cost_estimate=cost(1, 1),
        name="finish_winds",
    )(own, edge, *arrived, *wait)


def finish_late_kernel(count, cut, own_ref, edge_ref, *refs):
    arrived_refs, (out_ref, result_ref, sems) = refs[:count], refs[len(refs) - 3 :]
    F, L, R, _ = own_ref.shape
    copies = []
    for g in range(cut, F * L):
        i = g % L
        finish_level(own_ref, edge_ref, arrived_refs, result_ref.at[i], F - 1, i, (g - cut) * (R - 2))
        copies.append(pltpu.make_async_copy(result_ref.at[i], out_ref.at[i], sems.at[i]))
        copies[-1].start()
    for copy in copies:
        copy.wait()


def finish_late(own, arrived, edge, cut, out):
    L = own.shape[1]
    return pl.pallas_call(
        functools.partial(finish_late_kernel, len(arrived), cut),
        in_specs=[VMEM] * (2 + len(arrived)) + after([out]),
        out_specs=pl.BlockSpec(memory_space=pl.ANY),
        out_shape=jax.ShapeDtypeStruct(out.shape, jnp.float32),
        input_output_aliases={2 + len(arrived): 0},
        scratch_shapes=[pltpu.VMEM(out.shape, jnp.float32), pltpu.SemaphoreType.DMA((L,))],
        compiler_params=params(),
        cost_estimate=cost(1, 1),
        name="finish_late",
    )(own, edge, *arrived, out)


def edge_kernel(thick_hbm, u_hbm, v_hbm, tracer_hbm, *refs):
    last_ref, leading_ref, top_ref, low_ref, tracer_ref, sems = refs[-6:]
    T, L, R, _ = tracer_hbm.shape
    top = pl.ds(R - 8, 8)
    copies = [
        pltpu.make_async_copy(thick_hbm.at[:, top], top_ref.at[0], sems.at[0]),
        pltpu.make_async_copy(v_hbm.at[:, top], top_ref.at[1], sems.at[1]),
        pltpu.make_async_copy(thick_hbm.at[:, pl.ds(0, 8)], low_ref.at[0], sems.at[2]),
        pltpu.make_async_copy(u_hbm.at[:, pl.ds(0, 8)], low_ref.at[1], sems.at[3]),
        pltpu.make_async_copy(v_hbm.at[:, pl.ds(0, 8)], low_ref.at[2], sems.at[4]),
        pltpu.make_async_copy(tracer_hbm.at[:, :, top], tracer_ref.at[0], sems.at[5]),
        pltpu.make_async_copy(tracer_hbm.at[:, :, pl.ds(0, 8)], tracer_ref.at[1], sems.at[6]),
    ]
    for copy in copies:
        copy.start()
    for copy in copies:
        copy.wait()
    last_ref[0:2] = top_ref[:, :, 7:8]
    last_ref[2 : 2 + T] = tracer_ref[0, :, :, 7:8]
    leading_ref[0] = low_ref[0, :, 0:1]
    leading_ref[1] = low_ref[0, :, 1:2]
    leading_ref[2:4] = low_ref[1:3, :, 0:1]
    leading_ref[4 : 4 + T] = tracer_ref[1, :, :, 0:1]


def edge_rows(thickness, wind_u, wind_v, tracers, wait):
    L, R, N = thickness.shape
    T = tracers.shape[0]
    operands = [pltpu.with_memory_space_constraint(a, pltpu.HBM) for a in (thickness, wind_u, wind_v, tracers)]
    return pl.pallas_call(
        edge_kernel,
        in_specs=after(operands) + after(wait),
        out_specs=[VMEM] * 2,
        out_shape=[
            jax.ShapeDtypeStruct((2 + T, L, 1, N), jnp.float32),
            jax.ShapeDtypeStruct((4 + T, L, 1, N), jnp.float32),
        ],
        scratch_shapes=[
            pltpu.VMEM((2, L, 8, N), jnp.float32),
            pltpu.VMEM((3, L, 8, N), jnp.float32),
            pltpu.VMEM((2, T, L, 8, N), jnp.float32),
            pltpu.SemaphoreType.DMA((7,)),
        ],
        compiler_params=params(),
        cost_estimate=cost(1e10, 1e9),
        name="edge_rows",
    )(*operands, *wait)


def shifted(value, lev_count, sub_count, s, t):
    if t == 0:
        return lax.ppermute(value, "lev", [(i, (i + s) % lev_count) for i in range(lev_count)])
    if s == 0:
        return lax.ppermute(value, "sub", [(i, (i + t) % sub_count) for i in range(sub_count)])
    pairs = [
        (i * sub_count + j, (i + s) % lev_count * sub_count + (j + t) % sub_count)
        for i in range(lev_count)
        for j in range(sub_count)
    ]
    return lax.ppermute(value, ("lev", "sub"), pairs)


def per_device(thickness, wind_u, wind_v, tracers, level_weights, cutoff):
    L, R, N = thickness.shape
    lat_count = lax.axis_size("lat")
    C, S = lax.axis_size("lev"), lax.axis_size("sub")
    lat_rows = R * lat_count
    send = functools.partial(shifted, lev_count=C, sub_count=S)

    T = tracers.shape[0]
    northward = [(i, i + 1) for i in range(lat_count - 1)]
    southward = [(j, i) for i, j in northward]
    table = jnp.asarray(geometry_table(lat_rows, R))
    weights = jnp.broadcast_to(level_weights[:, None, None], (level_weights.shape[0], 8, LANES))
    away = range(1, C)

    def with_others_of_chip(own):
        return [own] + [send(own, s=0, t=t) for t in range(1, S)]

    def sent(parts):
        return [send(part, s=s, t=0) for s, part in zip(away, parts)]

    remap = functools.partial(remap_parts, (C, S), weights)

    new, both, near_new, *arguments = first_step(table, thickness, wind_u, wind_v, tracers)
    both = [send(both, s=s, t=0) for s in away]
    inner, near, near_rest = inner_step(table, new, *arguments)
    group = with_others_of_chip(inner)
    near = [near] + [send(near, s=s, t=0) for s in away]
    near_rest = [near_rest] + [send(near_rest, s=s, t=0) for s in away]
    parted = [part(each, (L, R, N), [near[0]]) for each in both]
    near_new = [near_new] + [each[1] for each in parted]
    others = other_chips((C, S), [a for each in parted for a in with_others_of_chip(each[0])])
    tracer_fields = [(0, 1 + c) for c in range(T)]
    away_parts = remap(group, [group], others, tracer_fields, away, near_rows(R)[1])
    arrived = sent(away_parts)

    last, leading = edge_rows(
        thickness, wind_u, wind_v, tracers, [away_parts[0], *near[1:2], *near_rest[1:2]]
    )
    up = lax.ppermute(last, "lat", northward)
    down = lax.ppermute(leading, "lat", southward)
    u, v, edge = second_step(table, lat_rows, thickness, wind_u, wind_v, tracers, up, down, cutoff)
    edges = [edge] + [send(edge, s=s, t=0) for s in away]
    winds = [with_others_of_chip(u), with_others_of_chip(v)]
    cut = 2 * L - 3
    tracers_own, thick_inner = remap(group, [group], others, tracer_fields, (0,), (0, 0), with_thickness=True, wait=[edge])
    near_new, near, near_rest = (
        [a for own in sources for a in with_others_of_chip(own)] for sources in (near_new, near, near_rest)
    )
    near_out = remap_near((C, S), weights, T, near_new, near, near_rest, wait=[tracers_own])
    winds_own, *winds_away = remap(
        group, winds, others, [(0, 0), (1, 0)], range(C), (1, 1), cut=cut, wait=[near_out, *arrived[:1]]
    )
    winds_arrived, late_arrived = sent(winds_away[0::2]), sent(winds_away[1::2])
    edges = [a for own in edges for a in with_others_of_chip(own)]
    edge_out, thick_edge = remap_edges((C, S), weights, edges, wait=winds_away[:1])

    tracers_out, thickness_out, token = finish_tracers(
        tracers_own, near_out, edge_out, thick_inner, thick_edge, arrived
    )
    u_out, v_out = finish_winds(winds_own, winds_arrived, edge_out, cut, [token])
    v_out = finish_late(winds_own, late_arrived, edge_out, cut, v_out)
    return thickness_out, u_out, v_out, tracers_out


def solution(mesh):
    placed = (
        P(("member", "lev", "sub"), "lat", None),
        P(("member", "lev", "sub"), "lat", None),
        P(("member", "lev", "sub"), "lat", None),
        P("member", ("lev", "sub"), "lat", None),
        P(),
        P("lat"),
    )
    return jax.shard_map(
        per_device,
        mesh=mesh,
        in_specs=placed,
        out_specs=(
            P(("member", "lev", "sub"), "lat", None),
            P(("member", "lev", "sub"), "lat", None),
            P(("member", "lev", "sub"), "lat", None),
            P("member", ("lev", "sub"), "lat", None),
        ),
        check_vma=False,
    )
```

```python
import functools

import jax
import jax.numpy as jnp
import ml_dtypes
import numpy as np
from jax import lax
from jax.experimental import pallas as pl
from jax.experimental.pallas import tpu as pltpu
from jax.sharding import PartitionSpec as P

LANES = 128
VMEM = pl.BlockSpec(memory_space=pltpu.VMEM)


def params():
    return pltpu.CompilerParams(vmem_limit_bytes=16 * 1024 * 1024)


def cost(flops, bytes_accessed):
    return pl.CostEstimate(flops=int(flops), bytes_accessed=int(bytes_accessed), transcendentals=0)


def after(arrays):
    return [pl.BlockSpec(memory_space=pl.ANY)] * len(arrays)


def near_rows(rows):
    return (1, 2, rows - 2), (3, 2)


def geometry_table(lat_rows, band_rows):
    bands = lat_rows // band_rows
    table = np.zeros((bands, band_rows + 8, LANES), np.float32)
    for band in range(bands):
        for j in range(band_rows + 1):
            row = band * band_rows + j
            south = np.sin(row * np.pi / lat_rows) if 0 < row < lat_rows else 0.0
            north = np.sin((row + 1) * np.pi / lat_rows) if row + 1 < lat_rows else 0.0
            table[band, j, 0] = south
            table[band, j, 1] = north
            table[band, j, 2] = 1.0 / np.sin((row + 0.5) * np.pi / lat_rows)
    return table


def east_of(value):
    return pltpu.roll(value, value.shape[1] - 1, 1)


def west_of(value):
    return pltpu.roll(value, 1, 1)


def row_ids(shape):
    return lax.broadcasted_iota(jnp.int32, shape, 0)


def north_of(value, beyond):
    rows = value.shape[0]
    rolled = pltpu.roll(value, rows - 1, 0)
    return rolled if beyond is None else jnp.where(row_ids(value.shape) == rows - 1, beyond, rolled)


def south_of(value, beyond):
    rolled = pltpu.roll(value, 1, 0)
    return rolled if beyond is None else jnp.where(row_ids(value.shape) == 0, beyond, rolled)


def fluxes(geo, thick, u, v, thick_s, v_s, thick_n):
    rows = thick.shape[0]
    east = u * jnp.where(u > 0, thick, east_of(thick))
    north = v * jnp.where(v > 0, thick, north_of(thick, thick_n)) * geo[0:rows, 1:2]
    below = None if v_s is None else v_s * jnp.where(v_s > 0, thick_s, thick[0:1]) * geo[0:1, 0:1]
    return east, north, below


def tracer_change(q, q_s, q_n, thick, u, v, v_s, east, north, below, inverse):
    t_east = east * jnp.where(u > 0, q, east_of(q))
    t_north = north * jnp.where(v > 0, q, north_of(q, q_n))
    t_below = None if v_s is None else below * jnp.where(v_s > 0, q_s, q[0:1])
    change = thick * q - (t_east - west_of(t_east))
    return change - (t_north - south_of(t_north, t_below)) * inverse


def packed_at(rows, levels, width):
    near = len(near_rows(rows)[0])
    size = rows - 2 + levels * near
    for a in range(width // LANES):
        yield a, a * size, [a * size + rows - 2 + k * near for k in range(levels)]


def first_kernel(table_hbm, thick_hbm, u_hbm, v_hbm, tracer_hbm, *refs):
    new_ref, both_ref, near_ref, thick_ref, u_ref, v_ref, tracer_ref, sum_ref, geo_ref, sems = refs
    L, rows, _ = thick_ref.shape
    near, _ = near_rows(rows)
    table_copy = pltpu.make_async_copy(table_hbm.at[lax.axis_index("lat")], geo_ref, sems.at[3, 0])
    table_copy.start()
    pairs = ((thick_hbm, thick_ref), (u_hbm, u_ref), (v_hbm, v_ref))

    def copies(k):
        return [pltpu.make_async_copy(a.at[k], b.at[k], sems.at[i, k]) for i, (a, b) in enumerate(pairs)]

    for k in range(L):
        for copy in copies(k):
            copy.start()
    tracer_copy = pltpu.make_async_copy(tracer_hbm, tracer_ref, sems.at[3, 1])
    tracer_copy.start()
    table_copy.wait()
    geo = geo_ref[...]
    sum_ref[...] = jnp.zeros_like(sum_ref)

    def level(k, carry):
        for copy in copies(k):
            copy.wait()
        thick, u, v = thick_ref[k], u_ref[k], v_ref[k]
        east, north, _ = fluxes(geo, thick, u, v, None, None, None)
        new = thick - (east - west_of(east)) - (north - south_of(north, None)) * geo[0:rows, 2:3]
        new_ref[k] = new
        for j, row in enumerate(near):
            near_ref[0, k, j : j + 1] = new[row : row + 1]
        sum_ref[...] += new
        return carry

    lax.fori_loop(0, L, level, 0)
    for a, at, each in packed_at(rows, L, thick_ref.shape[2]):
        lanes = slice(a * LANES, (a + 1) * LANES)
        both_ref[at : at + rows - 2] = sum_ref[1 : rows - 1, lanes]
        for k in range(L):
            both_ref[each[k] : each[k] + len(near)] = near_ref[0, k, :, lanes]
    tracer_copy.wait()


def first_step(table, thickness, wind_u, wind_v, tracers):
    L, R, N = thickness.shape
    arguments = (thickness, wind_u, wind_v, tracers)
    operands = [pltpu.with_memory_space_constraint(a, pltpu.HBM) for a in (table, *arguments)]
    near = len(near_rows(R)[0])
    shapes = [(L, R, N), ((R - 2 + L * near) * N // LANES, LANES), (1, L, near, N)] + [a.shape for a in arguments]
    return pl.pallas_call(
        first_kernel,
        in_specs=after(operands),
        out_specs=[VMEM] * len(shapes),
        out_shape=[jax.ShapeDtypeStruct(shape, jnp.float32) for shape in shapes],
        scratch_shapes=[
            pltpu.VMEM((R, N), jnp.float32),
            pltpu.VMEM(table.shape[1:], jnp.float32),
            pltpu.SemaphoreType.DMA((4, max(L, 2))),
        ],
        compiler_params=params(),
        cost_estimate=cost(40 * L * R * N, 4 * L * R * N * (7 + 2 * tracers.shape[0])),
        name="first_step",
    )(*operands)


def inner_kernel(table_ref, new_ref, thick_ref, u_ref, v_ref, tracer_ref, out_ref, near_ref, near_rest_ref):
    T, L, rows, _ = tracer_ref.shape
    near, _ = near_rows(rows)
    geo = table_ref[lax.axis_index("lat")]
    inverse = geo[0:rows, 2:3]

    def level(k, carry):
        thick, u, v, new = thick_ref[k], u_ref[k], v_ref[k], new_ref[k]
        east, north, _ = fluxes(geo, thick, u, v, None, None, None)

        out_ref[0, k] = new
        scale = 1.0 / new
        for c in range(T):
            change = tracer_change(
                tracer_ref[c, k], None, None, thick, u, v, None, east, north, None, inverse
            )
            value = change * scale
            out_ref[1 + c, k] = value
            ref, at = (near_ref, c) if c < T // 2 else (near_rest_ref, c - T // 2)
            for j, row in enumerate(near):
                ref[pl.ds((at * L + k) * len(near) + j, 1)] = value[row : row + 1]
        return carry

    lax.fori_loop(0, L, level, 0)


def inner_step(table, new, thickness, wind_u, wind_v, tracers):
    L, R, N = thickness.shape
    T = tracers.shape[0]
    rows = lambda n: jax.ShapeDtypeStruct((n * L * len(near_rows(R)[0]), N), jnp.float32)
    shape = lambda n, rows: jax.ShapeDtypeStruct((n, L, rows, N), jnp.float32)
    return pl.pallas_call(
        inner_kernel,
        in_specs=[VMEM] * 6,
        out_specs=[VMEM] * 3,
        out_shape=[shape(1 + T, R), rows(T // 2), rows(T - T // 2)],
        compiler_params=params(),
        cost_estimate=cost(130 * L * R * N, 4 * L * R * N * (8 + 2 * T)),
        name="inner_step",
    )(table, new, thickness, wind_u, wind_v, tracers)


def filter_tables(N):
    A = N // LANES
    b = np.arange(LANES)[:, None]
    p = np.arange(LANES)[None, :]
    tables = []
    for q in range(A // 2 + 1):
        angle = 2.0 * np.pi * ((b * (A * p + q)) % N) / N
        c, s = np.cos(angle), np.sin(angle)
        tables.append(np.block([[c, -s], [s, c]]))
    table = np.stack(tables)
    high = table.astype(np.float32).astype(ml_dtypes.bfloat16)
    low = (table - high.astype(np.float64)).astype(np.float32).astype(ml_dtypes.bfloat16)
    return high, low


def split(value):
    high = value.astype(jnp.bfloat16)
    return high, (value - high.astype(jnp.float32)).astype(jnp.bfloat16)


def product(value, high, low, transposed):
    dims = (((1,), (1 if transposed else 0,)), ((), ()))
    dot = lambda x, y: lax.dot_general(x, y, dims, preferred_element_type=jnp.float32)
    v_high, v_low = split(value)
    return dot(v_high, high) + (dot(v_high, low) + dot(v_low, high))


def filter_rows(x, cutoff, high_ref, low_ref):
    A = len(x)
    N = A * LANES
    half = A // 2
    even = [x[a] + x[A - a] for a in range(1, half + 1)]
    odd = [x[a] - x[A - a] for a in range(1, half + 1)]
    angle = lambda q, a: 2.0 * np.pi * ((q * a) % A) / A
    p = lax.broadcasted_iota(jnp.int32, cutoff.shape, 1)
    real, imag = [], []
    for q in range(half + 1):
        re = x[0]
        for a in range(1, half + 1):
            re = re + (even[a - 1] if q == 0 else float(np.cos(angle(q, a))) * even[a - 1])
        if q == 0:
            high, low = high_ref[0, 0:LANES], low_ref[0, 0:LANES]
            spectrum = product(re, high, low, False)
        else:
            high, low = high_ref[q], low_ref[q]
            im = -float(np.sin(angle(q, 1))) * odd[0]
            for a in range(2, half + 1):
                im = im - float(np.sin(angle(q, a))) * odd[a - 1]
            spectrum = product(jnp.concatenate([re, im], axis=1), high, low, False)
        mode = A * p + q
        factor = 1.0 / N if q == 0 else 2.0 / N
        kept = jnp.where(jnp.minimum(mode, N - mode) <= cutoff, factor, 0.0)
        back = product(spectrum * jnp.concatenate([kept, kept], axis=1), high, low, True)
        real.append(back[:, :LANES])
        imag.append(back[:, LANES:])
    out = [None] * A
    out[0] = functools.reduce(jnp.add, real)
    for a in range(1, half + 1):
        even_part, odd_part = real[0], None
        for q in range(1, half + 1):
            even_part = even_part + float(np.cos(angle(q, a))) * real[q]
            term = float(np.sin(angle(q, a))) * imag[q]
            odd_part = term if odd_part is None else odd_part + term
        out[a] = even_part - odd_part
        out[A - a] = even_part + odd_part
    return out


def second_kernel(
    lat_rows, table_ref, thick_ref, u_ref, v_ref, tracer_ref, up_ref, down_ref, cutoff_ref, high_ref, low_ref, *refs
):
    *wind_refs, edge_ref, new_wind = refs
    k = pl.program_id(0)
    _, L, rows, width = new_wind.shape
    band = lax.axis_index("lat")
    geo = table_ref[band]
    thick, u, v = thick_ref[0], u_ref[0], v_ref[0]
    thick_s, v_s = up_ref[0, 0], up_ref[1, 0]
    thick_n, thick_nn, u_n, v_n = (down_ref[i, 0] for i in range(4))
    east, north, below = fluxes(geo, thick, u, v, thick_s, v_s, thick_n)
    inverse = geo[0:rows, 2:3]
    new = thick - (east - west_of(east)) - (north - south_of(north, below)) * inverse
    east_n = u_n * jnp.where(u_n > 0, thick_n, east_of(thick_n))
    north_n = v_n * jnp.where(v_n > 0, thick_n, thick_nn) * geo[rows : rows + 1, 1:2]
    new_n = (
        thick_n
        - (east_n - west_of(east_n))
        - (north_n - north[rows - 1 : rows]) * geo[rows : rows + 1, 2:3]
    )
    new_wind[0, k] = u - 0.05 * (east_of(new) - new)
    inside = band * rows + row_ids(new.shape) < lat_rows - 1
    new_wind[1, k] = jnp.where(inside, v - 0.05 * (north_of(new, new_n) - new), 0.0)

    def store_edges(field, level, value):
        edge_ref[field, level, 0:1] = value[0:1]
        edge_ref[field, level, 1:2] = value[rows - 1 : rows]

    store_edges(0, k, new)
    scale = 1.0 / new
    for c in range(tracer_ref.shape[0]):
        change = tracer_change(
            tracer_ref[c, 0], up_ref[2 + c, 0], down_ref[4 + c, 0], thick, u, v, v_s, east, north, below, inverse
        )
        store_edges(3 + c, k, change * scale)

    @pl.when(k == L - 1)
    def _():
        pieces = [
            new_wind[:, :, :, a * LANES : (a + 1) * LANES].reshape(2 * L * rows, LANES) for a in range(width // LANES)
        ]
        cutoff = jnp.broadcast_to(cutoff_ref[...][None], (2 * L, rows, LANES)).reshape(2 * L * rows, LANES)
        for a, piece in enumerate(filter_rows(pieces, cutoff, high_ref, low_ref)):
            piece = piece.reshape(2, L, rows, LANES)
            for f in range(2):
                wind_refs[f][0, :, :, a * LANES : (a + 1) * LANES] = piece[f]
        for f in range(2):
            for level in range(L):
                store_edges(1 + f, level, wind_refs[f][0, level])


def second_step(table, lat_rows, thickness, wind_u, wind_v, tracers, up, down, cutoff):
    L, R, N = thickness.shape
    T = tracers.shape[0]
    high, low = filter_tables(N)
    level = pl.BlockSpec((1, R, N), lambda k: (k, 0, 0))
    some = lambda n, rows: pl.BlockSpec((n, 1, rows, N), lambda k: (0, k, 0, 0))
    whole = lambda shape: pl.BlockSpec(shape, lambda k: (0,) * len(shape))
    return pl.pallas_call(
        functools.partial(second_kernel, lat_rows),
        grid=(L,),
        in_specs=[whole(table.shape), level, level, level, some(T, R), some(2 + T, 1), some(4 + T, 1)]
        + [whole((R, LANES)), whole(high.shape), whole(low.shape)],
        out_specs=[whole((1, L, R, N)), whole((1, L, R, N)), whole((3 + T, L, 2, N))],
        out_shape=[
            jax.ShapeDtypeStruct((1, L, R, N), jnp.float32),
            jax.ShapeDtypeStruct((1, L, R, N), jnp.float32),
            jax.ShapeDtypeStruct((3 + T, L, 2, N), jnp.float32),
        ],
        scratch_shapes=[pltpu.VMEM((2, L, R, N), jnp.float32)],
        compiler_params=params(),
        cost_estimate=cost(12 * 2 * L * R * high.size, 4 * L * R * N * (8 + T)),
        name="second_step",
    )(
        table, thickness, wind_u, wind_v, tracers, up, down,
        jnp.broadcast_to(cutoff[:, None], (R, LANES)), jnp.asarray(high), jnp.asarray(low),
    )


def part_kernel(both_ref, *refs):
    sum_ref, near_ref = refs[-2:]
    rows, width = sum_ref.shape
    _, L, near, _ = near_ref.shape
    sum_ref[...] = jnp.zeros_like(sum_ref)
    for a, at, each in packed_at(rows, L, width):
        lanes = slice(a * LANES, (a + 1) * LANES)
        sum_ref[1 : rows - 1, lanes] = both_ref[at : at + rows - 2]
        for k in range(L):
            near_ref[0, k, :, lanes] = both_ref[each[k] : each[k] + near]


def part(both, shape, wait):
    L, R, N = shape
    return pl.pallas_call(
        part_kernel,
        in_specs=[VMEM] + after(wait),
        out_specs=[VMEM] * 2,
        out_shape=[
            jax.ShapeDtypeStruct((R, N), jnp.float32),
            jax.ShapeDtypeStruct((1, L, len(near_rows(R)[0]), N), jnp.float32),
        ],
        compiler_params=params(),
        cost_estimate=cost(1e11, 1e9),
        name="part",
    )(both, *wait)


def mass_kernel(C, S, *refs):
    other_refs, (base_ref, mass_ref) = refs[: (C - 1) * S], refs[(C - 1) * S :]
    lev = lax.axis_index("lev")
    others_mass, base = None, None
    for s in range(1, C):
        other = functools.reduce(jnp.add, [ref[...] for ref in other_refs[(s - 1) * S : s * S]])
        below = jnp.where(lev >= s, other, 0.0)
        others_mass = other if others_mass is None else others_mass + other
        base = below if base is None else base + below
    base_ref[...] = base
    mass_ref[...] = others_mass


def other_chips(counts, others):
    return pl.pallas_call(
        functools.partial(mass_kernel, *counts),
        in_specs=[VMEM] * len(others),
        out_specs=[VMEM] * 2,
        out_shape=[jax.ShapeDtypeStruct(others[0].shape, jnp.float32)] * 2,
        compiler_params=params(),
        cost_estimate=cost(1, 1),
        name="other_chips",
    )(*others)


def add_weights(weight_ref, sum_ref):
    total = jnp.zeros(weight_ref.shape[1:], jnp.float32)
    for k in range(weight_ref.shape[0]):
        sum_ref[k] = total
        total = total + weight_ref[k]
    sum_ref[weight_ref.shape[0]] = total
    return total


def source_levels(place, counts, thick, others):
    C, S = counts
    lev, sub = place
    spot = [lax.rem(lev - g // S + C, C) * S + lax.rem(sub - g % S + S, S) for g in range(len(thick))]
    group = [functools.reduce(jnp.add, levels) for levels in thick]
    mass = functools.reduce(jnp.add, group)
    base = jnp.zeros_like(mass)
    if others:
        base, mass = others[0], mass + others[1]
    sources = []
    for g, levels in enumerate(thick):
        low = base
        for other in range(len(thick)):
            if other != g:
                low = low + jnp.where(spot[other] < spot[g], group[other], 0.0)
        for m, value in enumerate(levels):
            sources.append((g, m, low, value))
            low = low + value
    return mass, sources


def covered(top, sources):
    return [jnp.minimum(jnp.maximum(top - low, 0.0), value) for _, _, low, value in sources]


def level_of(ref, index):
    return lambda m, at, columns: ref[index, m, at, columns]


def packed_level_of(ref, index, L, rows):
    return lambda m, at, columns: ref[(index * L + m) * rows : (index * L + m + 1) * rows, columns]


def remap_rows(weight_ref, sum_ref, counts, steps, thick_refs, field_refs, other_refs, store):
    C, S = counts
    _, L, R, N = thick_refs[0].shape
    rows = min(R, 8)
    place = lev, sub = lax.axis_index("lev"), lax.axis_index("sub")
    firsts = [(lax.rem(lev + s, C) * S + sub) * L for s in steps]
    weight_sum = add_weights(weight_ref, sum_ref)[0:rows]

    def tile(at, columns):
        thick = [[ref[0, m, at, columns] for m in range(L)] for ref in thick_refs]
        others = [ref[at, columns] for ref in other_refs]
        mass, sources = source_levels(place, counts, thick, others)
        unit = mass / weight_sum
        for index, s in enumerate(steps):
            below = covered(unit * sum_ref[firsts[index], 0:rows], sources)
            for i in range(L):
                upto = covered(unit * sum_ref[firsts[index] + i + 1, 0:rows], sources)
                part = [a - b for a, b in zip(upto, below)]
                below = upto
                target = unit * weight_ref[firsts[index] + i, 0:rows]
                scale = 1.0 / target
                means = []
                for refs in field_refs:
                    terms = [refs[g](m, at, columns) * w for (g, m, _, _), w in zip(sources, part)]
                    means.append(functools.reduce(jnp.add, terms) * scale)
                store(s, i, at, columns, target, means)

    for r in range(0, R, rows):

        def body(c, carry):
            tile(slice(r, r + rows), pl.ds(pl.multiple_of(c * LANES, LANES), LANES))
            return carry

        lax.fori_loop(0, N // LANES, body, 0)


def inner_part(at, margin, rows):
    return max(at.start, margin[0]), min(at.stop, rows - margin[1])


def remap_kernel(counts, steps, fields, margin, with_thickness, sizes, weight_ref, *refs):
    *refs, sum_ref = refs
    C, S = counts
    thick_refs, refs = refs[:S], refs[S:]
    bundles = []
    for _ in range(sizes[0]):
        bundles.append(refs[:S])
        refs = refs[S:]
    other_refs, out_refs = refs[:2], refs[len(refs) - len(steps) - with_thickness :]
    _, L, R, _ = thick_refs[0].shape
    thick_out_ref = out_refs[-1]
    field_refs = [[level_of(ref, index) for ref in bundles[which]] for which, index in fields]

    def store(s, i, at, columns, target, means):
        out_ref = out_refs[steps.index(s)]
        if with_thickness and s == 0:
            thick_out_ref[i, at, columns] = target
        for f, value in enumerate(means):
            if s == 0:
                out_ref[f, i, at, columns] = value
            else:
                lower, upper = inner_part(at, margin, R)
                start = (f * L + i) * (R - sum(margin)) - margin[0]
                out_ref[start + lower : start + upper, columns] = value[lower - at.start : upper - at.start]

    remap_rows(
        weight_ref, sum_ref, counts, steps, thick_refs, field_refs, other_refs, store
    )


def remap_parts(counts, weights, thick, bundles, others, fields, steps, margin, with_thickness=False, wait=()):
    C, S = counts
    _, L, R, N = thick[0].shape
    F = len(fields)
    whole = jax.ShapeDtypeStruct((F, L, R, N), jnp.float32)
    inner = jax.ShapeDtypeStruct((F * L * (R - sum(margin)), N), jnp.float32)
    flat = [a for bundle in bundles for a in bundle]
    out_shape = [whole if s == 0 else inner for s in steps]
    if with_thickness:
        out_shape.append(jax.ShapeDtypeStruct((L, R, N), jnp.float32))
    return pl.pallas_call(
        functools.partial(remap_kernel, counts, tuple(steps), tuple(fields), margin, with_thickness, (len(bundles),)),
        in_specs=[VMEM] * (1 + len(thick) + len(flat) + len(others)) + after(wait),
        out_specs=[VMEM] * len(out_shape),
        out_shape=out_shape,
        scratch_shapes=[pltpu.VMEM((weights.shape[0] + 1, 8, LANES), jnp.float32)],
        compiler_params=params(),
        cost_estimate=cost(len(steps) * S * L * L * R * N * (5 + 2 * F), 4 * R * N * L * (F + 1) * (S + len(steps))),
        name="remap_parts",
    )(weights, *thick, *flat, *others, *wait)


def remap_edge_kernel(counts, near_fields, weight_ref, *refs):
    *refs, sum_ref = refs
    G = counts[0] * counts[1]
    edge_refs, near_refs = refs[:G], refs[G : 2 * G]
    bundles = (refs[2 * G : 3 * G], refs[3 * G : 4 * G])
    edge_out_ref, thick_out_ref, near_out_ref = refs[-3:]

    def store_edge(s, i, at, columns, target, means):
        thick_out_ref[i, at, columns] = target
        for f, value in enumerate(means):
            edge_out_ref[f, i, at, columns] = value

    def store_near(s, i, at, columns, target, means):
        for f, value in enumerate(means):
            near_out_ref[f, i, at, columns] = value

    fields = [[level_of(ref, f) for ref in edge_refs] for f in range(1, edge_refs[0].shape[0])]
    remap_rows(weight_ref, sum_ref, counts, (0,), edge_refs, fields, [], store_edge)
    _, L, R, _ = near_refs[0].shape
    fields = [[packed_level_of(ref, index, L, R) for ref in bundles[which]] for which, index in near_fields]
    remap_rows(weight_ref, sum_ref, counts, (0,), near_refs, fields, [], store_near)


def remap_edges(counts, weights, edges, near_new, near, near_rest, wait=()):
    F, L, R, N = edges[0].shape
    T = F - 3
    near_fields = tuple((0, f) if f < T // 2 else (1, f - T // 2) for f in range(T))
    operands = [*edges, *near_new, *near, *near_rest]
    return pl.pallas_call(
        functools.partial(remap_edge_kernel, counts, near_fields),
        in_specs=[VMEM] * (1 + len(operands)) + after(wait),
        out_specs=[VMEM] * 3,
        out_shape=[
            jax.ShapeDtypeStruct((F - 1, L, R, N), jnp.float32),
            jax.ShapeDtypeStruct((L, R, N), jnp.float32),
            jax.ShapeDtypeStruct((T, *near_new[0].shape[1:]), jnp.float32),
        ],
        scratch_shapes=[pltpu.VMEM((weights.shape[0] + 1, 8, LANES), jnp.float32)],
        compiler_params=params(),
        cost_estimate=cost(len(edges) * L * L * R * N * 40, 4 * R * N * L * len(operands) * F),
        name="remap_edges",
    )(weights, *operands, *wait)


def finish_kernel(margin, own_ref, near_ref, edge_ref, thick_ref, thick_edge_ref, *refs):
    *arrived_refs, out_ref, thick_out_ref, token_ref = refs
    token_ref[...] = jnp.zeros_like(token_ref)
    T, L, R, _ = out_ref.shape
    thick_out_ref[...] = thick_ref[...]
    for i in range(L):
        for row, j in ((0, 0), (R - 1, 1)):
            thick_out_ref[i, row : row + 1] = thick_edge_ref[i, j : j + 1]
    for f in range(T):
        for i in range(L):
            start, first, end = (f * L + i) * (R - sum(margin)), margin[0], R - margin[1]
            total = own_ref[f, i, first:end]
            for ref in arrived_refs:
                total = total + ref[start : start + end - first]
            out_ref[f, i, first:end] = total
            for row, j in ((0, 0), (R - 1, 1)):
                out_ref[f, i, row : row + 1] = edge_ref[2 + f, i, j : j + 1]
            for j, row in enumerate(near_rows(R)[0]):
                out_ref[f, i, row : row + 1] = near_ref[f, i, j : j + 1]


def finish_tracers(own, near, edge, thick, thick_edge, arrived):
    return pl.pallas_call(
        functools.partial(finish_kernel, near_rows(own.shape[2])[1]),
        in_specs=[VMEM] * (5 + len(arrived)),
        out_specs=[VMEM] * 3,
        out_shape=[
            jax.ShapeDtypeStruct(own.shape, jnp.float32),
            jax.ShapeDtypeStruct(thick.shape, jnp.float32),
            jax.ShapeDtypeStruct((8, LANES), jnp.float32),
        ],
        compiler_params=params(),
        cost_estimate=cost(2 * own.size, 12 * own.size),
        name="finish_tracers",
    )(own, near, edge, thick, thick_edge, *arrived)


def finish_winds_kernel(count, own_ref, edge_ref, *refs):
    arrived_refs, out_refs = refs[:count], refs[-2:]
    _, L, R, N = own_ref.shape
    for f, out_ref in enumerate(out_refs):
        for i in range(L):
            start = (f * L + i) * (R - 2)
            total = own_ref[f, i, 1 : R - 1]
            for ref in arrived_refs:
                total = total + ref[start : start + R - 2]
            out_ref[i, 1 : R - 1] = total
            out_ref[i, 0:1] = edge_ref[f, i, 0:1]
            out_ref[i, R - 1 : R] = edge_ref[f, i, 1:2]


def finish_winds(own, arrived, edge, wait):
    return pl.pallas_call(
        functools.partial(finish_winds_kernel, len(arrived)),
        in_specs=[VMEM] * (2 + len(arrived)) + after(wait),
        out_specs=[VMEM] * 2,
        out_shape=[jax.ShapeDtypeStruct(own.shape[1:], jnp.float32)] * 2,
        compiler_params=params(),
        cost_estimate=cost(own.size, 12 * own.size),
        name="finish_winds",
    )(own, edge, *arrived, *wait)


def edge_kernel(thick_hbm, u_hbm, v_hbm, tracer_hbm, *refs):
    last_ref, leading_ref, top_ref, low_ref, tracer_ref, sems = refs[-6:]
    T, L, R, _ = tracer_hbm.shape
    top = pl.ds(R - 8, 8)
    copies = [
        pltpu.make_async_copy(thick_hbm.at[:, top], top_ref.at[0], sems.at[0]),
        pltpu.make_async_copy(v_hbm.at[:, top], top_ref.at[1], sems.at[1]),
        pltpu.make_async_copy(thick_hbm.at[:, pl.ds(0, 8)], low_ref.at[0], sems.at[2]),
        pltpu.make_async_copy(u_hbm.at[:, pl.ds(0, 8)], low_ref.at[1], sems.at[3]),
        pltpu.make_async_copy(v_hbm.at[:, pl.ds(0, 8)], low_ref.at[2], sems.at[4]),
        pltpu.make_async_copy(tracer_hbm.at[:, :, top], tracer_ref.at[0], sems.at[5]),
        pltpu.make_async_copy(tracer_hbm.at[:, :, pl.ds(0, 8)], tracer_ref.at[1], sems.at[6]),
    ]
    for copy in copies:
        copy.start()
    for copy in copies:
        copy.wait()
    last_ref[0:2] = top_ref[:, :, 7:8]
    last_ref[2 : 2 + T] = tracer_ref[0, :, :, 7:8]
    leading_ref[0] = low_ref[0, :, 0:1]
    leading_ref[1] = low_ref[0, :, 1:2]
    leading_ref[2:4] = low_ref[1:3, :, 0:1]
    leading_ref[4 : 4 + T] = tracer_ref[1, :, :, 0:1]


def edge_rows(thickness, wind_u, wind_v, tracers, wait):
    L, R, N = thickness.shape
    T = tracers.shape[0]
    operands = [pltpu.with_memory_space_constraint(a, pltpu.HBM) for a in (thickness, wind_u, wind_v, tracers)]
    return pl.pallas_call(
        edge_kernel,
        in_specs=after(operands) + after(wait),
        out_specs=[VMEM] * 2,
        out_shape=[
            jax.ShapeDtypeStruct((2 + T, L, 1, N), jnp.float32),
            jax.ShapeDtypeStruct((4 + T, L, 1, N), jnp.float32),
        ],
        scratch_shapes=[
            pltpu.VMEM((2, L, 8, N), jnp.float32),
            pltpu.VMEM((3, L, 8, N), jnp.float32),
            pltpu.VMEM((2, T, L, 8, N), jnp.float32),
            pltpu.SemaphoreType.DMA((7,)),
        ],
        compiler_params=params(),
        cost_estimate=cost(1e10, 1e9),
        name="edge_rows",
    )(*operands, *wait)


def shifted(value, lev_count, sub_count, s, t):
    if t == 0:
        return lax.ppermute(value, "lev", [(i, (i + s) % lev_count) for i in range(lev_count)])
    if s == 0:
        return lax.ppermute(value, "sub", [(i, (i + t) % sub_count) for i in range(sub_count)])
    pairs = [
        (i * sub_count + j, (i + s) % lev_count * sub_count + (j + t) % sub_count)
        for i in range(lev_count)
        for j in range(sub_count)
    ]
    return lax.ppermute(value, ("lev", "sub"), pairs)


def per_device(thickness, wind_u, wind_v, tracers, level_weights, cutoff):
    L, R, N = thickness.shape
    lat_count = lax.axis_size("lat")
    C, S = lax.axis_size("lev"), lax.axis_size("sub")
    lat_rows = R * lat_count
    send = functools.partial(shifted, lev_count=C, sub_count=S)

    T = tracers.shape[0]
    northward = [(i, i + 1) for i in range(lat_count - 1)]
    southward = [(j, i) for i, j in northward]
    table = jnp.asarray(geometry_table(lat_rows, R))
    weights = jnp.broadcast_to(level_weights[:, None, None], (level_weights.shape[0], 8, LANES))
    away = range(1, C)

    def with_others_of_chip(own):
        return [own] + [send(own, s=0, t=t) for t in range(1, S)]

    def sent(parts):
        return [send(part, s=s, t=0) for s, part in zip(away, parts)]

    remap = functools.partial(remap_parts, (C, S), weights)

    new, both, near_new, *arguments = first_step(table, thickness, wind_u, wind_v, tracers)
    both = [send(both, s=s, t=0) for s in away]
    inner, near, near_rest = inner_step(table, new, *arguments)
    group = with_others_of_chip(inner)
    near = [near] + [send(near, s=s, t=0) for s in away]
    near_rest = [near_rest] + [send(near_rest, s=s, t=0) for s in away]
    parted = [part(each, (L, R, N), [near[0]]) for each in both]
    near_new = [near_new] + [each[1] for each in parted]
    others = other_chips((C, S), [a for each in parted for a in with_others_of_chip(each[0])])
    tracer_fields = [(0, 1 + c) for c in range(T)]
    away_parts = remap(group, [group], others, tracer_fields, away, near_rows(R)[1])
    arrived = sent(away_parts)

    last, leading = edge_rows(
        thickness, wind_u, wind_v, tracers, [away_parts[0], *near[1:2], *near_rest[1:2]]
    )
    up = lax.ppermute(last, "lat", northward)
    down = lax.ppermute(leading, "lat", southward)
    u, v, edge = second_step(table, lat_rows, thickness, wind_u, wind_v, tracers, up, down, cutoff)
    edges = [edge] + [send(edge, s=s, t=0) for s in away]
    winds = [with_others_of_chip(u), with_others_of_chip(v)]
    tracers_own, thick_inner = remap(group, [group], others, tracer_fields, (0,), (0, 0), with_thickness=True, wait=[edge])
    winds_own, *winds_away = remap(
        group, winds, others, [(0, 0), (1, 0)], range(C), (1, 1), wait=[tracers_own, *arrived[:1]]
    )
    winds_arrived = sent(winds_away)
    near_new, near, near_rest, edges = (
        [a for own in sources for a in with_others_of_chip(own)] for sources in (near_new, near, near_rest, edges)
    )
    edge_out, thick_edge, near_out = remap_edges(
        (C, S), weights, edges, near_new, near, near_rest, wait=winds_away[:1]
    )

    tracers_out, thickness_out, token = finish_tracers(
        tracers_own, near_out, edge_out, thick_inner, thick_edge, arrived
    )
    u_out, v_out = finish_winds(winds_own, winds_arrived, edge_out, [token])
    return thickness_out, u_out, v_out, tracers_out


def solution(mesh):
    placed = (
        P(("member", "lev", "sub"), "lat", None),
        P(("member", "lev", "sub"), "lat", None),
        P(("member", "lev", "sub"), "lat", None),
        P("member", ("lev", "sub"), "lat", None),
        P(),
        P("lat"),
    )
    return jax.shard_map(
        per_device,
        mesh=mesh,
        in_specs=placed,
        out_specs=(
            P(("member", "lev", "sub"), "lat", None),
            P(("member", "lev", "sub"), "lat", None),
            P(("member", "lev", "sub"), "lat", None),
            P("member", ("lev", "sub"), "lat", None),
        ),
        check_vma=False,
    )
```

```python
import functools

import jax
import jax.numpy as jnp
import ml_dtypes
import numpy as np
from jax import lax
from jax.experimental import pallas as pl
from jax.experimental.pallas import tpu as pltpu
from jax.sharding import PartitionSpec as P

LANES = 128
VMEM = pl.BlockSpec(memory_space=pltpu.VMEM)


def params():
    return pltpu.CompilerParams(vmem_limit_bytes=16 * 1024 * 1024)


def cost(flops, bytes_accessed):
    return pl.CostEstimate(flops=int(flops), bytes_accessed=int(bytes_accessed), transcendentals=0)


def after(arrays):
    return [pl.BlockSpec(memory_space=pl.ANY)] * len(arrays)


def near_rows(rows):
    return (1, 2, rows - 2), (3, 2)


def geometry_table(lat_rows, band_rows):
    bands = lat_rows // band_rows
    table = np.zeros((bands, band_rows + 8, LANES), np.float32)
    for band in range(bands):
        for j in range(band_rows + 1):
            row = band * band_rows + j
            south = np.sin(row * np.pi / lat_rows) if 0 < row < lat_rows else 0.0
            north = np.sin((row + 1) * np.pi / lat_rows) if row + 1 < lat_rows else 0.0
            table[band, j, 0] = south
            table[band, j, 1] = north
            table[band, j, 2] = 1.0 / np.sin((row + 0.5) * np.pi / lat_rows)
    return table


def east_of(value):
    return pltpu.roll(value, value.shape[1] - 1, 1)


def west_of(value):
    return pltpu.roll(value, 1, 1)


def row_ids(shape):
    return lax.broadcasted_iota(jnp.int32, shape, 0)


def north_of(value, beyond):
    rows = value.shape[0]
    rolled = pltpu.roll(value, rows - 1, 0)
    return rolled if beyond is None else jnp.where(row_ids(value.shape) == rows - 1, beyond, rolled)


def south_of(value, beyond):
    rolled = pltpu.roll(value, 1, 0)
    return rolled if beyond is None else jnp.where(row_ids(value.shape) == 0, beyond, rolled)


def fluxes(geo, thick, u, v, thick_s, v_s, thick_n):
    rows = thick.shape[0]
    east = u * jnp.where(u > 0, thick, east_of(thick))
    north = v * jnp.where(v > 0, thick, north_of(thick, thick_n)) * geo[0:rows, 1:2]
    below = None if v_s is None else v_s * jnp.where(v_s > 0, thick_s, thick[0:1]) * geo[0:1, 0:1]
    return east, north, below


def tracer_change(q, q_s, q_n, thick, u, v, v_s, east, north, below, inverse):
    t_east = east * jnp.where(u > 0, q, east_of(q))
    t_north = north * jnp.where(v > 0, q, north_of(q, q_n))
    t_below = None if v_s is None else below * jnp.where(v_s > 0, q_s, q[0:1])
    change = thick * q - (t_east - west_of(t_east))
    return change - (t_north - south_of(t_north, t_below)) * inverse


def packed_at(rows, levels, width):
    near = len(near_rows(rows)[0])
    size = rows - 2 + levels * near
    for a in range(width // LANES):
        yield a, a * size, [a * size + rows - 2 + k * near for k in range(levels)]


def first_kernel(table_hbm, thick_hbm, u_hbm, v_hbm, tracer_hbm, *refs):
    new_ref, both_ref, near_ref, thick_ref, u_ref, v_ref, tracer_ref, sum_ref, geo_ref, sems = refs
    L, rows, _ = thick_ref.shape
    near, _ = near_rows(rows)
    table_copy = pltpu.make_async_copy(table_hbm.at[lax.axis_index("lat")], geo_ref, sems.at[3, 0])
    table_copy.start()
    pairs = ((thick_hbm, thick_ref), (u_hbm, u_ref), (v_hbm, v_ref))

    def copies(k):
        return [pltpu.make_async_copy(a.at[k], b.at[k], sems.at[i, k]) for i, (a, b) in enumerate(pairs)]

    for k in range(L):
        for copy in copies(k):
            copy.start()
    tracer_copy = pltpu.make_async_copy(tracer_hbm, tracer_ref, sems.at[3, 1])
    tracer_copy.start()
    table_copy.wait()
    geo = geo_ref[...]
    sum_ref[...] = jnp.zeros_like(sum_ref)

    def level(k, carry):
        for copy in copies(k):
            copy.wait()
        thick, u, v = thick_ref[k], u_ref[k], v_ref[k]
        east, north, _ = fluxes(geo, thick, u, v, None, None, None)
        new = thick - (east - west_of(east)) - (north - south_of(north, None)) * geo[0:rows, 2:3]
        new_ref[k] = new
        for j, row in enumerate(near):
            near_ref[0, k, j : j + 1] = new[row : row + 1]
        sum_ref[...] += new
        return carry

    lax.fori_loop(0, L, level, 0)
    for a, at, each in packed_at(rows, L, thick_ref.shape[2]):
        lanes = slice(a * LANES, (a + 1) * LANES)
        both_ref[at : at + rows - 2] = sum_ref[1 : rows - 1, lanes]
        for k in range(L):
            both_ref[each[k] : each[k] + len(near)] = near_ref[0, k, :, lanes]
    tracer_copy.wait()


def first_step(table, thickness, wind_u, wind_v, tracers):
    L, R, N = thickness.shape
    arguments = (thickness, wind_u, wind_v, tracers)
    operands = [pltpu.with_memory_space_constraint(a, pltpu.HBM) for a in (table, *arguments)]
    near = len(near_rows(R)[0])
    shapes = [(L, R, N), ((R - 2 + L * near) * N // LANES, LANES), (1, L, near, N)] + [a.shape for a in arguments]
    return pl.pallas_call(
        first_kernel,
        in_specs=after(operands),
        out_specs=[VMEM] * len(shapes),
        out_shape=[jax.ShapeDtypeStruct(shape, jnp.float32) for shape in shapes],
        scratch_shapes=[
            pltpu.VMEM((R, N), jnp.float32),
            pltpu.VMEM(table.shape[1:], jnp.float32),
            pltpu.SemaphoreType.DMA((4, max(L, 2))),
        ],
        compiler_params=params(),
        cost_estimate=cost(40 * L * R * N, 4 * L * R * N * (7 + 2 * tracers.shape[0])),
        name="first_step",
    )(*operands)


def inner_kernel(table_ref, new_ref, thick_ref, u_ref, v_ref, tracer_ref, out_ref, near_ref):
    T, L, rows, _ = tracer_ref.shape
    near, _ = near_rows(rows)
    geo = table_ref[lax.axis_index("lat")]
    inverse = geo[0:rows, 2:3]

    def level(k, carry):
        thick, u, v, new = thick_ref[k], u_ref[k], v_ref[k], new_ref[k]
        east, north, _ = fluxes(geo, thick, u, v, None, None, None)

        out_ref[0, k] = new
        scale = 1.0 / new
        for c in range(T):
            change = tracer_change(
                tracer_ref[c, k], None, None, thick, u, v, None, east, north, None, inverse
            )
            value = change * scale
            out_ref[1 + c, k] = value
            for j, row in enumerate(near):
                near_ref[pl.ds((c * L + k) * len(near) + j, 1)] = value[row : row + 1]
        return carry

    lax.fori_loop(0, L, level, 0)


def inner_step(table, new, thickness, wind_u, wind_v, tracers):
    L, R, N = thickness.shape
    T = tracers.shape[0]
    rows = jax.ShapeDtypeStruct((T * L * len(near_rows(R)[0]), N), jnp.float32)
    shape = lambda n, rows: jax.ShapeDtypeStruct((n, L, rows, N), jnp.float32)
    return pl.pallas_call(
        inner_kernel,
        in_specs=[VMEM] * 6,
        out_specs=[VMEM] * 2,
        out_shape=[shape(1 + T, R), rows],
        compiler_params=params(),
        cost_estimate=cost(130 * L * R * N, 4 * L * R * N * (8 + 2 * T)),
        name="inner_step",
    )(table, new, thickness, wind_u, wind_v, tracers)


def filter_tables(N):
    A = N // LANES
    b = np.arange(LANES)[:, None]
    p = np.arange(LANES)[None, :]
    tables = []
    for q in range(A // 2 + 1):
        angle = 2.0 * np.pi * ((b * (A * p + q)) % N) / N
        c, s = np.cos(angle), np.sin(angle)
        tables.append(np.block([[c, -s], [s, c]]))
    table = np.stack(tables)
    high = table.astype(np.float32).astype(ml_dtypes.bfloat16)
    low = (table - high.astype(np.float64)).astype(np.float32).astype(ml_dtypes.bfloat16)
    return high, low


def split(value):
    high = value.astype(jnp.bfloat16)
    return high, (value - high.astype(jnp.float32)).astype(jnp.bfloat16)


def product(value, high, low, transposed):
    dims = (((1,), (1 if transposed else 0,)), ((), ()))
    dot = lambda x, y: lax.dot_general(x, y, dims, preferred_element_type=jnp.float32)
    v_high, v_low = split(value)
    return dot(v_high, high) + (dot(v_high, low) + dot(v_low, high))


def filter_rows(x, cutoff, high_ref, low_ref):
    A = len(x)
    N = A * LANES
    half = A // 2
    even = [x[a] + x[A - a] for a in range(1, half + 1)]
    odd = [x[a] - x[A - a] for a in range(1, half + 1)]
    angle = lambda q, a: 2.0 * np.pi * ((q * a) % A) / A
    p = lax.broadcasted_iota(jnp.int32, cutoff.shape, 1)
    real, imag = [], []
    for q in range(half + 1):
        re = x[0]
        for a in range(1, half + 1):
            re = re + (even[a - 1] if q == 0 else float(np.cos(angle(q, a))) * even[a - 1])
        if q == 0:
            high, low = high_ref[0, 0:LANES], low_ref[0, 0:LANES]
            spectrum = product(re, high, low, False)
        else:
            high, low = high_ref[q], low_ref[q]
            im = -float(np.sin(angle(q, 1))) * odd[0]
            for a in range(2, half + 1):
                im = im - float(np.sin(angle(q, a))) * odd[a - 1]
            spectrum = product(jnp.concatenate([re, im], axis=1), high, low, False)
        mode = A * p + q
        factor = 1.0 / N if q == 0 else 2.0 / N
        kept = jnp.where(jnp.minimum(mode, N - mode) <= cutoff, factor, 0.0)
        back = product(spectrum * jnp.concatenate([kept, kept], axis=1), high, low, True)
        real.append(back[:, :LANES])
        imag.append(back[:, LANES:])
    out = [None] * A
    out[0] = functools.reduce(jnp.add, real)
    for a in range(1, half + 1):
        even_part, odd_part = real[0], None
        for q in range(1, half + 1):
            even_part = even_part + float(np.cos(angle(q, a))) * real[q]
            term = float(np.sin(angle(q, a))) * imag[q]
            odd_part = term if odd_part is None else odd_part + term
        out[a] = even_part - odd_part
        out[A - a] = even_part + odd_part
    return out


def second_kernel(
    lat_rows, table_ref, thick_ref, u_ref, v_ref, tracer_ref, up_ref, down_ref, cutoff_ref, high_ref, low_ref, *refs
):
    *wind_refs, edge_ref, new_wind = refs
    k = pl.program_id(0)
    _, L, rows, width = new_wind.shape
    band = lax.axis_index("lat")
    geo = table_ref[band]
    thick, u, v = thick_ref[0], u_ref[0], v_ref[0]
    thick_s, v_s = up_ref[0, 0], up_ref[1, 0]
    thick_n, thick_nn, u_n, v_n = (down_ref[i, 0] for i in range(4))
    east, north, below = fluxes(geo, thick, u, v, thick_s, v_s, thick_n)
    inverse = geo[0:rows, 2:3]
    new = thick - (east - west_of(east)) - (north - south_of(north, below)) * inverse
    east_n = u_n * jnp.where(u_n > 0, thick_n, east_of(thick_n))
    north_n = v_n * jnp.where(v_n > 0, thick_n, thick_nn) * geo[rows : rows + 1, 1:2]
    new_n = (
        thick_n
        - (east_n - west_of(east_n))
        - (north_n - north[rows - 1 : rows]) * geo[rows : rows + 1, 2:3]
    )
    new_wind[0, k] = u - 0.05 * (east_of(new) - new)
    inside = band * rows + row_ids(new.shape) < lat_rows - 1
    new_wind[1, k] = jnp.where(inside, v - 0.05 * (north_of(new, new_n) - new), 0.0)

    def store_edges(field, level, value):
        edge_ref[field, level, 0:1] = value[0:1]
        edge_ref[field, level, 1:2] = value[rows - 1 : rows]

    store_edges(0, k, new)
    scale = 1.0 / new
    for c in range(tracer_ref.shape[0]):
        change = tracer_change(
            tracer_ref[c, 0], up_ref[2 + c, 0], down_ref[4 + c, 0], thick, u, v, v_s, east, north, below, inverse
        )
        store_edges(3 + c, k, change * scale)

    @pl.when(k == L - 1)
    def _():
        pieces = [
            new_wind[:, :, :, a * LANES : (a + 1) * LANES].reshape(2 * L * rows, LANES) for a in range(width // LANES)
        ]
        cutoff = jnp.broadcast_to(cutoff_ref[...][None], (2 * L, rows, LANES)).reshape(2 * L * rows, LANES)
        for a, piece in enumerate(filter_rows(pieces, cutoff, high_ref, low_ref)):
            piece = piece.reshape(2, L, rows, LANES)
            for f in range(2):
                wind_refs[f][0, :, :, a * LANES : (a + 1) * LANES] = piece[f]
        for f in range(2):
            for level in range(L):
                store_edges(1 + f, level, wind_refs[f][0, level])


def second_step(table, lat_rows, thickness, wind_u, wind_v, tracers, up, down, cutoff):
    L, R, N = thickness.shape
    T = tracers.shape[0]
    high, low = filter_tables(N)
    level = pl.BlockSpec((1, R, N), lambda k: (k, 0, 0))
    some = lambda n, rows: pl.BlockSpec((n, 1, rows, N), lambda k: (0, k, 0, 0))
    whole = lambda shape: pl.BlockSpec(shape, lambda k: (0,) * len(shape))
    return pl.pallas_call(
        functools.partial(second_kernel, lat_rows),
        grid=(L,),
        in_specs=[whole(table.shape), level, level, level, some(T, R), some(2 + T, 1), some(4 + T, 1)]
        + [whole((R, LANES)), whole(high.shape), whole(low.shape)],
        out_specs=[whole((1, L, R, N)), whole((1, L, R, N)), whole((3 + T, L, 2, N))],
        out_shape=[
            jax.ShapeDtypeStruct((1, L, R, N), jnp.float32),
            jax.ShapeDtypeStruct((1, L, R, N), jnp.float32),
            jax.ShapeDtypeStruct((3 + T, L, 2, N), jnp.float32),
        ],
        scratch_shapes=[pltpu.VMEM((2, L, R, N), jnp.float32)],
        compiler_params=params(),
        cost_estimate=cost(12 * 2 * L * R * high.size, 4 * L * R * N * (8 + T)),
        name="second_step",
    )(
        table, thickness, wind_u, wind_v, tracers, up, down,
        jnp.broadcast_to(cutoff[:, None], (R, LANES)), jnp.asarray(high), jnp.asarray(low),
    )


def part_kernel(both_ref, *refs):
    sum_ref, near_ref = refs[-2:]
    rows, width = sum_ref.shape
    _, L, near, _ = near_ref.shape
    sum_ref[...] = jnp.zeros_like(sum_ref)
    for a, at, each in packed_at(rows, L, width):
        lanes = slice(a * LANES, (a + 1) * LANES)
        sum_ref[1 : rows - 1, lanes] = both_ref[at : at + rows - 2]
        for k in range(L):
            near_ref[0, k, :, lanes] = both_ref[each[k] : each[k] + near]


def part(both, shape, wait):
    L, R, N = shape
    return pl.pallas_call(
        part_kernel,
        in_specs=[VMEM] + after(wait),
        out_specs=[VMEM] * 2,
        out_shape=[
            jax.ShapeDtypeStruct((R, N), jnp.float32),
            jax.ShapeDtypeStruct((1, L, len(near_rows(R)[0]), N), jnp.float32),
        ],
        compiler_params=params(),
        cost_estimate=cost(1e11, 1e9),
        name="part",
    )(both, *wait)


def mass_kernel(C, S, *refs):
    other_refs, (base_ref, mass_ref) = refs[: (C - 1) * S], refs[(C - 1) * S :]
    lev = lax.axis_index("lev")
    others_mass, base = None, None
    for s in range(1, C):
        other = functools.reduce(jnp.add, [ref[...] for ref in other_refs[(s - 1) * S : s * S]])
        below = jnp.where(lev >= s, other, 0.0)
        others_mass = other if others_mass is None else others_mass + other
        base = below if base is None else base + below
    base_ref[...] = base
    mass_ref[...] = others_mass


def other_chips(counts, others):
    return pl.pallas_call(
        functools.partial(mass_kernel, *counts),
        in_specs=[VMEM] * len(others),
        out_specs=[VMEM] * 2,
        out_shape=[jax.ShapeDtypeStruct(others[0].shape, jnp.float32)] * 2,
        compiler_params=params(),
        cost_estimate=cost(1, 1),
        name="other_chips",
    )(*others)


def add_weights(weight_ref, sum_ref):
    total = jnp.zeros(weight_ref.shape[1:], jnp.float32)
    for k in range(weight_ref.shape[0]):
        sum_ref[k] = total
        total = total + weight_ref[k]
    sum_ref[weight_ref.shape[0]] = total
    return total


def source_levels(place, counts, thick, others):
    C, S = counts
    lev, sub = place
    spot = [lax.rem(lev - g // S + C, C) * S + lax.rem(sub - g % S + S, S) for g in range(len(thick))]
    group = [functools.reduce(jnp.add, levels) for levels in thick]
    mass = functools.reduce(jnp.add, group)
    base = jnp.zeros_like(mass)
    if others:
        base, mass = others[0], mass + others[1]
    sources = []
    for g, levels in enumerate(thick):
        low = base
        for other in range(len(thick)):
            if other != g:
                low = low + jnp.where(spot[other] < spot[g], group[other], 0.0)
        for m, value in enumerate(levels):
            sources.append((g, m, low, value))
            low = low + value
    return mass, sources


def covered(top, sources):
    return [jnp.minimum(jnp.maximum(top - low, 0.0), value) for _, _, low, value in sources]


def level_of(ref, index):
    return lambda m, at, columns: ref[index, m, at, columns]


def packed_level_of(ref, index, L, rows):
    return lambda m, at, columns: ref[(index * L + m) * rows : (index * L + m + 1) * rows, columns]


def remap_rows(weight_ref, sum_ref, counts, steps, thick_refs, field_refs, other_refs, store):
    C, S = counts
    _, L, R, N = thick_refs[0].shape
    rows = min(R, 8)
    place = lev, sub = lax.axis_index("lev"), lax.axis_index("sub")
    firsts = [(lax.rem(lev + s, C) * S + sub) * L for s in steps]
    weight_sum = add_weights(weight_ref, sum_ref)[0:rows]

    def tile(at, columns):
        thick = [[ref[0, m, at, columns] for m in range(L)] for ref in thick_refs]
        others = [ref[at, columns] for ref in other_refs]
        mass, sources = source_levels(place, counts, thick, others)
        unit = mass / weight_sum
        for index, s in enumerate(steps):
            below = covered(unit * sum_ref[firsts[index], 0:rows], sources)
            for i in range(L):
                upto = covered(unit * sum_ref[firsts[index] + i + 1, 0:rows], sources)
                part = [a - b for a, b in zip(upto, below)]
                below = upto
                target = unit * weight_ref[firsts[index] + i, 0:rows]
                scale = 1.0 / target
                means = []
                for refs in field_refs:
                    terms = [refs[g](m, at, columns) * w for (g, m, _, _), w in zip(sources, part)]
                    means.append(functools.reduce(jnp.add, terms) * scale)
                store(s, i, at, columns, target, means)

    for r in range(0, R, rows):

        def body(c, carry):
            tile(slice(r, r + rows), pl.ds(pl.multiple_of(c * LANES, LANES), LANES))
            return carry

        lax.fori_loop(0, N // LANES, body, 0)


def inner_part(at, margin, rows):
    return max(at.start, margin[0]), min(at.stop, rows - margin[1])


def remap_kernel(counts, steps, fields, margin, with_thickness, sizes, weight_ref, *refs):
    *refs, sum_ref = refs
    C, S = counts
    thick_refs, refs = refs[:S], refs[S:]
    bundles = []
    for _ in range(sizes[0]):
        bundles.append(refs[:S])
        refs = refs[S:]
    other_refs, out_refs = refs[:2], refs[len(refs) - len(steps) - with_thickness :]
    _, L, R, _ = thick_refs[0].shape
    thick_out_ref = out_refs[-1]
    field_refs = [[level_of(ref, index) for ref in bundles[which]] for which, index in fields]

    def store(s, i, at, columns, target, means):
        out_ref = out_refs[steps.index(s)]
        if with_thickness and s == 0:
            thick_out_ref[i, at, columns] = target
        for f, value in enumerate(means):
            if s == 0:
                out_ref[f, i, at, columns] = value
            else:
                lower, upper = inner_part(at, margin, R)
                start = (f * L + i) * (R - sum(margin)) - margin[0]
                out_ref[start + lower : start + upper, columns] = value[lower - at.start : upper - at.start]

    remap_rows(
        weight_ref, sum_ref, counts, steps, thick_refs, field_refs, other_refs, store
    )


def remap_parts(counts, weights, thick, bundles, others, fields, steps, margin, with_thickness=False, wait=()):
    C, S = counts
    _, L, R, N = thick[0].shape
    F = len(fields)
    whole = jax.ShapeDtypeStruct((F, L, R, N), jnp.float32)
    inner = jax.ShapeDtypeStruct((F * L * (R - sum(margin)), N), jnp.float32)
    flat = [a for bundle in bundles for a in bundle]
    out_shape = [whole if s == 0 else inner for s in steps]
    if with_thickness:
        out_shape.append(jax.ShapeDtypeStruct((L, R, N), jnp.float32))
    return pl.pallas_call(
        functools.partial(remap_kernel, counts, tuple(steps), tuple(fields), margin, with_thickness, (len(bundles),)),
        in_specs=[VMEM] * (1 + len(thick) + len(flat) + len(others)) + after(wait),
        out_specs=[VMEM] * len(out_shape),
        out_shape=out_shape,
        scratch_shapes=[pltpu.VMEM((weights.shape[0] + 1, 8, LANES), jnp.float32)],
        compiler_params=params(),
        cost_estimate=cost(len(steps) * S * L * L * R * N * (5 + 2 * F), 4 * R * N * L * (F + 1) * (S + len(steps))),
        name="remap_parts",
    )(weights, *thick, *flat, *others, *wait)


def remap_edge_kernel(counts, weight_ref, *refs):
    *refs, sum_ref = refs
    G = counts[0] * counts[1]
    edge_refs, near_refs, tracer_refs = refs[:G], refs[G : 2 * G], refs[2 * G : 3 * G]
    edge_out_ref, thick_out_ref, near_out_ref = refs[-3:]

    def store_edge(s, i, at, columns, target, means):
        thick_out_ref[i, at, columns] = target
        for f, value in enumerate(means):
            edge_out_ref[f, i, at, columns] = value

    def store_near(s, i, at, columns, target, means):
        for f, value in enumerate(means):
            near_out_ref[f, i, at, columns] = value

    fields = [[level_of(ref, f) for ref in edge_refs] for f in range(1, edge_refs[0].shape[0])]
    remap_rows(weight_ref, sum_ref, counts, (0,), edge_refs, fields, [], store_edge)
    _, L, R, _ = near_refs[0].shape
    fields = [[packed_level_of(ref, f, L, R) for ref in tracer_refs] for f in range(near_out_ref.shape[0])]
    remap_rows(weight_ref, sum_ref, counts, (0,), near_refs, fields, [], store_near)


def remap_edges(counts, weights, edges, near_new, near, wait=()):
    F, L, R, N = edges[0].shape
    T = F - 3
    operands = [*edges, *near_new, *near]
    return pl.pallas_call(
        functools.partial(remap_edge_kernel, counts),
        in_specs=[VMEM] * (1 + len(operands)) + after(wait),
        out_specs=[VMEM] * 3,
        out_shape=[
            jax.ShapeDtypeStruct((F - 1, L, R, N), jnp.float32),
            jax.ShapeDtypeStruct((L, R, N), jnp.float32),
            jax.ShapeDtypeStruct((T, *near_new[0].shape[1:]), jnp.float32),
        ],
        scratch_shapes=[pltpu.VMEM((weights.shape[0] + 1, 8, LANES), jnp.float32)],
        compiler_params=params(),
        cost_estimate=cost(len(edges) * L * L * R * N * 40, 4 * R * N * L * len(operands) * F),
        name="remap_edges",
    )(weights, *operands, *wait)


def finish_kernel(margin, own_ref, near_ref, edge_ref, thick_ref, thick_edge_ref, *refs):
    *arrived_refs, out_ref, thick_out_ref, token_ref = refs
    token_ref[...] = jnp.zeros_like(token_ref)
    T, L, R, _ = out_ref.shape
    thick_out_ref[...] = thick_ref[...]
    for i in range(L):
        for row, j in ((0, 0), (R - 1, 1)):
            thick_out_ref[i, row : row + 1] = thick_edge_ref[i, j : j + 1]
    for f in range(T):
        for i in range(L):
            start, first, end = (f * L + i) * (R - sum(margin)), margin[0], R - margin[1]
            total = own_ref[f, i, first:end]
            for ref in arrived_refs:
                total = total + ref[start : start + end - first]
            out_ref[f, i, first:end] = total
            for row, j in ((0, 0), (R - 1, 1)):
                out_ref[f, i, row : row + 1] = edge_ref[2 + f, i, j : j + 1]
            for j, row in enumerate(near_rows(R)[0]):
                out_ref[f, i, row : row + 1] = near_ref[f, i, j : j + 1]


def finish_tracers(own, near, edge, thick, thick_edge, arrived):
    return pl.pallas_call(
        functools.partial(finish_kernel, near_rows(own.shape[2])[1]),
        in_specs=[VMEM] * (5 + len(arrived)),
        out_specs=[VMEM] * 3,
        out_shape=[
            jax.ShapeDtypeStruct(own.shape, jnp.float32),
            jax.ShapeDtypeStruct(thick.shape, jnp.float32),
            jax.ShapeDtypeStruct((8, LANES), jnp.float32),
        ],
        compiler_params=params(),
        cost_estimate=cost(2 * own.size, 12 * own.size),
        name="finish_tracers",
    )(own, near, edge, thick, thick_edge, *arrived)


def finish_winds_kernel(count, own_ref, edge_ref, *refs):
    arrived_refs, out_refs = refs[:count], refs[-2:]
    _, L, R, N = own_ref.shape
    for f, out_ref in enumerate(out_refs):
        for i in range(L):
            start = (f * L + i) * (R - 2)
            total = own_ref[f, i, 1 : R - 1]
            for ref in arrived_refs:
                total = total + ref[start : start + R - 2]
            out_ref[i, 1 : R - 1] = total
            out_ref[i, 0:1] = edge_ref[f, i, 0:1]
            out_ref[i, R - 1 : R] = edge_ref[f, i, 1:2]


def finish_winds(own, arrived, edge, wait):
    return pl.pallas_call(
        functools.partial(finish_winds_kernel, len(arrived)),
        in_specs=[VMEM] * (2 + len(arrived)) + after(wait),
        out_specs=[VMEM] * 2,
        out_shape=[jax.ShapeDtypeStruct(own.shape[1:], jnp.float32)] * 2,
        compiler_params=params(),
        cost_estimate=cost(own.size, 12 * own.size),
        name="finish_winds",
    )(own, edge, *arrived, *wait)


def edge_kernel(thick_hbm, u_hbm, v_hbm, tracer_hbm, *refs):
    last_ref, leading_ref, top_ref, low_ref, tracer_ref, sems = refs[-6:]
    T, L, R, _ = tracer_hbm.shape
    top = pl.ds(R - 8, 8)
    copies = [
        pltpu.make_async_copy(thick_hbm.at[:, top], top_ref.at[0], sems.at[0]),
        pltpu.make_async_copy(v_hbm.at[:, top], top_ref.at[1], sems.at[1]),
        pltpu.make_async_copy(thick_hbm.at[:, pl.ds(0, 8)], low_ref.at[0], sems.at[2]),
        pltpu.make_async_copy(u_hbm.at[:, pl.ds(0, 8)], low_ref.at[1], sems.at[3]),
        pltpu.make_async_copy(v_hbm.at[:, pl.ds(0, 8)], low_ref.at[2], sems.at[4]),
        pltpu.make_async_copy(tracer_hbm.at[:, :, top], tracer_ref.at[0], sems.at[5]),
        pltpu.make_async_copy(tracer_hbm.at[:, :, pl.ds(0, 8)], tracer_ref.at[1], sems.at[6]),
    ]
    for copy in copies:
        copy.start()
    for copy in copies:
        copy.wait()
    last_ref[0:2] = top_ref[:, :, 7:8]
    last_ref[2 : 2 + T] = tracer_ref[0, :, :, 7:8]
    leading_ref[0] = low_ref[0, :, 0:1]
    leading_ref[1] = low_ref[0, :, 1:2]
    leading_ref[2:4] = low_ref[1:3, :, 0:1]
    leading_ref[4 : 4 + T] = tracer_ref[1, :, :, 0:1]


def edge_rows(thickness, wind_u, wind_v, tracers, wait):
    L, R, N = thickness.shape
    T = tracers.shape[0]
    operands = [pltpu.with_memory_space_constraint(a, pltpu.HBM) for a in (thickness, wind_u, wind_v, tracers)]
    return pl.pallas_call(
        edge_kernel,
        in_specs=after(operands) + after(wait),
        out_specs=[VMEM] * 2,
        out_shape=[
            jax.ShapeDtypeStruct((2 + T, L, 1, N), jnp.float32),
            jax.ShapeDtypeStruct((4 + T, L, 1, N), jnp.float32),
        ],
        scratch_shapes=[
            pltpu.VMEM((2, L, 8, N), jnp.float32),
            pltpu.VMEM((3, L, 8, N), jnp.float32),
            pltpu.VMEM((2, T, L, 8, N), jnp.float32),
            pltpu.SemaphoreType.DMA((7,)),
        ],
        compiler_params=params(),
        cost_estimate=cost(1e10, 1e9),
        name="edge_rows",
    )(*operands, *wait)


def shifted(value, lev_count, sub_count, s, t):
    if t == 0:
        return lax.ppermute(value, "lev", [(i, (i + s) % lev_count) for i in range(lev_count)])
    if s == 0:
        return lax.ppermute(value, "sub", [(i, (i + t) % sub_count) for i in range(sub_count)])
    pairs = [
        (i * sub_count + j, (i + s) % lev_count * sub_count + (j + t) % sub_count)
        for i in range(lev_count)
        for j in range(sub_count)
    ]
    return lax.ppermute(value, ("lev", "sub"), pairs)


def per_device(thickness, wind_u, wind_v, tracers, level_weights, cutoff):
    L, R, N = thickness.shape
    lat_count = lax.axis_size("lat")
    C, S = lax.axis_size("lev"), lax.axis_size("sub")
    lat_rows = R * lat_count
    send = functools.partial(shifted, lev_count=C, sub_count=S)

    T = tracers.shape[0]
    northward = [(i, i + 1) for i in range(lat_count - 1)]
    southward = [(j, i) for i, j in northward]
    table = jnp.asarray(geometry_table(lat_rows, R))
    weights = jnp.broadcast_to(level_weights[:, None, None], (level_weights.shape[0], 8, LANES))
    away = range(1, C)

    def with_others_of_chip(own):
        return [own] + [send(own, s=0, t=t) for t in range(1, S)]

    def sent(parts):
        return [send(part, s=s, t=0) for s, part in zip(away, parts)]

    remap = functools.partial(remap_parts, (C, S), weights)

    new, both, near_new, *arguments = first_step(table, thickness, wind_u, wind_v, tracers)
    both = [send(both, s=s, t=0) for s in away]
    inner, near = inner_step(table, new, *arguments)
    group = with_others_of_chip(inner)
    near = [near] + [send(near, s=s, t=0) for s in away]
    parted = [part(each, (L, R, N), [near[0]]) for each in both]
    near_new = [near_new] + [each[1] for each in parted]
    others = other_chips((C, S), [a for each in parted for a in with_others_of_chip(each[0])])
    tracer_fields = [(0, 1 + c) for c in range(T)]
    away_parts = remap(group, [group], others, tracer_fields, away, near_rows(R)[1])
    arrived = sent(away_parts)

    last, leading = edge_rows(
        thickness, wind_u, wind_v, tracers, [away_parts[0], *near[1:2]]
    )
    up = lax.ppermute(last, "lat", northward)
    down = lax.ppermute(leading, "lat", southward)
    u, v, edge = second_step(table, lat_rows, thickness, wind_u, wind_v, tracers, up, down, cutoff)
    edges = [edge] + [send(edge, s=s, t=0) for s in away]
    winds = [with_others_of_chip(u), with_others_of_chip(v)]
    tracers_own, thick_inner = remap(group, [group], others, tracer_fields, (0,), (0, 0), with_thickness=True, wait=[edge])
    winds_own, *winds_away = remap(
        group, winds, others, [(0, 0), (1, 0)], range(C), (1, 1), wait=[tracers_own, *arrived[:1]]
    )
    winds_arrived = sent(winds_away)
    near_new, near, edges = (
        [a for own in sources for a in with_others_of_chip(own)] for sources in (near_new, near, edges)
    )
    edge_out, thick_edge, near_out = remap_edges(
        (C, S), weights, edges, near_new, near, wait=winds_away[:1]
    )

    tracers_out, thickness_out, token = finish_tracers(
        tracers_own, near_out, edge_out, thick_inner, thick_edge, arrived
    )
    u_out, v_out = finish_winds(winds_own, winds_arrived, edge_out, [token])
    return thickness_out, u_out, v_out, tracers_out


def solution(mesh):
    placed = (
        P(("member", "lev", "sub"), "lat", None),
        P(("member", "lev", "sub"), "lat", None),
        P(("member", "lev", "sub"), "lat", None),
        P("member", ("lev", "sub"), "lat", None),
        P(),
        P("lat"),
    )
    return jax.shard_map(
        per_device,
        mesh=mesh,
        in_specs=placed,
        out_specs=(
            P(("member", "lev", "sub"), "lat", None),
            P(("member", "lev", "sub"), "lat", None),
            P(("member", "lev", "sub"), "lat", None),
            P("member", ("lev", "sub"), "lat", None),
        ),
        check_vma=False,
    )
```

```python
import functools

import jax
import jax.numpy as jnp
import ml_dtypes
import numpy as np
from jax import lax
from jax.experimental import pallas as pl
from jax.experimental.pallas import tpu as pltpu
from jax.sharding import PartitionSpec as P

LANES = 128
VMEM = pl.BlockSpec(memory_space=pltpu.VMEM)


def params():
    return pltpu.CompilerParams(vmem_limit_bytes=16 * 1024 * 1024)


def cost(flops, bytes_accessed):
    return pl.CostEstimate(flops=int(flops), bytes_accessed=int(bytes_accessed), transcendentals=0)


def after(arrays):
    return [pl.BlockSpec(memory_space=pl.ANY)] * len(arrays)


def near_rows(rows):
    return (1, 2, rows - 2), (3, 2)


def geometry_table(lat_rows, band_rows):
    bands = lat_rows // band_rows
    table = np.zeros((bands, band_rows + 8, LANES), np.float32)
    for band in range(bands):
        for j in range(band_rows + 1):
            row = band * band_rows + j
            south = np.sin(row * np.pi / lat_rows) if 0 < row < lat_rows else 0.0
            north = np.sin((row + 1) * np.pi / lat_rows) if row + 1 < lat_rows else 0.0
            table[band, j, 0] = south
            table[band, j, 1] = north
            table[band, j, 2] = 1.0 / np.sin((row + 0.5) * np.pi / lat_rows)
    return table


def east_of(value):
    return pltpu.roll(value, value.shape[1] - 1, 1)


def west_of(value):
    return pltpu.roll(value, 1, 1)


def row_ids(shape):
    return lax.broadcasted_iota(jnp.int32, shape, 0)


def north_of(value, beyond):
    rows = value.shape[0]
    rolled = pltpu.roll(value, rows - 1, 0)
    return rolled if beyond is None else jnp.where(row_ids(value.shape) == rows - 1, beyond, rolled)


def south_of(value, beyond):
    rolled = pltpu.roll(value, 1, 0)
    return rolled if beyond is None else jnp.where(row_ids(value.shape) == 0, beyond, rolled)


def fluxes(geo, thick, u, v, thick_s, v_s, thick_n):
    rows = thick.shape[0]
    east = u * jnp.where(u > 0, thick, east_of(thick))
    north = v * jnp.where(v > 0, thick, north_of(thick, thick_n)) * geo[0:rows, 1:2]
    below = None if v_s is None else v_s * jnp.where(v_s > 0, thick_s, thick[0:1]) * geo[0:1, 0:1]
    return east, north, below


def tracer_change(q, q_s, q_n, thick, u, v, v_s, east, north, below, inverse):
    t_east = east * jnp.where(u > 0, q, east_of(q))
    t_north = north * jnp.where(v > 0, q, north_of(q, q_n))
    t_below = None if v_s is None else below * jnp.where(v_s > 0, q_s, q[0:1])
    change = thick * q - (t_east - west_of(t_east))
    return change - (t_north - south_of(t_north, t_below)) * inverse


def packed_at(rows, levels, width):
    near = len(near_rows(rows)[0])
    size = rows - 2 + levels * near
    for a in range(width // LANES):
        yield a, a * size, [a * size + rows - 2 + k * near for k in range(levels)]


def first_kernel(table_hbm, thick_hbm, u_hbm, v_hbm, tracer_hbm, *refs):
    new_ref, both_ref, near_ref, thick_ref, u_ref, v_ref, tracer_ref, sum_ref, geo_ref, sems = refs
    L, rows, _ = thick_ref.shape
    near, _ = near_rows(rows)
    pairs = ((thick_hbm, thick_ref), (u_hbm, u_ref), (v_hbm, v_ref), (table_hbm.at[lax.axis_index("lat")], geo_ref))
    copies = [pltpu.make_async_copy(a, b, sems.at[i]) for i, (a, b) in enumerate(pairs)]
    for copy in copies:
        copy.start()
    tracer_copy = pltpu.make_async_copy(tracer_hbm, tracer_ref, sems.at[len(copies)])
    tracer_copy.start()
    for copy in copies:
        copy.wait()
    geo = geo_ref[...]
    sum_ref[...] = jnp.zeros_like(sum_ref)

    def level(k, carry):
        thick, u, v = thick_ref[k], u_ref[k], v_ref[k]
        east, north, _ = fluxes(geo, thick, u, v, None, None, None)
        new = thick - (east - west_of(east)) - (north - south_of(north, None)) * geo[0:rows, 2:3]
        new_ref[k] = new
        for j, row in enumerate(near):
            near_ref[0, k, j : j + 1] = new[row : row + 1]
        sum_ref[...] += new
        return carry

    lax.fori_loop(0, L, level, 0)
    for a, at, each in packed_at(rows, L, thick_ref.shape[2]):
        lanes = slice(a * LANES, (a + 1) * LANES)
        both_ref[at : at + rows - 2] = sum_ref[1 : rows - 1, lanes]
        for k in range(L):
            both_ref[each[k] : each[k] + len(near)] = near_ref[0, k, :, lanes]
    tracer_copy.wait()


def first_step(table, thickness, wind_u, wind_v, tracers):
    L, R, N = thickness.shape
    arguments = (thickness, wind_u, wind_v, tracers)
    operands = [pltpu.with_memory_space_constraint(a, pltpu.HBM) for a in (table, *arguments)]
    near = len(near_rows(R)[0])
    shapes = [(L, R, N), ((R - 2 + L * near) * N // LANES, LANES), (1, L, near, N)] + [a.shape for a in arguments]
    return pl.pallas_call(
        first_kernel,
        in_specs=after(operands),
        out_specs=[VMEM] * len(shapes),
        out_shape=[jax.ShapeDtypeStruct(shape, jnp.float32) for shape in shapes],
        scratch_shapes=[
            pltpu.VMEM((R, N), jnp.float32),
            pltpu.VMEM(table.shape[1:], jnp.float32),
            pltpu.SemaphoreType.DMA((5,)),
        ],
        compiler_params=params(),
        cost_estimate=cost(40 * L * R * N, 4 * L * R * N * (7 + 2 * tracers.shape[0])),
        name="first_step",
    )(*operands)


def inner_kernel(table_ref, new_ref, thick_ref, u_ref, v_ref, tracer_ref, out_ref, near_ref):
    T, L, rows, _ = tracer_ref.shape
    near, _ = near_rows(rows)
    geo = table_ref[lax.axis_index("lat")]
    inverse = geo[0:rows, 2:3]

    def level(k, carry):
        thick, u, v, new = thick_ref[k], u_ref[k], v_ref[k], new_ref[k]
        east, north, _ = fluxes(geo, thick, u, v, None, None, None)

        out_ref[0, k] = new
        scale = 1.0 / new
        for c in range(T):
            change = tracer_change(
                tracer_ref[c, k], None, None, thick, u, v, None, east, north, None, inverse
            )
            value = change * scale
            out_ref[1 + c, k] = value
            for j, row in enumerate(near):
                near_ref[pl.ds((c * L + k) * len(near) + j, 1)] = value[row : row + 1]
        return carry

    lax.fori_loop(0, L, level, 0)


def inner_step(table, new, thickness, wind_u, wind_v, tracers):
    L, R, N = thickness.shape
    T = tracers.shape[0]
    rows = jax.ShapeDtypeStruct((T * L * len(near_rows(R)[0]), N), jnp.float32)
    shape = lambda n, rows: jax.ShapeDtypeStruct((n, L, rows, N), jnp.float32)
    return pl.pallas_call(
        inner_kernel,
        in_specs=[VMEM] * 6,
        out_specs=[VMEM] * 2,
        out_shape=[shape(1 + T, R), rows],
        compiler_params=params(),
        cost_estimate=cost(130 * L * R * N, 4 * L * R * N * (8 + 2 * T)),
        name="inner_step",
    )(table, new, thickness, wind_u, wind_v, tracers)


def filter_tables(N):
    A = N // LANES
    b = np.arange(LANES)[:, None]
    p = np.arange(LANES)[None, :]
    tables = []
    for q in range(A // 2 + 1):
        angle = 2.0 * np.pi * ((b * (A * p + q)) % N) / N
        c, s = np.cos(angle), np.sin(angle)
        tables.append(np.block([[c, -s], [s, c]]))
    table = np.stack(tables)
    high = table.astype(np.float32).astype(ml_dtypes.bfloat16)
    low = (table - high.astype(np.float64)).astype(np.float32).astype(ml_dtypes.bfloat16)
    return high, low


def split(value):
    high = value.astype(jnp.bfloat16)
    return high, (value - high.astype(jnp.float32)).astype(jnp.bfloat16)


def product(value, high, low, transposed):
    dims = (((1,), (1 if transposed else 0,)), ((), ()))
    dot = lambda x, y: lax.dot_general(x, y, dims, preferred_element_type=jnp.float32)
    v_high, v_low = split(value)
    return dot(v_high, high) + (dot(v_high, low) + dot(v_low, high))


def filter_rows(x, cutoff, high_ref, low_ref):
    A = len(x)
    N = A * LANES
    half = A // 2
    even = [x[a] + x[A - a] for a in range(1, half + 1)]
    odd = [x[a] - x[A - a] for a in range(1, half + 1)]
    angle = lambda q, a: 2.0 * np.pi * ((q * a) % A) / A
    p = lax.broadcasted_iota(jnp.int32, cutoff.shape, 1)
    real, imag = [], []
    for q in range(half + 1):
        re = x[0]
        for a in range(1, half + 1):
            re = re + (even[a - 1] if q == 0 else float(np.cos(angle(q, a))) * even[a - 1])
        if q == 0:
            high, low = high_ref[0, 0:LANES], low_ref[0, 0:LANES]
            spectrum = product(re, high, low, False)
        else:
            high, low = high_ref[q], low_ref[q]
            im = -float(np.sin(angle(q, 1))) * odd[0]
            for a in range(2, half + 1):
                im = im - float(np.sin(angle(q, a))) * odd[a - 1]
            spectrum = product(jnp.concatenate([re, im], axis=1), high, low, False)
        mode = A * p + q
        factor = 1.0 / N if q == 0 else 2.0 / N
        kept = jnp.where(jnp.minimum(mode, N - mode) <= cutoff, factor, 0.0)
        back = product(spectrum * jnp.concatenate([kept, kept], axis=1), high, low, True)
        real.append(back[:, :LANES])
        imag.append(back[:, LANES:])
    out = [None] * A
    out[0] = functools.reduce(jnp.add, real)
    for a in range(1, half + 1):
        even_part, odd_part = real[0], None
        for q in range(1, half + 1):
            even_part = even_part + float(np.cos(angle(q, a))) * real[q]
            term = float(np.sin(angle(q, a))) * imag[q]
            odd_part = term if odd_part is None else odd_part + term
        out[a] = even_part - odd_part
        out[A - a] = even_part + odd_part
    return out


def second_kernel(
    lat_rows, table_ref, thick_ref, u_ref, v_ref, tracer_ref, up_ref, down_ref, cutoff_ref, high_ref, low_ref, *refs
):
    *wind_refs, edge_ref, new_wind = refs
    k = pl.program_id(0)
    _, L, rows, width = new_wind.shape
    band = lax.axis_index("lat")
    geo = table_ref[band]
    thick, u, v = thick_ref[0], u_ref[0], v_ref[0]
    thick_s, v_s = up_ref[0, 0], up_ref[1, 0]
    thick_n, thick_nn, u_n, v_n = (down_ref[i, 0] for i in range(4))
    east, north, below = fluxes(geo, thick, u, v, thick_s, v_s, thick_n)
    inverse = geo[0:rows, 2:3]
    new = thick - (east - west_of(east)) - (north - south_of(north, below)) * inverse
    east_n = u_n * jnp.where(u_n > 0, thick_n, east_of(thick_n))
    north_n = v_n * jnp.where(v_n > 0, thick_n, thick_nn) * geo[rows : rows + 1, 1:2]
    new_n = (
        thick_n
        - (east_n - west_of(east_n))
        - (north_n - north[rows - 1 : rows]) * geo[rows : rows + 1, 2:3]
    )
    new_wind[0, k] = u - 0.05 * (east_of(new) - new)
    inside = band * rows + row_ids(new.shape) < lat_rows - 1
    new_wind[1, k] = jnp.where(inside, v - 0.05 * (north_of(new, new_n) - new), 0.0)

    def store_edges(field, level, value):
        edge_ref[field, level, 0:1] = value[0:1]
        edge_ref[field, level, 1:2] = value[rows - 1 : rows]

    store_edges(0, k, new)
    scale = 1.0 / new
    for c in range(tracer_ref.shape[0]):
        change = tracer_change(
            tracer_ref[c, 0], up_ref[2 + c, 0], down_ref[4 + c, 0], thick, u, v, v_s, east, north, below, inverse
        )
        store_edges(3 + c, k, change * scale)

    @pl.when(k == L - 1)
    def _():
        pieces = [
            new_wind[:, :, :, a * LANES : (a + 1) * LANES].reshape(2 * L * rows, LANES) for a in range(width // LANES)
        ]
        cutoff = jnp.broadcast_to(cutoff_ref[...][None], (2 * L, rows, LANES)).reshape(2 * L * rows, LANES)
        for a, piece in enumerate(filter_rows(pieces, cutoff, high_ref, low_ref)):
            piece = piece.reshape(2, L, rows, LANES)
            for f in range(2):
                wind_refs[f][0, :, :, a * LANES : (a + 1) * LANES] = piece[f]
        for f in range(2):
            for level in range(L):
                store_edges(1 + f, level, wind_refs[f][0, level])


def second_step(table, lat_rows, thickness, wind_u, wind_v, tracers, up, down, cutoff):
    L, R, N = thickness.shape
    T = tracers.shape[0]
    high, low = filter_tables(N)
    level = pl.BlockSpec((1, R, N), lambda k: (k, 0, 0))
    some = lambda n, rows: pl.BlockSpec((n, 1, rows, N), lambda k: (0, k, 0, 0))
    whole = lambda shape: pl.BlockSpec(shape, lambda k: (0,) * len(shape))
    return pl.pallas_call(
        functools.partial(second_kernel, lat_rows),
        grid=(L,),
        in_specs=[whole(table.shape), level, level, level, some(T, R), some(2 + T, 1), some(4 + T, 1)]
        + [whole((R, LANES)), whole(high.shape), whole(low.shape)],
        out_specs=[whole((1, L, R, N)), whole((1, L, R, N)), whole((3 + T, L, 2, N))],
        out_shape=[
            jax.ShapeDtypeStruct((1, L, R, N), jnp.float32),
            jax.ShapeDtypeStruct((1, L, R, N), jnp.float32),
            jax.ShapeDtypeStruct((3 + T, L, 2, N), jnp.float32),
        ],
        scratch_shapes=[pltpu.VMEM((2, L, R, N), jnp.float32)],
        compiler_params=params(),
        cost_estimate=cost(12 * 2 * L * R * high.size, 4 * L * R * N * (8 + T)),
        name="second_step",
    )(
        table, thickness, wind_u, wind_v, tracers, up, down,
        jnp.broadcast_to(cutoff[:, None], (R, LANES)), jnp.asarray(high), jnp.asarray(low),
    )


def part_kernel(both_ref, *refs):
    sum_ref, near_ref = refs[-2:]
    rows, width = sum_ref.shape
    _, L, near, _ = near_ref.shape
    sum_ref[...] = jnp.zeros_like(sum_ref)
    for a, at, each in packed_at(rows, L, width):
        lanes = slice(a * LANES, (a + 1) * LANES)
        sum_ref[1 : rows - 1, lanes] = both_ref[at : at + rows - 2]
        for k in range(L):
            near_ref[0, k, :, lanes] = both_ref[each[k] : each[k] + near]


def part(both, shape, wait):
    L, R, N = shape
    return pl.pallas_call(
        part_kernel,
        in_specs=[VMEM] + after(wait),
        out_specs=[VMEM] * 2,
        out_shape=[
            jax.ShapeDtypeStruct((R, N), jnp.float32),
            jax.ShapeDtypeStruct((1, L, len(near_rows(R)[0]), N), jnp.float32),
        ],
        compiler_params=params(),
        cost_estimate=cost(1e11, 1e9),
        name="part",
    )(both, *wait)


def mass_kernel(C, S, *refs):
    other_refs, (base_ref, mass_ref) = refs[: (C - 1) * S], refs[(C - 1) * S :]
    lev = lax.axis_index("lev")
    others_mass, base = None, None
    for s in range(1, C):
        other = functools.reduce(jnp.add, [ref[...] for ref in other_refs[(s - 1) * S : s * S]])
        below = jnp.where(lev >= s, other, 0.0)
        others_mass = other if others_mass is None else others_mass + other
        base = below if base is None else base + below
    base_ref[...] = base
    mass_ref[...] = others_mass


def other_chips(counts, others):
    return pl.pallas_call(
        functools.partial(mass_kernel, *counts),
        in_specs=[VMEM] * len(others),
        out_specs=[VMEM] * 2,
        out_shape=[jax.ShapeDtypeStruct(others[0].shape, jnp.float32)] * 2,
        compiler_params=params(),
        cost_estimate=cost(1, 1),
        name="other_chips",
    )(*others)


def add_weights(weight_ref, sum_ref):
    total = jnp.zeros(weight_ref.shape[1:], jnp.float32)
    for k in range(weight_ref.shape[0]):
        sum_ref[k] = total
        total = total + weight_ref[k]
    sum_ref[weight_ref.shape[0]] = total
    return total


def source_levels(place, counts, thick, others):
    C, S = counts
    lev, sub = place
    spot = [lax.rem(lev - g // S + C, C) * S + lax.rem(sub - g % S + S, S) for g in range(len(thick))]
    group = [functools.reduce(jnp.add, levels) for levels in thick]
    mass = functools.reduce(jnp.add, group)
    base = jnp.zeros_like(mass)
    if others:
        base, mass = others[0], mass + others[1]
    sources = []
    for g, levels in enumerate(thick):
        low = base
        for other in range(len(thick)):
            if other != g:
                low = low + jnp.where(spot[other] < spot[g], group[other], 0.0)
        for m, value in enumerate(levels):
            sources.append((g, m, low, value))
            low = low + value
    return mass, sources


def covered(top, sources):
    return [jnp.minimum(jnp.maximum(top - low, 0.0), value) for _, _, low, value in sources]


def level_of(ref, index):
    return lambda m, at, columns: ref[index, m, at, columns]


def packed_level_of(ref, index, L, rows):
    return lambda m, at, columns: ref[(index * L + m) * rows : (index * L + m + 1) * rows, columns]


def remap_rows(weight_ref, sum_ref, counts, steps, thick_refs, field_refs, other_refs, store):
    C, S = counts
    _, L, R, N = thick_refs[0].shape
    rows = min(R, 8)
    place = lev, sub = lax.axis_index("lev"), lax.axis_index("sub")
    firsts = [(lax.rem(lev + s, C) * S + sub) * L for s in steps]
    weight_sum = add_weights(weight_ref, sum_ref)[0:rows]

    def tile(at, columns):
        thick = [[ref[0, m, at, columns] for m in range(L)] for ref in thick_refs]
        others = [ref[at, columns] for ref in other_refs]
        mass, sources = source_levels(place, counts, thick, others)
        unit = mass / weight_sum
        for index, s in enumerate(steps):
            below = covered(unit * sum_ref[firsts[index], 0:rows], sources)
            for i in range(L):
                upto = covered(unit * sum_ref[firsts[index] + i + 1, 0:rows], sources)
                part = [a - b for a, b in zip(upto, below)]
                below = upto
                target = unit * weight_ref[firsts[index] + i, 0:rows]
                scale = 1.0 / target
                means = []
                for refs in field_refs:
                    terms = [refs[g](m, at, columns) * w for (g, m, _, _), w in zip(sources, part)]
                    means.append(functools.reduce(jnp.add, terms) * scale)
                store(s, i, at, columns, target, means)

    for r in range(0, R, rows):

        def body(c, carry):
            tile(slice(r, r + rows), pl.ds(pl.multiple_of(c * LANES, LANES), LANES))
            return carry

        lax.fori_loop(0, N // LANES, body, 0)


def inner_part(at, margin, rows):
    return max(at.start, margin[0]), min(at.stop, rows - margin[1])


def remap_kernel(counts, steps, fields, margin, with_thickness, sizes, weight_ref, *refs):
    *refs, sum_ref = refs
    C, S = counts
    thick_refs, refs = refs[:S], refs[S:]
    bundles = []
    for _ in range(sizes[0]):
        bundles.append(refs[:S])
        refs = refs[S:]
    other_refs, out_refs = refs[:2], refs[len(refs) - len(steps) - with_thickness :]
    _, L, R, _ = thick_refs[0].shape
    thick_out_ref = out_refs[-1]
    field_refs = [[level_of(ref, index) for ref in bundles[which]] for which, index in fields]

    def store(s, i, at, columns, target, means):
        out_ref = out_refs[steps.index(s)]
        if with_thickness and s == 0:
            thick_out_ref[i, at, columns] = target
        for f, value in enumerate(means):
            if s == 0:
                out_ref[f, i, at, columns] = value
            else:
                lower, upper = inner_part(at, margin, R)
                start = (f * L + i) * (R - sum(margin)) - margin[0]
                out_ref[start + lower : start + upper, columns] = value[lower - at.start : upper - at.start]

    remap_rows(
        weight_ref, sum_ref, counts, steps, thick_refs, field_refs, other_refs, store
    )


def remap_parts(counts, weights, thick, bundles, others, fields, steps, margin, with_thickness=False, wait=()):
    C, S = counts
    _, L, R, N = thick[0].shape
    F = len(fields)
    whole = jax.ShapeDtypeStruct((F, L, R, N), jnp.float32)
    inner = jax.ShapeDtypeStruct((F * L * (R - sum(margin)), N), jnp.float32)
    flat = [a for bundle in bundles for a in bundle]
    out_shape = [whole if s == 0 else inner for s in steps]
    if with_thickness:
        out_shape.append(jax.ShapeDtypeStruct((L, R, N), jnp.float32))
    return pl.pallas_call(
        functools.partial(remap_kernel, counts, tuple(steps), tuple(fields), margin, with_thickness, (len(bundles),)),
        in_specs=[VMEM] * (1 + len(thick) + len(flat) + len(others)) + after(wait),
        out_specs=[VMEM] * len(out_shape),
        out_shape=out_shape,
        scratch_shapes=[pltpu.VMEM((weights.shape[0] + 1, 8, LANES), jnp.float32)],
        compiler_params=params(),
        cost_estimate=cost(len(steps) * S * L * L * R * N * (5 + 2 * F), 4 * R * N * L * (F + 1) * (S + len(steps))),
        name="remap_parts",
    )(weights, *thick, *flat, *others, *wait)


def remap_edge_kernel(counts, weight_ref, *refs):
    *refs, sum_ref = refs
    G = counts[0] * counts[1]
    edge_refs, near_refs, tracer_refs = refs[:G], refs[G : 2 * G], refs[2 * G : 3 * G]
    edge_out_ref, thick_out_ref, near_out_ref = refs[-3:]

    def store_edge(s, i, at, columns, target, means):
        thick_out_ref[i, at, columns] = target
        for f, value in enumerate(means):
            edge_out_ref[f, i, at, columns] = value

    def store_near(s, i, at, columns, target, means):
        for f, value in enumerate(means):
            near_out_ref[f, i, at, columns] = value

    fields = [[level_of(ref, f) for ref in edge_refs] for f in range(1, edge_refs[0].shape[0])]
    remap_rows(weight_ref, sum_ref, counts, (0,), edge_refs, fields, [], store_edge)
    _, L, R, _ = near_refs[0].shape
    fields = [[packed_level_of(ref, f, L, R) for ref in tracer_refs] for f in range(near_out_ref.shape[0])]
    remap_rows(weight_ref, sum_ref, counts, (0,), near_refs, fields, [], store_near)


def remap_edges(counts, weights, edges, near_new, near, wait=()):
    F, L, R, N = edges[0].shape
    T = F - 3
    operands = [*edges, *near_new, *near]
    return pl.pallas_call(
        functools.partial(remap_edge_kernel, counts),
        in_specs=[VMEM] * (1 + len(operands)) + after(wait),
        out_specs=[VMEM] * 3,
        out_shape=[
            jax.ShapeDtypeStruct((F - 1, L, R, N), jnp.float32),
            jax.ShapeDtypeStruct((L, R, N), jnp.float32),
            jax.ShapeDtypeStruct((T, *near_new[0].shape[1:]), jnp.float32),
        ],
        scratch_shapes=[pltpu.VMEM((weights.shape[0] + 1, 8, LANES), jnp.float32)],
        compiler_params=params(),
        cost_estimate=cost(len(edges) * L * L * R * N * 40, 4 * R * N * L * len(operands) * F),
        name="remap_edges",
    )(weights, *operands, *wait)


def finish_kernel(margin, own_ref, near_ref, edge_ref, thick_ref, thick_edge_ref, *refs):
    *arrived_refs, out_ref, thick_out_ref, token_ref = refs
    token_ref[...] = jnp.zeros_like(token_ref)
    T, L, R, _ = out_ref.shape
    thick_out_ref[...] = thick_ref[...]
    for i in range(L):
        for row, j in ((0, 0), (R - 1, 1)):
            thick_out_ref[i, row : row + 1] = thick_edge_ref[i, j : j + 1]
    for f in range(T):
        for i in range(L):
            start, first, end = (f * L + i) * (R - sum(margin)), margin[0], R - margin[1]
            total = own_ref[f, i, first:end]
            for ref in arrived_refs:
                total = total + ref[start : start + end - first]
            out_ref[f, i, first:end] = total
            for row, j in ((0, 0), (R - 1, 1)):
                out_ref[f, i, row : row + 1] = edge_ref[2 + f, i, j : j + 1]
            for j, row in enumerate(near_rows(R)[0]):
                out_ref[f, i, row : row + 1] = near_ref[f, i, j : j + 1]


def finish_tracers(own, near, edge, thick, thick_edge, arrived):
    return pl.pallas_call(
        functools.partial(finish_kernel, near_rows(own.shape[2])[1]),
        in_specs=[VMEM] * (5 + len(arrived)),
        out_specs=[VMEM] * 3,
        out_shape=[
            jax.ShapeDtypeStruct(own.shape, jnp.float32),
            jax.ShapeDtypeStruct(thick.shape, jnp.float32),
            jax.ShapeDtypeStruct((8, LANES), jnp.float32),
        ],
        compiler_params=params(),
        cost_estimate=cost(2 * own.size, 12 * own.size),
        name="finish_tracers",
    )(own, near, edge, thick, thick_edge, *arrived)


def finish_winds_kernel(count, own_ref, edge_ref, *refs):
    arrived_refs, out_refs = refs[:count], refs[-2:]
    _, L, R, N = own_ref.shape
    for f, out_ref in enumerate(out_refs):
        for i in range(L):
            start = (f * L + i) * (R - 2)
            total = own_ref[f, i, 1 : R - 1]
            for ref in arrived_refs:
                total = total + ref[start : start + R - 2]
            out_ref[i, 1 : R - 1] = total
            out_ref[i, 0:1] = edge_ref[f, i, 0:1]
            out_ref[i, R - 1 : R] = edge_ref[f, i, 1:2]


def finish_winds(own, arrived, edge, wait):
    return pl.pallas_call(
        functools.partial(finish_winds_kernel, len(arrived)),
        in_specs=[VMEM] * (2 + len(arrived)) + after(wait),
        out_specs=[VMEM] * 2,
        out_shape=[jax.ShapeDtypeStruct(own.shape[1:], jnp.float32)] * 2,
        compiler_params=params(),
        cost_estimate=cost(own.size, 12 * own.size),
        name="finish_winds",
    )(own, edge, *arrived, *wait)


def edge_kernel(thick_hbm, u_hbm, v_hbm, tracer_hbm, *refs):
    last_ref, leading_ref, top_ref, low_ref, tracer_ref, sems = refs[-6:]
    T, L, R, _ = tracer_hbm.shape
    top = pl.ds(R - 8, 8)
    copies = [
        pltpu.make_async_copy(thick_hbm.at[:, top], top_ref.at[0], sems.at[0]),
        pltpu.make_async_copy(v_hbm.at[:, top], top_ref.at[1], sems.at[1]),
        pltpu.make_async_copy(thick_hbm.at[:, pl.ds(0, 8)], low_ref.at[0], sems.at[2]),
        pltpu.make_async_copy(u_hbm.at[:, pl.ds(0, 8)], low_ref.at[1], sems.at[3]),
        pltpu.make_async_copy(v_hbm.at[:, pl.ds(0, 8)], low_ref.at[2], sems.at[4]),
        pltpu.make_async_copy(tracer_hbm.at[:, :, top], tracer_ref.at[0], sems.at[5]),
        pltpu.make_async_copy(tracer_hbm.at[:, :, pl.ds(0, 8)], tracer_ref.at[1], sems.at[6]),
    ]
    for copy in copies:
        copy.start()
    for copy in copies:
        copy.wait()
    last_ref[0:2] = top_ref[:, :, 7:8]
    last_ref[2 : 2 + T] = tracer_ref[0, :, :, 7:8]
    leading_ref[0] = low_ref[0, :, 0:1]
    leading_ref[1] = low_ref[0, :, 1:2]
    leading_ref[2:4] = low_ref[1:3, :, 0:1]
    leading_ref[4 : 4 + T] = tracer_ref[1, :, :, 0:1]


def edge_rows(thickness, wind_u, wind_v, tracers, wait):
    L, R, N = thickness.shape
    T = tracers.shape[0]
    operands = [pltpu.with_memory_space_constraint(a, pltpu.HBM) for a in (thickness, wind_u, wind_v, tracers)]
    return pl.pallas_call(
        edge_kernel,
        in_specs=after(operands) + after(wait),
        out_specs=[VMEM] * 2,
        out_shape=[
            jax.ShapeDtypeStruct((2 + T, L, 1, N), jnp.float32),
            jax.ShapeDtypeStruct((4 + T, L, 1, N), jnp.float32),
        ],
        scratch_shapes=[
            pltpu.VMEM((2, L, 8, N), jnp.float32),
            pltpu.VMEM((3, L, 8, N), jnp.float32),
            pltpu.VMEM((2, T, L, 8, N), jnp.float32),
            pltpu.SemaphoreType.DMA((7,)),
        ],
        compiler_params=params(),
        cost_estimate=cost(1e10, 1e9),
        name="edge_rows",
    )(*operands, *wait)


def shifted(value, lev_count, sub_count, s, t):
    if t == 0:
        return lax.ppermute(value, "lev", [(i, (i + s) % lev_count) for i in range(lev_count)])
    if s == 0:
        return lax.ppermute(value, "sub", [(i, (i + t) % sub_count) for i in range(sub_count)])
    pairs = [
        (i * sub_count + j, (i + s) % lev_count * sub_count + (j + t) % sub_count)
        for i in range(lev_count)
        for j in range(sub_count)
    ]
    return lax.ppermute(value, ("lev", "sub"), pairs)


def per_device(thickness, wind_u, wind_v, tracers, level_weights, cutoff):
    L, R, N = thickness.shape
    lat_count = lax.axis_size("lat")
    C, S = lax.axis_size("lev"), lax.axis_size("sub")
    lat_rows = R * lat_count
    send = functools.partial(shifted, lev_count=C, sub_count=S)

    T = tracers.shape[0]
    northward = [(i, i + 1) for i in range(lat_count - 1)]
    southward = [(j, i) for i, j in northward]
    table = jnp.asarray(geometry_table(lat_rows, R))
    weights = jnp.broadcast_to(level_weights[:, None, None], (level_weights.shape[0], 8, LANES))
    away = range(1, C)

    def with_others_of_chip(own):
        return [own] + [send(own, s=0, t=t) for t in range(1, S)]

    def sent(parts):
        return [send(part, s=s, t=0) for s, part in zip(away, parts)]

    remap = functools.partial(remap_parts, (C, S), weights)

    new, both, near_new, *arguments = first_step(table, thickness, wind_u, wind_v, tracers)
    both = [send(both, s=s, t=0) for s in away]
    inner, near = inner_step(table, new, *arguments)
    group = with_others_of_chip(inner)
    near = [near] + [send(near, s=s, t=0) for s in away]
    parted = [part(each, (L, R, N), [near[0]]) for each in both]
    near_new = [near_new] + [each[1] for each in parted]
    others = other_chips((C, S), [a for each in parted for a in with_others_of_chip(each[0])])
    tracer_fields = [(0, 1 + c) for c in range(T)]
    away_parts = remap(group, [group], others, tracer_fields, away, near_rows(R)[1])
    arrived = sent(away_parts)

    last, leading = edge_rows(
        thickness, wind_u, wind_v, tracers, [away_parts[0], *near[1:2]]
    )
    up = lax.ppermute(last, "lat", northward)
    down = lax.ppermute(leading, "lat", southward)
    u, v, edge = second_step(table, lat_rows, thickness, wind_u, wind_v, tracers, up, down, cutoff)
    edges = [edge] + [send(edge, s=s, t=0) for s in away]
    winds = [with_others_of_chip(u), with_others_of_chip(v)]
    tracers_own, thick_inner = remap(group, [group], others, tracer_fields, (0,), (0, 0), with_thickness=True, wait=[edge])
    winds_own, *winds_away = remap(
        group, winds, others, [(0, 0), (1, 0)], range(C), (1, 1), wait=[tracers_own, *arrived[:1]]
    )
    winds_arrived = sent(winds_away)
    near_new, near, edges = (
        [a for own in sources for a in with_others_of_chip(own)] for sources in (near_new, near, edges)
    )
    edge_out, thick_edge, near_out = remap_edges(
        (C, S), weights, edges, near_new, near, wait=winds_away[:1]
    )

    tracers_out, thickness_out, token = finish_tracers(
        tracers_own, near_out, edge_out, thick_inner, thick_edge, arrived
    )
    u_out, v_out = finish_winds(winds_own, winds_arrived, edge_out, [token])
    return thickness_out, u_out, v_out, tracers_out


def solution(mesh):
    placed = (
        P(("member", "lev", "sub"), "lat", None),
        P(("member", "lev", "sub"), "lat", None),
        P(("member", "lev", "sub"), "lat", None),
        P("member", ("lev", "sub"), "lat", None),
        P(),
        P("lat"),
    )
    return jax.shard_map(
        per_device,
        mesh=mesh,
        in_specs=placed,
        out_specs=(
            P(("member", "lev", "sub"), "lat", None),
            P(("member", "lev", "sub"), "lat", None),
            P(("member", "lev", "sub"), "lat", None),
            P("member", ("lev", "sub"), "lat", None),
        ),
        check_vma=False,
    )
```

```python
import functools

import jax
import jax.numpy as jnp
import ml_dtypes
import numpy as np
from jax import lax
from jax.experimental import pallas as pl
from jax.experimental.pallas import tpu as pltpu
from jax.sharding import PartitionSpec as P

LANES = 128
VMEM = pl.BlockSpec(memory_space=pltpu.VMEM)


def params():
    return pltpu.CompilerParams(vmem_limit_bytes=16 * 1024 * 1024)


def cost(flops, bytes_accessed):
    return pl.CostEstimate(flops=int(flops), bytes_accessed=int(bytes_accessed), transcendentals=0)


def after(arrays):
    return [pl.BlockSpec(memory_space=pl.ANY)] * len(arrays)


def near_rows(rows):
    return (1, 2, rows - 2), (3, 2)


def geometry_table(lat_rows, band_rows):
    bands = lat_rows // band_rows
    table = np.zeros((bands, band_rows + 8, LANES), np.float32)
    for band in range(bands):
        for j in range(band_rows + 1):
            row = band * band_rows + j
            south = np.sin(row * np.pi / lat_rows) if 0 < row < lat_rows else 0.0
            north = np.sin((row + 1) * np.pi / lat_rows) if row + 1 < lat_rows else 0.0
            table[band, j, 0] = south
            table[band, j, 1] = north
            table[band, j, 2] = 1.0 / np.sin((row + 0.5) * np.pi / lat_rows)
    return table


def east_of(value):
    return pltpu.roll(value, value.shape[1] - 1, 1)


def west_of(value):
    return pltpu.roll(value, 1, 1)


def row_ids(shape):
    return lax.broadcasted_iota(jnp.int32, shape, 0)


def north_of(value, beyond):
    rows = value.shape[0]
    rolled = pltpu.roll(value, rows - 1, 0)
    return rolled if beyond is None else jnp.where(row_ids(value.shape) == rows - 1, beyond, rolled)


def south_of(value, beyond):
    rolled = pltpu.roll(value, 1, 0)
    return rolled if beyond is None else jnp.where(row_ids(value.shape) == 0, beyond, rolled)


def fluxes(geo, thick, u, v, thick_s, v_s, thick_n):
    rows = thick.shape[0]
    east = u * jnp.where(u > 0, thick, east_of(thick))
    north = v * jnp.where(v > 0, thick, north_of(thick, thick_n)) * geo[0:rows, 1:2]
    below = None if v_s is None else v_s * jnp.where(v_s > 0, thick_s, thick[0:1]) * geo[0:1, 0:1]
    return east, north, below


def tracer_change(q, q_s, q_n, thick, u, v, v_s, east, north, below, inverse):
    t_east = east * jnp.where(u > 0, q, east_of(q))
    t_north = north * jnp.where(v > 0, q, north_of(q, q_n))
    t_below = None if v_s is None else below * jnp.where(v_s > 0, q_s, q[0:1])
    change = thick * q - (t_east - west_of(t_east))
    return change - (t_north - south_of(t_north, t_below)) * inverse


def packed_at(rows, levels, width):
    near = len(near_rows(rows)[0])
    size = rows - 2 + levels * near
    for a in range(width // LANES):
        yield a, a * size, [a * size + rows - 2 + k * near for k in range(levels)]


def first_kernel(table_hbm, thick_hbm, u_hbm, v_hbm, tracer_hbm, *refs):
    new_ref, both_ref, near_ref, thick_ref, u_ref, v_ref, tracer_ref, sum_ref, geo_ref, sems = refs
    L, rows, _ = thick_ref.shape
    near, _ = near_rows(rows)
    table_copy = pltpu.make_async_copy(table_hbm.at[lax.axis_index("lat")], geo_ref, sems.at[3, 0])
    table_copy.start()
    pairs = ((thick_hbm, thick_ref), (u_hbm, u_ref), (v_hbm, v_ref))

    def copies(k):
        return [pltpu.make_async_copy(a.at[k], b.at[k], sems.at[i, k]) for i, (a, b) in enumerate(pairs)]

    for k in range(L):
        for copy in copies(k):
            copy.start()
    tracer_copy = pltpu.make_async_copy(tracer_hbm, tracer_ref, sems.at[3, 1])
    tracer_copy.start()
    table_copy.wait()
    geo = geo_ref[...]
    sum_ref[...] = jnp.zeros_like(sum_ref)

    def level(k, carry):
        for copy in copies(k):
            copy.wait()
        thick, u, v = thick_ref[k], u_ref[k], v_ref[k]
        east, north, _ = fluxes(geo, thick, u, v, None, None, None)
        new = thick - (east - west_of(east)) - (north - south_of(north, None)) * geo[0:rows, 2:3]
        new_ref[k] = new
        for j, row in enumerate(near):
            near_ref[0, k, j : j + 1] = new[row : row + 1]
        sum_ref[...] += new
        return carry

    lax.fori_loop(0, L, level, 0)
    for a, at, each in packed_at(rows, L, thick_ref.shape[2]):
        lanes = slice(a * LANES, (a + 1) * LANES)
        both_ref[at : at + rows - 2] = sum_ref[1 : rows - 1, lanes]
        for k in range(L):
            both_ref[each[k] : each[k] + len(near)] = near_ref[0, k, :, lanes]
    tracer_copy.wait()


def first_step(table, thickness, wind_u, wind_v, tracers):
    L, R, N = thickness.shape
    arguments = (thickness, wind_u, wind_v, tracers)
    operands = [pltpu.with_memory_space_constraint(a, pltpu.HBM) for a in (table, *arguments)]
    near = len(near_rows(R)[0])
    shapes = [(L, R, N), ((R - 2 + L * near) * N // LANES, LANES), (1, L, near, N)] + [a.shape for a in arguments]
    return pl.pallas_call(
        first_kernel,
        in_specs=after(operands),
        out_specs=[VMEM] * len(shapes),
        out_shape=[jax.ShapeDtypeStruct(shape, jnp.float32) for shape in shapes],
        scratch_shapes=[
            pltpu.VMEM((R, N), jnp.float32),
            pltpu.VMEM(table.shape[1:], jnp.float32),
            pltpu.SemaphoreType.DMA((4, max(L, 2))),
        ],
        compiler_params=params(),
        cost_estimate=cost(40 * L * R * N, 4 * L * R * N * (7 + 2 * tracers.shape[0])),
        name="first_step",
    )(*operands)


def inner_kernel(table_ref, new_ref, thick_ref, u_ref, v_ref, tracer_ref, out_ref, near_ref):
    T, L, rows, _ = tracer_ref.shape
    near, _ = near_rows(rows)
    geo = table_ref[lax.axis_index("lat")]
    inverse = geo[0:rows, 2:3]

    def level(k, carry):
        thick, u, v, new = thick_ref[k], u_ref[k], v_ref[k], new_ref[k]
        east, north, _ = fluxes(geo, thick, u, v, None, None, None)

        out_ref[0, k] = new
        scale = 1.0 / new
        for c in range(T):
            change = tracer_change(
                tracer_ref[c, k], None, None, thick, u, v, None, east, north, None, inverse
            )
            value = change * scale
            out_ref[1 + c, k] = value
            for j, row in enumerate(near):
                near_ref[pl.ds((c * L + k) * len(near) + j, 1)] = value[row : row + 1]
        return carry

    lax.fori_loop(0, L, level, 0)


def inner_step(table, new, thickness, wind_u, wind_v, tracers):
    L, R, N = thickness.shape
    T = tracers.shape[0]
    rows = jax.ShapeDtypeStruct((T * L * len(near_rows(R)[0]), N), jnp.float32)
    shape = lambda n, rows: jax.ShapeDtypeStruct((n, L, rows, N), jnp.float32)
    return pl.pallas_call(
        inner_kernel,
        in_specs=[VMEM] * 6,
        out_specs=[VMEM] * 2,
        out_shape=[shape(1 + T, R), rows],
        compiler_params=params(),
        cost_estimate=cost(130 * L * R * N, 4 * L * R * N * (8 + 2 * T)),
        name="inner_step",
    )(table, new, thickness, wind_u, wind_v, tracers)


def filter_tables(N):
    A = N // LANES
    b = np.arange(LANES)[:, None]
    p = np.arange(LANES)[None, :]
    tables = []
    for q in range(A // 2 + 1):
        angle = 2.0 * np.pi * ((b * (A * p + q)) % N) / N
        c, s = np.cos(angle), np.sin(angle)
        tables.append(np.block([[c, -s], [s, c]]))
    table = np.stack(tables)
    high = table.astype(np.float32).astype(ml_dtypes.bfloat16)
    low = (table - high.astype(np.float64)).astype(np.float32).astype(ml_dtypes.bfloat16)
    return high, low


def split(value):
    high = value.astype(jnp.bfloat16)
    return high, (value - high.astype(jnp.float32)).astype(jnp.bfloat16)


def product(value, high, low, transposed):
    dims = (((1,), (1 if transposed else 0,)), ((), ()))
    dot = lambda x, y: lax.dot_general(x, y, dims, preferred_element_type=jnp.float32)
    v_high, v_low = split(value)
    return dot(v_high, high) + (dot(v_high, low) + dot(v_low, high))


def filter_rows(x, cutoff, high_ref, low_ref):
    A = len(x)
    N = A * LANES
    half = A // 2
    even = [x[a] + x[A - a] for a in range(1, half + 1)]
    odd = [x[a] - x[A - a] for a in range(1, half + 1)]
    angle = lambda q, a: 2.0 * np.pi * ((q * a) % A) / A
    p = lax.broadcasted_iota(jnp.int32, cutoff.shape, 1)
    real, imag = [], []
    for q in range(half + 1):
        re = x[0]
        for a in range(1, half + 1):
            re = re + (even[a - 1] if q == 0 else float(np.cos(angle(q, a))) * even[a - 1])
        if q == 0:
            high, low = high_ref[0, 0:LANES], low_ref[0, 0:LANES]
            spectrum = product(re, high, low, False)
        else:
            high, low = high_ref[q], low_ref[q]
            im = -float(np.sin(angle(q, 1))) * odd[0]
            for a in range(2, half + 1):
                im = im - float(np.sin(angle(q, a))) * odd[a - 1]
            spectrum = product(jnp.concatenate([re, im], axis=1), high, low, False)
        mode = A * p + q
        factor = 1.0 / N if q == 0 else 2.0 / N
        kept = jnp.where(jnp.minimum(mode, N - mode) <= cutoff, factor, 0.0)
        back = product(spectrum * jnp.concatenate([kept, kept], axis=1), high, low, True)
        real.append(back[:, :LANES])
        imag.append(back[:, LANES:])
    out = [None] * A
    out[0] = functools.reduce(jnp.add, real)
    for a in range(1, half + 1):
        even_part, odd_part = real[0], None
        for q in range(1, half + 1):
            even_part = even_part + float(np.cos(angle(q, a))) * real[q]
            term = float(np.sin(angle(q, a))) * imag[q]
            odd_part = term if odd_part is None else odd_part + term
        out[a] = even_part - odd_part
        out[A - a] = even_part + odd_part
    return out


def second_kernel(
    lat_rows, table_ref, thick_ref, u_ref, v_ref, tracer_ref, up_ref, down_ref, cutoff_ref, high_ref, low_ref, *refs
):
    *wind_refs, edge_ref, new_wind = refs
    k = pl.program_id(0)
    _, L, rows, width = new_wind.shape
    band = lax.axis_index("lat")
    geo = table_ref[band]
    thick, u, v = thick_ref[0], u_ref[0], v_ref[0]
    thick_s, v_s = up_ref[0, 0], up_ref[1, 0]
    thick_n, thick_nn, u_n, v_n = (down_ref[i, 0] for i in range(4))
    east, north, below = fluxes(geo, thick, u, v, thick_s, v_s, thick_n)
    inverse = geo[0:rows, 2:3]
    new = thick - (east - west_of(east)) - (north - south_of(north, below)) * inverse
    east_n = u_n * jnp.where(u_n > 0, thick_n, east_of(thick_n))
    north_n = v_n * jnp.where(v_n > 0, thick_n, thick_nn) * geo[rows : rows + 1, 1:2]
    new_n = (
        thick_n
        - (east_n - west_of(east_n))
        - (north_n - north[rows - 1 : rows]) * geo[rows : rows + 1, 2:3]
    )
    new_wind[0, k] = u - 0.05 * (east_of(new) - new)
    inside = band * rows + row_ids(new.shape) < lat_rows - 1
    new_wind[1, k] = jnp.where(inside, v - 0.05 * (north_of(new, new_n) - new), 0.0)

    def store_edges(field, level, value):
        edge_ref[field, level, 0:1] = value[0:1]
        edge_ref[field, level, 1:2] = value[rows - 1 : rows]

    store_edges(0, k, new)
    scale = 1.0 / new
    for c in range(tracer_ref.shape[0]):
        change = tracer_change(
            tracer_ref[c, 0], up_ref[2 + c, 0], down_ref[4 + c, 0], thick, u, v, v_s, east, north, below, inverse
        )
        store_edges(3 + c, k, change * scale)

    @pl.when(k == L - 1)
    def _():
        pieces = [
            new_wind[:, :, :, a * LANES : (a + 1) * LANES].reshape(2 * L * rows, LANES) for a in range(width // LANES)
        ]
        cutoff = jnp.broadcast_to(cutoff_ref[...][None], (2 * L, rows, LANES)).reshape(2 * L * rows, LANES)
        for a, piece in enumerate(filter_rows(pieces, cutoff, high_ref, low_ref)):
            piece = piece.reshape(2, L, rows, LANES)
            for f in range(2):
                wind_refs[f][0, :, :, a * LANES : (a + 1) * LANES] = piece[f]
        for f in range(2):
            for level in range(L):
                store_edges(1 + f, level, wind_refs[f][0, level])


def second_step(table, lat_rows, thickness, wind_u, wind_v, tracers, up, down, cutoff):
    L, R, N = thickness.shape
    T = tracers.shape[0]
    high, low = filter_tables(N)
    level = pl.BlockSpec((1, R, N), lambda k: (k, 0, 0))
    some = lambda n, rows: pl.BlockSpec((n, 1, rows, N), lambda k: (0, k, 0, 0))
    whole = lambda shape: pl.BlockSpec(shape, lambda k: (0,) * len(shape))
    return pl.pallas_call(
        functools.partial(second_kernel, lat_rows),
        grid=(L,),
        in_specs=[whole(table.shape), level, level, level, some(T, R), some(2 + T, 1), some(4 + T, 1)]
        + [whole((R, LANES)), whole(high.shape), whole(low.shape)],
        out_specs=[whole((1, L, R, N)), whole((1, L, R, N)), whole((3 + T, L, 2, N))],
        out_shape=[
            jax.ShapeDtypeStruct((1, L, R, N), jnp.float32),
            jax.ShapeDtypeStruct((1, L, R, N), jnp.float32),
            jax.ShapeDtypeStruct((3 + T, L, 2, N), jnp.float32),
        ],
        scratch_shapes=[pltpu.VMEM((2, L, R, N), jnp.float32)],
        compiler_params=params(),
        cost_estimate=cost(12 * 2 * L * R * high.size, 4 * L * R * N * (8 + T)),
        name="second_step",
    )(
        table, thickness, wind_u, wind_v, tracers, up, down,
        jnp.broadcast_to(cutoff[:, None], (R, LANES)), jnp.asarray(high), jnp.asarray(low),
    )


def part_kernel(both_ref, *refs):
    sum_ref, near_ref = refs[-2:]
    rows, width = sum_ref.shape
    _, L, near, _ = near_ref.shape
    sum_ref[...] = jnp.zeros_like(sum_ref)
    for a, at, each in packed_at(rows, L, width):
        lanes = slice(a * LANES, (a + 1) * LANES)
        sum_ref[1 : rows - 1, lanes] = both_ref[at : at + rows - 2]
        for k in range(L):
            near_ref[0, k, :, lanes] = both_ref[each[k] : each[k] + near]


def part(both, shape, wait):
    L, R, N = shape
    return pl.pallas_call(
        part_kernel,
        in_specs=[VMEM] + after(wait),
        out_specs=[VMEM] * 2,
        out_shape=[
            jax.ShapeDtypeStruct((R, N), jnp.float32),
            jax.ShapeDtypeStruct((1, L, len(near_rows(R)[0]), N), jnp.float32),
        ],
        compiler_params=params(),
        cost_estimate=cost(1e11, 1e9),
        name="part",
    )(both, *wait)


def mass_kernel(C, S, *refs):
    other_refs, (base_ref, mass_ref) = refs[: (C - 1) * S], refs[(C - 1) * S :]
    lev = lax.axis_index("lev")
    others_mass, base = None, None
    for s in range(1, C):
        other = functools.reduce(jnp.add, [ref[...] for ref in other_refs[(s - 1) * S : s * S]])
        below = jnp.where(lev >= s, other, 0.0)
        others_mass = other if others_mass is None else others_mass + other
        base = below if base is None else base + below
    base_ref[...] = base
    mass_ref[...] = others_mass


def other_chips(counts, others):
    return pl.pallas_call(
        functools.partial(mass_kernel, *counts),
        in_specs=[VMEM] * len(others),
        out_specs=[VMEM] * 2,
        out_shape=[jax.ShapeDtypeStruct(others[0].shape, jnp.float32)] * 2,
        compiler_params=params(),
        cost_estimate=cost(1, 1),
        name="other_chips",
    )(*others)


def add_weights(weight_ref, sum_ref):
    total = jnp.zeros(weight_ref.shape[1:], jnp.float32)
    for k in range(weight_ref.shape[0]):
        sum_ref[k] = total
        total = total + weight_ref[k]
    sum_ref[weight_ref.shape[0]] = total
    return total


def source_levels(place, counts, thick, others):
    C, S = counts
    lev, sub = place
    spot = [lax.rem(lev - g // S + C, C) * S + lax.rem(sub - g % S + S, S) for g in range(len(thick))]
    group = [functools.reduce(jnp.add, levels) for levels in thick]
    mass = functools.reduce(jnp.add, group)
    base = jnp.zeros_like(mass)
    if others:
        base, mass = others[0], mass + others[1]
    sources = []
    for g, levels in enumerate(thick):
        low = base
        for other in range(len(thick)):
            if other != g:
                low = low + jnp.where(spot[other] < spot[g], group[other], 0.0)
        for m, value in enumerate(levels):
            sources.append((g, m, low, value))
            low = low + value
    return mass, sources


def covered(top, sources):
    return [jnp.minimum(jnp.maximum(top - low, 0.0), value) for _, _, low, value in sources]


def level_of(ref, index):
    return lambda m, at, columns: ref[index, m, at, columns]


def packed_level_of(ref, index, L, rows):
    return lambda m, at, columns: ref[(index * L + m) * rows : (index * L + m + 1) * rows, columns]


def remap_rows(weight_ref, sum_ref, counts, steps, thick_refs, field_refs, other_refs, store):
    C, S = counts
    _, L, R, N = thick_refs[0].shape
    rows = min(R, 8)
    place = lev, sub = lax.axis_index("lev"), lax.axis_index("sub")
    firsts = [(lax.rem(lev + s, C) * S + sub) * L for s in steps]
    weight_sum = add_weights(weight_ref, sum_ref)[0:rows]

    def tile(at, columns):
        thick = [[ref[0, m, at, columns] for m in range(L)] for ref in thick_refs]
        others = [ref[at, columns] for ref in other_refs]
        mass, sources = source_levels(place, counts, thick, others)
        unit = mass / weight_sum
        for index, s in enumerate(steps):
            below = covered(unit * sum_ref[firsts[index], 0:rows], sources)
            for i in range(L):
                upto = covered(unit * sum_ref[firsts[index] + i + 1, 0:rows], sources)
                part = [a - b for a, b in zip(upto, below)]
                below = upto
                target = unit * weight_ref[firsts[index] + i, 0:rows]
                scale = 1.0 / target
                means = []
                for refs in field_refs:
                    terms = [refs[g](m, at, columns) * w for (g, m, _, _), w in zip(sources, part)]
                    means.append(functools.reduce(jnp.add, terms) * scale)
                store(s, i, at, columns, target, means)

    for r in range(0, R, rows):

        def body(c, carry):
            tile(slice(r, r + rows), pl.ds(pl.multiple_of(c * LANES, LANES), LANES))
            return carry

        lax.fori_loop(0, N // LANES, body, 0)


def inner_part(at, margin, rows):
    return max(at.start, margin[0]), min(at.stop, rows - margin[1])


def remap_kernel(counts, steps, fields, margin, with_thickness, sizes, weight_ref, *refs):
    *refs, sum_ref = refs
    C, S = counts
    thick_refs, refs = refs[:S], refs[S:]
    bundles = []
    for _ in range(sizes[0]):
        bundles.append(refs[:S])
        refs = refs[S:]
    other_refs, out_refs = refs[:2], refs[len(refs) - len(steps) - with_thickness :]
    _, L, R, _ = thick_refs[0].shape
    thick_out_ref = out_refs[-1]
    field_refs = [[level_of(ref, index) for ref in bundles[which]] for which, index in fields]

    def store(s, i, at, columns, target, means):
        out_ref = out_refs[steps.index(s)]
        if with_thickness and s == 0:
            thick_out_ref[i, at, columns] = target
        for f, value in enumerate(means):
            if s == 0:
                out_ref[f, i, at, columns] = value
            else:
                lower, upper = inner_part(at, margin, R)
                start = (f * L + i) * (R - sum(margin)) - margin[0]
                out_ref[start + lower : start + upper, columns] = value[lower - at.start : upper - at.start]

    remap_rows(
        weight_ref, sum_ref, counts, steps, thick_refs, field_refs, other_refs, store
    )


def remap_parts(counts, weights, thick, bundles, others, fields, steps, margin, with_thickness=False, wait=()):
    C, S = counts
    _, L, R, N = thick[0].shape
    F = len(fields)
    whole = jax.ShapeDtypeStruct((F, L, R, N), jnp.float32)
    inner = jax.ShapeDtypeStruct((F * L * (R - sum(margin)), N), jnp.float32)
    flat = [a for bundle in bundles for a in bundle]
    out_shape = [whole if s == 0 else inner for s in steps]
    if with_thickness:
        out_shape.append(jax.ShapeDtypeStruct((L, R, N), jnp.float32))
    return pl.pallas_call(
        functools.partial(remap_kernel, counts, tuple(steps), tuple(fields), margin, with_thickness, (len(bundles),)),
        in_specs=[VMEM] * (1 + len(thick) + len(flat) + len(others)) + after(wait),
        out_specs=[VMEM] * len(out_shape),
        out_shape=out_shape,
        scratch_shapes=[pltpu.VMEM((weights.shape[0] + 1, 8, LANES), jnp.float32)],
        compiler_params=params(),
        cost_estimate=cost(len(steps) * S * L * L * R * N * (5 + 2 * F), 4 * R * N * L * (F + 1) * (S + len(steps))),
        name="remap_parts",
    )(weights, *thick, *flat, *others, *wait)


def remap_edge_kernel(counts, weight_ref, *refs):
    *refs, sum_ref = refs
    G = counts[0] * counts[1]
    edge_refs, near_refs, tracer_refs = refs[:G], refs[G : 2 * G], refs[2 * G : 3 * G]
    edge_out_ref, thick_out_ref, near_out_ref = refs[-3:]

    def store_edge(s, i, at, columns, target, means):
        thick_out_ref[i, at, columns] = target
        for f, value in enumerate(means):
            edge_out_ref[f, i, at, columns] = value

    def store_near(s, i, at, columns, target, means):
        for f, value in enumerate(means):
            near_out_ref[f, i, at, columns] = value

    fields = [[level_of(ref, f) for ref in edge_refs] for f in range(1, edge_refs[0].shape[0])]
    remap_rows(weight_ref, sum_ref, counts, (0,), edge_refs, fields, [], store_edge)
    _, L, R, _ = near_refs[0].shape
    fields = [[packed_level_of(ref, f, L, R) for ref in tracer_refs] for f in range(near_out_ref.shape[0])]
    remap_rows(weight_ref, sum_ref, counts, (0,), near_refs, fields, [], store_near)


def remap_edges(counts, weights, edges, near_new, near, wait=()):
    F, L, R, N = edges[0].shape
    T = F - 3
    operands = [*edges, *near_new, *near]
    return pl.pallas_call(
        functools.partial(remap_edge_kernel, counts),
        in_specs=[VMEM] * (1 + len(operands)) + after(wait),
        out_specs=[VMEM] * 3,
        out_shape=[
            jax.ShapeDtypeStruct((F - 1, L, R, N), jnp.float32),
            jax.ShapeDtypeStruct((L, R, N), jnp.float32),
            jax.ShapeDtypeStruct((T, *near_new[0].shape[1:]), jnp.float32),
        ],
        scratch_shapes=[pltpu.VMEM((weights.shape[0] + 1, 8, LANES), jnp.float32)],
        compiler_params=params(),
        cost_estimate=cost(len(edges) * L * L * R * N * 40, 4 * R * N * L * len(operands) * F),
        name="remap_edges",
    )(weights, *operands, *wait)


def finish_kernel(margin, own_ref, near_ref, edge_ref, thick_ref, thick_edge_ref, *refs):
    *arrived_refs, out_ref, thick_out_ref, token_ref = refs
    token_ref[...] = jnp.zeros_like(token_ref)
    T, L, R, _ = out_ref.shape
    thick_out_ref[...] = thick_ref[...]
    for i in range(L):
        for row, j in ((0, 0), (R - 1, 1)):
            thick_out_ref[i, row : row + 1] = thick_edge_ref[i, j : j + 1]
    for f in range(T):
        for i in range(L):
            start, first, end = (f * L + i) * (R - sum(margin)), margin[0], R - margin[1]
            total = own_ref[f, i, first:end]
            for ref in arrived_refs:
                total = total + ref[start : start + end - first]
            out_ref[f, i, first:end] = total
            for row, j in ((0, 0), (R - 1, 1)):
                out_ref[f, i, row : row + 1] = edge_ref[2 + f, i, j : j + 1]
            for j, row in enumerate(near_rows(R)[0]):
                out_ref[f, i, row : row + 1] = near_ref[f, i, j : j + 1]


def finish_tracers(own, near, edge, thick, thick_edge, arrived):
    return pl.pallas_call(
        functools.partial(finish_kernel, near_rows(own.shape[2])[1]),
        in_specs=[VMEM] * (5 + len(arrived)),
        out_specs=[VMEM] * 3,
        out_shape=[
            jax.ShapeDtypeStruct(own.shape, jnp.float32),
            jax.ShapeDtypeStruct(thick.shape, jnp.float32),
            jax.ShapeDtypeStruct((8, LANES), jnp.float32),
        ],
        compiler_params=params(),
        cost_estimate=cost(2 * own.size, 12 * own.size),
        name="finish_tracers",
    )(own, near, edge, thick, thick_edge, *arrived)


def finish_winds_kernel(count, own_ref, edge_ref, *refs):
    arrived_refs, (*out_refs, result_ref, sems) = refs[:count], refs[len(refs) - 4 :]
    _, L, R, N = own_ref.shape
    row = row_ids((R, N))
    copies = []
    for f, out_ref in enumerate(out_refs):
        for i in range(L):
            start = (f * L + i) * (R - 2)
            first = start // 8 * 8
            total = own_ref[f, i]
            for ref in arrived_refs:
                size = min(R + 8, ref.shape[0] - first)
                total = total + pltpu.roll(ref[first : first + size], (1 - (start - first)) % size, 0)[0:R]
            total = jnp.where(row == 0, edge_ref[f, i, 0:1], jnp.where(row == R - 1, edge_ref[f, i, 1:2], total))
            result_ref[f, i] = total
            copies.append(pltpu.make_async_copy(result_ref.at[f, i], out_ref.at[i], sems.at[f, i]))
            copies[-1].start()
    for copy in copies:
        copy.wait()


def finish_winds(own, arrived, edge, wait):
    F, L = own.shape[:2]
    return pl.pallas_call(
        functools.partial(finish_winds_kernel, len(arrived)),
        in_specs=[VMEM] * (2 + len(arrived)) + after(wait),
        out_specs=[pl.BlockSpec(memory_space=pl.ANY)] * F,
        out_shape=[jax.ShapeDtypeStruct(own.shape[1:], jnp.float32)] * F,
        scratch_shapes=[pltpu.VMEM(own.shape, jnp.float32), pltpu.SemaphoreType.DMA((F, L))],
        compiler_params=params(),
        cost_estimate=cost(own.size, 12 * own.size),
        name="finish_winds",
    )(own, edge, *arrived, *wait)


def edge_kernel(thick_hbm, u_hbm, v_hbm, tracer_hbm, *refs):
    last_ref, leading_ref, top_ref, low_ref, tracer_ref, sems = refs[-6:]
    T, L, R, _ = tracer_hbm.shape
    top = pl.ds(R - 8, 8)
    copies = [
        pltpu.make_async_copy(thick_hbm.at[:, top], top_ref.at[0], sems.at[0]),
        pltpu.make_async_copy(v_hbm.at[:, top], top_ref.at[1], sems.at[1]),
        pltpu.make_async_copy(thick_hbm.at[:, pl.ds(0, 8)], low_ref.at[0], sems.at[2]),
        pltpu.make_async_copy(u_hbm.at[:, pl.ds(0, 8)], low_ref.at[1], sems.at[3]),
        pltpu.make_async_copy(v_hbm.at[:, pl.ds(0, 8)], low_ref.at[2], sems.at[4]),
        pltpu.make_async_copy(tracer_hbm.at[:, :, top], tracer_ref.at[0], sems.at[5]),
        pltpu.make_async_copy(tracer_hbm.at[:, :, pl.ds(0, 8)], tracer_ref.at[1], sems.at[6]),
    ]
    for copy in copies:
        copy.start()
    for copy in copies:
        copy.wait()
    last_ref[0:2] = top_ref[:, :, 7:8]
    last_ref[2 : 2 + T] = tracer_ref[0, :, :, 7:8]
    leading_ref[0] = low_ref[0, :, 0:1]
    leading_ref[1] = low_ref[0, :, 1:2]
    leading_ref[2:4] = low_ref[1:3, :, 0:1]
    leading_ref[4 : 4 + T] = tracer_ref[1, :, :, 0:1]


def edge_rows(thickness, wind_u, wind_v, tracers, wait):
    L, R, N = thickness.shape
    T = tracers.shape[0]
    operands = [pltpu.with_memory_space_constraint(a, pltpu.HBM) for a in (thickness, wind_u, wind_v, tracers)]
    return pl.pallas_call(
        edge_kernel,
        in_specs=after(operands) + after(wait),
        out_specs=[VMEM] * 2,
        out_shape=[
            jax.ShapeDtypeStruct((2 + T, L, 1, N), jnp.float32),
            jax.ShapeDtypeStruct((4 + T, L, 1, N), jnp.float32),
        ],
        scratch_shapes=[
            pltpu.VMEM((2, L, 8, N), jnp.float32),
            pltpu.VMEM((3, L, 8, N), jnp.float32),
            pltpu.VMEM((2, T, L, 8, N), jnp.float32),
            pltpu.SemaphoreType.DMA((7,)),
        ],
        compiler_params=params(),
        cost_estimate=cost(1e10, 1e9),
        name="edge_rows",
    )(*operands, *wait)


def shifted(value, lev_count, sub_count, s, t):
    if t == 0:
        return lax.ppermute(value, "lev", [(i, (i + s) % lev_count) for i in range(lev_count)])
    if s == 0:
        return lax.ppermute(value, "sub", [(i, (i + t) % sub_count) for i in range(sub_count)])
    pairs = [
        (i * sub_count + j, (i + s) % lev_count * sub_count + (j + t) % sub_count)
        for i in range(lev_count)
        for j in range(sub_count)
    ]
    return lax.ppermute(value, ("lev", "sub"), pairs)


def per_device(thickness, wind_u, wind_v, tracers, level_weights, cutoff):
    L, R, N = thickness.shape
    lat_count = lax.axis_size("lat")
    C, S = lax.axis_size("lev"), lax.axis_size("sub")
    lat_rows = R * lat_count
    send = functools.partial(shifted, lev_count=C, sub_count=S)

    T = tracers.shape[0]
    northward = [(i, i + 1) for i in range(lat_count - 1)]
    southward = [(j, i) for i, j in northward]
    table = jnp.asarray(geometry_table(lat_rows, R))
    weights = jnp.broadcast_to(level_weights[:, None, None], (level_weights.shape[0], 8, LANES))
    away = range(1, C)

    def with_others_of_chip(own):
        return [own] + [send(own, s=0, t=t) for t in range(1, S)]

    def sent(parts):
        return [send(part, s=s, t=0) for s, part in zip(away, parts)]

    remap = functools.partial(remap_parts, (C, S), weights)

    new, both, near_new, *arguments = first_step(table, thickness, wind_u, wind_v, tracers)
    both = [send(both, s=s, t=0) for s in away]
    inner, near = inner_step(table, new, *arguments)
    group = with_others_of_chip(inner)
    near = [near] + [send(near, s=s, t=0) for s in away]
    parted = [part(each, (L, R, N), [near[0]]) for each in both]
    near_new = [near_new] + [each[1] for each in parted]
    others = other_chips((C, S), [a for each in parted for a in with_others_of_chip(each[0])])
    tracer_fields = [(0, 1 + c) for c in range(T)]
    away_parts = remap(group, [group], others, tracer_fields, away, near_rows(R)[1])
    arrived = sent(away_parts)

    last, leading = edge_rows(
        thickness, wind_u, wind_v, tracers, [away_parts[0], *near[1:2]]
    )
    up = lax.ppermute(last, "lat", northward)
    down = lax.ppermute(leading, "lat", southward)
    u, v, edge = second_step(table, lat_rows, thickness, wind_u, wind_v, tracers, up, down, cutoff)
    edges = [edge] + [send(edge, s=s, t=0) for s in away]
    winds = [with_others_of_chip(u), with_others_of_chip(v)]
    tracers_own, thick_inner = remap(group, [group], others, tracer_fields, (0,), (0, 0), with_thickness=True, wait=[edge])
    winds_own, *winds_away = remap(
        group, winds, others, [(0, 0), (1, 0)], range(C), (1, 1), wait=[tracers_own, *arrived[:1]]
    )
    winds_arrived = sent(winds_away)
    near_new, near, edges = (
        [a for own in sources for a in with_others_of_chip(own)] for sources in (near_new, near, edges)
    )
    edge_out, thick_edge, near_out = remap_edges(
        (C, S), weights, edges, near_new, near, wait=winds_away[:1]
    )

    tracers_out, thickness_out, token = finish_tracers(
        tracers_own, near_out, edge_out, thick_inner, thick_edge, arrived
    )
    u_out, v_out = finish_winds(winds_own, winds_arrived, edge_out, [token])
    return thickness_out, u_out, v_out, tracers_out


def solution(mesh):
    placed = (
        P(("member", "lev", "sub"), "lat", None),
        P(("member", "lev", "sub"), "lat", None),
        P(("member", "lev", "sub"), "lat", None),
        P("member", ("lev", "sub"), "lat", None),
        P(),
        P("lat"),
    )
    return jax.shard_map(
        per_device,
        mesh=mesh,
        in_specs=placed,
        out_specs=(
            P(("member", "lev", "sub"), "lat", None),
            P(("member", "lev", "sub"), "lat", None),
            P(("member", "lev", "sub"), "lat", None),
            P("member", ("lev", "sub"), "lat", None),
        ),
        check_vma=False,
    )
```

```python
import functools

import jax
import jax.numpy as jnp
import ml_dtypes
import numpy as np
from jax import lax
from jax.experimental import pallas as pl
from jax.experimental.pallas import tpu as pltpu
from jax.sharding import PartitionSpec as P

LANES = 128
VMEM = pl.BlockSpec(memory_space=pltpu.VMEM)


def params():
    return pltpu.CompilerParams(vmem_limit_bytes=16 * 1024 * 1024)


def cost(flops, bytes_accessed):
    return pl.CostEstimate(flops=int(flops), bytes_accessed=int(bytes_accessed), transcendentals=0)


def after(arrays):
    return [pl.BlockSpec(memory_space=pl.ANY)] * len(arrays)


def near_rows(rows):
    return (1, 2, rows - 2), (3, 2)


def geometry_table(lat_rows, band_rows):
    bands = lat_rows // band_rows
    table = np.zeros((bands, band_rows + 8, LANES), np.float32)
    for band in range(bands):
        for j in range(band_rows + 1):
            row = band * band_rows + j
            south = np.sin(row * np.pi / lat_rows) if 0 < row < lat_rows else 0.0
            north = np.sin((row + 1) * np.pi / lat_rows) if row + 1 < lat_rows else 0.0
            table[band, j, 0] = south
            table[band, j, 1] = north
            table[band, j, 2] = 1.0 / np.sin((row + 0.5) * np.pi / lat_rows)
    return table


def east_of(value):
    return pltpu.roll(value, value.shape[1] - 1, 1)


def west_of(value):
    return pltpu.roll(value, 1, 1)


def row_ids(shape):
    return lax.broadcasted_iota(jnp.int32, shape, 0)


def north_of(value, beyond):
    rows = value.shape[0]
    rolled = pltpu.roll(value, rows - 1, 0)
    return rolled if beyond is None else jnp.where(row_ids(value.shape) == rows - 1, beyond, rolled)


def south_of(value, beyond):
    rolled = pltpu.roll(value, 1, 0)
    return rolled if beyond is None else jnp.where(row_ids(value.shape) == 0, beyond, rolled)


def fluxes(geo, thick, u, v, thick_s, v_s, thick_n):
    rows = thick.shape[0]
    east = u * jnp.where(u > 0, thick, east_of(thick))
    north = v * jnp.where(v > 0, thick, north_of(thick, thick_n)) * geo[0:rows, 1:2]
    below = None if v_s is None else v_s * jnp.where(v_s > 0, thick_s, thick[0:1]) * geo[0:1, 0:1]
    return east, north, below


def tracer_change(q, q_s, q_n, thick, u, v, v_s, east, north, below, inverse):
    t_east = east * jnp.where(u > 0, q, east_of(q))
    t_north = north * jnp.where(v > 0, q, north_of(q, q_n))
    t_below = None if v_s is None else below * jnp.where(v_s > 0, q_s, q[0:1])
    change = thick * q - (t_east - west_of(t_east))
    return change - (t_north - south_of(t_north, t_below)) * inverse


def packed_at(rows, levels, width):
    near = len(near_rows(rows)[0])
    size = rows - 2 + levels * near
    for a in range(width // LANES):
        yield a, a * size, [a * size + rows - 2 + k * near for k in range(levels)]


def first_kernel(table_hbm, thick_hbm, u_hbm, v_hbm, tracer_hbm, *refs):
    new_ref, both_ref, near_ref, thick_ref, u_ref, v_ref, tracer_ref, sum_ref, geo_ref, sems = refs
    L, rows, _ = thick_ref.shape
    near, _ = near_rows(rows)
    table_copy = pltpu.make_async_copy(table_hbm.at[lax.axis_index("lat")], geo_ref, sems.at[3, 0])
    table_copy.start()
    pairs = ((thick_hbm, thick_ref), (u_hbm, u_ref), (v_hbm, v_ref))

    def copies(k):
        return [pltpu.make_async_copy(a.at[k], b.at[k], sems.at[i, k]) for i, (a, b) in enumerate(pairs)]

    for k in range(L):
        for copy in copies(k):
            copy.start()
    tracer_copy = pltpu.make_async_copy(tracer_hbm, tracer_ref, sems.at[3, 1])
    tracer_copy.start()
    table_copy.wait()
    geo = geo_ref[...]
    sum_ref[...] = jnp.zeros_like(sum_ref)

    def level(k, carry):
        for copy in copies(k):
            copy.wait()
        thick, u, v = thick_ref[k], u_ref[k], v_ref[k]
        east, north, _ = fluxes(geo, thick, u, v, None, None, None)
        new = thick - (east - west_of(east)) - (north - south_of(north, None)) * geo[0:rows, 2:3]
        new_ref[k] = new
        for j, row in enumerate(near):
            near_ref[0, k, j : j + 1] = new[row : row + 1]
        sum_ref[...] += new
        return carry

    lax.fori_loop(0, L, level, 0)
    for a, at, each in packed_at(rows, L, thick_ref.shape[2]):
        lanes = slice(a * LANES, (a + 1) * LANES)
        both_ref[at : at + rows - 2] = sum_ref[1 : rows - 1, lanes]
        for k in range(L):
            both_ref[each[k] : each[k] + len(near)] = near_ref[0, k, :, lanes]
    tracer_copy.wait()


def first_step(table, thickness, wind_u, wind_v, tracers):
    L, R, N = thickness.shape
    arguments = (thickness, wind_u, wind_v, tracers)
    operands = [pltpu.with_memory_space_constraint(a, pltpu.HBM) for a in (table, *arguments)]
    near = len(near_rows(R)[0])
    shapes = [(L, R, N), ((R - 2 + L * near) * N // LANES, LANES), (1, L, near, N)] + [a.shape for a in arguments]
    return pl.pallas_call(
        first_kernel,
        in_specs=after(operands),
        out_specs=[VMEM] * len(shapes),
        out_shape=[jax.ShapeDtypeStruct(shape, jnp.float32) for shape in shapes],
        scratch_shapes=[
            pltpu.VMEM((R, N), jnp.float32),
            pltpu.VMEM(table.shape[1:], jnp.float32),
            pltpu.SemaphoreType.DMA((4, max(L, 2))),
        ],
        compiler_params=params(),
        cost_estimate=cost(40 * L * R * N, 4 * L * R * N * (7 + 2 * tracers.shape[0])),
        name="first_step",
    )(*operands)


def inner_kernel(table_ref, new_ref, thick_ref, u_ref, v_ref, tracer_ref, out_ref, near_ref):
    T, L, rows, _ = tracer_ref.shape
    near, _ = near_rows(rows)
    geo = table_ref[lax.axis_index("lat")]
    inverse = geo[0:rows, 2:3]

    def level(k, carry):
        thick, u, v, new = thick_ref[k], u_ref[k], v_ref[k], new_ref[k]
        east, north, _ = fluxes(geo, thick, u, v, None, None, None)

        out_ref[0, k] = new
        scale = 1.0 / new
        for c in range(T):
            change = tracer_change(
                tracer_ref[c, k], None, None, thick, u, v, None, east, north, None, inverse
            )
            value = change * scale
            out_ref[1 + c, k] = value
            for j, row in enumerate(near):
                near_ref[pl.ds((c * L + k) * len(near) + j, 1)] = value[row : row + 1]
        return carry

    lax.fori_loop(0, L, level, 0)


def inner_step(table, new, thickness, wind_u, wind_v, tracers):
    L, R, N = thickness.shape
    T = tracers.shape[0]
    rows = jax.ShapeDtypeStruct((T * L * len(near_rows(R)[0]), N), jnp.float32)
    shape = lambda n, rows: jax.ShapeDtypeStruct((n, L, rows, N), jnp.float32)
    return pl.pallas_call(
        inner_kernel,
        in_specs=[VMEM] * 6,
        out_specs=[VMEM] * 2,
        out_shape=[shape(1 + T, R), rows],
        compiler_params=params(),
        cost_estimate=cost(130 * L * R * N, 4 * L * R * N * (8 + 2 * T)),
        name="inner_step",
    )(table, new, thickness, wind_u, wind_v, tracers)


def filter_tables(N):
    A = N // LANES
    b = np.arange(LANES)[:, None]
    p = np.arange(LANES)[None, :]
    tables = []
    for q in range(A // 2 + 1):
        angle = 2.0 * np.pi * ((b * (A * p + q)) % N) / N
        c, s = np.cos(angle), np.sin(angle)
        tables.append(np.block([[c, -s], [s, c]]))
    table = np.stack(tables)
    high = table.astype(np.float32).astype(ml_dtypes.bfloat16)
    low = (table - high.astype(np.float64)).astype(np.float32).astype(ml_dtypes.bfloat16)
    return high, low


def split(value):
    high = value.astype(jnp.bfloat16)
    return high, (value - high.astype(jnp.float32)).astype(jnp.bfloat16)


def product(value, high, low, transposed):
    dims = (((1,), (1 if transposed else 0,)), ((), ()))
    dot = lambda x, y: lax.dot_general(x, y, dims, preferred_element_type=jnp.float32)
    v_high, v_low = split(value)
    return dot(v_high, high) + (dot(v_high, low) + dot(v_low, high))


def filter_rows(x, cutoff, high_ref, low_ref):
    A = len(x)
    N = A * LANES
    half = A // 2
    even = [x[a] + x[A - a] for a in range(1, half + 1)]
    odd = [x[a] - x[A - a] for a in range(1, half + 1)]
    angle = lambda q, a: 2.0 * np.pi * ((q * a) % A) / A
    p = lax.broadcasted_iota(jnp.int32, cutoff.shape, 1)
    real, imag = [], []
    for q in range(half + 1):
        re = x[0]
        for a in range(1, half + 1):
            re = re + (even[a - 1] if q == 0 else float(np.cos(angle(q, a))) * even[a - 1])
        if q == 0:
            high, low = high_ref[0, 0:LANES], low_ref[0, 0:LANES]
            spectrum = product(re, high, low, False)
        else:
            high, low = high_ref[q], low_ref[q]
            im = -float(np.sin(angle(q, 1))) * odd[0]
            for a in range(2, half + 1):
                im = im - float(np.sin(angle(q, a))) * odd[a - 1]
            spectrum = product(jnp.concatenate([re, im], axis=1), high, low, False)
        mode = A * p + q
        factor = 1.0 / N if q == 0 else 2.0 / N
        kept = jnp.where(jnp.minimum(mode, N - mode) <= cutoff, factor, 0.0)
        back = product(spectrum * jnp.concatenate([kept, kept], axis=1), high, low, True)
        real.append(back[:, :LANES])
        imag.append(back[:, LANES:])
    out = [None] * A
    out[0] = functools.reduce(jnp.add, real)
    for a in range(1, half + 1):
        even_part, odd_part = real[0], None
        for q in range(1, half + 1):
            even_part = even_part + float(np.cos(angle(q, a))) * real[q]
            term = float(np.sin(angle(q, a))) * imag[q]
            odd_part = term if odd_part is None else odd_part + term
        out[a] = even_part - odd_part
        out[A - a] = even_part + odd_part
    return out


def second_kernel(
    lat_rows, table_ref, thick_ref, u_ref, v_ref, tracer_ref, up_ref, down_ref, cutoff_ref, high_ref, low_ref, *refs
):
    *wind_refs, edge_ref, new_wind = refs
    k = pl.program_id(0)
    _, L, rows, width = new_wind.shape
    band = lax.axis_index("lat")
    geo = table_ref[band]
    thick, u, v = thick_ref[0], u_ref[0], v_ref[0]
    thick_s, v_s = up_ref[0, 0], up_ref[1, 0]
    thick_n, thick_nn, u_n, v_n = (down_ref[i, 0] for i in range(4))
    east, north, below = fluxes(geo, thick, u, v, thick_s, v_s, thick_n)
    inverse = geo[0:rows, 2:3]
    new = thick - (east - west_of(east)) - (north - south_of(north, below)) * inverse
    east_n = u_n * jnp.where(u_n > 0, thick_n, east_of(thick_n))
    north_n = v_n * jnp.where(v_n > 0, thick_n, thick_nn) * geo[rows : rows + 1, 1:2]
    new_n = (
        thick_n
        - (east_n - west_of(east_n))
        - (north_n - north[rows - 1 : rows]) * geo[rows : rows + 1, 2:3]
    )
    new_wind[0, k] = u - 0.05 * (east_of(new) - new)
    inside = band * rows + row_ids(new.shape) < lat_rows - 1
    new_wind[1, k] = jnp.where(inside, v - 0.05 * (north_of(new, new_n) - new), 0.0)

    def store_edges(field, level, value):
        edge_ref[field, level, 0:1] = value[0:1]
        edge_ref[field, level, 1:2] = value[rows - 1 : rows]

    store_edges(0, k, new)
    scale = 1.0 / new
    for c in range(tracer_ref.shape[0]):
        change = tracer_change(
            tracer_ref[c, 0], up_ref[2 + c, 0], down_ref[4 + c, 0], thick, u, v, v_s, east, north, below, inverse
        )
        store_edges(3 + c, k, change * scale)

    @pl.when(k == L - 1)
    def _():
        pieces = [
            new_wind[:, :, :, a * LANES : (a + 1) * LANES].reshape(2 * L * rows, LANES) for a in range(width // LANES)
        ]
        cutoff = jnp.broadcast_to(cutoff_ref[...][None], (2 * L, rows, LANES)).reshape(2 * L * rows, LANES)
        for a, piece in enumerate(filter_rows(pieces, cutoff, high_ref, low_ref)):
            piece = piece.reshape(2, L, rows, LANES)
            for f in range(2):
                wind_refs[f][0, :, :, a * LANES : (a + 1) * LANES] = piece[f]
        for f in range(2):
            for level in range(L):
                store_edges(1 + f, level, wind_refs[f][0, level])


def second_step(table, lat_rows, thickness, wind_u, wind_v, tracers, up, down, cutoff):
    L, R, N = thickness.shape
    T = tracers.shape[0]
    high, low = filter_tables(N)
    level = pl.BlockSpec((1, R, N), lambda k: (k, 0, 0))
    some = lambda n, rows: pl.BlockSpec((n, 1, rows, N), lambda k: (0, k, 0, 0))
    whole = lambda shape: pl.BlockSpec(shape, lambda k: (0,) * len(shape))
    return pl.pallas_call(
        functools.partial(second_kernel, lat_rows),
        grid=(L,),
        in_specs=[whole(table.shape), level, level, level, some(T, R), some(2 + T, 1), some(4 + T, 1)]
        + [whole((R, LANES)), whole(high.shape), whole(low.shape)],
        out_specs=[whole((1, L, R, N)), whole((1, L, R, N)), whole((3 + T, L, 2, N))],
        out_shape=[
            jax.ShapeDtypeStruct((1, L, R, N), jnp.float32),
            jax.ShapeDtypeStruct((1, L, R, N), jnp.float32),
            jax.ShapeDtypeStruct((3 + T, L, 2, N), jnp.float32),
        ],
        scratch_shapes=[pltpu.VMEM((2, L, R, N), jnp.float32)],
        compiler_params=params(),
        cost_estimate=cost(12 * 2 * L * R * high.size, 4 * L * R * N * (8 + T)),
        name="second_step",
    )(
        table, thickness, wind_u, wind_v, tracers, up, down,
        jnp.broadcast_to(cutoff[:, None], (R, LANES)), jnp.asarray(high), jnp.asarray(low),
    )


def part_kernel(both_ref, *refs):
    sum_ref, near_ref = refs[-2:]
    rows, width = sum_ref.shape
    _, L, near, _ = near_ref.shape
    sum_ref[...] = jnp.zeros_like(sum_ref)
    for a, at, each in packed_at(rows, L, width):
        lanes = slice(a * LANES, (a + 1) * LANES)
        sum_ref[1 : rows - 1, lanes] = both_ref[at : at + rows - 2]
        for k in range(L):
            near_ref[0, k, :, lanes] = both_ref[each[k] : each[k] + near]


def part(both, shape, wait):
    L, R, N = shape
    return pl.pallas_call(
        part_kernel,
        in_specs=[VMEM] + after(wait),
        out_specs=[VMEM] * 2,
        out_shape=[
            jax.ShapeDtypeStruct((R, N), jnp.float32),
            jax.ShapeDtypeStruct((1, L, len(near_rows(R)[0]), N), jnp.float32),
        ],
        compiler_params=params(),
        cost_estimate=cost(1e11, 1e9),
        name="part",
    )(both, *wait)


def mass_kernel(C, S, *refs):
    other_refs, (base_ref, mass_ref) = refs[: (C - 1) * S], refs[(C - 1) * S :]
    lev = lax.axis_index("lev")
    others_mass, base = None, None
    for s in range(1, C):
        other = functools.reduce(jnp.add, [ref[...] for ref in other_refs[(s - 1) * S : s * S]])
        below = jnp.where(lev >= s, other, 0.0)
        others_mass = other if others_mass is None else others_mass + other
        base = below if base is None else base + below
    base_ref[...] = base
    mass_ref[...] = others_mass


def other_chips(counts, others):
    return pl.pallas_call(
        functools.partial(mass_kernel, *counts),
        in_specs=[VMEM] * len(others),
        out_specs=[VMEM] * 2,
        out_shape=[jax.ShapeDtypeStruct(others[0].shape, jnp.float32)] * 2,
        compiler_params=params(),
        cost_estimate=cost(1, 1),
        name="other_chips",
    )(*others)


def add_weights(weight_ref, sum_ref):
    total = jnp.zeros(weight_ref.shape[1:], jnp.float32)
    for k in range(weight_ref.shape[0]):
        sum_ref[k] = total
        total = total + weight_ref[k]
    sum_ref[weight_ref.shape[0]] = total
    return total


def source_levels(place, counts, thick, others):
    C, S = counts
    lev, sub = place
    spot = [lax.rem(lev - g // S + C, C) * S + lax.rem(sub - g % S + S, S) for g in range(len(thick))]
    group = [functools.reduce(jnp.add, levels) for levels in thick]
    mass = functools.reduce(jnp.add, group)
    base = jnp.zeros_like(mass)
    if others:
        base, mass = others[0], mass + others[1]
    sources = []
    for g, levels in enumerate(thick):
        low = base
        for other in range(len(thick)):
            if other != g:
                low = low + jnp.where(spot[other] < spot[g], group[other], 0.0)
        for m, value in enumerate(levels):
            sources.append((g, m, low, value))
            low = low + value
    return mass, sources


def covered(top, sources):
    return [jnp.minimum(jnp.maximum(top - low, 0.0), value) for _, _, low, value in sources]


def level_of(ref, index):
    return lambda m, at, columns: ref[index, m, at, columns]


def packed_level_of(ref, index, L, rows):
    return lambda m, at, columns: ref[(index * L + m) * rows : (index * L + m + 1) * rows, columns]


def remap_rows(weight_ref, sum_ref, counts, steps, thick_refs, field_refs, other_refs, store):
    C, S = counts
    _, L, R, N = thick_refs[0].shape
    rows = min(R, 8)
    place = lev, sub = lax.axis_index("lev"), lax.axis_index("sub")
    firsts = [(lax.rem(lev + s, C) * S + sub) * L for s in steps]
    weight_sum = add_weights(weight_ref, sum_ref)[0:rows]

    def tile(at, columns):
        thick = [[ref[0, m, at, columns] for m in range(L)] for ref in thick_refs]
        others = [ref[at, columns] for ref in other_refs]
        mass, sources = source_levels(place, counts, thick, others)
        unit = mass / weight_sum
        for index, s in enumerate(steps):
            below = covered(unit * sum_ref[firsts[index], 0:rows], sources)
            for i in range(L):
                upto = covered(unit * sum_ref[firsts[index] + i + 1, 0:rows], sources)
                part = [a - b for a, b in zip(upto, below)]
                below = upto
                target = unit * weight_ref[firsts[index] + i, 0:rows]
                scale = 1.0 / target
                means = []
                for refs in field_refs:
                    terms = [refs[g](m, at, columns) * w for (g, m, _, _), w in zip(sources, part)]
                    means.append(functools.reduce(jnp.add, terms) * scale)
                store(s, i, at, columns, target, means)

    for r in range(0, R, rows):

        def body(c, carry):
            tile(slice(r, r + rows), pl.ds(pl.multiple_of(c * LANES, LANES), LANES))
            return carry

        lax.fori_loop(0, N // LANES, body, 0)


def inner_part(at, margin, rows):
    return max(at.start, margin[0]), min(at.stop, rows - margin[1])


def remap_kernel(counts, steps, fields, margin, with_thickness, sizes, weight_ref, *refs):
    *refs, sum_ref = refs
    C, S = counts
    thick_refs, refs = refs[:S], refs[S:]
    bundles = []
    for _ in range(sizes[0]):
        bundles.append(refs[:S])
        refs = refs[S:]
    other_refs, out_refs = refs[:2], refs[len(refs) - len(steps) - with_thickness :]
    _, L, R, _ = thick_refs[0].shape
    thick_out_ref = out_refs[-1]
    field_refs = [[level_of(ref, index) for ref in bundles[which]] for which, index in fields]

    def store(s, i, at, columns, target, means):
        out_ref = out_refs[steps.index(s)]
        if with_thickness and s == 0:
            thick_out_ref[i, at, columns] = target
        for f, value in enumerate(means):
            if s == 0:
                out_ref[f, i, at, columns] = value
            else:
                lower, upper = inner_part(at, margin, R)
                start = (f * L + i) * (R - sum(margin)) - margin[0]
                out_ref[start + lower : start + upper, columns] = value[lower - at.start : upper - at.start]

    remap_rows(
        weight_ref, sum_ref, counts, steps, thick_refs, field_refs, other_refs, store
    )


def remap_parts(counts, weights, thick, bundles, others, fields, steps, margin, with_thickness=False, wait=()):
    C, S = counts
    _, L, R, N = thick[0].shape
    F = len(fields)
    whole = jax.ShapeDtypeStruct((F, L, R, N), jnp.float32)
    inner = jax.ShapeDtypeStruct((F * L * (R - sum(margin)), N), jnp.float32)
    flat = [a for bundle in bundles for a in bundle]
    out_shape = [whole if s == 0 else inner for s in steps]
    if with_thickness:
        out_shape.append(jax.ShapeDtypeStruct((L, R, N), jnp.float32))
    return pl.pallas_call(
        functools.partial(remap_kernel, counts, tuple(steps), tuple(fields), margin, with_thickness, (len(bundles),)),
        in_specs=[VMEM] * (1 + len(thick) + len(flat) + len(others)) + after(wait),
        out_specs=[VMEM] * len(out_shape),
        out_shape=out_shape,
        scratch_shapes=[pltpu.VMEM((weights.shape[0] + 1, 8, LANES), jnp.float32)],
        compiler_params=params(),
        cost_estimate=cost(len(steps) * S * L * L * R * N * (5 + 2 * F), 4 * R * N * L * (F + 1) * (S + len(steps))),
        name="remap_parts",
    )(weights, *thick, *flat, *others, *wait)


def remap_edge_kernel(counts, weight_ref, *refs):
    *refs, sum_ref = refs
    G = counts[0] * counts[1]
    edge_refs, near_refs, tracer_refs = refs[:G], refs[G : 2 * G], refs[2 * G : 3 * G]
    edge_out_ref, thick_out_ref, near_out_ref = refs[-3:]

    def store_edge(s, i, at, columns, target, means):
        thick_out_ref[i, at, columns] = target
        for f, value in enumerate(means):
            edge_out_ref[f, i, at, columns] = value

    def store_near(s, i, at, columns, target, means):
        for f, value in enumerate(means):
            near_out_ref[f, i, at, columns] = value

    fields = [[level_of(ref, f) for ref in edge_refs] for f in range(1, edge_refs[0].shape[0])]
    remap_rows(weight_ref, sum_ref, counts, (0,), edge_refs, fields, [], store_edge)
    _, L, R, _ = near_refs[0].shape
    fields = [[packed_level_of(ref, f, L, R) for ref in tracer_refs] for f in range(near_out_ref.shape[0])]
    remap_rows(weight_ref, sum_ref, counts, (0,), near_refs, fields, [], store_near)


def remap_edges(counts, weights, edges, near_new, near, wait=()):
    F, L, R, N = edges[0].shape
    T = F - 3
    operands = [*edges, *near_new, *near]
    return pl.pallas_call(
        functools.partial(remap_edge_kernel, counts),
        in_specs=[VMEM] * (1 + len(operands)) + after(wait),
        out_specs=[VMEM] * 3,
        out_shape=[
            jax.ShapeDtypeStruct((F - 1, L, R, N), jnp.float32),
            jax.ShapeDtypeStruct((L, R, N), jnp.float32),
            jax.ShapeDtypeStruct((T, *near_new[0].shape[1:]), jnp.float32),
        ],
        scratch_shapes=[pltpu.VMEM((weights.shape[0] + 1, 8, LANES), jnp.float32)],
        compiler_params=params(),
        cost_estimate=cost(len(edges) * L * L * R * N * 40, 4 * R * N * L * len(operands) * F),
        name="remap_edges",
    )(weights, *operands, *wait)


def finish_kernel(margin, own_ref, near_ref, edge_ref, thick_ref, thick_edge_ref, *refs):
    *arrived_refs, out_ref, thick_out_ref, token_ref = refs
    token_ref[...] = jnp.zeros_like(token_ref)
    T, L, R, _ = out_ref.shape
    thick_out_ref[...] = thick_ref[...]
    for i in range(L):
        for row, j in ((0, 0), (R - 1, 1)):
            thick_out_ref[i, row : row + 1] = thick_edge_ref[i, j : j + 1]
    for f in range(T):
        for i in range(L):
            start, first, end = (f * L + i) * (R - sum(margin)), margin[0], R - margin[1]
            total = own_ref[f, i, first:end]
            for ref in arrived_refs:
                total = total + ref[start : start + end - first]
            out_ref[f, i, first:end] = total
            for row, j in ((0, 0), (R - 1, 1)):
                out_ref[f, i, row : row + 1] = edge_ref[2 + f, i, j : j + 1]
            for j, row in enumerate(near_rows(R)[0]):
                out_ref[f, i, row : row + 1] = near_ref[f, i, j : j + 1]


def finish_tracers(own, near, edge, thick, thick_edge, arrived):
    return pl.pallas_call(
        functools.partial(finish_kernel, near_rows(own.shape[2])[1]),
        in_specs=[VMEM] * (5 + len(arrived)),
        out_specs=[VMEM] * 3,
        out_shape=[
            jax.ShapeDtypeStruct(own.shape, jnp.float32),
            jax.ShapeDtypeStruct(thick.shape, jnp.float32),
            jax.ShapeDtypeStruct((8, LANES), jnp.float32),
        ],
        compiler_params=params(),
        cost_estimate=cost(2 * own.size, 12 * own.size),
        name="finish_tracers",
    )(own, near, edge, thick, thick_edge, *arrived)


def finish_winds_kernel(count, own_ref, edge_ref, *refs):
    arrived_refs, (*out_refs, result_ref, sems) = refs[:count], refs[len(refs) - 4 :]
    _, L, R, N = own_ref.shape
    row = row_ids((R, N))
    copies = []
    for f, out_ref in enumerate(out_refs):
        for i in range(L):
            start = (f * L + i) * (R - 2)
            first = start // 8 * 8
            total = own_ref[f, i]
            for ref in arrived_refs:
                size = min(R + 8, ref.shape[0] - first)
                total = total + pltpu.roll(ref[first : first + size], (1 - (start - first)) % size, 0)[0:R]
            total = jnp.where(row == 0, edge_ref[f, i, 0:1], jnp.where(row == R - 1, edge_ref[f, i, 1:2], total))
            result_ref[f, i] = total
            copies.append(pltpu.make_async_copy(result_ref.at[f, i], out_ref.at[i], sems.at[f, i]))
            copies[-1].start()
    for copy in copies:
        copy.wait()


def finish_winds(own, arrived, edge, wait):
    F, L = own.shape[:2]
    return pl.pallas_call(
        functools.partial(finish_winds_kernel, len(arrived)),
        in_specs=[VMEM] * (2 + len(arrived)) + after(wait),
        out_specs=[pl.BlockSpec(memory_space=pl.ANY)] * F,
        out_shape=[jax.ShapeDtypeStruct(own.shape[1:], jnp.float32)] * F,
        scratch_shapes=[pltpu.VMEM(own.shape, jnp.float32), pltpu.SemaphoreType.DMA((F, L))],
        compiler_params=params(),
        cost_estimate=cost(own.size, 12 * own.size),
        name="finish_winds",
    )(own, edge, *arrived, *wait)


def edge_kernel(thick_any, u_any, v_any, tracer_any, *refs):
    last_ref, leading_ref, top_ref, low_ref, tracer_ref, sems = refs[-6:]
    T, L, R, _ = tracer_any.shape
    top = pl.ds(R - 8, 8)
    copies = [
        pltpu.make_async_copy(thick_any.at[:, top], top_ref.at[0], sems.at[0]),
        pltpu.make_async_copy(v_any.at[:, top], top_ref.at[1], sems.at[1]),
        pltpu.make_async_copy(thick_any.at[:, pl.ds(0, 8)], low_ref.at[0], sems.at[2]),
        pltpu.make_async_copy(u_any.at[:, pl.ds(0, 8)], low_ref.at[1], sems.at[3]),
        pltpu.make_async_copy(v_any.at[:, pl.ds(0, 8)], low_ref.at[2], sems.at[4]),
        pltpu.make_async_copy(tracer_any.at[:, :, top], tracer_ref.at[0], sems.at[5]),
        pltpu.make_async_copy(tracer_any.at[:, :, pl.ds(0, 8)], tracer_ref.at[1], sems.at[6]),
    ]
    for copy in copies:
        copy.start()
    for copy in copies:
        copy.wait()
    last_ref[0:2] = top_ref[:, :, 7:8]
    last_ref[2 : 2 + T] = tracer_ref[0, :, :, 7:8]
    leading_ref[0] = low_ref[0, :, 0:1]
    leading_ref[1] = low_ref[0, :, 1:2]
    leading_ref[2:4] = low_ref[1:3, :, 0:1]
    leading_ref[4 : 4 + T] = tracer_ref[1, :, :, 0:1]


def edge_rows(thickness, wind_u, wind_v, tracers, wait):
    L, R, N = thickness.shape
    T = tracers.shape[0]
    operands = [thickness, wind_u, wind_v, tracers]
    return pl.pallas_call(
        edge_kernel,
        in_specs=after(operands) + after(wait),
        out_specs=[VMEM] * 2,
        out_shape=[
            jax.ShapeDtypeStruct((2 + T, L, 1, N), jnp.float32),
            jax.ShapeDtypeStruct((4 + T, L, 1, N), jnp.float32),
        ],
        scratch_shapes=[
            pltpu.VMEM((2, L, 8, N), jnp.float32),
            pltpu.VMEM((3, L, 8, N), jnp.float32),
            pltpu.VMEM((2, T, L, 8, N), jnp.float32),
            pltpu.SemaphoreType.DMA((7,)),
        ],
        compiler_params=params(),
        cost_estimate=cost(1e10, 1e9),
        name="edge_rows",
    )(*operands, *wait)


def shifted(value, lev_count, sub_count, s, t):
    if t == 0:
        return lax.ppermute(value, "lev", [(i, (i + s) % lev_count) for i in range(lev_count)])
    if s == 0:
        return lax.ppermute(value, "sub", [(i, (i + t) % sub_count) for i in range(sub_count)])
    pairs = [
        (i * sub_count + j, (i + s) % lev_count * sub_count + (j + t) % sub_count)
        for i in range(lev_count)
        for j in range(sub_count)
    ]
    return lax.ppermute(value, ("lev", "sub"), pairs)


def per_device(thickness, wind_u, wind_v, tracers, level_weights, cutoff):
    L, R, N = thickness.shape
    lat_count = lax.axis_size("lat")
    C, S = lax.axis_size("lev"), lax.axis_size("sub")
    lat_rows = R * lat_count
    send = functools.partial(shifted, lev_count=C, sub_count=S)

    T = tracers.shape[0]
    northward = [(i, i + 1) for i in range(lat_count - 1)]
    southward = [(j, i) for i, j in northward]
    table = jnp.asarray(geometry_table(lat_rows, R))
    weights = jnp.broadcast_to(level_weights[:, None, None], (level_weights.shape[0], 8, LANES))
    away = range(1, C)

    def with_others_of_chip(own):
        return [own] + [send(own, s=0, t=t) for t in range(1, S)]

    def sent(parts):
        return [send(part, s=s, t=0) for s, part in zip(away, parts)]

    remap = functools.partial(remap_parts, (C, S), weights)

    new, both, near_new, *arguments = first_step(table, thickness, wind_u, wind_v, tracers)
    both = [send(both, s=s, t=0) for s in away]
    inner, near = inner_step(table, new, *arguments)
    group = with_others_of_chip(inner)
    near = [near] + [send(near, s=s, t=0) for s in away]
    parted = [part(each, (L, R, N), [near[0]]) for each in both]
    near_new = [near_new] + [each[1] for each in parted]
    others = other_chips((C, S), [a for each in parted for a in with_others_of_chip(each[0])])
    tracer_fields = [(0, 1 + c) for c in range(T)]
    away_parts = remap(group, [group], others, tracer_fields, away, near_rows(R)[1])
    arrived = sent(away_parts)

    last, leading = edge_rows(
        *arguments, [away_parts[0], *near[1:2]]
    )
    up = lax.ppermute(last, "lat", northward)
    down = lax.ppermute(leading, "lat", southward)
    u, v, edge = second_step(table, lat_rows, *arguments, up, down, cutoff)
    edges = [edge] + [send(edge, s=s, t=0) for s in away]
    winds = [with_others_of_chip(u), with_others_of_chip(v)]
    tracers_own, thick_inner = remap(group, [group], others, tracer_fields, (0,), (0, 0), with_thickness=True, wait=[edge])
    winds_own, *winds_away = remap(
        group, winds, others, [(0, 0), (1, 0)], range(C), (1, 1), wait=[tracers_own, *arrived[:1]]
    )
    winds_arrived = sent(winds_away)
    near_new, near, edges = (
        [a for own in sources for a in with_others_of_chip(own)] for sources in (near_new, near, edges)
    )
    edge_out, thick_edge, near_out = remap_edges(
        (C, S), weights, edges, near_new, near, wait=winds_away[:1]
    )

    tracers_out, thickness_out, token = finish_tracers(
        tracers_own, near_out, edge_out, thick_inner, thick_edge, arrived
    )
    u_out, v_out = finish_winds(winds_own, winds_arrived, edge_out, [token])
    return thickness_out, u_out, v_out, tracers_out


def solution(mesh):
    placed = (
        P(("member", "lev", "sub"), "lat", None),
        P(("member", "lev", "sub"), "lat", None),
        P(("member", "lev", "sub"), "lat", None),
        P("member", ("lev", "sub"), "lat", None),
        P(),
        P("lat"),
    )
    return jax.shard_map(
        per_device,
        mesh=mesh,
        in_specs=placed,
        out_specs=(
            P(("member", "lev", "sub"), "lat", None),
            P(("member", "lev", "sub"), "lat", None),
            P(("member", "lev", "sub"), "lat", None),
            P("member", ("lev", "sub"), "lat", None),
        ),
        check_vma=False,
    )
```

```python
import functools

import jax
import jax.numpy as jnp
import ml_dtypes
import numpy as np
from jax import lax
from jax.experimental import pallas as pl
from jax.experimental.pallas import tpu as pltpu
from jax.sharding import PartitionSpec as P

LANES = 128
VMEM = pl.BlockSpec(memory_space=pltpu.VMEM)


def params():
    return pltpu.CompilerParams(vmem_limit_bytes=16 * 1024 * 1024)


def cost(flops, bytes_accessed):
    return pl.CostEstimate(flops=int(flops), bytes_accessed=int(bytes_accessed), transcendentals=0)


def after(arrays):
    return [pl.BlockSpec(memory_space=pl.ANY)] * len(arrays)


def near_rows(rows):
    return (1, 2, rows - 2), (3, 2)


def geometry_table(lat_rows, band_rows):
    bands = lat_rows // band_rows
    table = np.zeros((bands, band_rows + 8, LANES), np.float32)
    for band in range(bands):
        for j in range(band_rows + 1):
            row = band * band_rows + j
            south = np.sin(row * np.pi / lat_rows) if 0 < row < lat_rows else 0.0
            north = np.sin((row + 1) * np.pi / lat_rows) if row + 1 < lat_rows else 0.0
            table[band, j, 0] = south
            table[band, j, 1] = north
            table[band, j, 2] = 1.0 / np.sin((row + 0.5) * np.pi / lat_rows)
    return table


def east_of(value):
    return pltpu.roll(value, value.shape[1] - 1, 1)


def west_of(value):
    return pltpu.roll(value, 1, 1)


def row_ids(shape):
    return lax.broadcasted_iota(jnp.int32, shape, 0)


def north_of(value, beyond):
    rows = value.shape[0]
    rolled = pltpu.roll(value, rows - 1, 0)
    return rolled if beyond is None else jnp.where(row_ids(value.shape) == rows - 1, beyond, rolled)


def south_of(value, beyond):
    rolled = pltpu.roll(value, 1, 0)
    return rolled if beyond is None else jnp.where(row_ids(value.shape) == 0, beyond, rolled)


def fluxes(geo, thick, u, v, thick_s, v_s, thick_n):
    rows = thick.shape[0]
    east = u * jnp.where(u > 0, thick, east_of(thick))
    north = v * jnp.where(v > 0, thick, north_of(thick, thick_n)) * geo[0:rows, 1:2]
    below = None if v_s is None else v_s * jnp.where(v_s > 0, thick_s, thick[0:1]) * geo[0:1, 0:1]
    return east, north, below


def tracer_change(q, q_s, q_n, thick, u, v, v_s, east, north, below, inverse):
    t_east = east * jnp.where(u > 0, q, east_of(q))
    t_north = north * jnp.where(v > 0, q, north_of(q, q_n))
    t_below = None if v_s is None else below * jnp.where(v_s > 0, q_s, q[0:1])
    change = thick * q - (t_east - west_of(t_east))
    return change - (t_north - south_of(t_north, t_below)) * inverse


def packed_at(rows, levels, width):
    near = len(near_rows(rows)[0])
    size = rows - 2 + levels * near
    for a in range(width // LANES):
        yield a, a * size, [a * size + rows - 2 + k * near for k in range(levels)]


def first_kernel(table_hbm, thick_hbm, u_hbm, v_hbm, tracer_hbm, *refs):
    new_ref, both_ref, near_ref, east_ref, north_ref, thick_ref, u_ref, v_ref, tracer_ref, sum_ref, geo_ref, sems = refs
    L, rows, _ = thick_ref.shape
    near, _ = near_rows(rows)
    table_copy = pltpu.make_async_copy(table_hbm.at[lax.axis_index("lat")], geo_ref, sems.at[3, 0])
    table_copy.start()
    pairs = ((thick_hbm, thick_ref), (u_hbm, u_ref), (v_hbm, v_ref))

    def copies(k):
        return [pltpu.make_async_copy(a.at[k], b.at[k], sems.at[i, k]) for i, (a, b) in enumerate(pairs)]

    for k in range(L):
        for copy in copies(k):
            copy.start()
    tracer_copy = pltpu.make_async_copy(tracer_hbm, tracer_ref, sems.at[3, 1])
    tracer_copy.start()
    table_copy.wait()
    geo = geo_ref[...]
    sum_ref[...] = jnp.zeros_like(sum_ref)

    def level(k, carry):
        for copy in copies(k):
            copy.wait()
        thick, u, v = thick_ref[k], u_ref[k], v_ref[k]
        east, north, _ = fluxes(geo, thick, u, v, None, None, None)
        new = thick - (east - west_of(east)) - (north - south_of(north, None)) * geo[0:rows, 2:3]
        new_ref[k] = new
        east_ref[k] = east
        north_ref[k] = north
        for j, row in enumerate(near):
            near_ref[0, k, j : j + 1] = new[row : row + 1]
        sum_ref[...] += new
        return carry

    lax.fori_loop(0, L, level, 0)
    for a, at, each in packed_at(rows, L, thick_ref.shape[2]):
        lanes = slice(a * LANES, (a + 1) * LANES)
        both_ref[at : at + rows - 2] = sum_ref[1 : rows - 1, lanes]
        for k in range(L):
            both_ref[each[k] : each[k] + len(near)] = near_ref[0, k, :, lanes]
    tracer_copy.wait()


def first_step(table, thickness, wind_u, wind_v, tracers):
    L, R, N = thickness.shape
    arguments = (thickness, wind_u, wind_v, tracers)
    operands = [pltpu.with_memory_space_constraint(a, pltpu.HBM) for a in (table, *arguments)]
    near = len(near_rows(R)[0])
    shapes = [(L, R, N), ((R - 2 + L * near) * N // LANES, LANES), (1, L, near, N), (L, R, N), (L, R, N)] + [a.shape for a in arguments]
    return pl.pallas_call(
        first_kernel,
        in_specs=after(operands),
        out_specs=[VMEM] * len(shapes),
        out_shape=[jax.ShapeDtypeStruct(shape, jnp.float32) for shape in shapes],
        scratch_shapes=[
            pltpu.VMEM((R, N), jnp.float32),
            pltpu.VMEM(table.shape[1:], jnp.float32),
            pltpu.SemaphoreType.DMA((4, max(L, 2))),
        ],
        compiler_params=params(),
        cost_estimate=cost(40 * L * R * N, 4 * L * R * N * (7 + 2 * tracers.shape[0])),
        name="first_step",
    )(*operands)


def inner_kernel(table_ref, new_ref, east_ref, north_ref, thick_ref, u_ref, v_ref, tracer_ref, out_ref, near_ref):
    T, L, rows, _ = tracer_ref.shape
    near, _ = near_rows(rows)
    geo = table_ref[lax.axis_index("lat")]
    inverse = geo[0:rows, 2:3]

    def level(k, carry):
        thick, u, v, new = thick_ref[k], u_ref[k], v_ref[k], new_ref[k]
        east, north = east_ref[k], north_ref[k]

        out_ref[0, k] = new
        scale = 1.0 / new
        for c in range(T):
            change = tracer_change(
                tracer_ref[c, k], None, None, thick, u, v, None, east, north, None, inverse
            )
            value = change * scale
            out_ref[1 + c, k] = value
            for j, row in enumerate(near):
                near_ref[pl.ds((c * L + k) * len(near) + j, 1)] = value[row : row + 1]
        return carry

    lax.fori_loop(0, L, level, 0)


def inner_step(table, new, east, north, thickness, wind_u, wind_v, tracers):
    L, R, N = thickness.shape
    T = tracers.shape[0]
    rows = jax.ShapeDtypeStruct((T * L * len(near_rows(R)[0]), N), jnp.float32)
    shape = lambda n, rows: jax.ShapeDtypeStruct((n, L, rows, N), jnp.float32)
    return pl.pallas_call(
        inner_kernel,
        in_specs=[VMEM] * 8,
        out_specs=[VMEM] * 2,
        out_shape=[shape(1 + T, R), rows],
        compiler_params=params(),
        cost_estimate=cost(130 * L * R * N, 4 * L * R * N * (8 + 2 * T)),
        name="inner_step",
    )(table, new, east, north, thickness, wind_u, wind_v, tracers)


def filter_tables(N):
    A = N // LANES
    b = np.arange(LANES)[:, None]
    p = np.arange(LANES)[None, :]
    tables = []
    for q in range(A // 2 + 1):
        angle = 2.0 * np.pi * ((b * (A * p + q)) % N) / N
        c, s = np.cos(angle), np.sin(angle)
        tables.append(np.block([[c, -s], [s, c]]))
    table = np.stack(tables)
    high = table.astype(np.float32).astype(ml_dtypes.bfloat16)
    low = (table - high.astype(np.float64)).astype(np.float32).astype(ml_dtypes.bfloat16)
    return high, low


def split(value):
    high = value.astype(jnp.bfloat16)
    return high, (value - high.astype(jnp.float32)).astype(jnp.bfloat16)


def product(value, high, low, transposed):
    dims = (((1,), (1 if transposed else 0,)), ((), ()))
    dot = lambda x, y: lax.dot_general(x, y, dims, preferred_element_type=jnp.float32)
    v_high, v_low = split(value)
    return dot(v_high, high) + (dot(v_high, low) + dot(v_low, high))


def filter_rows(x, cutoff, high_ref, low_ref):
    A = len(x)
    N = A * LANES
    half = A // 2
    even = [x[a] + x[A - a] for a in range(1, half + 1)]
    odd = [x[a] - x[A - a] for a in range(1, half + 1)]
    angle = lambda q, a: 2.0 * np.pi * ((q * a) % A) / A
    p = lax.broadcasted_iota(jnp.int32, cutoff.shape, 1)
    real, imag = [], []
    for q in range(half + 1):
        re = x[0]
        for a in range(1, half + 1):
            re = re + (even[a - 1] if q == 0 else float(np.cos(angle(q, a))) * even[a - 1])
        if q == 0:
            high, low = high_ref[0, 0:LANES], low_ref[0, 0:LANES]
            spectrum = product(re, high, low, False)
        else:
            high, low = high_ref[q], low_ref[q]
            im = -float(np.sin(angle(q, 1))) * odd[0]
            for a in range(2, half + 1):
                im = im - float(np.sin(angle(q, a))) * odd[a - 1]
            spectrum = product(jnp.concatenate([re, im], axis=1), high, low, False)
        mode = A * p + q
        factor = 1.0 / N if q == 0 else 2.0 / N
        kept = jnp.where(jnp.minimum(mode, N - mode) <= cutoff, factor, 0.0)
        back = product(spectrum * jnp.concatenate([kept, kept], axis=1), high, low, True)
        real.append(back[:, :LANES])
        imag.append(back[:, LANES:])
    out = [None] * A
    out[0] = functools.reduce(jnp.add, real)
    for a in range(1, half + 1):
        even_part, odd_part = real[0], None
        for q in range(1, half + 1):
            even_part = even_part + float(np.cos(angle(q, a))) * real[q]
            term = float(np.sin(angle(q, a))) * imag[q]
            odd_part = term if odd_part is None else odd_part + term
        out[a] = even_part - odd_part
        out[A - a] = even_part + odd_part
    return out


def second_kernel(
    lat_rows, table_ref, thick_ref, u_ref, v_ref, tracer_ref, up_ref, down_ref, cutoff_ref, high_ref, low_ref, *refs
):
    *wind_refs, edge_ref, new_wind = refs
    k = pl.program_id(0)
    _, L, rows, width = new_wind.shape
    band = lax.axis_index("lat")
    geo = table_ref[band]
    thick, u, v = thick_ref[0], u_ref[0], v_ref[0]
    thick_s, v_s = up_ref[0, 0], up_ref[1, 0]
    thick_n, thick_nn, u_n, v_n = (down_ref[i, 0] for i in range(4))
    east, north, below = fluxes(geo, thick, u, v, thick_s, v_s, thick_n)
    inverse = geo[0:rows, 2:3]
    new = thick - (east - west_of(east)) - (north - south_of(north, below)) * inverse
    east_n = u_n * jnp.where(u_n > 0, thick_n, east_of(thick_n))
    north_n = v_n * jnp.where(v_n > 0, thick_n, thick_nn) * geo[rows : rows + 1, 1:2]
    new_n = (
        thick_n
        - (east_n - west_of(east_n))
        - (north_n - north[rows - 1 : rows]) * geo[rows : rows + 1, 2:3]
    )
    new_wind[0, k] = u - 0.05 * (east_of(new) - new)
    inside = band * rows + row_ids(new.shape) < lat_rows - 1
    new_wind[1, k] = jnp.where(inside, v - 0.05 * (north_of(new, new_n) - new), 0.0)

    def store_edges(field, level, value):
        edge_ref[field, level, 0:1] = value[0:1]
        edge_ref[field, level, 1:2] = value[rows - 1 : rows]

    store_edges(0, k, new)
    scale = 1.0 / new
    for c in range(tracer_ref.shape[0]):
        change = tracer_change(
            tracer_ref[c, 0], up_ref[2 + c, 0], down_ref[4 + c, 0], thick, u, v, v_s, east, north, below, inverse
        )
        store_edges(3 + c, k, change * scale)

    @pl.when(k == L - 1)
    def _():
        pieces = [
            new_wind[:, :, :, a * LANES : (a + 1) * LANES].reshape(2 * L * rows, LANES) for a in range(width // LANES)
        ]
        cutoff = jnp.broadcast_to(cutoff_ref[...][None], (2 * L, rows, LANES)).reshape(2 * L * rows, LANES)
        for a, piece in enumerate(filter_rows(pieces, cutoff, high_ref, low_ref)):
            piece = piece.reshape(2, L, rows, LANES)
            for f in range(2):
                wind_refs[f][0, :, :, a * LANES : (a + 1) * LANES] = piece[f]
        for f in range(2):
            for level in range(L):
                store_edges(1 + f, level, wind_refs[f][0, level])


def second_step(table, lat_rows, thickness, wind_u, wind_v, tracers, up, down, cutoff):
    L, R, N = thickness.shape
    T = tracers.shape[0]
    high, low = filter_tables(N)
    level = pl.BlockSpec((1, R, N), lambda k: (k, 0, 0))
    some = lambda n, rows: pl.BlockSpec((n, 1, rows, N), lambda k: (0, k, 0, 0))
    whole = lambda shape: pl.BlockSpec(shape, lambda k: (0,) * len(shape))
    return pl.pallas_call(
        functools.partial(second_kernel, lat_rows),
        grid=(L,),
        in_specs=[whole(table.shape), level, level, level, some(T, R), some(2 + T, 1), some(4 + T, 1)]
        + [whole((R, LANES)), whole(high.shape), whole(low.shape)],
        out_specs=[whole((1, L, R, N)), whole((1, L, R, N)), whole((3 + T, L, 2, N))],
        out_shape=[
            jax.ShapeDtypeStruct((1, L, R, N), jnp.float32),
            jax.ShapeDtypeStruct((1, L, R, N), jnp.float32),
            jax.ShapeDtypeStruct((3 + T, L, 2, N), jnp.float32),
        ],
        scratch_shapes=[pltpu.VMEM((2, L, R, N), jnp.float32)],
        compiler_params=params(),
        cost_estimate=cost(12 * 2 * L * R * high.size, 4 * L * R * N * (8 + T)),
        name="second_step",
    )(
        table, thickness, wind_u, wind_v, tracers, up, down,
        jnp.broadcast_to(cutoff[:, None], (R, LANES)), jnp.asarray(high), jnp.asarray(low),
    )


def part_kernel(both_ref, *refs):
    sum_ref, near_ref = refs[-2:]
    rows, width = sum_ref.shape
    _, L, near, _ = near_ref.shape
    sum_ref[...] = jnp.zeros_like(sum_ref)
    for a, at, each in packed_at(rows, L, width):
        lanes = slice(a * LANES, (a + 1) * LANES)
        sum_ref[1 : rows - 1, lanes] = both_ref[at : at + rows - 2]
        for k in range(L):
            near_ref[0, k, :, lanes] = both_ref[each[k] : each[k] + near]


def part(both, shape, wait):
    L, R, N = shape
    return pl.pallas_call(
        part_kernel,
        in_specs=[VMEM] + after(wait),
        out_specs=[VMEM] * 2,
        out_shape=[
            jax.ShapeDtypeStruct((R, N), jnp.float32),
            jax.ShapeDtypeStruct((1, L, len(near_rows(R)[0]), N), jnp.float32),
        ],
        compiler_params=params(),
        cost_estimate=cost(1e11, 1e9),
        name="part",
    )(both, *wait)


def mass_kernel(C, S, *refs):
    other_refs, (base_ref, mass_ref) = refs[: (C - 1) * S], refs[(C - 1) * S :]
    lev = lax.axis_index("lev")
    others_mass, base = None, None
    for s in range(1, C):
        other = functools.reduce(jnp.add, [ref[...] for ref in other_refs[(s - 1) * S : s * S]])
        below = jnp.where(lev >= s, other, 0.0)
        others_mass = other if others_mass is None else others_mass + other
        base = below if base is None else base + below
    base_ref[...] = base
    mass_ref[...] = others_mass


def other_chips(counts, others):
    return pl.pallas_call(
        functools.partial(mass_kernel, *counts),
        in_specs=[VMEM] * len(others),
        out_specs=[VMEM] * 2,
        out_shape=[jax.ShapeDtypeStruct(others[0].shape, jnp.float32)] * 2,
        compiler_params=params(),
        cost_estimate=cost(1, 1),
        name="other_chips",
    )(*others)


def add_weights(weight_ref, sum_ref):
    total = jnp.zeros(weight_ref.shape[1:], jnp.float32)
    for k in range(weight_ref.shape[0]):
        sum_ref[k] = total
        total = total + weight_ref[k]
    sum_ref[weight_ref.shape[0]] = total
    return total


def source_levels(place, counts, thick, others):
    C, S = counts
    lev, sub = place
    spot = [lax.rem(lev - g // S + C, C) * S + lax.rem(sub - g % S + S, S) for g in range(len(thick))]
    group = [functools.reduce(jnp.add, levels) for levels in thick]
    mass = functools.reduce(jnp.add, group)
    base = jnp.zeros_like(mass)
    if others:
        base, mass = others[0], mass + others[1]
    sources = []
    for g, levels in enumerate(thick):
        low = base
        for other in range(len(thick)):
            if other != g:
                low = low + jnp.where(spot[other] < spot[g], group[other], 0.0)
        for m, value in enumerate(levels):
            sources.append((g, m, low, value))
            low = low + value
    return mass, sources


def covered(top, sources):
    return [jnp.minimum(jnp.maximum(top - low, 0.0), value) for _, _, low, value in sources]


def level_of(ref, index):
    return lambda m, at, columns: ref[index, m, at, columns]


def packed_level_of(ref, index, L, rows):
    return lambda m, at, columns: ref[(index * L + m) * rows : (index * L + m + 1) * rows, columns]


def remap_rows(weight_ref, sum_ref, counts, steps, thick_refs, field_refs, other_refs, store):
    C, S = counts
    _, L, R, N = thick_refs[0].shape
    rows = min(R, 8)
    place = lev, sub = lax.axis_index("lev"), lax.axis_index("sub")
    firsts = [(lax.rem(lev + s, C) * S + sub) * L for s in steps]
    weight_sum = add_weights(weight_ref, sum_ref)[0:rows]

    def tile(at, columns):
        thick = [[ref[0, m, at, columns] for m in range(L)] for ref in thick_refs]
        others = [ref[at, columns] for ref in other_refs]
        mass, sources = source_levels(place, counts, thick, others)
        unit = mass / weight_sum
        for index, s in enumerate(steps):
            below = covered(unit * sum_ref[firsts[index], 0:rows], sources)
            for i in range(L):
                upto = covered(unit * sum_ref[firsts[index] + i + 1, 0:rows], sources)
                part = [a - b for a, b in zip(upto, below)]
                below = upto
                target = unit * weight_ref[firsts[index] + i, 0:rows]
                scale = 1.0 / target
                means = []
                for refs in field_refs:
                    terms = [refs[g](m, at, columns) * w for (g, m, _, _), w in zip(sources, part)]
                    means.append(functools.reduce(jnp.add, terms) * scale)
                store(s, i, at, columns, target, means)

    for r in range(0, R, rows):

        def body(c, carry):
            tile(slice(r, r + rows), pl.ds(pl.multiple_of(c * LANES, LANES), LANES))
            return carry

        lax.fori_loop(0, N // LANES, body, 0)


def inner_part(at, margin, rows):
    return max(at.start, margin[0]), min(at.stop, rows - margin[1])


def remap_kernel(counts, steps, fields, margin, with_thickness, sizes, weight_ref, *refs):
    *refs, sum_ref = refs
    C, S = counts
    thick_refs, refs = refs[:S], refs[S:]
    bundles = []
    for _ in range(sizes[0]):
        bundles.append(refs[:S])
        refs = refs[S:]
    other_refs, out_refs = refs[:2], refs[len(refs) - len(steps) - with_thickness :]
    _, L, R, _ = thick_refs[0].shape
    thick_out_ref = out_refs[-1]
    field_refs = [[level_of(ref, index) for ref in bundles[which]] for which, index in fields]

    def store(s, i, at, columns, target, means):
        out_ref = out_refs[steps.index(s)]
        if with_thickness and s == 0:
            thick_out_ref[i, at, columns] = target
        for f, value in enumerate(means):
            if s == 0:
                out_ref[f, i, at, columns] = value
            else:
                lower, upper = inner_part(at, margin, R)
                start = (f * L + i) * (R - sum(margin)) - margin[0]
                out_ref[start + lower : start + upper, columns] = value[lower - at.start : upper - at.start]

    remap_rows(
        weight_ref, sum_ref, counts, steps, thick_refs, field_refs, other_refs, store
    )


def remap_parts(counts, weights, thick, bundles, others, fields, steps, margin, with_thickness=False, wait=()):
    C, S = counts
    _, L, R, N = thick[0].shape
    F = len(fields)
    whole = jax.ShapeDtypeStruct((F, L, R, N), jnp.float32)
    inner = jax.ShapeDtypeStruct((F * L * (R - sum(margin)), N), jnp.float32)
    flat = [a for bundle in bundles for a in bundle]
    out_shape = [whole if s == 0 else inner for s in steps]
    if with_thickness:
        out_shape.append(jax.ShapeDtypeStruct((L, R, N), jnp.float32))
    return pl.pallas_call(
        functools.partial(remap_kernel, counts, tuple(steps), tuple(fields), margin, with_thickness, (len(bundles),)),
        in_specs=[VMEM] * (1 + len(thick) + len(flat) + len(others)) + after(wait),
        out_specs=[VMEM] * len(out_shape),
        out_shape=out_shape,
        scratch_shapes=[pltpu.VMEM((weights.shape[0] + 1, 8, LANES), jnp.float32)],
        compiler_params=params(),
        cost_estimate=cost(len(steps) * S * L * L * R * N * (5 + 2 * F), 4 * R * N * L * (F + 1) * (S + len(steps))),
        name="remap_parts",
    )(weights, *thick, *flat, *others, *wait)


def remap_edge_kernel(counts, weight_ref, *refs):
    *refs, sum_ref = refs
    G = counts[0] * counts[1]
    edge_refs, near_refs, tracer_refs = refs[:G], refs[G : 2 * G], refs[2 * G : 3 * G]
    edge_out_ref, thick_out_ref, near_out_ref = refs[-3:]

    def store_edge(s, i, at, columns, target, means):
        thick_out_ref[i, at, columns] = target
        for f, value in enumerate(means):
            edge_out_ref[f, i, at, columns] = value

    def store_near(s, i, at, columns, target, means):
        for f, value in enumerate(means):
            near_out_ref[f, i, at, columns] = value

    fields = [[level_of(ref, f) for ref in edge_refs] for f in range(1, edge_refs[0].shape[0])]
    remap_rows(weight_ref, sum_ref, counts, (0,), edge_refs, fields, [], store_edge)
    _, L, R, _ = near_refs[0].shape
    fields = [[packed_level_of(ref, f, L, R) for ref in tracer_refs] for f in range(near_out_ref.shape[0])]
    remap_rows(weight_ref, sum_ref, counts, (0,), near_refs, fields, [], store_near)


def remap_edges(counts, weights, edges, near_new, near, wait=()):
    F, L, R, N = edges[0].shape
    T = F - 3
    operands = [*edges, *near_new, *near]
    return pl.pallas_call(
        functools.partial(remap_edge_kernel, counts),
        in_specs=[VMEM] * (1 + len(operands)) + after(wait),
        out_specs=[VMEM] * 3,
        out_shape=[
            jax.ShapeDtypeStruct((F - 1, L, R, N), jnp.float32),
            jax.ShapeDtypeStruct((L, R, N), jnp.float32),
            jax.ShapeDtypeStruct((T, *near_new[0].shape[1:]), jnp.float32),
        ],
        scratch_shapes=[pltpu.VMEM((weights.shape[0] + 1, 8, LANES), jnp.float32)],
        compiler_params=params(),
        cost_estimate=cost(len(edges) * L * L * R * N * 40, 4 * R * N * L * len(operands) * F),
        name="remap_edges",
    )(weights, *operands, *wait)


def finish_kernel(margin, own_ref, near_ref, edge_ref, thick_ref, thick_edge_ref, *refs):
    *arrived_refs, out_ref, thick_out_ref, token_ref = refs
    token_ref[...] = jnp.zeros_like(token_ref)
    T, L, R, _ = out_ref.shape
    thick_out_ref[...] = thick_ref[...]
    for i in range(L):
        for row, j in ((0, 0), (R - 1, 1)):
            thick_out_ref[i, row : row + 1] = thick_edge_ref[i, j : j + 1]
    for f in range(T):
        for i in range(L):
            start, first, end = (f * L + i) * (R - sum(margin)), margin[0], R - margin[1]
            total = own_ref[f, i, first:end]
            for ref in arrived_refs:
                total = total + ref[start : start + end - first]
            out_ref[f, i, first:end] = total
            for row, j in ((0, 0), (R - 1, 1)):
                out_ref[f, i, row : row + 1] = edge_ref[2 + f, i, j : j + 1]
            for j, row in enumerate(near_rows(R)[0]):
                out_ref[f, i, row : row + 1] = near_ref[f, i, j : j + 1]


def finish_tracers(own, near, edge, thick, thick_edge, arrived):
    return pl.pallas_call(
        functools.partial(finish_kernel, near_rows(own.shape[2])[1]),
        in_specs=[VMEM] * (5 + len(arrived)),
        out_specs=[VMEM] * 3,
        out_shape=[
            jax.ShapeDtypeStruct(own.shape, jnp.float32),
            jax.ShapeDtypeStruct(thick.shape, jnp.float32),
            jax.ShapeDtypeStruct((8, LANES), jnp.float32),
        ],
        compiler_params=params(),
        cost_estimate=cost(2 * own.size, 12 * own.size),
        name="finish_tracers",
    )(own, near, edge, thick, thick_edge, *arrived)


def finish_winds_kernel(count, own_ref, edge_ref, *refs):
    arrived_refs, (*out_refs, result_ref, sems) = refs[:count], refs[len(refs) - 4 :]
    _, L, R, N = own_ref.shape
    row = row_ids((R, N))
    copies = []
    for f, out_ref in enumerate(out_refs):
        for i in range(L):
            start = (f * L + i) * (R - 2)
            first = start // 8 * 8
            total = own_ref[f, i]
            for ref in arrived_refs:
                size = min(R + 8, ref.shape[0] - first)
                total = total + pltpu.roll(ref[first : first + size], (1 - (start - first)) % size, 0)[0:R]
            total = jnp.where(row == 0, edge_ref[f, i, 0:1], jnp.where(row == R - 1, edge_ref[f, i, 1:2], total))
            result_ref[f, i] = total
            copies.append(pltpu.make_async_copy(result_ref.at[f, i], out_ref.at[i], sems.at[f, i]))
            copies[-1].start()
    for copy in copies:
        copy.wait()


def finish_winds(own, arrived, edge, wait):
    F, L = own.shape[:2]
    return pl.pallas_call(
        functools.partial(finish_winds_kernel, len(arrived)),
        in_specs=[VMEM] * (2 + len(arrived)) + after(wait),
        out_specs=[pl.BlockSpec(memory_space=pl.ANY)] * F,
        out_shape=[jax.ShapeDtypeStruct(own.shape[1:], jnp.float32)] * F,
        scratch_shapes=[pltpu.VMEM(own.shape, jnp.float32), pltpu.SemaphoreType.DMA((F, L))],
        compiler_params=params(),
        cost_estimate=cost(own.size, 12 * own.size),
        name="finish_winds",
    )(own, edge, *arrived, *wait)


def edge_kernel(thick_any, u_any, v_any, tracer_any, *refs):
    last_ref, leading_ref, top_ref, low_ref, tracer_ref, sems = refs[-6:]
    T, L, R, _ = tracer_any.shape
    top = pl.ds(R - 8, 8)
    copies = [
        pltpu.make_async_copy(thick_any.at[:, top], top_ref.at[0], sems.at[0]),
        pltpu.make_async_copy(v_any.at[:, top], top_ref.at[1], sems.at[1]),
        pltpu.make_async_copy(thick_any.at[:, pl.ds(0, 8)], low_ref.at[0], sems.at[2]),
        pltpu.make_async_copy(u_any.at[:, pl.ds(0, 8)], low_ref.at[1], sems.at[3]),
        pltpu.make_async_copy(v_any.at[:, pl.ds(0, 8)], low_ref.at[2], sems.at[4]),
        pltpu.make_async_copy(tracer_any.at[:, :, top], tracer_ref.at[0], sems.at[5]),
        pltpu.make_async_copy(tracer_any.at[:, :, pl.ds(0, 8)], tracer_ref.at[1], sems.at[6]),
    ]
    for copy in copies:
        copy.start()
    for copy in copies:
        copy.wait()
    last_ref[0:2] = top_ref[:, :, 7:8]
    last_ref[2 : 2 + T] = tracer_ref[0, :, :, 7:8]
    leading_ref[0] = low_ref[0, :, 0:1]
    leading_ref[1] = low_ref[0, :, 1:2]
    leading_ref[2:4] = low_ref[1:3, :, 0:1]
    leading_ref[4 : 4 + T] = tracer_ref[1, :, :, 0:1]


def edge_rows(thickness, wind_u, wind_v, tracers, wait):
    L, R, N = thickness.shape
    T = tracers.shape[0]
    operands = [thickness, wind_u, wind_v, tracers]
    return pl.pallas_call(
        edge_kernel,
        in_specs=after(operands) + after(wait),
        out_specs=[VMEM] * 2,
        out_shape=[
            jax.ShapeDtypeStruct((2 + T, L, 1, N), jnp.float32),
            jax.ShapeDtypeStruct((4 + T, L, 1, N), jnp.float32),
        ],
        scratch_shapes=[
            pltpu.VMEM((2, L, 8, N), jnp.float32),
            pltpu.VMEM((3, L, 8, N), jnp.float32),
            pltpu.VMEM((2, T, L, 8, N), jnp.float32),
            pltpu.SemaphoreType.DMA((7,)),
        ],
        compiler_params=params(),
        cost_estimate=cost(1e10, 1e9),
        name="edge_rows",
    )(*operands, *wait)


def shifted(value, lev_count, sub_count, s, t):
    if t == 0:
        return lax.ppermute(value, "lev", [(i, (i + s) % lev_count) for i in range(lev_count)])
    if s == 0:
        return lax.ppermute(value, "sub", [(i, (i + t) % sub_count) for i in range(sub_count)])
    pairs = [
        (i * sub_count + j, (i + s) % lev_count * sub_count + (j + t) % sub_count)
        for i in range(lev_count)
        for j in range(sub_count)
    ]
    return lax.ppermute(value, ("lev", "sub"), pairs)


def per_device(thickness, wind_u, wind_v, tracers, level_weights, cutoff):
    L, R, N = thickness.shape
    lat_count = lax.axis_size("lat")
    C, S = lax.axis_size("lev"), lax.axis_size("sub")
    lat_rows = R * lat_count
    send = functools.partial(shifted, lev_count=C, sub_count=S)

    T = tracers.shape[0]
    northward = [(i, i + 1) for i in range(lat_count - 1)]
    southward = [(j, i) for i, j in northward]
    table = jnp.asarray(geometry_table(lat_rows, R))
    weights = jnp.broadcast_to(level_weights[:, None, None], (level_weights.shape[0], 8, LANES))
    away = range(1, C)

    def with_others_of_chip(own):
        return [own] + [send(own, s=0, t=t) for t in range(1, S)]

    def sent(parts):
        return [send(part, s=s, t=0) for s, part in zip(away, parts)]

    remap = functools.partial(remap_parts, (C, S), weights)

    new, both, near_new, east, north, *arguments = first_step(table, thickness, wind_u, wind_v, tracers)
    both = [send(both, s=s, t=0) for s in away]
    inner, near = inner_step(table, new, east, north, *arguments)
    group = with_others_of_chip(inner)
    near = [near] + [send(near, s=s, t=0) for s in away]
    parted = [part(each, (L, R, N), [near[0]]) for each in both]
    near_new = [near_new] + [each[1] for each in parted]
    others = other_chips((C, S), [a for each in parted for a in with_others_of_chip(each[0])])
    tracer_fields = [(0, 1 + c) for c in range(T)]
    away_parts = remap(group, [group], others, tracer_fields, away, near_rows(R)[1])
    arrived = sent(away_parts)

    last, leading = edge_rows(
        *arguments, [away_parts[0], *near[1:2]]
    )
    up = lax.ppermute(last, "lat", northward)
    down = lax.ppermute(leading, "lat", southward)
    u, v, edge = second_step(table, lat_rows, *arguments, up, down, cutoff)
    edges = [edge] + [send(edge, s=s, t=0) for s in away]
    winds = [with_others_of_chip(u), with_others_of_chip(v)]
    tracers_own, thick_inner = remap(group, [group], others, tracer_fields, (0,), (0, 0), with_thickness=True, wait=[edge])
    winds_own, *winds_away = remap(
        group, winds, others, [(0, 0), (1, 0)], range(C), (1, 1), wait=[tracers_own, *arrived[:1]]
    )
    winds_arrived = sent(winds_away)
    near_new, near, edges = (
        [a for own in sources for a in with_others_of_chip(own)] for sources in (near_new, near, edges)
    )
    edge_out, thick_edge, near_out = remap_edges(
        (C, S), weights, edges, near_new, near, wait=winds_away[:1]
    )

    tracers_out, thickness_out, token = finish_tracers(
        tracers_own, near_out, edge_out, thick_inner, thick_edge, arrived
    )
    u_out, v_out = finish_winds(winds_own, winds_arrived, edge_out, [token])
    return thickness_out, u_out, v_out, tracers_out


def solution(mesh):
    placed = (
        P(("member", "lev", "sub"), "lat", None),
        P(("member", "lev", "sub"), "lat", None),
        P(("member", "lev", "sub"), "lat", None),
        P("member", ("lev", "sub"), "lat", None),
        P(),
        P("lat"),
    )
    return jax.shard_map(
        per_device,
        mesh=mesh,
        in_specs=placed,
        out_specs=(
            P(("member", "lev", "sub"), "lat", None),
            P(("member", "lev", "sub"), "lat", None),
            P(("member", "lev", "sub"), "lat", None),
            P("member", ("lev", "sub"), "lat", None),
        ),
        check_vma=False,
    )
```

```python
import functools

import jax
import jax.numpy as jnp
import ml_dtypes
import numpy as np
from jax import lax
from jax.experimental import pallas as pl
from jax.experimental.pallas import tpu as pltpu
from jax.sharding import PartitionSpec as P

LANES = 128
VMEM = pl.BlockSpec(memory_space=pltpu.VMEM)


def params():
    return pltpu.CompilerParams(vmem_limit_bytes=16 * 1024 * 1024)


def cost(flops, bytes_accessed):
    return pl.CostEstimate(flops=int(flops), bytes_accessed=int(bytes_accessed), transcendentals=0)


def after(arrays):
    return [pl.BlockSpec(memory_space=pl.ANY)] * len(arrays)


def near_rows(rows):
    return (1, rows - 2), (2, 2)


def geometry_table(lat_rows, band_rows):
    bands = lat_rows // band_rows
    table = np.zeros((bands, band_rows + 8, LANES), np.float32)
    for band in range(bands):
        for j in range(band_rows + 1):
            row = band * band_rows + j
            south = np.sin(row * np.pi / lat_rows) if 0 < row < lat_rows else 0.0
            north = np.sin((row + 1) * np.pi / lat_rows) if row + 1 < lat_rows else 0.0
            table[band, j, 0] = south
            table[band, j, 1] = north
            table[band, j, 2] = 1.0 / np.sin((row + 0.5) * np.pi / lat_rows)
    return table


def east_of(value):
    return pltpu.roll(value, value.shape[1] - 1, 1)


def west_of(value):
    return pltpu.roll(value, 1, 1)


def row_ids(shape):
    return lax.broadcasted_iota(jnp.int32, shape, 0)


def north_of(value, beyond):
    rows = value.shape[0]
    rolled = pltpu.roll(value, rows - 1, 0)
    return rolled if beyond is None else jnp.where(row_ids(value.shape) == rows - 1, beyond, rolled)


def south_of(value, beyond):
    rolled = pltpu.roll(value, 1, 0)
    return rolled if beyond is None else jnp.where(row_ids(value.shape) == 0, beyond, rolled)


def fluxes(geo, thick, u, v, thick_s, v_s, thick_n):
    rows = thick.shape[0]
    east = u * jnp.where(u > 0, thick, east_of(thick))
    north = v * jnp.where(v > 0, thick, north_of(thick, thick_n)) * geo[0:rows, 1:2]
    below = None if v_s is None else v_s * jnp.where(v_s > 0, thick_s, thick[0:1]) * geo[0:1, 0:1]
    return east, north, below


def tracer_change(q, q_s, q_n, thick, u, v, v_s, east, north, below, inverse):
    t_east = east * jnp.where(u > 0, q, east_of(q))
    t_north = north * jnp.where(v > 0, q, north_of(q, q_n))
    t_below = None if v_s is None else below * jnp.where(v_s > 0, q_s, q[0:1])
    change = thick * q - (t_east - west_of(t_east))
    return change - (t_north - south_of(t_north, t_below)) * inverse


def packed_at(rows, levels, width):
    near = len(near_rows(rows)[0])
    size = rows - 2 + levels * near
    for a in range(width // LANES):
        yield a, a * size, [a * size + rows - 2 + k * near for k in range(levels)]


def first_kernel(table_hbm, thick_hbm, u_hbm, v_hbm, tracer_hbm, *refs):
    new_ref, both_ref, near_ref, east_ref, north_ref, thick_ref, u_ref, v_ref, tracer_ref, sum_ref, geo_ref, sems = refs
    L, rows, _ = thick_ref.shape
    near, _ = near_rows(rows)
    table_copy = pltpu.make_async_copy(table_hbm.at[lax.axis_index("lat")], geo_ref, sems.at[3, 0])
    table_copy.start()
    pairs = ((thick_hbm, thick_ref), (u_hbm, u_ref), (v_hbm, v_ref))

    def copies(k):
        return [pltpu.make_async_copy(a.at[k], b.at[k], sems.at[i, k]) for i, (a, b) in enumerate(pairs)]

    for k in range(L):
        for copy in copies(k):
            copy.start()
    tracer_copy = pltpu.make_async_copy(tracer_hbm, tracer_ref, sems.at[3, 1])
    tracer_copy.start()
    table_copy.wait()
    geo = geo_ref[...]
    sum_ref[...] = jnp.zeros_like(sum_ref)

    def level(k, carry):
        for copy in copies(k):
            copy.wait()
        thick, u, v = thick_ref[k], u_ref[k], v_ref[k]
        east, north, _ = fluxes(geo, thick, u, v, None, None, None)
        new = thick - (east - west_of(east)) - (north - south_of(north, None)) * geo[0:rows, 2:3]
        new_ref[k] = new
        east_ref[k] = east
        north_ref[k] = north
        for j, row in enumerate(near):
            near_ref[0, k, j : j + 1] = new[row : row + 1]
        sum_ref[...] += new
        return carry

    lax.fori_loop(0, L, level, 0)
    for a, at, each in packed_at(rows, L, thick_ref.shape[2]):
        lanes = slice(a * LANES, (a + 1) * LANES)
        both_ref[at : at + rows - 2] = sum_ref[1 : rows - 1, lanes]
        for k in range(L):
            both_ref[each[k] : each[k] + len(near)] = near_ref[0, k, :, lanes]
    tracer_copy.wait()


def first_step(table, thickness, wind_u, wind_v, tracers):
    L, R, N = thickness.shape
    arguments = (thickness, wind_u, wind_v, tracers)
    operands = [pltpu.with_memory_space_constraint(a, pltpu.HBM) for a in (table, *arguments)]
    near = len(near_rows(R)[0])
    shapes = [(L, R, N), ((R - 2 + L * near) * N // LANES, LANES), (1, L, near, N), (L, R, N), (L, R, N)] + [a.shape for a in arguments]
    return pl.pallas_call(
        first_kernel,
        in_specs=after(operands),
        out_specs=[VMEM] * len(shapes),
        out_shape=[jax.ShapeDtypeStruct(shape, jnp.float32) for shape in shapes],
        scratch_shapes=[
            pltpu.VMEM((R, N), jnp.float32),
            pltpu.VMEM(table.shape[1:], jnp.float32),
            pltpu.SemaphoreType.DMA((4, max(L, 2))),
        ],
        compiler_params=params(),
        cost_estimate=cost(40 * L * R * N, 4 * L * R * N * (7 + 2 * tracers.shape[0])),
        name="first_step",
    )(*operands)


def inner_kernel(table_ref, new_ref, east_ref, north_ref, thick_ref, u_ref, v_ref, tracer_ref, out_ref, near_ref):
    T, L, rows, _ = tracer_ref.shape
    near, _ = near_rows(rows)
    geo = table_ref[lax.axis_index("lat")]
    inverse = geo[0:rows, 2:3]

    def level(k, carry):
        thick, u, v, new = thick_ref[k], u_ref[k], v_ref[k], new_ref[k]
        east, north = east_ref[k], north_ref[k]

        out_ref[0, k] = new
        scale = 1.0 / new
        for c in range(T):
            change = tracer_change(
                tracer_ref[c, k], None, None, thick, u, v, None, east, north, None, inverse
            )
            value = change * scale
            out_ref[1 + c, k] = value
            for j, row in enumerate(near):
                near_ref[pl.ds((c * L + k) * len(near) + j, 1)] = value[row : row + 1]
        return carry

    lax.fori_loop(0, L, level, 0)


def inner_step(table, new, east, north, thickness, wind_u, wind_v, tracers):
    L, R, N = thickness.shape
    T = tracers.shape[0]
    rows = jax.ShapeDtypeStruct((T * L * len(near_rows(R)[0]), N), jnp.float32)
    shape = lambda n, rows: jax.ShapeDtypeStruct((n, L, rows, N), jnp.float32)
    return pl.pallas_call(
        inner_kernel,
        in_specs=[VMEM] * 8,
        out_specs=[VMEM] * 2,
        out_shape=[shape(1 + T, R), rows],
        compiler_params=params(),
        cost_estimate=cost(130 * L * R * N, 4 * L * R * N * (8 + 2 * T)),
        name="inner_step",
    )(table, new, east, north, thickness, wind_u, wind_v, tracers)


def filter_tables(N):
    A = N // LANES
    b = np.arange(LANES)[:, None]
    p = np.arange(LANES)[None, :]
    tables = []
    for q in range(A // 2 + 1):
        angle = 2.0 * np.pi * ((b * (A * p + q)) % N) / N
        c, s = np.cos(angle), np.sin(angle)
        tables.append(np.block([[c, -s], [s, c]]))
    table = np.stack(tables)
    high = table.astype(np.float32).astype(ml_dtypes.bfloat16)
    low = (table - high.astype(np.float64)).astype(np.float32).astype(ml_dtypes.bfloat16)
    return high, low


def split(value):
    high = value.astype(jnp.bfloat16)
    return high, (value - high.astype(jnp.float32)).astype(jnp.bfloat16)


def product(value, high, low, transposed):
    dims = (((1,), (1 if transposed else 0,)), ((), ()))
    dot = lambda x, y: lax.dot_general(x, y, dims, preferred_element_type=jnp.float32)
    v_high, v_low = split(value)
    return dot(v_high, high) + (dot(v_high, low) + dot(v_low, high))


def filter_rows(x, cutoff, high_ref, low_ref):
    A = len(x)
    N = A * LANES
    half = A // 2
    even = [x[a] + x[A - a] for a in range(1, half + 1)]
    odd = [x[a] - x[A - a] for a in range(1, half + 1)]
    angle = lambda q, a: 2.0 * np.pi * ((q * a) % A) / A
    p = lax.broadcasted_iota(jnp.int32, cutoff.shape, 1)
    real, imag = [], []
    for q in range(half + 1):
        re = x[0]
        for a in range(1, half + 1):
            re = re + (even[a - 1] if q == 0 else float(np.cos(angle(q, a))) * even[a - 1])
        if q == 0:
            high, low = high_ref[0, 0:LANES], low_ref[0, 0:LANES]
            spectrum = product(re, high, low, False)
        else:
            high, low = high_ref[q], low_ref[q]
            im = -float(np.sin(angle(q, 1))) * odd[0]
            for a in range(2, half + 1):
                im = im - float(np.sin(angle(q, a))) * odd[a - 1]
            spectrum = product(jnp.concatenate([re, im], axis=1), high, low, False)
        mode = A * p + q
        factor = 1.0 / N if q == 0 else 2.0 / N
        kept = jnp.where(jnp.minimum(mode, N - mode) <= cutoff, factor, 0.0)
        back = product(spectrum * jnp.concatenate([kept, kept], axis=1), high, low, True)
        real.append(back[:, :LANES])
        imag.append(back[:, LANES:])
    out = [None] * A
    out[0] = functools.reduce(jnp.add, real)
    for a in range(1, half + 1):
        even_part, odd_part = real[0], None
        for q in range(1, half + 1):
            even_part = even_part + float(np.cos(angle(q, a))) * real[q]
            term = float(np.sin(angle(q, a))) * imag[q]
            odd_part = term if odd_part is None else odd_part + term
        out[a] = even_part - odd_part
        out[A - a] = even_part + odd_part
    return out


def second_kernel(
    lat_rows, table_ref, thick_ref, u_ref, v_ref, tracer_ref, up_ref, down_ref, cutoff_ref, high_ref, low_ref, *refs
):
    *wind_refs, edge_ref, new_wind = refs
    k = pl.program_id(0)
    _, L, rows, width = new_wind.shape
    band = lax.axis_index("lat")
    geo = table_ref[band]
    thick, u, v = thick_ref[0], u_ref[0], v_ref[0]
    thick_s, v_s = up_ref[0, 0], up_ref[1, 0]
    thick_n, thick_nn, u_n, v_n = (down_ref[i, 0] for i in range(4))
    east, north, below = fluxes(geo, thick, u, v, thick_s, v_s, thick_n)
    inverse = geo[0:rows, 2:3]
    new = thick - (east - west_of(east)) - (north - south_of(north, below)) * inverse
    east_n = u_n * jnp.where(u_n > 0, thick_n, east_of(thick_n))
    north_n = v_n * jnp.where(v_n > 0, thick_n, thick_nn) * geo[rows : rows + 1, 1:2]
    new_n = (
        thick_n
        - (east_n - west_of(east_n))
        - (north_n - north[rows - 1 : rows]) * geo[rows : rows + 1, 2:3]
    )
    new_wind[0, k] = u - 0.05 * (east_of(new) - new)
    inside = band * rows + row_ids(new.shape) < lat_rows - 1
    new_wind[1, k] = jnp.where(inside, v - 0.05 * (north_of(new, new_n) - new), 0.0)

    def store_edges(field, level, value):
        edge_ref[field, level, 0:1] = value[0:1]
        edge_ref[field, level, 1:2] = value[rows - 1 : rows]

    store_edges(0, k, new)
    scale = 1.0 / new
    for c in range(tracer_ref.shape[0]):
        change = tracer_change(
            tracer_ref[c, 0], up_ref[2 + c, 0], down_ref[4 + c, 0], thick, u, v, v_s, east, north, below, inverse
        )
        store_edges(3 + c, k, change * scale)

    @pl.when(k == L - 1)
    def _():
        pieces = [
            new_wind[:, :, :, a * LANES : (a + 1) * LANES].reshape(2 * L * rows, LANES) for a in range(width // LANES)
        ]
        cutoff = jnp.broadcast_to(cutoff_ref[...][None], (2 * L, rows, LANES)).reshape(2 * L * rows, LANES)
        for a, piece in enumerate(filter_rows(pieces, cutoff, high_ref, low_ref)):
            piece = piece.reshape(2, L, rows, LANES)
            for f in range(2):
                wind_refs[f][0, :, :, a * LANES : (a + 1) * LANES] = piece[f]
        for f in range(2):
            for level in range(L):
                store_edges(1 + f, level, wind_refs[f][0, level])


def second_step(table, lat_rows, thickness, wind_u, wind_v, tracers, up, down, cutoff):
    L, R, N = thickness.shape
    T = tracers.shape[0]
    high, low = filter_tables(N)
    level = pl.BlockSpec((1, R, N), lambda k: (k, 0, 0))
    some = lambda n, rows: pl.BlockSpec((n, 1, rows, N), lambda k: (0, k, 0, 0))
    whole = lambda shape: pl.BlockSpec(shape, lambda k: (0,) * len(shape))
    return pl.pallas_call(
        functools.partial(second_kernel, lat_rows),
        grid=(L,),
        in_specs=[whole(table.shape), level, level, level, some(T, R), some(2 + T, 1), some(4 + T, 1)]
        + [whole((R, LANES)), whole(high.shape), whole(low.shape)],
        out_specs=[whole((1, L, R, N)), whole((1, L, R, N)), whole((3 + T, L, 2, N))],
        out_shape=[
            jax.ShapeDtypeStruct((1, L, R, N), jnp.float32),
            jax.ShapeDtypeStruct((1, L, R, N), jnp.float32),
            jax.ShapeDtypeStruct((3 + T, L, 2, N), jnp.float32),
        ],
        scratch_shapes=[pltpu.VMEM((2, L, R, N), jnp.float32)],
        compiler_params=params(),
        cost_estimate=cost(12 * 2 * L * R * high.size, 4 * L * R * N * (8 + T)),
        name="second_step",
    )(
        table, thickness, wind_u, wind_v, tracers, up, down,
        jnp.broadcast_to(cutoff[:, None], (R, LANES)), jnp.asarray(high), jnp.asarray(low),
    )


def part_kernel(both_ref, *refs):
    sum_ref, near_ref = refs[-2:]
    rows, width = sum_ref.shape
    _, L, near, _ = near_ref.shape
    sum_ref[...] = jnp.zeros_like(sum_ref)
    for a, at, each in packed_at(rows, L, width):
        lanes = slice(a * LANES, (a + 1) * LANES)
        sum_ref[1 : rows - 1, lanes] = both_ref[at : at + rows - 2]
        for k in range(L):
            near_ref[0, k, :, lanes] = both_ref[each[k] : each[k] + near]


def part(both, shape, wait):
    L, R, N = shape
    return pl.pallas_call(
        part_kernel,
        in_specs=[VMEM] + after(wait),
        out_specs=[VMEM] * 2,
        out_shape=[
            jax.ShapeDtypeStruct((R, N), jnp.float32),
            jax.ShapeDtypeStruct((1, L, len(near_rows(R)[0]), N), jnp.float32),
        ],
        compiler_params=params(),
        cost_estimate=cost(1e11, 1e9),
        name="part",
    )(both, *wait)


def mass_kernel(C, S, *refs):
    other_refs, (base_ref, mass_ref) = refs[: (C - 1) * S], refs[(C - 1) * S :]
    lev = lax.axis_index("lev")
    others_mass, base = None, None
    for s in range(1, C):
        other = functools.reduce(jnp.add, [ref[...] for ref in other_refs[(s - 1) * S : s * S]])
        below = jnp.where(lev >= s, other, 0.0)
        others_mass = other if others_mass is None else others_mass + other
        base = below if base is None else base + below
    base_ref[...] = base
    mass_ref[...] = others_mass


def other_chips(counts, others):
    return pl.pallas_call(
        functools.partial(mass_kernel, *counts),
        in_specs=[VMEM] * len(others),
        out_specs=[VMEM] * 2,
        out_shape=[jax.ShapeDtypeStruct(others[0].shape, jnp.float32)] * 2,
        compiler_params=params(),
        cost_estimate=cost(1, 1),
        name="other_chips",
    )(*others)


def add_weights(weight_ref, sum_ref):
    total = jnp.zeros(weight_ref.shape[1:], jnp.float32)
    for k in range(weight_ref.shape[0]):
        sum_ref[k] = total
        total = total + weight_ref[k]
    sum_ref[weight_ref.shape[0]] = total
    return total


def source_levels(place, counts, thick, others):
    C, S = counts
    lev, sub = place
    spot = [lax.rem(lev - g // S + C, C) * S + lax.rem(sub - g % S + S, S) for g in range(len(thick))]
    group = [functools.reduce(jnp.add, levels) for levels in thick]
    mass = functools.reduce(jnp.add, group)
    base = jnp.zeros_like(mass)
    if others:
        base, mass = others[0], mass + others[1]
    sources = []
    for g, levels in enumerate(thick):
        low = base
        for other in range(len(thick)):
            if other != g:
                low = low + jnp.where(spot[other] < spot[g], group[other], 0.0)
        for m, value in enumerate(levels):
            sources.append((g, m, low, value))
            low = low + value
    return mass, sources


def covered(top, sources):
    return [jnp.minimum(jnp.maximum(top - low, 0.0), value) for _, _, low, value in sources]


def level_of(ref, index):
    return lambda m, at, columns: ref[index, m, at, columns]


def packed_level_of(ref, index, L, rows):
    return lambda m, at, columns: ref[(index * L + m) * rows : (index * L + m + 1) * rows, columns]


def remap_rows(weight_ref, sum_ref, counts, steps, thick_refs, field_refs, other_refs, store):
    C, S = counts
    _, L, R, N = thick_refs[0].shape
    rows = min(R, 8)
    place = lev, sub = lax.axis_index("lev"), lax.axis_index("sub")
    firsts = [(lax.rem(lev + s, C) * S + sub) * L for s in steps]
    weight_sum = add_weights(weight_ref, sum_ref)[0:rows]

    def tile(at, columns):
        thick = [[ref[0, m, at, columns] for m in range(L)] for ref in thick_refs]
        others = [ref[at, columns] for ref in other_refs]
        mass, sources = source_levels(place, counts, thick, others)
        unit = mass / weight_sum
        for index, s in enumerate(steps):
            below = covered(unit * sum_ref[firsts[index], 0:rows], sources)
            for i in range(L):
                upto = covered(unit * sum_ref[firsts[index] + i + 1, 0:rows], sources)
                part = [a - b for a, b in zip(upto, below)]
                below = upto
                target = unit * weight_ref[firsts[index] + i, 0:rows]
                scale = 1.0 / target
                means = []
                for refs in field_refs:
                    terms = [refs[g](m, at, columns) * w for (g, m, _, _), w in zip(sources, part)]
                    means.append(functools.reduce(jnp.add, terms) * scale)
                store(s, i, at, columns, target, means)

    for r in range(0, R, rows):

        def body(c, carry):
            tile(slice(r, r + rows), pl.ds(pl.multiple_of(c * LANES, LANES), LANES))
            return carry

        lax.fori_loop(0, N // LANES, body, 0)


def inner_part(at, margin, rows):
    return max(at.start, margin[0]), min(at.stop, rows - margin[1])


def remap_kernel(counts, steps, fields, margin, with_thickness, sizes, weight_ref, *refs):
    *refs, sum_ref = refs
    C, S = counts
    thick_refs, refs = refs[:S], refs[S:]
    bundles = []
    for _ in range(sizes[0]):
        bundles.append(refs[:S])
        refs = refs[S:]
    other_refs, out_refs = refs[:2], refs[len(refs) - len(steps) - with_thickness :]
    _, L, R, _ = thick_refs[0].shape
    thick_out_ref = out_refs[-1]
    field_refs = [[level_of(ref, index) for ref in bundles[which]] for which, index in fields]

    def store(s, i, at, columns, target, means):
        out_ref = out_refs[steps.index(s)]
        if with_thickness and s == 0:
            thick_out_ref[i, at, columns] = target
        for f, value in enumerate(means):
            if s == 0:
                out_ref[f, i, at, columns] = value
            else:
                lower, upper = inner_part(at, margin, R)
                start = (f * L + i) * (R - sum(margin)) - margin[0]
                out_ref[start + lower : start + upper, columns] = value[lower - at.start : upper - at.start]

    remap_rows(
        weight_ref, sum_ref, counts, steps, thick_refs, field_refs, other_refs, store
    )


def remap_parts(counts, weights, thick, bundles, others, fields, steps, margin, with_thickness=False, wait=()):
    C, S = counts
    _, L, R, N = thick[0].shape
    F = len(fields)
    whole = jax.ShapeDtypeStruct((F, L, R, N), jnp.float32)
    inner = jax.ShapeDtypeStruct((F * L * (R - sum(margin)), N), jnp.float32)
    flat = [a for bundle in bundles for a in bundle]
    out_shape = [whole if s == 0 else inner for s in steps]
    if with_thickness:
        out_shape.append(jax.ShapeDtypeStruct((L, R, N), jnp.float32))
    return pl.pallas_call(
        functools.partial(remap_kernel, counts, tuple(steps), tuple(fields), margin, with_thickness, (len(bundles),)),
        in_specs=[VMEM] * (1 + len(thick) + len(flat) + len(others)) + after(wait),
        out_specs=[VMEM] * len(out_shape),
        out_shape=out_shape,
        scratch_shapes=[pltpu.VMEM((weights.shape[0] + 1, 8, LANES), jnp.float32)],
        compiler_params=params(),
        cost_estimate=cost(len(steps) * S * L * L * R * N * (5 + 2 * F), 4 * R * N * L * (F + 1) * (S + len(steps))),
        name="remap_parts",
    )(weights, *thick, *flat, *others, *wait)


def remap_edge_kernel(counts, weight_ref, *refs):
    *refs, sum_ref = refs
    G = counts[0] * counts[1]
    edge_refs, near_refs, tracer_refs = refs[:G], refs[G : 2 * G], refs[2 * G : 3 * G]
    edge_out_ref, thick_out_ref, near_out_ref = refs[-3:]

    def store_edge(s, i, at, columns, target, means):
        thick_out_ref[i, at, columns] = target
        for f, value in enumerate(means):
            edge_out_ref[f, i, at, columns] = value

    def store_near(s, i, at, columns, target, means):
        for f, value in enumerate(means):
            near_out_ref[f, i, at, columns] = value

    fields = [[level_of(ref, f) for ref in edge_refs] for f in range(1, edge_refs[0].shape[0])]
    remap_rows(weight_ref, sum_ref, counts, (0,), edge_refs, fields, [], store_edge)
    _, L, R, _ = near_refs[0].shape
    fields = [[packed_level_of(ref, f, L, R) for ref in tracer_refs] for f in range(near_out_ref.shape[0])]
    remap_rows(weight_ref, sum_ref, counts, (0,), near_refs, fields, [], store_near)


def remap_edges(counts, weights, edges, near_new, near, wait=()):
    F, L, R, N = edges[0].shape
    T = F - 3
    operands = [*edges, *near_new, *near]
    return pl.pallas_call(
        functools.partial(remap_edge_kernel, counts),
        in_specs=[VMEM] * (1 + len(operands)) + after(wait),
        out_specs=[VMEM] * 3,
        out_shape=[
            jax.ShapeDtypeStruct((F - 1, L, R, N), jnp.float32),
            jax.ShapeDtypeStruct((L, R, N), jnp.float32),
            jax.ShapeDtypeStruct((T, *near_new[0].shape[1:]), jnp.float32),
        ],
        scratch_shapes=[pltpu.VMEM((weights.shape[0] + 1, 8, LANES), jnp.float32)],
        compiler_params=params(),
        cost_estimate=cost(len(edges) * L * L * R * N * 40, 4 * R * N * L * len(operands) * F),
        name="remap_edges",
    )(weights, *operands, *wait)


def finish_kernel(margin, own_ref, near_ref, edge_ref, thick_ref, thick_edge_ref, *refs):
    *arrived_refs, out_ref, thick_out_ref, token_ref = refs
    token_ref[...] = jnp.zeros_like(token_ref)
    T, L, R, _ = out_ref.shape
    thick_out_ref[...] = thick_ref[...]
    for i in range(L):
        for row, j in ((0, 0), (R - 1, 1)):
            thick_out_ref[i, row : row + 1] = thick_edge_ref[i, j : j + 1]
    for f in range(T):
        for i in range(L):
            start, first, end = (f * L + i) * (R - sum(margin)), margin[0], R - margin[1]
            total = own_ref[f, i, first:end]
            for ref in arrived_refs:
                total = total + ref[start : start + end - first]
            out_ref[f, i, first:end] = total
            for row, j in ((0, 0), (R - 1, 1)):
                out_ref[f, i, row : row + 1] = edge_ref[2 + f, i, j : j + 1]
            for j, row in enumerate(near_rows(R)[0]):
                out_ref[f, i, row : row + 1] = near_ref[f, i, j : j + 1]


def finish_tracers(own, near, edge, thick, thick_edge, arrived):
    return pl.pallas_call(
        functools.partial(finish_kernel, near_rows(own.shape[2])[1]),
        in_specs=[VMEM] * (5 + len(arrived)),
        out_specs=[VMEM] * 3,
        out_shape=[
            jax.ShapeDtypeStruct(own.shape, jnp.float32),
            jax.ShapeDtypeStruct(thick.shape, jnp.float32),
            jax.ShapeDtypeStruct((8, LANES), jnp.float32),
        ],
        compiler_params=params(),
        cost_estimate=cost(2 * own.size, 12 * own.size),
        name="finish_tracers",
    )(own, near, edge, thick, thick_edge, *arrived)


def finish_winds_kernel(count, own_ref, edge_ref, *refs):
    arrived_refs, (*out_refs, result_ref, sems) = refs[:count], refs[len(refs) - 4 :]
    _, L, R, N = own_ref.shape
    row = row_ids((R, N))
    copies = []
    for f, out_ref in enumerate(out_refs):
        for i in range(L):
            start = (f * L + i) * (R - 2)
            first = start // 8 * 8
            total = own_ref[f, i]
            for ref in arrived_refs:
                size = min(R + 8, ref.shape[0] - first)
                total = total + pltpu.roll(ref[first : first + size], (1 - (start - first)) % size, 0)[0:R]
            total = jnp.where(row == 0, edge_ref[f, i, 0:1], jnp.where(row == R - 1, edge_ref[f, i, 1:2], total))
            result_ref[f, i] = total
            copies.append(pltpu.make_async_copy(result_ref.at[f, i], out_ref.at[i], sems.at[f, i]))
            copies[-1].start()
    for copy in copies:
        copy.wait()


def finish_winds(own, arrived, edge, wait):
    F, L = own.shape[:2]
    return pl.pallas_call(
        functools.partial(finish_winds_kernel, len(arrived)),
        in_specs=[VMEM] * (2 + len(arrived)) + after(wait),
        out_specs=[pl.BlockSpec(memory_space=pl.ANY)] * F,
        out_shape=[jax.ShapeDtypeStruct(own.shape[1:], jnp.float32)] * F,
        scratch_shapes=[pltpu.VMEM(own.shape, jnp.float32), pltpu.SemaphoreType.DMA((F, L))],
        compiler_params=params(),
        cost_estimate=cost(own.size, 12 * own.size),
        name="finish_winds",
    )(own, edge, *arrived, *wait)


def edge_kernel(thick_any, u_any, v_any, tracer_any, *refs):
    last_ref, leading_ref, top_ref, low_ref, tracer_ref, sems = refs[-6:]
    T, L, R, _ = tracer_any.shape
    top = pl.ds(R - 8, 8)
    copies = [
        pltpu.make_async_copy(thick_any.at[:, top], top_ref.at[0], sems.at[0]),
        pltpu.make_async_copy(v_any.at[:, top], top_ref.at[1], sems.at[1]),
        pltpu.make_async_copy(thick_any.at[:, pl.ds(0, 8)], low_ref.at[0], sems.at[2]),
        pltpu.make_async_copy(u_any.at[:, pl.ds(0, 8)], low_ref.at[1], sems.at[3]),
        pltpu.make_async_copy(v_any.at[:, pl.ds(0, 8)], low_ref.at[2], sems.at[4]),
        pltpu.make_async_copy(tracer_any.at[:, :, top], tracer_ref.at[0], sems.at[5]),
        pltpu.make_async_copy(tracer_any.at[:, :, pl.ds(0, 8)], tracer_ref.at[1], sems.at[6]),
    ]
    for copy in copies:
        copy.start()
    for copy in copies:
        copy.wait()
    last_ref[0:2] = top_ref[:, :, 7:8]
    last_ref[2 : 2 + T] = tracer_ref[0, :, :, 7:8]
    leading_ref[0] = low_ref[0, :, 0:1]
    leading_ref[1] = low_ref[0, :, 1:2]
    leading_ref[2:4] = low_ref[1:3, :, 0:1]
    leading_ref[4 : 4 + T] = tracer_ref[1, :, :, 0:1]


def edge_rows(thickness, wind_u, wind_v, tracers, wait):
    L, R, N = thickness.shape
    T = tracers.shape[0]
    operands = [thickness, wind_u, wind_v, tracers]
    return pl.pallas_call(
        edge_kernel,
        in_specs=after(operands) + after(wait),
        out_specs=[VMEM] * 2,
        out_shape=[
            jax.ShapeDtypeStruct((2 + T, L, 1, N), jnp.float32),
            jax.ShapeDtypeStruct((4 + T, L, 1, N), jnp.float32),
        ],
        scratch_shapes=[
            pltpu.VMEM((2, L, 8, N), jnp.float32),
            pltpu.VMEM((3, L, 8, N), jnp.float32),
            pltpu.VMEM((2, T, L, 8, N), jnp.float32),
            pltpu.SemaphoreType.DMA((7,)),
        ],
        compiler_params=params(),
        cost_estimate=cost(1e10, 1e9),
        name="edge_rows",
    )(*operands, *wait)


def shifted(value, lev_count, sub_count, s, t):
    if t == 0:
        return lax.ppermute(value, "lev", [(i, (i + s) % lev_count) for i in range(lev_count)])
    if s == 0:
        return lax.ppermute(value, "sub", [(i, (i + t) % sub_count) for i in range(sub_count)])
    pairs = [
        (i * sub_count + j, (i + s) % lev_count * sub_count + (j + t) % sub_count)
        for i in range(lev_count)
        for j in range(sub_count)
    ]
    return lax.ppermute(value, ("lev", "sub"), pairs)


def per_device(thickness, wind_u, wind_v, tracers, level_weights, cutoff):
    L, R, N = thickness.shape
    lat_count = lax.axis_size("lat")
    C, S = lax.axis_size("lev"), lax.axis_size("sub")
    lat_rows = R * lat_count
    send = functools.partial(shifted, lev_count=C, sub_count=S)

    T = tracers.shape[0]
    northward = [(i, i + 1) for i in range(lat_count - 1)]
    southward = [(j, i) for i, j in northward]
    table = jnp.asarray(geometry_table(lat_rows, R))
    weights = jnp.broadcast_to(level_weights[:, None, None], (level_weights.shape[0], 8, LANES))
    away = range(1, C)

    def with_others_of_chip(own):
        return [own] + [send(own, s=0, t=t) for t in range(1, S)]

    def sent(parts):
        return [send(part, s=s, t=0) for s, part in zip(away, parts)]

    remap = functools.partial(remap_parts, (C, S), weights)

    new, both, near_new, east, north, *arguments = first_step(table, thickness, wind_u, wind_v, tracers)
    both = [send(both, s=s, t=0) for s in away]
    inner, near = inner_step(table, new, east, north, *arguments)
    group = with_others_of_chip(inner)
    near = [near] + [send(near, s=s, t=0) for s in away]
    parted = [part(each, (L, R, N), [near[0]]) for each in both]
    near_new = [near_new] + [each[1] for each in parted]
    others = other_chips((C, S), [a for each in parted for a in with_others_of_chip(each[0])])
    tracer_fields = [(0, 1 + c) for c in range(T)]
    away_parts = remap(group, [group], others, tracer_fields, away, near_rows(R)[1])
    arrived = sent(away_parts)

    last, leading = edge_rows(
        *arguments, [away_parts[0], *near[1:2]]
    )
    up = lax.ppermute(last, "lat", northward)
    down = lax.ppermute(leading, "lat", southward)
    u, v, edge = second_step(table, lat_rows, *arguments, up, down, cutoff)
    edges = [edge] + [send(edge, s=s, t=0) for s in away]
    winds = [with_others_of_chip(u), with_others_of_chip(v)]
    tracers_own, thick_inner = remap(group, [group], others, tracer_fields, (0,), (0, 0), with_thickness=True, wait=[edge])
    winds_own, *winds_away = remap(
        group, winds, others, [(0, 0), (1, 0)], range(C), (1, 1), wait=[tracers_own, *arrived[:1]]
    )
    winds_arrived = sent(winds_away)
    near_new, near, edges = (
        [a for own in sources for a in with_others_of_chip(own)] for sources in (near_new, near, edges)
    )
    edge_out, thick_edge, near_out = remap_edges(
        (C, S), weights, edges, near_new, near, wait=winds_away[:1]
    )

    tracers_out, thickness_out, token = finish_tracers(
        tracers_own, near_out, edge_out, thick_inner, thick_edge, arrived
    )
    u_out, v_out = finish_winds(winds_own, winds_arrived, edge_out, [token])
    return thickness_out, u_out, v_out, tracers_out


def solution(mesh):
    placed = (
        P(("member", "lev", "sub"), "lat", None),
        P(("member", "lev", "sub"), "lat", None),
        P(("member", "lev", "sub"), "lat", None),
        P("member", ("lev", "sub"), "lat", None),
        P(),
        P("lat"),
    )
    return jax.shard_map(
        per_device,
        mesh=mesh,
        in_specs=placed,
        out_specs=(
            P(("member", "lev", "sub"), "lat", None),
            P(("member", "lev", "sub"), "lat", None),
            P(("member", "lev", "sub"), "lat", None),
            P("member", ("lev", "sub"), "lat", None),
        ),
        check_vma=False,
    )
```

```python
import functools

import jax
import jax.numpy as jnp
import ml_dtypes
import numpy as np
from jax import lax
from jax.experimental import pallas as pl
from jax.experimental.pallas import tpu as pltpu
from jax.sharding import PartitionSpec as P

LANES = 128
VMEM = pl.BlockSpec(memory_space=pltpu.VMEM)


def params():
    return pltpu.CompilerParams(vmem_limit_bytes=16 * 1024 * 1024)


def cost(flops, bytes_accessed):
    return pl.CostEstimate(flops=int(flops), bytes_accessed=int(bytes_accessed), transcendentals=0)


def after(arrays):
    return [pl.BlockSpec(memory_space=pl.ANY)] * len(arrays)


def near_rows(rows):
    return (1, 2, rows - 3, rows - 2), (3, 3)


def geometry_table(lat_rows, band_rows):
    bands = lat_rows // band_rows
    table = np.zeros((bands, band_rows + 8, LANES), np.float32)
    for band in range(bands):
        for j in range(band_rows + 1):
            row = band * band_rows + j
            south = np.sin(row * np.pi / lat_rows) if 0 < row < lat_rows else 0.0
            north = np.sin((row + 1) * np.pi / lat_rows) if row + 1 < lat_rows else 0.0
            table[band, j, 0] = south
            table[band, j, 1] = north
            table[band, j, 2] = 1.0 / np.sin((row + 0.5) * np.pi / lat_rows)
    return table


def east_of(value):
    return pltpu.roll(value, value.shape[1] - 1, 1)


def west_of(value):
    return pltpu.roll(value, 1, 1)


def row_ids(shape):
    return lax.broadcasted_iota(jnp.int32, shape, 0)


def north_of(value, beyond):
    rows = value.shape[0]
    rolled = pltpu.roll(value, rows - 1, 0)
    return rolled if beyond is None else jnp.where(row_ids(value.shape) == rows - 1, beyond, rolled)


def south_of(value, beyond):
    rolled = pltpu.roll(value, 1, 0)
    return rolled if beyond is None else jnp.where(row_ids(value.shape) == 0, beyond, rolled)


def fluxes(geo, thick, u, v, thick_s, v_s, thick_n):
    rows = thick.shape[0]
    east = u * jnp.where(u > 0, thick, east_of(thick))
    north = v * jnp.where(v > 0, thick, north_of(thick, thick_n)) * geo[0:rows, 1:2]
    below = None if v_s is None else v_s * jnp.where(v_s > 0, thick_s, thick[0:1]) * geo[0:1, 0:1]
    return east, north, below


def tracer_change(q, q_s, q_n, thick, u, v, v_s, east, north, below, inverse):
    t_east = east * jnp.where(u > 0, q, east_of(q))
    t_north = north * jnp.where(v > 0, q, north_of(q, q_n))
    t_below = None if v_s is None else below * jnp.where(v_s > 0, q_s, q[0:1])
    change = thick * q - (t_east - west_of(t_east))
    return change - (t_north - south_of(t_north, t_below)) * inverse


def packed_at(rows, levels, width):
    near = len(near_rows(rows)[0])
    size = rows - 2 + levels * near
    for a in range(width // LANES):
        yield a, a * size, [a * size + rows - 2 + k * near for k in range(levels)]


def first_kernel(table_hbm, thick_hbm, u_hbm, v_hbm, tracer_hbm, *refs):
    new_ref, both_ref, near_ref, east_ref, north_ref, thick_ref, u_ref, v_ref, tracer_ref, sum_ref, geo_ref, sems = refs
    L, rows, _ = thick_ref.shape
    near, _ = near_rows(rows)
    table_copy = pltpu.make_async_copy(table_hbm.at[lax.axis_index("lat")], geo_ref, sems.at[3, 0])
    table_copy.start()
    pairs = ((thick_hbm, thick_ref), (u_hbm, u_ref), (v_hbm, v_ref))

    def copies(k):
        return [pltpu.make_async_copy(a.at[k], b.at[k], sems.at[i, k]) for i, (a, b) in enumerate(pairs)]

    for k in range(L):
        for copy in copies(k):
            copy.start()
    tracer_copy = pltpu.make_async_copy(tracer_hbm, tracer_ref, sems.at[3, 1])
    tracer_copy.start()
    table_copy.wait()
    geo = geo_ref[...]
    sum_ref[...] = jnp.zeros_like(sum_ref)

    def level(k, carry):
        for copy in copies(k):
            copy.wait()
        thick, u, v = thick_ref[k], u_ref[k], v_ref[k]
        east, north, _ = fluxes(geo, thick, u, v, None, None, None)
        new = thick - (east - west_of(east)) - (north - south_of(north, None)) * geo[0:rows, 2:3]
        new_ref[k] = new
        east_ref[k] = east
        north_ref[k] = north
        for j, row in enumerate(near):
            near_ref[0, k, j : j + 1] = new[row : row + 1]
        sum_ref[...] += new
        return carry

    lax.fori_loop(0, L, level, 0)
    for a, at, each in packed_at(rows, L, thick_ref.shape[2]):
        lanes = slice(a * LANES, (a + 1) * LANES)
        both_ref[at : at + rows - 2] = sum_ref[1 : rows - 1, lanes]
        for k in range(L):
            both_ref[each[k] : each[k] + len(near)] = near_ref[0, k, :, lanes]
    tracer_copy.wait()


def first_step(table, thickness, wind_u, wind_v, tracers):
    L, R, N = thickness.shape
    arguments = (thickness, wind_u, wind_v, tracers)
    operands = [pltpu.with_memory_space_constraint(a, pltpu.HBM) for a in (table, *arguments)]
    near = len(near_rows(R)[0])
    shapes = [(L, R, N), ((R - 2 + L * near) * N // LANES, LANES), (1, L, near, N), (L, R, N), (L, R, N)] + [a.shape for a in arguments]
    return pl.pallas_call(
        first_kernel,
        in_specs=after(operands),
        out_specs=[VMEM] * len(shapes),
        out_shape=[jax.ShapeDtypeStruct(shape, jnp.float32) for shape in shapes],
        scratch_shapes=[
            pltpu.VMEM((R, N), jnp.float32),
            pltpu.VMEM(table.shape[1:], jnp.float32),
            pltpu.SemaphoreType.DMA((4, max(L, 2))),
        ],
        compiler_params=params(),
        cost_estimate=cost(40 * L * R * N, 4 * L * R * N * (7 + 2 * tracers.shape[0])),
        name="first_step",
    )(*operands)


def inner_kernel(table_ref, new_ref, east_ref, north_ref, thick_ref, u_ref, v_ref, tracer_ref, out_ref, near_ref):
    T, L, rows, _ = tracer_ref.shape
    near, _ = near_rows(rows)
    geo = table_ref[lax.axis_index("lat")]
    inverse = geo[0:rows, 2:3]

    def level(k, carry):
        thick, u, v, new = thick_ref[k], u_ref[k], v_ref[k], new_ref[k]
        east, north = east_ref[k], north_ref[k]

        out_ref[0, k] = new
        scale = 1.0 / new
        for c in range(T):
            change = tracer_change(
                tracer_ref[c, k], None, None, thick, u, v, None, east, north, None, inverse
            )
            value = change * scale
            out_ref[1 + c, k] = value
            for j, row in enumerate(near):
                near_ref[pl.ds((c * L + k) * len(near) + j, 1)] = value[row : row + 1]
        return carry

    lax.fori_loop(0, L, level, 0)


def inner_step(table, new, east, north, thickness, wind_u, wind_v, tracers):
    L, R, N = thickness.shape
    T = tracers.shape[0]
    rows = jax.ShapeDtypeStruct((T * L * len(near_rows(R)[0]), N), jnp.float32)
    shape = lambda n, rows: jax.ShapeDtypeStruct((n, L, rows, N), jnp.float32)
    return pl.pallas_call(
        inner_kernel,
        in_specs=[VMEM] * 8,
        out_specs=[VMEM] * 2,
        out_shape=[shape(1 + T, R), rows],
        compiler_params=params(),
        cost_estimate=cost(130 * L * R * N, 4 * L * R * N * (8 + 2 * T)),
        name="inner_step",
    )(table, new, east, north, thickness, wind_u, wind_v, tracers)


def filter_tables(N):
    A = N // LANES
    b = np.arange(LANES)[:, None]
    p = np.arange(LANES)[None, :]
    tables = []
    for q in range(A // 2 + 1):
        angle = 2.0 * np.pi * ((b * (A * p + q)) % N) / N
        c, s = np.cos(angle), np.sin(angle)
        tables.append(np.block([[c, -s], [s, c]]))
    table = np.stack(tables)
    high = table.astype(np.float32).astype(ml_dtypes.bfloat16)
    low = (table - high.astype(np.float64)).astype(np.float32).astype(ml_dtypes.bfloat16)
    return high, low


def split(value):
    high = value.astype(jnp.bfloat16)
    return high, (value - high.astype(jnp.float32)).astype(jnp.bfloat16)


def product(value, high, low, transposed):
    dims = (((1,), (1 if transposed else 0,)), ((), ()))
    dot = lambda x, y: lax.dot_general(x, y, dims, preferred_element_type=jnp.float32)
    v_high, v_low = split(value)
    return dot(v_high, high) + (dot(v_high, low) + dot(v_low, high))


def filter_rows(x, cutoff, high_ref, low_ref):
    A = len(x)
    N = A * LANES
    half = A // 2
    even = [x[a] + x[A - a] for a in range(1, half + 1)]
    odd = [x[a] - x[A - a] for a in range(1, half + 1)]
    angle = lambda q, a: 2.0 * np.pi * ((q * a) % A) / A
    p = lax.broadcasted_iota(jnp.int32, cutoff.shape, 1)
    real, imag = [], []
    for q in range(half + 1):
        re = x[0]
        for a in range(1, half + 1):
            re = re + (even[a - 1] if q == 0 else float(np.cos(angle(q, a))) * even[a - 1])
        if q == 0:
            high, low = high_ref[0, 0:LANES], low_ref[0, 0:LANES]
            spectrum = product(re, high, low, False)
        else:
            high, low = high_ref[q], low_ref[q]
            im = -float(np.sin(angle(q, 1))) * odd[0]
            for a in range(2, half + 1):
                im = im - float(np.sin(angle(q, a))) * odd[a - 1]
            spectrum = product(jnp.concatenate([re, im], axis=1), high, low, False)
        mode = A * p + q
        factor = 1.0 / N if q == 0 else 2.0 / N
        kept = jnp.where(jnp.minimum(mode, N - mode) <= cutoff, factor, 0.0)
        back = product(spectrum * jnp.concatenate([kept, kept], axis=1), high, low, True)
        real.append(back[:, :LANES])
        imag.append(back[:, LANES:])
    out = [None] * A
    out[0] = functools.reduce(jnp.add, real)
    for a in range(1, half + 1):
        even_part, odd_part = real[0], None
        for q in range(1, half + 1):
            even_part = even_part + float(np.cos(angle(q, a))) * real[q]
            term = float(np.sin(angle(q, a))) * imag[q]
            odd_part = term if odd_part is None else odd_part + term
        out[a] = even_part - odd_part
        out[A - a] = even_part + odd_part
    return out


def second_kernel(
    lat_rows, table_ref, thick_ref, u_ref, v_ref, tracer_ref, up_ref, down_ref, cutoff_ref, high_ref, low_ref, *refs
):
    *wind_refs, edge_ref, new_wind = refs
    k = pl.program_id(0)
    _, L, rows, width = new_wind.shape
    band = lax.axis_index("lat")
    geo = table_ref[band]
    thick, u, v = thick_ref[0], u_ref[0], v_ref[0]
    thick_s, v_s = up_ref[0, 0], up_ref[1, 0]
    thick_n, thick_nn, u_n, v_n = (down_ref[i, 0] for i in range(4))
    east, north, below = fluxes(geo, thick, u, v, thick_s, v_s, thick_n)
    inverse = geo[0:rows, 2:3]
    new = thick - (east - west_of(east)) - (north - south_of(north, below)) * inverse
    east_n = u_n * jnp.where(u_n > 0, thick_n, east_of(thick_n))
    north_n = v_n * jnp.where(v_n > 0, thick_n, thick_nn) * geo[rows : rows + 1, 1:2]
    new_n = (
        thick_n
        - (east_n - west_of(east_n))
        - (north_n - north[rows - 1 : rows]) * geo[rows : rows + 1, 2:3]
    )
    new_wind[0, k] = u - 0.05 * (east_of(new) - new)
    inside = band * rows + row_ids(new.shape) < lat_rows - 1
    new_wind[1, k] = jnp.where(inside, v - 0.05 * (north_of(new, new_n) - new), 0.0)

    def store_edges(field, level, value):
        edge_ref[field, level, 0:1] = value[0:1]
        edge_ref[field, level, 1:2] = value[rows - 1 : rows]

    store_edges(0, k, new)
    scale = 1.0 / new
    for c in range(tracer_ref.shape[0]):
        change = tracer_change(
            tracer_ref[c, 0], up_ref[2 + c, 0], down_ref[4 + c, 0], thick, u, v, v_s, east, north, below, inverse
        )
        store_edges(3 + c, k, change * scale)

    @pl.when(k == L - 1)
    def _():
        pieces = [
            new_wind[:, :, :, a * LANES : (a + 1) * LANES].reshape(2 * L * rows, LANES) for a in range(width // LANES)
        ]
        cutoff = jnp.broadcast_to(cutoff_ref[...][None], (2 * L, rows, LANES)).reshape(2 * L * rows, LANES)
        for a, piece in enumerate(filter_rows(pieces, cutoff, high_ref, low_ref)):
            piece = piece.reshape(2, L, rows, LANES)
            for f in range(2):
                wind_refs[f][0, :, :, a * LANES : (a + 1) * LANES] = piece[f]
        for f in range(2):
            for level in range(L):
                store_edges(1 + f, level, wind_refs[f][0, level])


def second_step(table, lat_rows, thickness, wind_u, wind_v, tracers, up, down, cutoff):
    L, R, N = thickness.shape
    T = tracers.shape[0]
    high, low = filter_tables(N)
    level = pl.BlockSpec((1, R, N), lambda k: (k, 0, 0))
    some = lambda n, rows: pl.BlockSpec((n, 1, rows, N), lambda k: (0, k, 0, 0))
    whole = lambda shape: pl.BlockSpec(shape, lambda k: (0,) * len(shape))
    return pl.pallas_call(
        functools.partial(second_kernel, lat_rows),
        grid=(L,),
        in_specs=[whole(table.shape), level, level, level, some(T, R), some(2 + T, 1), some(4 + T, 1)]
        + [whole((R, LANES)), whole(high.shape), whole(low.shape)],
        out_specs=[whole((1, L, R, N)), whole((1, L, R, N)), whole((3 + T, L, 2, N))],
        out_shape=[
            jax.ShapeDtypeStruct((1, L, R, N), jnp.float32),
            jax.ShapeDtypeStruct((1, L, R, N), jnp.float32),
            jax.ShapeDtypeStruct((3 + T, L, 2, N), jnp.float32),
        ],
        scratch_shapes=[pltpu.VMEM((2, L, R, N), jnp.float32)],
        compiler_params=params(),
        cost_estimate=cost(12 * 2 * L * R * high.size, 4 * L * R * N * (8 + T)),
        name="second_step",
    )(
        table, thickness, wind_u, wind_v, tracers, up, down,
        jnp.broadcast_to(cutoff[:, None], (R, LANES)), jnp.asarray(high), jnp.asarray(low),
    )


def part_kernel(both_ref, *refs):
    sum_ref, near_ref = refs[-2:]
    rows, width = sum_ref.shape
    _, L, near, _ = near_ref.shape
    sum_ref[...] = jnp.zeros_like(sum_ref)
    for a, at, each in packed_at(rows, L, width):
        lanes = slice(a * LANES, (a + 1) * LANES)
        sum_ref[1 : rows - 1, lanes] = both_ref[at : at + rows - 2]
        for k in range(L):
            near_ref[0, k, :, lanes] = both_ref[each[k] : each[k] + near]


def part(both, shape, wait):
    L, R, N = shape
    return pl.pallas_call(
        part_kernel,
        in_specs=[VMEM] + after(wait),
        out_specs=[VMEM] * 2,
        out_shape=[
            jax.ShapeDtypeStruct((R, N), jnp.float32),
            jax.ShapeDtypeStruct((1, L, len(near_rows(R)[0]), N), jnp.float32),
        ],
        compiler_params=params(),
        cost_estimate=cost(1e11, 1e9),
        name="part",
    )(both, *wait)


def mass_kernel(C, S, *refs):
    other_refs, (base_ref, mass_ref) = refs[: (C - 1) * S], refs[(C - 1) * S :]
    lev = lax.axis_index("lev")
    others_mass, base = None, None
    for s in range(1, C):
        other = functools.reduce(jnp.add, [ref[...] for ref in other_refs[(s - 1) * S : s * S]])
        below = jnp.where(lev >= s, other, 0.0)
        others_mass = other if others_mass is None else others_mass + other
        base = below if base is None else base + below
    base_ref[...] = base
    mass_ref[...] = others_mass


def other_chips(counts, others):
    return pl.pallas_call(
        functools.partial(mass_kernel, *counts),
        in_specs=[VMEM] * len(others),
        out_specs=[VMEM] * 2,
        out_shape=[jax.ShapeDtypeStruct(others[0].shape, jnp.float32)] * 2,
        compiler_params=params(),
        cost_estimate=cost(1, 1),
        name="other_chips",
    )(*others)


def add_weights(weight_ref, sum_ref):
    total = jnp.zeros(weight_ref.shape[1:], jnp.float32)
    for k in range(weight_ref.shape[0]):
        sum_ref[k] = total
        total = total + weight_ref[k]
    sum_ref[weight_ref.shape[0]] = total
    return total


def source_levels(place, counts, thick, others):
    C, S = counts
    lev, sub = place
    spot = [lax.rem(lev - g // S + C, C) * S + lax.rem(sub - g % S + S, S) for g in range(len(thick))]
    group = [functools.reduce(jnp.add, levels) for levels in thick]
    mass = functools.reduce(jnp.add, group)
    base = jnp.zeros_like(mass)
    if others:
        base, mass = others[0], mass + others[1]
    sources = []
    for g, levels in enumerate(thick):
        low = base
        for other in range(len(thick)):
            if other != g:
                low = low + jnp.where(spot[other] < spot[g], group[other], 0.0)
        for m, value in enumerate(levels):
            sources.append((g, m, low, value))
            low = low + value
    return mass, sources


def covered(top, sources):
    return [jnp.minimum(jnp.maximum(top - low, 0.0), value) for _, _, low, value in sources]


def level_of(ref, index):
    return lambda m, at, columns: ref[index, m, at, columns]


def packed_level_of(ref, index, L, rows):
    return lambda m, at, columns: ref[(index * L + m) * rows : (index * L + m + 1) * rows, columns]


def remap_rows(weight_ref, sum_ref, counts, steps, thick_refs, field_refs, other_refs, store):
    C, S = counts
    _, L, R, N = thick_refs[0].shape
    rows = min(R, 8)
    place = lev, sub = lax.axis_index("lev"), lax.axis_index("sub")
    firsts = [(lax.rem(lev + s, C) * S + sub) * L for s in steps]
    weight_sum = add_weights(weight_ref, sum_ref)[0:rows]

    def tile(at, columns):
        thick = [[ref[0, m, at, columns] for m in range(L)] for ref in thick_refs]
        others = [ref[at, columns] for ref in other_refs]
        mass, sources = source_levels(place, counts, thick, others)
        unit = mass / weight_sum
        for index, s in enumerate(steps):
            below = covered(unit * sum_ref[firsts[index], 0:rows], sources)
            for i in range(L):
                upto = covered(unit * sum_ref[firsts[index] + i + 1, 0:rows], sources)
                part = [a - b for a, b in zip(upto, below)]
                below = upto
                target = unit * weight_ref[firsts[index] + i, 0:rows]
                scale = 1.0 / target
                means = []
                for refs in field_refs:
                    terms = [refs[g](m, at, columns) * w for (g, m, _, _), w in zip(sources, part)]
                    means.append(functools.reduce(jnp.add, terms) * scale)
                store(s, i, at, columns, target, means)

    for r in range(0, R, rows):

        def body(c, carry):
            tile(slice(r, r + rows), pl.ds(pl.multiple_of(c * LANES, LANES), LANES))
            return carry

        lax.fori_loop(0, N // LANES, body, 0)


def inner_part(at, margin, rows):
    return max(at.start, margin[0]), min(at.stop, rows - margin[1])


def remap_kernel(counts, steps, fields, margin, with_thickness, sizes, weight_ref, *refs):
    *refs, sum_ref = refs
    C, S = counts
    thick_refs, refs = refs[:S], refs[S:]
    bundles = []
    for _ in range(sizes[0]):
        bundles.append(refs[:S])
        refs = refs[S:]
    other_refs, out_refs = refs[:2], refs[len(refs) - len(steps) - with_thickness :]
    _, L, R, _ = thick_refs[0].shape
    thick_out_ref = out_refs[-1]
    field_refs = [[level_of(ref, index) for ref in bundles[which]] for which, index in fields]

    def store(s, i, at, columns, target, means):
        out_ref = out_refs[steps.index(s)]
        if with_thickness and s == 0:
            thick_out_ref[i, at, columns] = target
        for f, value in enumerate(means):
            if s == 0:
                out_ref[f, i, at, columns] = value
            else:
                lower, upper = inner_part(at, margin, R)
                start = (f * L + i) * (R - sum(margin)) - margin[0]
                out_ref[start + lower : start + upper, columns] = value[lower - at.start : upper - at.start]

    remap_rows(
        weight_ref, sum_ref, counts, steps, thick_refs, field_refs, other_refs, store
    )


def remap_parts(counts, weights, thick, bundles, others, fields, steps, margin, with_thickness=False, wait=()):
    C, S = counts
    _, L, R, N = thick[0].shape
    F = len(fields)
    whole = jax.ShapeDtypeStruct((F, L, R, N), jnp.float32)
    inner = jax.ShapeDtypeStruct((F * L * (R - sum(margin)), N), jnp.float32)
    flat = [a for bundle in bundles for a in bundle]
    out_shape = [whole if s == 0 else inner for s in steps]
    if with_thickness:
        out_shape.append(jax.ShapeDtypeStruct((L, R, N), jnp.float32))
    return pl.pallas_call(
        functools.partial(remap_kernel, counts, tuple(steps), tuple(fields), margin, with_thickness, (len(bundles),)),
        in_specs=[VMEM] * (1 + len(thick) + len(flat) + len(others)) + after(wait),
        out_specs=[VMEM] * len(out_shape),
        out_shape=out_shape,
        scratch_shapes=[pltpu.VMEM((weights.shape[0] + 1, 8, LANES), jnp.float32)],
        compiler_params=params(),
        cost_estimate=cost(len(steps) * S * L * L * R * N * (5 + 2 * F), 4 * R * N * L * (F + 1) * (S + len(steps))),
        name="remap_parts",
    )(weights, *thick, *flat, *others, *wait)


def remap_edge_kernel(counts, weight_ref, *refs):
    *refs, sum_ref = refs
    G = counts[0] * counts[1]
    edge_refs, near_refs, tracer_refs = refs[:G], refs[G : 2 * G], refs[2 * G : 3 * G]
    edge_out_ref, thick_out_ref, near_out_ref = refs[-3:]

    def store_edge(s, i, at, columns, target, means):
        thick_out_ref[i, at, columns] = target
        for f, value in enumerate(means):
            edge_out_ref[f, i, at, columns] = value

    def store_near(s, i, at, columns, target, means):
        for f, value in enumerate(means):
            near_out_ref[f, i, at, columns] = value

    fields = [[level_of(ref, f) for ref in edge_refs] for f in range(1, edge_refs[0].shape[0])]
    remap_rows(weight_ref, sum_ref, counts, (0,), edge_refs, fields, [], store_edge)
    _, L, R, _ = near_refs[0].shape
    fields = [[packed_level_of(ref, f, L, R) for ref in tracer_refs] for f in range(near_out_ref.shape[0])]
    remap_rows(weight_ref, sum_ref, counts, (0,), near_refs, fields, [], store_near)


def remap_edges(counts, weights, edges, near_new, near, wait=()):
    F, L, R, N = edges[0].shape
    T = F - 3
    operands = [*edges, *near_new, *near]
    return pl.pallas_call(
        functools.partial(remap_edge_kernel, counts),
        in_specs=[VMEM] * (1 + len(operands)) + after(wait),
        out_specs=[VMEM] * 3,
        out_shape=[
            jax.ShapeDtypeStruct((F - 1, L, R, N), jnp.float32),
            jax.ShapeDtypeStruct((L, R, N), jnp.float32),
            jax.ShapeDtypeStruct((T, *near_new[0].shape[1:]), jnp.float32),
        ],
        scratch_shapes=[pltpu.VMEM((weights.shape[0] + 1, 8, LANES), jnp.float32)],
        compiler_params=params(),
        cost_estimate=cost(len(edges) * L * L * R * N * 40, 4 * R * N * L * len(operands) * F),
        name="remap_edges",
    )(weights, *operands, *wait)


def finish_kernel(margin, own_ref, near_ref, edge_ref, thick_ref, thick_edge_ref, *refs):
    *arrived_refs, out_ref, thick_out_ref, token_ref = refs
    token_ref[...] = jnp.zeros_like(token_ref)
    T, L, R, _ = out_ref.shape
    thick_out_ref[...] = thick_ref[...]
    for i in range(L):
        for row, j in ((0, 0), (R - 1, 1)):
            thick_out_ref[i, row : row + 1] = thick_edge_ref[i, j : j + 1]
    for f in range(T):
        for i in range(L):
            start, first, end = (f * L + i) * (R - sum(margin)), margin[0], R - margin[1]
            total = own_ref[f, i, first:end]
            for ref in arrived_refs:
                total = total + ref[start : start + end - first]
            out_ref[f, i, first:end] = total
            for row, j in ((0, 0), (R - 1, 1)):
                out_ref[f, i, row : row + 1] = edge_ref[2 + f, i, j : j + 1]
            for j, row in enumerate(near_rows(R)[0]):
                out_ref[f, i, row : row + 1] = near_ref[f, i, j : j + 1]


def finish_tracers(own, near, edge, thick, thick_edge, arrived):
    return pl.pallas_call(
        functools.partial(finish_kernel, near_rows(own.shape[2])[1]),
        in_specs=[VMEM] * (5 + len(arrived)),
        out_specs=[VMEM] * 3,
        out_shape=[
            jax.ShapeDtypeStruct(own.shape, jnp.float32),
            jax.ShapeDtypeStruct(thick.shape, jnp.float32),
            jax.ShapeDtypeStruct((8, LANES), jnp.float32),
        ],
        compiler_params=params(),
        cost_estimate=cost(2 * own.size, 12 * own.size),
        name="finish_tracers",
    )(own, near, edge, thick, thick_edge, *arrived)


def finish_winds_kernel(count, own_ref, edge_ref, *refs):
    arrived_refs, (*out_refs, result_ref, sems) = refs[:count], refs[len(refs) - 4 :]
    _, L, R, N = own_ref.shape
    row = row_ids((R, N))
    copies = []
    for f, out_ref in enumerate(out_refs):
        for i in range(L):
            start = (f * L + i) * (R - 2)
            first = start // 8 * 8
            total = own_ref[f, i]
            for ref in arrived_refs:
                size = min(R + 8, ref.shape[0] - first)
                total = total + pltpu.roll(ref[first : first + size], (1 - (start - first)) % size, 0)[0:R]
            total = jnp.where(row == 0, edge_ref[f, i, 0:1], jnp.where(row == R - 1, edge_ref[f, i, 1:2], total))
            result_ref[f, i] = total
            copies.append(pltpu.make_async_copy(result_ref.at[f, i], out_ref.at[i], sems.at[f, i]))
            copies[-1].start()
    for copy in copies:
        copy.wait()


def finish_winds(own, arrived, edge, wait):
    F, L = own.shape[:2]
    return pl.pallas_call(
        functools.partial(finish_winds_kernel, len(arrived)),
        in_specs=[VMEM] * (2 + len(arrived)) + after(wait),
        out_specs=[pl.BlockSpec(memory_space=pl.ANY)] * F,
        out_shape=[jax.ShapeDtypeStruct(own.shape[1:], jnp.float32)] * F,
        scratch_shapes=[pltpu.VMEM(own.shape, jnp.float32), pltpu.SemaphoreType.DMA((F, L))],
        compiler_params=params(),
        cost_estimate=cost(own.size, 12 * own.size),
        name="finish_winds",
    )(own, edge, *arrived, *wait)


def edge_kernel(thick_any, u_any, v_any, tracer_any, *refs):
    last_ref, leading_ref, top_ref, low_ref, tracer_ref, sems = refs[-6:]
    T, L, R, _ = tracer_any.shape
    top = pl.ds(R - 8, 8)
    copies = [
        pltpu.make_async_copy(thick_any.at[:, top], top_ref.at[0], sems.at[0]),
        pltpu.make_async_copy(v_any.at[:, top], top_ref.at[1], sems.at[1]),
        pltpu.make_async_copy(thick_any.at[:, pl.ds(0, 8)], low_ref.at[0], sems.at[2]),
        pltpu.make_async_copy(u_any.at[:, pl.ds(0, 8)], low_ref.at[1], sems.at[3]),
        pltpu.make_async_copy(v_any.at[:, pl.ds(0, 8)], low_ref.at[2], sems.at[4]),
        pltpu.make_async_copy(tracer_any.at[:, :, top], tracer_ref.at[0], sems.at[5]),
        pltpu.make_async_copy(tracer_any.at[:, :, pl.ds(0, 8)], tracer_ref.at[1], sems.at[6]),
    ]
    for copy in copies:
        copy.start()
    for copy in copies:
        copy.wait()
    last_ref[0:2] = top_ref[:, :, 7:8]
    last_ref[2 : 2 + T] = tracer_ref[0, :, :, 7:8]
    leading_ref[0] = low_ref[0, :, 0:1]
    leading_ref[1] = low_ref[0, :, 1:2]
    leading_ref[2:4] = low_ref[1:3, :, 0:1]
    leading_ref[4 : 4 + T] = tracer_ref[1, :, :, 0:1]


def edge_rows(thickness, wind_u, wind_v, tracers, wait):
    L, R, N = thickness.shape
    T = tracers.shape[0]
    operands = [thickness, wind_u, wind_v, tracers]
    return pl.pallas_call(
        edge_kernel,
        in_specs=after(operands) + after(wait),
        out_specs=[VMEM] * 2,
        out_shape=[
            jax.ShapeDtypeStruct((2 + T, L, 1, N), jnp.float32),
            jax.ShapeDtypeStruct((4 + T, L, 1, N), jnp.float32),
        ],
        scratch_shapes=[
            pltpu.VMEM((2, L, 8, N), jnp.float32),
            pltpu.VMEM((3, L, 8, N), jnp.float32),
            pltpu.VMEM((2, T, L, 8, N), jnp.float32),
            pltpu.SemaphoreType.DMA((7,)),
        ],
        compiler_params=params(),
        cost_estimate=cost(1e10, 1e9),
        name="edge_rows",
    )(*operands, *wait)


def shifted(value, lev_count, sub_count, s, t):
    if t == 0:
        return lax.ppermute(value, "lev", [(i, (i + s) % lev_count) for i in range(lev_count)])
    if s == 0:
        return lax.ppermute(value, "sub", [(i, (i + t) % sub_count) for i in range(sub_count)])
    pairs = [
        (i * sub_count + j, (i + s) % lev_count * sub_count + (j + t) % sub_count)
        for i in range(lev_count)
        for j in range(sub_count)
    ]
    return lax.ppermute(value, ("lev", "sub"), pairs)


def per_device(thickness, wind_u, wind_v, tracers, level_weights, cutoff):
    L, R, N = thickness.shape
    lat_count = lax.axis_size("lat")
    C, S = lax.axis_size("lev"), lax.axis_size("sub")
    lat_rows = R * lat_count
    send = functools.partial(shifted, lev_count=C, sub_count=S)

    T = tracers.shape[0]
    northward = [(i, i + 1) for i in range(lat_count - 1)]
    southward = [(j, i) for i, j in northward]
    table = jnp.asarray(geometry_table(lat_rows, R))
    weights = jnp.broadcast_to(level_weights[:, None, None], (level_weights.shape[0], 8, LANES))
    away = range(1, C)

    def with_others_of_chip(own):
        return [own] + [send(own, s=0, t=t) for t in range(1, S)]

    def sent(parts):
        return [send(part, s=s, t=0) for s, part in zip(away, parts)]

    remap = functools.partial(remap_parts, (C, S), weights)

    new, both, near_new, east, north, *arguments = first_step(table, thickness, wind_u, wind_v, tracers)
    both = [send(both, s=s, t=0) for s in away]
    inner, near = inner_step(table, new, east, north, *arguments)
    group = with_others_of_chip(inner)
    near = [near] + [send(near, s=s, t=0) for s in away]
    parted = [part(each, (L, R, N), [near[0]]) for each in both]
    near_new = [near_new] + [each[1] for each in parted]
    others = other_chips((C, S), [a for each in parted for a in with_others_of_chip(each[0])])
    tracer_fields = [(0, 1 + c) for c in range(T)]
    away_parts = remap(group, [group], others, tracer_fields, away, near_rows(R)[1])
    arrived = sent(away_parts)

    last, leading = edge_rows(
        *arguments, [away_parts[0], *near[1:2]]
    )
    up = lax.ppermute(last, "lat", northward)
    down = lax.ppermute(leading, "lat", southward)
    u, v, edge = second_step(table, lat_rows, *arguments, up, down, cutoff)
    edges = [edge] + [send(edge, s=s, t=0) for s in away]
    winds = [with_others_of_chip(u), with_others_of_chip(v)]
    tracers_own, thick_inner = remap(group, [group], others, tracer_fields, (0,), (0, 0), with_thickness=True, wait=[edge])
    winds_own, *winds_away = remap(
        group, winds, others, [(0, 0), (1, 0)], range(C), (1, 1), wait=[tracers_own, *arrived[:1]]
    )
    winds_arrived = sent(winds_away)
    near_new, near, edges = (
        [a for own in sources for a in with_others_of_chip(own)] for sources in (near_new, near, edges)
    )
    edge_out, thick_edge, near_out = remap_edges(
        (C, S), weights, edges, near_new, near, wait=winds_away[:1]
    )

    tracers_out, thickness_out, token = finish_tracers(
        tracers_own, near_out, edge_out, thick_inner, thick_edge, arrived
    )
    u_out, v_out = finish_winds(winds_own, winds_arrived, edge_out, [token])
    return thickness_out, u_out, v_out, tracers_out


def solution(mesh):
    placed = (
        P(("member", "lev", "sub"), "lat", None),
        P(("member", "lev", "sub"), "lat", None),
        P(("member", "lev", "sub"), "lat", None),
        P("member", ("lev", "sub"), "lat", None),
        P(),
        P("lat"),
    )
    return jax.shard_map(
        per_device,
        mesh=mesh,
        in_specs=placed,
        out_specs=(
            P(("member", "lev", "sub"), "lat", None),
            P(("member", "lev", "sub"), "lat", None),
            P(("member", "lev", "sub"), "lat", None),
            P("member", ("lev", "sub"), "lat", None),
        ),
        check_vma=False,
    )
```

```python
import functools

import jax
import jax.numpy as jnp
import ml_dtypes
import numpy as np
from jax import lax
from jax.experimental import pallas as pl
from jax.experimental.pallas import tpu as pltpu
from jax.sharding import PartitionSpec as P

LANES = 128
VMEM = pl.BlockSpec(memory_space=pltpu.VMEM)


def params():
    return pltpu.CompilerParams(vmem_limit_bytes=16 * 1024 * 1024)


def cost(flops, bytes_accessed):
    return pl.CostEstimate(flops=int(flops), bytes_accessed=int(bytes_accessed), transcendentals=0)


def after(arrays):
    return [pl.BlockSpec(memory_space=pl.ANY)] * len(arrays)


def near_rows(rows):
    return (1, 2, rows - 2), (3, 2)


def geometry_table(lat_rows, band_rows):
    bands = lat_rows // band_rows
    table = np.zeros((bands, band_rows + 8, LANES), np.float32)
    for band in range(bands):
        for j in range(band_rows + 1):
            row = band * band_rows + j
            south = np.sin(row * np.pi / lat_rows) if 0 < row < lat_rows else 0.0
            north = np.sin((row + 1) * np.pi / lat_rows) if row + 1 < lat_rows else 0.0
            table[band, j, 0] = south
            table[band, j, 1] = north
            table[band, j, 2] = 1.0 / np.sin((row + 0.5) * np.pi / lat_rows)
    return table


def east_of(value):
    return pltpu.roll(value, value.shape[1] - 1, 1)


def west_of(value):
    return pltpu.roll(value, 1, 1)


def row_ids(shape):
    return lax.broadcasted_iota(jnp.int32, shape, 0)


def north_of(value, beyond):
    rows = value.shape[0]
    rolled = pltpu.roll(value, rows - 1, 0)
    return rolled if beyond is None else jnp.where(row_ids(value.shape) == rows - 1, beyond, rolled)


def south_of(value, beyond):
    rolled = pltpu.roll(value, 1, 0)
    return rolled if beyond is None else jnp.where(row_ids(value.shape) == 0, beyond, rolled)


def fluxes(geo, thick, u, v, thick_s, v_s, thick_n):
    rows = thick.shape[0]
    east = u * jnp.where(u > 0, thick, east_of(thick))
    north = v * jnp.where(v > 0, thick, north_of(thick, thick_n)) * geo[0:rows, 1:2]
    below = None if v_s is None else v_s * jnp.where(v_s > 0, thick_s, thick[0:1]) * geo[0:1, 0:1]
    return east, north, below


def tracer_change(q, q_s, q_n, thick, u, v, v_s, east, north, below, inverse):
    t_east = east * jnp.where(u > 0, q, east_of(q))
    t_north = north * jnp.where(v > 0, q, north_of(q, q_n))
    t_below = None if v_s is None else below * jnp.where(v_s > 0, q_s, q[0:1])
    change = thick * q - (t_east - west_of(t_east))
    return change - (t_north - south_of(t_north, t_below)) * inverse


def packed_at(rows, levels, width):
    near = len(near_rows(rows)[0])
    size = rows - 2 + levels * near
    for a in range(width // LANES):
        yield a, a * size, [a * size + rows - 2 + k * near for k in range(levels)]


def first_kernel(table_hbm, thick_hbm, u_hbm, v_hbm, tracer_hbm, *refs):
    new_ref, both_ref, near_ref, east_ref, north_ref, thick_ref, u_ref, v_ref, tracer_ref, sum_ref, geo_ref, sems = refs
    L, rows, _ = thick_ref.shape
    near, _ = near_rows(rows)
    table_copy = pltpu.make_async_copy(table_hbm.at[lax.axis_index("lat")], geo_ref, sems.at[3, 0])
    table_copy.start()
    pairs = ((thick_hbm, thick_ref), (u_hbm, u_ref), (v_hbm, v_ref))

    def copies(k):
        return [pltpu.make_async_copy(a.at[k], b.at[k], sems.at[i, k]) for i, (a, b) in enumerate(pairs)]

    for k in range(L):
        for copy in copies(k):
            copy.start()
    tracer_copy = pltpu.make_async_copy(tracer_hbm, tracer_ref, sems.at[3, 1])
    tracer_copy.start()
    table_copy.wait()
    geo = geo_ref[...]
    sum_ref[...] = jnp.zeros_like(sum_ref)

    def level(k, carry):
        for copy in copies(k):
            copy.wait()
        thick, u, v = thick_ref[k], u_ref[k], v_ref[k]
        east, north, _ = fluxes(geo, thick, u, v, None, None, None)
        new = thick - (east - west_of(east)) - (north - south_of(north, None)) * geo[0:rows, 2:3]
        new_ref[k] = new
        east_ref[k] = east
        north_ref[k] = north
        for j, row in enumerate(near):
            near_ref[0, k, j : j + 1] = new[row : row + 1]
        sum_ref[...] += new
        return carry

    lax.fori_loop(0, L, level, 0)
    for a, at, each in packed_at(rows, L, thick_ref.shape[2]):
        lanes = slice(a * LANES, (a + 1) * LANES)
        both_ref[at : at + rows - 2] = sum_ref[1 : rows - 1, lanes]
        for k in range(L):
            both_ref[each[k] : each[k] + len(near)] = near_ref[0, k, :, lanes]
    tracer_copy.wait()


def first_step(table, thickness, wind_u, wind_v, tracers):
    L, R, N = thickness.shape
    arguments = (thickness, wind_u, wind_v, tracers)
    operands = [pltpu.with_memory_space_constraint(a, pltpu.HBM) for a in (table, *arguments)]
    near = len(near_rows(R)[0])
    shapes = [(L, R, N), ((R - 2 + L * near) * N // LANES, LANES), (1, L, near, N), (L, R, N), (L, R, N)] + [a.shape for a in arguments]
    return pl.pallas_call(
        first_kernel,
        in_specs=after(operands),
        out_specs=[VMEM] * len(shapes),
        out_shape=[jax.ShapeDtypeStruct(shape, jnp.float32) for shape in shapes],
        scratch_shapes=[
            pltpu.VMEM((R, N), jnp.float32),
            pltpu.VMEM(table.shape[1:], jnp.float32),
            pltpu.SemaphoreType.DMA((4, max(L, 2))),
        ],
        compiler_params=params(),
        cost_estimate=cost(40 * L * R * N, 4 * L * R * N * (7 + 2 * tracers.shape[0])),
        name="first_step",
    )(*operands)


def inner_kernel(table_ref, new_ref, east_ref, north_ref, thick_ref, u_ref, v_ref, tracer_ref, out_ref, near_ref):
    T, L, rows, _ = tracer_ref.shape
    near, _ = near_rows(rows)
    geo = table_ref[lax.axis_index("lat")]
    inverse = geo[0:rows, 2:3]

    def level(k, carry):
        thick, u, v, new = thick_ref[k], u_ref[k], v_ref[k], new_ref[k]
        east, north = east_ref[k], north_ref[k]

        out_ref[0, k] = new
        scale = 1.0 / new
        for c in range(T):
            change = tracer_change(
                tracer_ref[c, k], None, None, thick, u, v, None, east, north, None, inverse
            )
            value = change * scale
            out_ref[1 + c, k] = value
            for j, row in enumerate(near):
                near_ref[pl.ds((c * L + k) * len(near) + j, 1)] = value[row : row + 1]
        return carry

    lax.fori_loop(0, L, level, 0)


def inner_step(table, new, east, north, thickness, wind_u, wind_v, tracers):
    L, R, N = thickness.shape
    T = tracers.shape[0]
    rows = jax.ShapeDtypeStruct((T * L * len(near_rows(R)[0]), N), jnp.float32)
    shape = lambda n, rows: jax.ShapeDtypeStruct((n, L, rows, N), jnp.float32)
    return pl.pallas_call(
        inner_kernel,
        in_specs=[VMEM] * 8,
        out_specs=[VMEM] * 2,
        out_shape=[shape(1 + T, R), rows],
        compiler_params=params(),
        cost_estimate=cost(130 * L * R * N, 4 * L * R * N * (8 + 2 * T)),
        name="inner_step",
    )(table, new, east, north, thickness, wind_u, wind_v, tracers)


def filter_tables(N):
    A = N // LANES
    b = np.arange(LANES)[:, None]
    p = np.arange(LANES)[None, :]
    tables = []
    for q in range(A // 2 + 1):
        angle = 2.0 * np.pi * ((b * (A * p + q)) % N) / N
        c, s = np.cos(angle), np.sin(angle)
        tables.append(np.block([[c, -s], [s, c]]))
    table = np.stack(tables)
    high = table.astype(np.float32).astype(ml_dtypes.bfloat16)
    low = (table - high.astype(np.float64)).astype(np.float32).astype(ml_dtypes.bfloat16)
    return high, low


def split(value):
    high = value.astype(jnp.bfloat16)
    return high, (value - high.astype(jnp.float32)).astype(jnp.bfloat16)


def product(value, high, low, transposed):
    dims = (((1,), (1 if transposed else 0,)), ((), ()))
    dot = lambda x, y: lax.dot_general(x, y, dims, preferred_element_type=jnp.float32)
    v_high, v_low = split(value)
    return dot(v_high, high) + (dot(v_high, low) + dot(v_low, high))


def filter_rows(x, cutoff, high_ref, low_ref):
    A = len(x)
    N = A * LANES
    half = A // 2
    even = [x[a] + x[A - a] for a in range(1, half + 1)]
    odd = [x[a] - x[A - a] for a in range(1, half + 1)]
    angle = lambda q, a: 2.0 * np.pi * ((q * a) % A) / A
    p = lax.broadcasted_iota(jnp.int32, cutoff.shape, 1)
    real, imag = [], []
    for q in range(half + 1):
        re = x[0]
        for a in range(1, half + 1):
            re = re + (even[a - 1] if q == 0 else float(np.cos(angle(q, a))) * even[a - 1])
        if q == 0:
            high, low = high_ref[0, 0:LANES], low_ref[0, 0:LANES]
            spectrum = product(re, high, low, False)
        else:
            high, low = high_ref[q], low_ref[q]
            im = -float(np.sin(angle(q, 1))) * odd[0]
            for a in range(2, half + 1):
                im = im - float(np.sin(angle(q, a))) * odd[a - 1]
            spectrum = product(jnp.concatenate([re, im], axis=1), high, low, False)
        mode = A * p + q
        factor = 1.0 / N if q == 0 else 2.0 / N
        kept = jnp.where(jnp.minimum(mode, N - mode) <= cutoff, factor, 0.0)
        back = product(spectrum * jnp.concatenate([kept, kept], axis=1), high, low, True)
        real.append(back[:, :LANES])
        imag.append(back[:, LANES:])
    out = [None] * A
    out[0] = functools.reduce(jnp.add, real)
    for a in range(1, half + 1):
        even_part, odd_part = real[0], None
        for q in range(1, half + 1):
            even_part = even_part + float(np.cos(angle(q, a))) * real[q]
            term = float(np.sin(angle(q, a))) * imag[q]
            odd_part = term if odd_part is None else odd_part + term
        out[a] = even_part - odd_part
        out[A - a] = even_part + odd_part
    return out


def second_kernel(
    lat_rows, table_ref, thick_ref, u_ref, v_ref, tracer_ref, up_ref, down_ref, cutoff_ref, high_ref, low_ref, *refs
):
    *wind_refs, edge_ref, new_wind = refs
    k = pl.program_id(0)
    _, L, rows, width = new_wind.shape
    band = lax.axis_index("lat")
    geo = table_ref[band]
    thick, u, v = thick_ref[0], u_ref[0], v_ref[0]
    thick_s, v_s = up_ref[0, 0], up_ref[1, 0]
    thick_n, thick_nn, u_n, v_n = (down_ref[i, 0] for i in range(4))
    east, north, below = fluxes(geo, thick, u, v, thick_s, v_s, thick_n)
    inverse = geo[0:rows, 2:3]
    new = thick - (east - west_of(east)) - (north - south_of(north, below)) * inverse
    east_n = u_n * jnp.where(u_n > 0, thick_n, east_of(thick_n))
    north_n = v_n * jnp.where(v_n > 0, thick_n, thick_nn) * geo[rows : rows + 1, 1:2]
    new_n = (
        thick_n
        - (east_n - west_of(east_n))
        - (north_n - north[rows - 1 : rows]) * geo[rows : rows + 1, 2:3]
    )
    new_wind[0, k] = u - 0.05 * (east_of(new) - new)
    inside = band * rows + row_ids(new.shape) < lat_rows - 1
    new_wind[1, k] = jnp.where(inside, v - 0.05 * (north_of(new, new_n) - new), 0.0)

    def store_edges(field, level, value):
        edge_ref[field, level, 0:1] = value[0:1]
        edge_ref[field, level, 1:2] = value[rows - 1 : rows]

    store_edges(0, k, new)
    scale = 1.0 / new
    for c in range(tracer_ref.shape[0]):
        change = tracer_change(
            tracer_ref[c, 0], up_ref[2 + c, 0], down_ref[4 + c, 0], thick, u, v, v_s, east, north, below, inverse
        )
        store_edges(3 + c, k, change * scale)

    @pl.when(k == L - 1)
    def _():
        pieces = [
            new_wind[:, :, :, a * LANES : (a + 1) * LANES].reshape(2 * L * rows, LANES) for a in range(width // LANES)
        ]
        cutoff = jnp.broadcast_to(cutoff_ref[...][None], (2 * L, rows, LANES)).reshape(2 * L * rows, LANES)
        for a, piece in enumerate(filter_rows(pieces, cutoff, high_ref, low_ref)):
            piece = piece.reshape(2, L, rows, LANES)
            for f in range(2):
                wind_refs[f][0, :, :, a * LANES : (a + 1) * LANES] = piece[f]
        for f in range(2):
            for level in range(L):
                store_edges(1 + f, level, wind_refs[f][0, level])


def second_step(table, lat_rows, thickness, wind_u, wind_v, tracers, up, down, cutoff):
    L, R, N = thickness.shape
    T = tracers.shape[0]
    high, low = filter_tables(N)
    level = pl.BlockSpec((1, R, N), lambda k: (k, 0, 0))
    some = lambda n, rows: pl.BlockSpec((n, 1, rows, N), lambda k: (0, k, 0, 0))
    whole = lambda shape: pl.BlockSpec(shape, lambda k: (0,) * len(shape))
    return pl.pallas_call(
        functools.partial(second_kernel, lat_rows),
        grid=(L,),
        in_specs=[whole(table.shape), level, level, level, some(T, R), some(2 + T, 1), some(4 + T, 1)]
        + [whole((R, LANES)), whole(high.shape), whole(low.shape)],
        out_specs=[whole((1, L, R, N)), whole((1, L, R, N)), whole((3 + T, L, 2, N))],
        out_shape=[
            jax.ShapeDtypeStruct((1, L, R, N), jnp.float32),
            jax.ShapeDtypeStruct((1, L, R, N), jnp.float32),
            jax.ShapeDtypeStruct((3 + T, L, 2, N), jnp.float32),
        ],
        scratch_shapes=[pltpu.VMEM((2, L, R, N), jnp.float32)],
        compiler_params=params(),
        cost_estimate=cost(12 * 2 * L * R * high.size, 4 * L * R * N * (8 + T)),
        name="second_step",
    )(
        table, thickness, wind_u, wind_v, tracers, up, down,
        jnp.broadcast_to(cutoff[:, None], (R, LANES)), jnp.asarray(high), jnp.asarray(low),
    )


def part_kernel(both_ref, *refs):
    sum_ref, near_ref = refs[-2:]
    rows, width = sum_ref.shape
    _, L, near, _ = near_ref.shape
    sum_ref[...] = jnp.zeros_like(sum_ref)
    for a, at, each in packed_at(rows, L, width):
        lanes = slice(a * LANES, (a + 1) * LANES)
        sum_ref[1 : rows - 1, lanes] = both_ref[at : at + rows - 2]
        for k in range(L):
            near_ref[0, k, :, lanes] = both_ref[each[k] : each[k] + near]


def part(both, shape, wait):
    L, R, N = shape
    return pl.pallas_call(
        part_kernel,
        in_specs=[VMEM] + after(wait),
        out_specs=[VMEM] * 2,
        out_shape=[
            jax.ShapeDtypeStruct((R, N), jnp.float32),
            jax.ShapeDtypeStruct((1, L, len(near_rows(R)[0]), N), jnp.float32),
        ],
        compiler_params=params(),
        cost_estimate=cost(1e11, 1e9),
        name="part",
    )(both, *wait)


def mass_kernel(C, S, *refs):
    other_refs, (base_ref, mass_ref) = refs[: (C - 1) * S], refs[(C - 1) * S :]
    lev = lax.axis_index("lev")
    others_mass, base = None, None
    for s in range(1, C):
        other = functools.reduce(jnp.add, [ref[...] for ref in other_refs[(s - 1) * S : s * S]])
        below = jnp.where(lev >= s, other, 0.0)
        others_mass = other if others_mass is None else others_mass + other
        base = below if base is None else base + below
    base_ref[...] = base
    mass_ref[...] = others_mass


def other_chips(counts, others):
    return pl.pallas_call(
        functools.partial(mass_kernel, *counts),
        in_specs=[VMEM] * len(others),
        out_specs=[VMEM] * 2,
        out_shape=[jax.ShapeDtypeStruct(others[0].shape, jnp.float32)] * 2,
        compiler_params=params(),
        cost_estimate=cost(1, 1),
        name="other_chips",
    )(*others)


def add_weights(weight_ref, sum_ref):
    total = jnp.zeros(weight_ref.shape[1:], jnp.float32)
    for k in range(weight_ref.shape[0]):
        sum_ref[k] = total
        total = total + weight_ref[k]
    sum_ref[weight_ref.shape[0]] = total
    return total


def source_levels(place, counts, thick, others):
    C, S = counts
    lev, sub = place
    spot = [lax.rem(lev - g // S + C, C) * S + lax.rem(sub - g % S + S, S) for g in range(len(thick))]
    group = [functools.reduce(jnp.add, levels) for levels in thick]
    mass = functools.reduce(jnp.add, group)
    base = jnp.zeros_like(mass)
    if others:
        base, mass = others[0], mass + others[1]
    sources = []
    for g, levels in enumerate(thick):
        low = base
        for other in range(len(thick)):
            if other != g:
                low = low + jnp.where(spot[other] < spot[g], group[other], 0.0)
        for m, value in enumerate(levels):
            sources.append((g, m, low, value))
            low = low + value
    return mass, sources


def covered(top, sources):
    return [jnp.minimum(jnp.maximum(top - low, 0.0), value) for _, _, low, value in sources]


def level_of(ref, index):
    return lambda m, at, columns: ref[index, m, at, columns]


def packed_level_of(ref, index, L, rows):
    return lambda m, at, columns: ref[(index * L + m) * rows : (index * L + m + 1) * rows, columns]


def remap_rows(weight_ref, sum_ref, counts, steps, thick_refs, field_refs, other_refs, store):
    C, S = counts
    _, L, R, N = thick_refs[0].shape
    rows = min(R, 8)
    place = lev, sub = lax.axis_index("lev"), lax.axis_index("sub")
    firsts = [(lax.rem(lev + s, C) * S + sub) * L for s in steps]
    weight_sum = add_weights(weight_ref, sum_ref)[0:rows]

    def tile(at, columns):
        thick = [[ref[0, m, at, columns] for m in range(L)] for ref in thick_refs]
        others = [ref[at, columns] for ref in other_refs]
        mass, sources = source_levels(place, counts, thick, others)
        unit = mass / weight_sum
        for index, s in enumerate(steps):
            below = covered(unit * sum_ref[firsts[index], 0:rows], sources)
            for i in range(L):
                upto = covered(unit * sum_ref[firsts[index] + i + 1, 0:rows], sources)
                part = [a - b for a, b in zip(upto, below)]
                below = upto
                target = unit * weight_ref[firsts[index] + i, 0:rows]
                scale = 1.0 / target
                means = []
                for refs in field_refs:
                    terms = [refs[g](m, at, columns) * w for (g, m, _, _), w in zip(sources, part)]
                    means.append(functools.reduce(jnp.add, terms) * scale)
                store(s, i, at, columns, target, means)

    for r in range(0, R, rows):

        def body(c, carry):
            tile(slice(r, r + rows), pl.ds(pl.multiple_of(c * LANES, LANES), LANES))
            return carry

        lax.fori_loop(0, N // LANES, body, 0)


def inner_part(at, margin, rows):
    return max(at.start, margin[0]), min(at.stop, rows - margin[1])


def remap_kernel(counts, steps, fields, margin, with_thickness, sizes, weight_ref, *refs):
    *refs, sum_ref = refs
    C, S = counts
    thick_refs, refs = refs[:S], refs[S:]
    bundles = []
    for _ in range(sizes[0]):
        bundles.append(refs[:S])
        refs = refs[S:]
    other_refs, out_refs = refs[:2], refs[len(refs) - len(steps) - with_thickness :]
    _, L, R, _ = thick_refs[0].shape
    thick_out_ref = out_refs[-1]
    field_refs = [[level_of(ref, index) for ref in bundles[which]] for which, index in fields]

    def store(s, i, at, columns, target, means):
        out_ref = out_refs[steps.index(s)]
        if with_thickness and s == 0:
            thick_out_ref[i, at, columns] = target
        for f, value in enumerate(means):
            if s == 0:
                out_ref[f, i, at, columns] = value
            else:
                lower, upper = inner_part(at, margin, R)
                start = (f * L + i) * (R - sum(margin)) - margin[0]
                out_ref[start + lower : start + upper, columns] = value[lower - at.start : upper - at.start]

    remap_rows(
        weight_ref, sum_ref, counts, steps, thick_refs, field_refs, other_refs, store
    )


def remap_parts(counts, weights, thick, bundles, others, fields, steps, margin, with_thickness=False, wait=()):
    C, S = counts
    _, L, R, N = thick[0].shape
    F = len(fields)
    whole = jax.ShapeDtypeStruct((F, L, R, N), jnp.float32)
    inner = jax.ShapeDtypeStruct((F * L * (R - sum(margin)), N), jnp.float32)
    flat = [a for bundle in bundles for a in bundle]
    out_shape = [whole if s == 0 else inner for s in steps]
    if with_thickness:
        out_shape.append(jax.ShapeDtypeStruct((L, R, N), jnp.float32))
    return pl.pallas_call(
        functools.partial(remap_kernel, counts, tuple(steps), tuple(fields), margin, with_thickness, (len(bundles),)),
        in_specs=[VMEM] * (1 + len(thick) + len(flat) + len(others)) + after(wait),
        out_specs=[VMEM] * len(out_shape),
        out_shape=out_shape,
        scratch_shapes=[pltpu.VMEM((weights.shape[0] + 1, 8, LANES), jnp.float32)],
        compiler_params=params(),
        cost_estimate=cost(len(steps) * S * L * L * R * N * (5 + 2 * F), 4 * R * N * L * (F + 1) * (S + len(steps))),
        name="remap_parts",
    )(weights, *thick, *flat, *others, *wait)


def remap_edge_kernel(counts, weight_ref, *refs):
    *refs, sum_ref = refs
    G = counts[0] * counts[1]
    edge_refs, near_refs, tracer_refs = refs[:G], refs[G : 2 * G], refs[2 * G : 3 * G]
    edge_out_ref, thick_out_ref, near_out_ref = refs[-3:]

    def store_edge(s, i, at, columns, target, means):
        thick_out_ref[i, at, columns] = target
        for f, value in enumerate(means):
            edge_out_ref[f, i, at, columns] = value

    def store_near(s, i, at, columns, target, means):
        for f, value in enumerate(means):
            near_out_ref[f, i, at, columns] = value

    fields = [[level_of(ref, f) for ref in edge_refs] for f in range(1, edge_refs[0].shape[0])]
    remap_rows(weight_ref, sum_ref, counts, (0,), edge_refs, fields, [], store_edge)
    _, L, R, _ = near_refs[0].shape
    fields = [[packed_level_of(ref, f, L, R) for ref in tracer_refs] for f in range(near_out_ref.shape[0])]
    remap_rows(weight_ref, sum_ref, counts, (0,), near_refs, fields, [], store_near)


def remap_edges(counts, weights, edges, near_new, near, wait=()):
    F, L, R, N = edges[0].shape
    T = F - 3
    operands = [*edges, *near_new, *near]
    return pl.pallas_call(
        functools.partial(remap_edge_kernel, counts),
        in_specs=[VMEM] * (1 + len(operands)) + after(wait),
        out_specs=[VMEM] * 3,
        out_shape=[
            jax.ShapeDtypeStruct((F - 1, L, R, N), jnp.float32),
            jax.ShapeDtypeStruct((L, R, N), jnp.float32),
            jax.ShapeDtypeStruct((T, *near_new[0].shape[1:]), jnp.float32),
        ],
        scratch_shapes=[pltpu.VMEM((weights.shape[0] + 1, 8, LANES), jnp.float32)],
        compiler_params=params(),
        cost_estimate=cost(len(edges) * L * L * R * N * 40, 4 * R * N * L * len(operands) * F),
        name="remap_edges",
    )(weights, *operands, *wait)


def finish_kernel(margin, own_ref, near_ref, edge_ref, thick_ref, thick_edge_ref, *refs):
    *arrived_refs, out_ref, thick_out_ref, token_ref = refs
    token_ref[...] = jnp.zeros_like(token_ref)
    T, L, R, _ = out_ref.shape
    thick_out_ref[...] = thick_ref[...]
    for i in range(L):
        for row, j in ((0, 0), (R - 1, 1)):
            thick_out_ref[i, row : row + 1] = thick_edge_ref[i, j : j + 1]
    for f in range(T):
        for i in range(L):
            start, first, end = (f * L + i) * (R - sum(margin)), margin[0], R - margin[1]
            total = own_ref[f, i, first:end]
            for ref in arrived_refs:
                total = total + ref[start : start + end - first]
            out_ref[f, i, first:end] = total
            for row, j in ((0, 0), (R - 1, 1)):
                out_ref[f, i, row : row + 1] = edge_ref[2 + f, i, j : j + 1]
            for j, row in enumerate(near_rows(R)[0]):
                out_ref[f, i, row : row + 1] = near_ref[f, i, j : j + 1]


def finish_tracers(own, near, edge, thick, thick_edge, arrived):
    return pl.pallas_call(
        functools.partial(finish_kernel, near_rows(own.shape[2])[1]),
        in_specs=[VMEM] * (5 + len(arrived)),
        out_specs=[VMEM] * 3,
        out_shape=[
            jax.ShapeDtypeStruct(own.shape, jnp.float32),
            jax.ShapeDtypeStruct(thick.shape, jnp.float32),
            jax.ShapeDtypeStruct((8, LANES), jnp.float32),
        ],
        compiler_params=params(),
        cost_estimate=cost(2 * own.size, 12 * own.size),
        name="finish_tracers",
    )(own, near, edge, thick, thick_edge, *arrived)


def finish_winds_kernel(count, own_ref, edge_ref, *refs):
    arrived_refs, (*out_refs, result_ref, sems) = refs[:count], refs[len(refs) - 4 :]
    _, L, R, N = own_ref.shape
    row = row_ids((R, N))
    copies = []
    for f, out_ref in enumerate(out_refs):
        for i in range(L):
            start = (f * L + i) * (R - 2)
            first = start // 8 * 8
            total = own_ref[f, i]
            for ref in arrived_refs:
                size = min(R + 8, ref.shape[0] - first)
                total = total + pltpu.roll(ref[first : first + size], (1 - (start - first)) % size, 0)[0:R]
            total = jnp.where(row == 0, edge_ref[f, i, 0:1], jnp.where(row == R - 1, edge_ref[f, i, 1:2], total))
            result_ref[f, i] = total
        copies.append(pltpu.make_async_copy(result_ref.at[f], out_ref, sems.at[f]))
        copies[-1].start()
    for copy in copies:
        copy.wait()


def finish_winds(own, arrived, edge, wait):
    F = own.shape[0]
    return pl.pallas_call(
        functools.partial(finish_winds_kernel, len(arrived)),
        in_specs=[VMEM] * (2 + len(arrived)) + after(wait),
        out_specs=[pl.BlockSpec(memory_space=pl.ANY)] * F,
        out_shape=[jax.ShapeDtypeStruct(own.shape[1:], jnp.float32)] * F,
        scratch_shapes=[pltpu.VMEM(own.shape, jnp.float32), pltpu.SemaphoreType.DMA((F,))],
        compiler_params=params(),
        cost_estimate=cost(own.size, 12 * own.size),
        name="finish_winds",
    )(own, edge, *arrived, *wait)


def edge_kernel(thick_any, u_any, v_any, tracer_any, *refs):
    last_ref, leading_ref, top_ref, low_ref, tracer_ref, sems = refs[-6:]
    T, L, R, _ = tracer_any.shape
    top = pl.ds(R - 8, 8)
    copies = [
        pltpu.make_async_copy(thick_any.at[:, top], top_ref.at[0], sems.at[0]),
        pltpu.make_async_copy(v_any.at[:, top], top_ref.at[1], sems.at[1]),
        pltpu.make_async_copy(thick_any.at[:, pl.ds(0, 8)], low_ref.at[0], sems.at[2]),
        pltpu.make_async_copy(u_any.at[:, pl.ds(0, 8)], low_ref.at[1], sems.at[3]),
        pltpu.make_async_copy(v_any.at[:, pl.ds(0, 8)], low_ref.at[2], sems.at[4]),
        pltpu.make_async_copy(tracer_any.at[:, :, top], tracer_ref.at[0], sems.at[5]),
        pltpu.make_async_copy(tracer_any.at[:, :, pl.ds(0, 8)], tracer_ref.at[1], sems.at[6]),
    ]
    for copy in copies:
        copy.start()
    for copy in copies:
        copy.wait()
    last_ref[0:2] = top_ref[:, :, 7:8]
    last_ref[2 : 2 + T] = tracer_ref[0, :, :, 7:8]
    leading_ref[0] = low_ref[0, :, 0:1]
    leading_ref[1] = low_ref[0, :, 1:2]
    leading_ref[2:4] = low_ref[1:3, :, 0:1]
    leading_ref[4 : 4 + T] = tracer_ref[1, :, :, 0:1]


def edge_rows(thickness, wind_u, wind_v, tracers, wait):
    L, R, N = thickness.shape
    T = tracers.shape[0]
    operands = [thickness, wind_u, wind_v, tracers]
    return pl.pallas_call(
        edge_kernel,
        in_specs=after(operands) + after(wait),
        out_specs=[VMEM] * 2,
        out_shape=[
            jax.ShapeDtypeStruct((2 + T, L, 1, N), jnp.float32),
            jax.ShapeDtypeStruct((4 + T, L, 1, N), jnp.float32),
        ],
        scratch_shapes=[
            pltpu.VMEM((2, L, 8, N), jnp.float32),
            pltpu.VMEM((3, L, 8, N), jnp.float32),
            pltpu.VMEM((2, T, L, 8, N), jnp.float32),
            pltpu.SemaphoreType.DMA((7,)),
        ],
        compiler_params=params(),
        cost_estimate=cost(1e10, 1e9),
        name="edge_rows",
    )(*operands, *wait)


def shifted(value, lev_count, sub_count, s, t):
    if t == 0:
        return lax.ppermute(value, "lev", [(i, (i + s) % lev_count) for i in range(lev_count)])
    if s == 0:
        return lax.ppermute(value, "sub", [(i, (i + t) % sub_count) for i in range(sub_count)])
    pairs = [
        (i * sub_count + j, (i + s) % lev_count * sub_count + (j + t) % sub_count)
        for i in range(lev_count)
        for j in range(sub_count)
    ]
    return lax.ppermute(value, ("lev", "sub"), pairs)


def per_device(thickness, wind_u, wind_v, tracers, level_weights, cutoff):
    L, R, N = thickness.shape
    lat_count = lax.axis_size("lat")
    C, S = lax.axis_size("lev"), lax.axis_size("sub")
    lat_rows = R * lat_count
    send = functools.partial(shifted, lev_count=C, sub_count=S)

    T = tracers.shape[0]
    northward = [(i, i + 1) for i in range(lat_count - 1)]
    southward = [(j, i) for i, j in northward]
    table = jnp.asarray(geometry_table(lat_rows, R))
    weights = jnp.broadcast_to(level_weights[:, None, None], (level_weights.shape[0], 8, LANES))
    away = range(1, C)

    def with_others_of_chip(own):
        return [own] + [send(own, s=0, t=t) for t in range(1, S)]

    def sent(parts):
        return [send(part, s=s, t=0) for s, part in zip(away, parts)]

    remap = functools.partial(remap_parts, (C, S), weights)

    new, both, near_new, east, north, *arguments = first_step(table, thickness, wind_u, wind_v, tracers)
    both = [send(both, s=s, t=0) for s in away]
    inner, near = inner_step(table, new, east, north, *arguments)
    group = with_others_of_chip(inner)
    near = [near] + [send(near, s=s, t=0) for s in away]
    parted = [part(each, (L, R, N), [near[0]]) for each in both]
    near_new = [near_new] + [each[1] for each in parted]
    others = other_chips((C, S), [a for each in parted for a in with_others_of_chip(each[0])])
    tracer_fields = [(0, 1 + c) for c in range(T)]
    away_parts = remap(group, [group], others, tracer_fields, away, near_rows(R)[1])
    arrived = sent(away_parts)

    last, leading = edge_rows(
        *arguments, [away_parts[0], *near[1:2]]
    )
    up = lax.ppermute(last, "lat", northward)
    down = lax.ppermute(leading, "lat", southward)
    u, v, edge = second_step(table, lat_rows, *arguments, up, down, cutoff)
    edges = [edge] + [send(edge, s=s, t=0) for s in away]
    winds = [with_others_of_chip(u), with_others_of_chip(v)]
    tracers_own, thick_inner = remap(group, [group], others, tracer_fields, (0,), (0, 0), with_thickness=True, wait=[edge])
    winds_own, *winds_away = remap(
        group, winds, others, [(0, 0), (1, 0)], range(C), (1, 1), wait=[tracers_own, *arrived[:1]]
    )
    winds_arrived = sent(winds_away)
    near_new, near, edges = (
        [a for own in sources for a in with_others_of_chip(own)] for sources in (near_new, near, edges)
    )
    edge_out, thick_edge, near_out = remap_edges(
        (C, S), weights, edges, near_new, near, wait=winds_away[:1]
    )

    tracers_out, thickness_out, token = finish_tracers(
        tracers_own, near_out, edge_out, thick_inner, thick_edge, arrived
    )
    u_out, v_out = finish_winds(winds_own, winds_arrived, edge_out, [token])
    return thickness_out, u_out, v_out, tracers_out


def solution(mesh):
    placed = (
        P(("member", "lev", "sub"), "lat", None),
        P(("member", "lev", "sub"), "lat", None),
        P(("member", "lev", "sub"), "lat", None),
        P("member", ("lev", "sub"), "lat", None),
        P(),
        P("lat"),
    )
    return jax.shard_map(
        per_device,
        mesh=mesh,
        in_specs=placed,
        out_specs=(
            P(("member", "lev", "sub"), "lat", None),
            P(("member", "lev", "sub"), "lat", None),
            P(("member", "lev", "sub"), "lat", None),
            P("member", ("lev", "sub"), "lat", None),
        ),
        check_vma=False,
    )
```
